32 devices in a mesh: ctx: 8 (over z, x), exp: 4 (over y, core).
Axes of the slice: x: 2, y: 2, z: 4, core: 2. Of those that a mesh axis runs over, the one named last changes fastest.
Arguments:
- seq_input: bfloat16 [2048, 4096], P('ctx', 'exp'), may hold values from -6 to 6
- b_input: bfloat16 [2048, 128], P('ctx'), may hold values from -6 to 6
- c_input: bfloat16 [2048, 128], P('ctx'), may hold values from -6 to 6
- conv_x: float32 [4, 4096], P(None, 'exp'), may hold values from -3 to 3
- conv_bc: float32 [4, 256], replicated, may hold values from -3 to 3
- log_decay: float32 [64, 2048], P('exp', 'ctx'), may hold values from -1 to 0, as said below
- skip_gain: float32 [64], P('exp'), may hold values from 0.5 to 8
- norm_gain: float32 [4096], P('exp'), may hold values from 0.1 to 1.9
- moe_input: bfloat16 [512, 4096], P('ctx', 'exp'), may hold values from -6 to 6
- expert_ids: int32 [512, 2], P('ctx'), may hold values from 0 to 3, all different within a row; in each aligned block of 64 rows (0 to 63, 64 to 127, ...) at most 64 rows name the same one
- w_gate: bfloat16 [4, 4096, 8192], P('exp', None, 'ctx'), may hold values from -0.09375 to 0.09375
- w_up: bfloat16 [4, 4096, 8192], P('exp', None, 'ctx'), may hold values from -0.09375 to 0.09375
Outputs:
- mixed: bfloat16 [2048, 4096], P('ctx', 'exp')
- expert_hidden: bfloat16 [4, 512, 8192], P('exp', None, 'ctx')
The draws below stay inside these ranges and needn't reach their ends.
Inputs may be any that keep to these rules, and one draw needn't show every extreme that they name: `log_decay`: every entry is negative. `expert_ids`: a row names two different experts; in each aligned block of 64 rows no expert is named by more than 64 rows.
All inputs are finite; a program needn't handle non-finite values.
Results may differ from the reference program's by a relative error of at most 0.001.
Values may be sent and summed in bfloat16 or wider, within the bound.
No kernel may reach another device: no remote copies, remote signals or barrier semaphores. Data moves between devices by JAX's collectives and lax.ppermute only.
A program may use at most 64 MiB of HBM per device.

```python
import math
import jax
import jax.numpy as jnp
import numpy as np
from jax import lax

D = 4096
FF = 8192
HEADS = 64
HDIM = 64
STATE = 128
KCONV = 4
BLOCK = 256
TOK_DEV = 256
MTOK_CTX = 64
EXPERTS = 4
CAP = 64
SEQ = 2048
MTOKENS = 512
CH = 4096
N_CTX = 8


def draw_log_decay(key, part):
    key = jax.random.fold_in(key, 11)
    keys = jax.random.split(key, 7)
    fast_share = 0.5
    is_fast = jax.random.uniform(keys[0], (HEADS,)) < fast_share
    fast_rate = jax.random.uniform(keys[1], (HEADS,), jnp.float32, 1.0 / 50.0, 1.0 / 30.0)
    slow_rate = jnp.exp(jax.random.uniform(keys[2], (HEADS,), jnp.float32, jnp.log(0.3), 0.0)) / SEQ
    decay_speed = jnp.where(is_fast, fast_rate, slow_rate)
    approximate_value = jax.random.uniform(keys[3], (HEADS, SEQ), jnp.float32, 0.5, 1.5)
    block_tiling = jax.random.uniform(keys[4], (HEADS, SEQ // TOK_DEV), jnp.float32, 0.5, 1.5)
    block_tiling = jnp.repeat(block_tiling, TOK_DEV, axis=1)
    slot_positions = jax.random.randint(keys[5], (3,), 0, SEQ)
    layer_depth_count = jax.random.uniform(keys[6], (3,), jnp.float32, 0.22, 0.69)
    expert_locations = jnp.arange(SEQ, dtype=jnp.int32)
    token_group_span = jnp.sum((expert_locations[None, :] == slot_positions[:, None]).astype(jnp.float32) * layer_depth_count[:, None], axis=0)
    return -(decay_speed[:, None] * approximate_value * block_tiling + token_group_span[None, :])


def shard_levels(key, extent, cuts, smallest, high):
    def one(dim, parts):
        heights = jax.random.uniform(jax.random.fold_in(jax.random.fold_in(key, 6), dim), (parts,), jnp.float32, smallest / len(cuts), high / len(cuts))
        return jnp.repeat(jnp.exp(heights), extent[dim] // parts).reshape((-1,) + (1,) * (len(extent) - dim - 1))

    loudness = one(*cuts[0])
    for cut in cuts[1:]:
        loudness = loudness * one(*cut)
    return loudness


def routed_block(own_key, own, number, rows, number_of, top, reach, lean):
    ranking = jax.random.permutation(own_key, number_of)
    heavy_load, common = shares(number_of, rows * top, reach, lean, True), shares(number_of, rows * top, reach, lean, False)
    places = jnp.arange(number_of)

    def named(lengths, offset_by):
        used = int((lengths > 0).sum())
        fixed = max(1, used // 4)
        moved = fixed + (places - fixed + offset_by * (used - fixed)) % max(1, number_of - fixed)
        return jnp.zeros((number_of,), jnp.int32).at[ranking[jnp.where(places < fixed, places, moved)]].set(jnp.asarray(lengths, jnp.int32))

    lengths = jnp.where(number % 4 == 0, named(heavy_load, number // 4), named(common, number - number // 4 - 1))
    mixed = jax.random.permutation(jax.random.fold_in(own, 3), number_of)
    source_of, taker = mixed[0:number_of // 2 * 2:2], mixed[1:number_of // 2 * 2:2]
    margin = jnp.minimum(lengths[source_of] - 1, reach - lengths[taker]) // 2
    margin = jnp.where((source_of == ranking[0]) | (taker == ranking[0]) | (lengths[taker] == 0), 0, jnp.maximum(margin, 0))
    moved = jax.random.randint(jax.random.fold_in(own, 4), (number_of // 2,), 0, 1 << 20) % (margin + 1)
    lengths = lengths.at[source_of].add(-moved).at[taker].add(moved)
    items = jnp.searchsorted(jnp.cumsum(lengths), jnp.arange(rows * top), side="right").astype(jnp.int32)
    grid = items.reshape(top, rows).T
    grid = grid[jax.random.permutation(jax.random.fold_in(own, 1), rows)]
    offset_by = jax.random.randint(jax.random.fold_in(own, 2), (rows, 1), 0, top)
    return jnp.take_along_axis(grid, (jnp.arange(top)[None, :] + offset_by) % top, axis=1)


def shares(amount, total, most, slope, full):
    weights = [(1 << 20) // math.isqrt(rank ** slope) + 1 for rank in range(1, amount + 1)]
    largest = most if full else min(most, max(-(-total // amount), total * weights[0] // sum(weights)))
    least = 1 if total - largest >= amount - 1 else 0
    counts, surplus = [largest] + [least] * (amount - 1), total - largest - least * (amount - 1)
    while surplus > 0:
        free = [i for i in range(1, amount) if counts[i] < largest] or [i for i in range(1, amount) if counts[i] < most]
        whole, remaining = sum([weights[i] for i in free]), surplus
        for i in free:
            more = min(most - counts[i], max(1, remaining * weights[i] // whole), surplus)
            counts[i] = counts[i] + more
            surplus = surplus - more
    return np.array(counts)


def bell_draw(stream_key, extent, spread, most, cuts=(), held_as=jnp.bfloat16):
    level = shard_levels(stream_key, extent, cuts, -0.22, 0.18) if cuts else 1.0
    drawn = jax.random.normal(stream_key, extent, jnp.float32) * spread * level
    return jnp.minimum(jnp.maximum(drawn, -most), most).astype(held_as)


def setup_inputs(seed: int = 0) -> dict:
    seeds = jax.random.split(jax.random.key(seed), 13)
    seq_input = bell_draw(seeds[0], (SEQ, CH), 1.0, 6.0, ((0, 8), (1, 4)))
    b_input = bell_draw(seeds[1], (SEQ, STATE), 1.0, 6.0, ((0, 8),))
    c_input = bell_draw(seeds[2], (SEQ, STATE), 1.0, 6.0, ((0, 8),))
    conv_x = bell_draw(seeds[3], (KCONV, CH), KCONV ** -0.5, 3.0, ((1, 4),), jnp.float32)
    conv_bc = bell_draw(seeds[4], (KCONV, 2 * STATE), KCONV ** -0.5, 3.0, (), jnp.float32)
    log_decay = draw_log_decay(jax.random.fold_in(seeds[12], 71), 0)
    skip_gain = jnp.clip(jnp.exp(math.log(8.0) - 2.7725887 * jax.random.uniform(seeds[6], (HEADS,), jnp.float32) ** shard_levels(seeds[6], (HEADS,), ((0, 4),), -0.2, 0.2)), 0.5, 8.0)
    norm_gain = jnp.clip(1.0 + 0.18 * jax.random.normal(seeds[7], (CH,), jnp.float32), 0.1, 1.9)
    moe_input = bell_draw(seeds[8], (MTOKENS, D), 1.0, 6.0, ((0, 8), (1, 4)))
    expert_ids_keys = jax.random.split(jax.random.fold_in(seeds[9], 1), MTOKENS // MTOK_CTX)
    expert_ids_turns = jax.random.permutation(jax.random.fold_in(seeds[9], 3), MTOKENS // MTOK_CTX)
    expert_ids = jax.vmap(lambda own, number: routed_block(jax.random.fold_in(seeds[9], 2), own, number, MTOK_CTX, EXPERTS, 2, CAP, 2))(expert_ids_keys, expert_ids_turns).reshape((MTOKENS, 2))
    w_gate = bell_draw(seeds[10], (EXPERTS, D, FF), D ** -0.5, 0.09375, ((0, 4), (2, 8)))
    w_up = bell_draw(seeds[11], (EXPERTS, D, FF), D ** -0.5, 0.09375, ((0, 4), (2, 8)))
    return dict(seq_input=seq_input, b_input=b_input, c_input=c_input, conv_x=conv_x, conv_bc=conv_bc, log_decay=log_decay, skip_gain=skip_gain, norm_gain=norm_gain, moe_input=moe_input, expert_ids=expert_ids, w_gate=w_gate, w_up=w_up)


HIGH = lax.Precision.HIGHEST

def causal_conv(padded, weights):
    length = padded.shape[0] - weights.shape[0] + 1
    total = jnp.zeros((length, padded.shape[1]), jnp.float32)
    for offset in range(weights.shape[0]):
        total = total + weights[offset][None, :].astype(jnp.float32) * padded[offset:offset + length].astype(jnp.float32)
    return jax.nn.silu(total)

def ssd_block(carry, pieces):
    drive, bmat, cmat, logs = pieces
    within = jnp.cumsum(logs, axis=1)
    length = logs.shape[1]
    lower = jnp.tril(jnp.ones((length, length), dtype=bool))[None]
    gaps = within[:, :, None] - within[:, None, :]
    decay = jnp.where(lower, jnp.exp(jnp.where(lower, gaps, 0.0)), 0.0)
    intersection = jnp.dot(cmat, bmat.T, precision=HIGH, preferred_element_type=jnp.float32)
    inner = jnp.einsum('hts,shp->thp', decay * intersection[None], drive, precision=HIGH)
    carried = jnp.einsum('tn,hpn->thp', cmat, carry, precision=HIGH) * jnp.exp(within).T[:, :, None]
    remain = jnp.exp(within[:, -1:] - within)
    fresh = jnp.einsum('thp,tn->hpn', drive * remain.T[:, :, None], bmat, precision=HIGH)
    updated = jnp.exp(within[:, -1])[:, None, None] * carry + fresh
    return (updated, inner + carried)

def expert_step(triple):
    rows, gate_w, up_w = triple
    gate = jnp.dot(rows, gate_w, preferred_element_type=jnp.float32)
    upper = jnp.dot(rows, up_w, preferred_element_type=jnp.float32)
    return (jax.nn.silu(gate) * upper).astype(jnp.bfloat16)

def reference(seq_input, b_input, c_input, conv_x, conv_bc, log_decay, skip_gain, norm_gain, moe_input, expert_ids, w_gate, w_up):
    rim = KCONV - 1
    xpad = jnp.concatenate([jnp.zeros((rim, CH), seq_input.dtype), seq_input], 0)
    xconv = causal_conv(xpad, conv_x)
    both = jnp.concatenate([b_input, c_input], 1)
    bpad = jnp.concatenate([jnp.zeros((rim, 2 * STATE), both.dtype), both], 0)
    bc = causal_conv(bpad, conv_bc)
    bconv = bc[:, :STATE]
    cconv = bc[:, STATE:]
    xheads = xconv.reshape(SEQ, HEADS, HDIM)
    inflow = jnp.sqrt(-jnp.expm1(2.0 * log_decay))
    drive = xheads * inflow.T[:, :, None]
    count = SEQ // BLOCK
    logs = log_decay.reshape(HEADS, count, BLOCK).transpose(1, 0, 2)
    start = jnp.zeros((HEADS, HDIM, STATE), jnp.float32)
    final, outputs = lax.scan(ssd_block, start, (drive.reshape(count, BLOCK, HEADS, HDIM), bconv.reshape(count, BLOCK, STATE), cconv.reshape(count, BLOCK, STATE), logs))
    pre = outputs.reshape(SEQ, HEADS, HDIM) + skip_gain[None, :, None] * xheads
    scale = lax.rsqrt(lax.optimization_barrier(jnp.mean(pre * pre, axis=2, keepdims=True)) + 1e-05)
    mixed = (pre * scale * norm_gain.reshape(HEADS, HDIM)[None]).reshape(SEQ, CH).astype(jnp.bfloat16)
    pairs = expert_ids.reshape(N_CTX, MTOK_CTX * 2)
    onehot = (pairs[:, :, None] == jnp.arange(EXPERTS, dtype=jnp.int32)[None, None, :]).astype(jnp.int32)
    before = jnp.cumsum(onehot, axis=1) - onehot
    position = lax.optimization_barrier(jnp.sum(before * onehot, axis=2))
    pos_hot = (position[:, :, None] == jnp.arange(CAP, dtype=jnp.int32)[None, None, :]).astype(jnp.float32)
    tok_hot = ((jnp.arange(2 * MTOK_CTX, dtype=jnp.int32) // 2)[:, None] == jnp.arange(MTOK_CTX, dtype=jnp.int32)[None, :]).astype(jnp.float32)
    dispatch = jnp.einsum('cae,caq,at->ceqt', onehot.astype(jnp.float32), pos_hot, tok_hot)
    blocks_in = moe_input.reshape(N_CTX, MTOK_CTX, D).astype(jnp.float32)
    rows = jnp.einsum('ceqt,ctd->ecqd', dispatch, blocks_in).astype(jnp.bfloat16).reshape(EXPERTS, N_CTX * CAP, D)
    expert_hidden = lax.map(expert_step, (rows, w_gate, w_up))
    return (mixed, expert_hidden)
```

```python
import jax
import jax.numpy as jnp
from jax import lax
from jax.sharding import PartitionSpec as P

HDIM = 64
STATE = 128
KCONV = 4

HIGH = lax.Precision.HIGHEST


def passed_along(block, axis, distance):
    devices = range(lax.axis_size(axis))
    route = [(i - distance, i) for i in devices if i - distance in devices]
    return lax.ppermute(block, axis, route)


def swapped(block, bit):
    return lax.ppermute(block, "exp", [(i, i ^ bit) for i in range(lax.axis_size("exp"))])


def causal_conv(padded, weights):
    length = padded.shape[0] - weights.shape[0] + 1
    total = jnp.zeros((length, padded.shape[1]), jnp.float32)
    for offset in range(weights.shape[0]):
        total = total + weights[offset][None, :] * padded[offset : offset + length].astype(
            jnp.float32
        )
    return jax.nn.silu(total)


def slot_matrix(pairs, expert, capacity):
    tokens = pairs.shape[0]
    named = jnp.any(pairs == expert, axis=1).astype(jnp.int32)
    position = jnp.cumsum(named) - named
    hit = (position[None, :] == jnp.arange(capacity, dtype=jnp.int32)[:, None]) & (
        named[None, :] > 0
    )
    return hit.astype(jnp.bfloat16)


def three_parts(value):
    high = lax.reduce_precision(value, 8, 7)
    rest = value - high
    middle = lax.reduce_precision(rest, 8, 7)
    low = rest - middle
    return jnp.stack([high, middle, low]).astype(jnp.bfloat16)


def experts_by_tokens(tokens, pairs, w_gate, w_up):
    blocks, rows, columns = tokens.shape
    me = lax.axis_index("exp")
    own = tokens.reshape(blocks * rows, columns)
    across = swapped(own, 2)
    beside = swapped(own, 1)
    corner = swapped(across, 1)
    whole = jnp.zeros((4,) + own.shape, own.dtype)
    for bit, piece in enumerate((own, beside, across, corner)):
        whole = lax.dynamic_update_slice(whole, piece[None], (me ^ bit, 0, 0))
    whole = whole.transpose(1, 0, 2).reshape(blocks * rows, 4 * columns)
    gate = jnp.dot(whole, w_gate[0], preferred_element_type=jnp.float32)
    upper = jnp.dot(whole, w_up[0], preferred_element_type=jnp.float32)
    hidden = (jax.nn.silu(gate) * upper).astype(jnp.bfloat16)
    pick = jax.vmap(lambda p: slot_matrix(p, me, rows))(pairs)
    slots = jnp.einsum(
        "bqt,btf->bqf",
        pick,
        hidden.reshape(blocks, rows, -1),
        preferred_element_type=jnp.float32,
    )
    return slots.astype(jnp.bfloat16).reshape(1, blocks * rows, -1)


def experts_by_slots(moe_input, pairs, w_gate, w_up):
    experts = lax.axis_size("exp")
    tokens, columns = moe_input.shape
    capacity = 4 * tokens // experts
    pick = jax.vmap(lambda e: slot_matrix(pairs, e, capacity))(jnp.arange(experts))
    slots = jnp.einsum("eqt,td->eqd", pick, moe_input, preferred_element_type=jnp.float32)
    routed = lax.all_to_all(
        slots.astype(jnp.bfloat16), "exp", split_axis=0, concat_axis=2, tiled=True
    )
    rows = lax.all_gather(routed[0], "ctx", axis=0, tiled=True)
    gate = jnp.dot(rows, w_gate[0], preferred_element_type=jnp.float32)
    upper = jnp.dot(rows, w_up[0], preferred_element_type=jnp.float32)
    return (jax.nn.silu(gate) * upper).astype(jnp.bfloat16)[None]


def on_device(
    seq_input,
    b_input,
    c_input,
    conv_x,
    conv_bc,
    log_decay,
    skip_gain,
    norm_gain,
    moe_input,
    expert_ids,
    w_gate,
    w_up,
):
    rim = KCONV - 1
    tokens, channels = seq_input.shape
    heads = skip_gain.shape[0]
    ctx = lax.axis_size("ctx")
    me = lax.axis_index("ctx")
    rows = moe_input.shape[0]
    by_tokens = lax.axis_size("exp") == 4

    extra = jnp.zeros((8, moe_input.shape[1]), jnp.bfloat16)
    extra = extra.at[0, : 2 * rows].set(expert_ids.reshape(-1).astype(jnp.bfloat16))
    extra = extra.at[1:4, :heads].set(three_parts(jnp.sum(log_decay, axis=1)))
    sent = jnp.concatenate([moe_input, extra], 0) if by_tokens else extra
    gathered = lax.all_gather(sent, "ctx", axis=0)
    lines = gathered[:, -8:]
    sums = jnp.sum(lines[:, 1:4, :heads].astype(jnp.float32), axis=1)

    ends = jnp.concatenate([a[tokens - rim :] for a in (seq_input, b_input, c_input)], 1)
    before = passed_along(ends, "ctx", 1)
    xconv = causal_conv(jnp.concatenate([before[:, :channels], seq_input], 0), conv_x)
    both = jnp.concatenate([before[:, channels:], jnp.concatenate([b_input, c_input], 1)], 0)
    bc = causal_conv(both, conv_bc)
    bconv = bc[:, :STATE]
    cconv = bc[:, STATE:]
    xheads = xconv.reshape(tokens, heads, HDIM)
    drive = xheads * jnp.sqrt(-jnp.expm1(2.0 * log_decay)).T[:, :, None]
    within = jnp.cumsum(log_decay, axis=1)
    remain = jnp.exp(within[:, -1:] - within)
    final = jnp.einsum("thp,tn->hpn", drive * remain.T[:, :, None], bconv, precision=HIGH)

    share = heads * HDIM // ctx
    parts = lax.all_to_all(
        final.reshape(ctx, share, STATE), "ctx", split_axis=0, concat_axis=0, tiled=True
    )
    through = jnp.repeat(jnp.exp(sums), HDIM, axis=1)
    through = lax.dynamic_slice(through, (0, me * share), (ctx, share))
    state = jnp.zeros_like(parts[0])
    starts = [state]
    for i in range(ctx - 1):
        state = through[i][:, None] * state + parts[i]
        starts.append(state)
    incoming = lax.all_to_all(
        jnp.stack(starts), "ctx", split_axis=0, concat_axis=0, tiled=True
    ).reshape(heads, HDIM, STATE)

    lower = jnp.tril(jnp.ones((tokens, tokens), dtype=bool))[None]
    gaps = within[:, :, None] - within[:, None, :]
    decay = jnp.where(lower, jnp.exp(jnp.where(lower, gaps, 0.0)), 0.0)
    meet = jnp.dot(cconv, bconv.T, precision=HIGH, preferred_element_type=jnp.float32)
    inner = jnp.einsum("hts,shp->thp", decay * meet[None], drive, precision=HIGH)
    carried = jnp.einsum("tn,hpn->thp", cconv, incoming, precision=HIGH)
    carried = carried * jnp.exp(within).T[:, :, None]
    pre = inner + carried + skip_gain[None, :, None] * xheads
    scale = lax.rsqrt(jnp.mean(pre * pre, axis=2, keepdims=True) + 1e-05)
    mixed = (
        (pre * scale * norm_gain.reshape(heads, HDIM)[None])
        .reshape(tokens, channels)
        .astype(jnp.bfloat16)
    )

    if by_tokens:
        pairs = lines[:, 0, : 2 * rows].astype(jnp.int32).reshape(ctx, rows, 2)
        hidden = experts_by_tokens(gathered[:, :rows], pairs, w_gate, w_up)
    else:
        hidden = experts_by_slots(moe_input, expert_ids, w_gate, w_up)
    return (mixed, hidden)


def solution(mesh):
    in_specs = (
        P("ctx", "exp"),
        P("ctx", None),
        P("ctx", None),
        P(None, "exp"),
        P(),
        P("exp", "ctx"),
        P("exp"),
        P("exp"),
        P("ctx", "exp"),
        P("ctx", None),
        P("exp", None, "ctx"),
        P("exp", None, "ctx"),
    )
    out_specs = (P("ctx", "exp"), P("exp", None, "ctx"))
    return jax.shard_map(
        on_device, mesh=mesh, in_specs=in_specs, out_specs=out_specs, check_vma=False
    )
```

```python
import functools

import jax
import jax.numpy as jnp
from jax import lax
from jax.experimental import pallas as pl
from jax.experimental.pallas import tpu as pltpu
from jax.sharding import PartitionSpec as P

HDIM = 64
STATE = 128
KCONV = 4
EDGE = 16
NOTES = 8

HIGH = lax.Precision.HIGHEST
F32 = jnp.float32
BF16 = jnp.bfloat16


def dot(a, b, contract=((1,), (0,))):
    return lax.dot_general(a, b, (contract, ((), ())), precision=HIGH, preferred_element_type=F32)


def dot16(a, b, contract=((1,), (0,))):
    return lax.dot_general(a, b, (contract, ((), ())), preferred_element_type=F32)


def halves(value):
    high = value.astype(BF16)
    return high, (value - high.astype(F32)).astype(BF16)


def iota(shape, axis):
    return lax.broadcasted_iota(jnp.int32, shape, axis)


def head_spread(heads):
    shape = (heads, heads * HDIM)
    return (iota(shape, 1) // HDIM == iota(shape, 0)).astype(F32)


def upper_ones(length):
    return (iota((length, length), 0) <= iota((length, length), 1)).astype(F32)


def silu(value):
    return value / (1.0 + jnp.exp(-value))


def full(shape):
    return pl.BlockSpec(shape, lambda *_: (0,) * len(shape))


def call(body, outs, args, specs=None, scratch=(), flops=0, name=None):
    moved = sum(a.size * a.dtype.itemsize for a in (*args, *outs))
    return pl.pallas_call(
        body,
        out_shape=outs,
        grid=(1,),
        in_specs=specs or [full(a.shape) for a in args],
        out_specs=[full(o.shape) for o in outs],
        scratch_shapes=list(scratch),
        compiler_params=pltpu.CompilerParams(vmem_limit_bytes=32 * 2**20),
        cost_estimate=pl.CostEstimate(flops=flops, bytes_accessed=moved, transcendentals=0),
        name=name,
    )(*args)


def pack_body(x_ref, b_ref, c_ref, moe_ref, ends_ref, copies_ref):
    channels = x_ref.shape[1]
    ends_ref[:, :channels] = x_ref[...]
    ends_ref[:, channels : channels + STATE] = b_ref[...]
    ends_ref[:, channels + STATE :] = c_ref[...]
    for i in range(copies_ref.shape[0]):
        copies_ref[i] = moe_ref[...]


def pack(seq_input, b_input, c_input, moe_input, copies):
    tokens, channels = seq_input.shape
    last = tokens // EDGE - 1
    args = (seq_input, b_input, c_input, moe_input)
    specs = [pl.BlockSpec((EDGE, a.shape[1]), lambda *_: (last, 0)) for a in args[:3]]
    specs.append(full(moe_input.shape))
    outs = [
        jax.ShapeDtypeStruct((EDGE, channels + 2 * STATE), BF16),
        jax.ShapeDtypeStruct((copies,) + moe_input.shape, BF16),
    ]
    return call(pack_body, outs, args, specs, name="pack")


def front_body(
    by_tokens,
    x_ref,
    b_ref,
    c_ref,
    ends_ref,
    taps_ref,
    taps_bc_ref,
    logs_ref,
    inflow_ref,
    skip_ref,
    ids_ref,
    drive_ref,
    direct_ref,
    bc_ref,
    slab_ref,
    pad_ref,
):
    tokens, channels = x_ref.shape
    heads = logs_ref.shape[0]
    pad_ref[0:8, :] = ends_ref[...].astype(F32)[EDGE - 8 : EDGE]
    pad_ref[8 : 8 + tokens, :channels] = x_ref[...].astype(F32)
    pad_ref[8 : 8 + tokens, channels : channels + STATE] = b_ref[...].astype(F32)
    pad_ref[8 : 8 + tokens, channels + STATE :] = c_ref[...].astype(F32)

    def conv(taps, start, stop):
        total = jnp.zeros((tokens, stop - start), F32)
        for k in range(KCONV):
            first = 8 - (KCONV - 1) + k
            total = total + taps[k : k + 1] * pad_ref[first : first + tokens, start:stop]
        return silu(total)

    bc = conv(taps_bc_ref[...], channels, channels + 2 * STATE)
    bc_ref[...] = bc
    bmat = bc[:, :STATE]

    logs = logs_ref[...]
    inflow = inflow_ref[...]
    within = dot(logs, upper_ones(tokens))
    total = within[:, tokens - 1 :]
    remain = jnp.exp(total - within)
    spread = head_spread(heads)
    xconv = conv(taps_ref[...], 0, channels)
    first = ((0,), (0,))
    drive_ref[...] = xconv * dot(inflow, spread, first)
    direct_ref[...] = xconv * dot(skip_ref[...], spread)
    state = dot(bmat, xconv * dot(inflow * remain, spread, first), first)
    notes = dot(jnp.exp(jnp.broadcast_to(total, (heads, NOTES))), spread, first)
    if not by_tokens:
        slab_ref[:STATE] = state
        slab_ref[STATE:] = notes
        return
    parts, _, share = slab_ref.shape
    ids = ids_ref[...].astype(F32)
    rows = ids.shape[0]
    shape = (rows, 2 * rows)
    column = jnp.where(iota(shape, 1) < rows, ids[:, 0:1], ids[:, 1:2])
    column = jnp.where(iota(shape, 1) % rows == iota(shape, 0), column, 0.0)
    line = jnp.sum(column, axis=0, keepdims=True)
    for i in range(parts):
        cut = slice(i * share, (i + 1) * share)
        slab_ref[i, :STATE] = state[:, cut]
        slab_ref[i, STATE:] = jnp.where(iota((NOTES, share), 0) == 1, line, notes[:, cut])


def inner_body(drive_ref, direct_ref, bc_ref, logs_ref, pre_ref):
    tokens = drive_ref.shape[0]
    heads = logs_ref.shape[0]
    logs = logs_ref[...]
    ones = upper_ones(tokens)
    row = dot(logs, ones)
    column = dot(ones, logs, ((0,), (1,)))
    meet = dot(bc_ref[:, STATE:], bc_ref[:, :STATE], ((1,), (1,)))
    lower = iota((tokens, tokens), 0) >= iota((tokens, tokens), 1)
    left = iota((tokens, 2 * HDIM), 1) < HDIM
    for pair in range(heads // 2):
        cut = slice(pair * 2 * HDIM, (pair + 1) * 2 * HDIM)
        d_high, d_low = halves(drive_ref[:, cut])
        both = []
        for h in (2 * pair, 2 * pair + 1):
            gap = column[:, h : h + 1] - row[h : h + 1, :]
            mix = jnp.where(lower, jnp.exp(gap), 0.0) * meet
            m_high, m_low = halves(mix)
            both.append(dot16(m_high, d_high) + dot16(m_high, d_low) + dot16(m_low, d_high))
        pre_ref[:, cut] = direct_ref[:, cut] + jnp.where(left, both[0], both[1])


def prefix_body(parts_ref, starts_ref):
    ctx, rows, share = starts_ref.shape
    state = jnp.zeros((rows, share), F32)
    for i in range(ctx):
        starts_ref[i] = state
        if i < ctx - 1:
            state = parts_ref[i, STATE : STATE + 1] * state + parts_ref[i, :STATE]


def back_body(cuts, pre_ref, start_ref, bc_ref, logs_ref, gain_ref, out_ref):
    tokens, channels = pre_ref.shape
    heads = logs_ref.shape[0]
    within = dot(logs_ref[...], upper_ones(tokens))
    decay = dot(jnp.exp(within), head_spread(heads), ((0,), (0,)))
    width = min(channels, 2 * HDIM)
    group = (iota((width, width), 0) // HDIM == iota((width, width), 1) // HDIM).astype(BF16)
    c_high, c_low = halves(bc_ref[:, STATE:])
    for i in range(channels // width):
        cut = slice(i * width, (i + 1) * width)
        s_high, s_low = halves(start_ref[i] if cuts else start_ref[:, cut])
        carried = dot16(c_high, s_high) + dot16(c_high, s_low) + dot16(c_low, s_high)
        pre = pre_ref[:, cut] + carried * decay[:, cut]
        q_high, q_low = halves(pre * pre)
        mean = (dot16(q_high, group) + dot16(q_low, group)) * (1.0 / HDIM)
        out_ref[:, cut] = (pre * lax.rsqrt(mean + 1e-05) * gain_ref[:, cut]).astype(BF16)


def mixing(seq_input, b_input, c_input, before, conv_x, conv_bc, log_decay, skip, gain, ids, flag):
    tokens, channels = seq_input.shape
    heads = skip.shape[0]
    ctx = lax.axis_size("ctx")
    share = channels // ctx
    cuts = share == 2 * HDIM
    inflow = jnp.sqrt(-jnp.expm1(2.0 * log_decay))
    square = jax.ShapeDtypeStruct((tokens, channels), F32)
    slabs = (ctx, STATE + NOTES, share) if cuts else (STATE + NOTES, channels)
    outs = [
        square,
        square,
        jax.ShapeDtypeStruct((tokens, 2 * STATE), F32),
        jax.ShapeDtypeStruct(slabs, F32),
    ]
    drive, direct, bc, slab = call(
        functools.partial(front_body, cuts),
        outs,
        (
            seq_input,
            b_input,
            c_input,
            before,
            conv_x,
            conv_bc,
            log_decay,
            inflow,
            skip.reshape(1, heads),
            ids,
        ),
        scratch=[pltpu.VMEM((8 + tokens, channels + 2 * STATE), F32)],
        flops=10**9,
        name="front",
    )
    if not cuts:
        slab = slab.reshape(STATE + NOTES, ctx, share).transpose(1, 0, 2)
    parts = lax.all_to_all(slab, "ctx", split_axis=0, concat_axis=0, tiled=True)
    starts = call(
        prefix_body,
        [jax.ShapeDtypeStruct((ctx, STATE, share), F32)],
        (parts,),
        flops=10**6,
        name="prefix",
    )[0]
    start = lax.all_to_all(starts, "ctx", split_axis=0, concat_axis=0, tiled=True)
    if not cuts:
        start = start.transpose(1, 0, 2).reshape(STATE, channels)
    pre = call(
        inner_body, [square], (drive, direct, bc, log_decay), flops=4 * 10**9, name="inner"
    )[0]
    mixed = call(
        functools.partial(back_body, cuts),
        [jax.ShapeDtypeStruct((tokens, channels), BF16)],
        (pre, start, bc, log_decay, gain.reshape(1, channels)),
        flops=10**9,
        name="back",
    )[0]
    return mixed, parts


def swapped(block, axis, bit):
    return lax.ppermute(block, axis, [(i, i ^ bit) for i in range(lax.axis_size(axis))])


def first_body(place_ref, z, x, cz, cx, g0, g1, u0, u1, gate_ref, up_ref):
    half = z.shape[0]
    for w0, w1, out in ((g0, g1, gate_ref), (u0, u1, up_ref)):
        out[:half] = dot16(z[...], w0[0]) + dot16(cz[...], w1[0])
        out[half:] = dot16(x[...], w0[0]) + dot16(cx[...], w1[0])


def second_body(
    place_ref, y, d0, d1, cy, cd0, cd1, gate_ref, up_ref, g0, g1, u0, u1, notes_ref, out_ref, hid
):
    half = y.shape[0]
    part = d0.shape[0]
    rows = hid.shape[0] // notes_ref.shape[0]
    me = place_ref[0]
    side = place_ref[1]
    for a, b, start in ((y, cy, 0), (d0, cd0, half), (d1, cd1, half + part)):
        cut = slice(start, start + a.shape[0])
        gate = gate_ref[cut] + dot16(a[...], g0[0]) + dot16(b[...], g1[0])
        upper = up_ref[cut] + dot16(a[...], u0[0]) + dot16(b[...], u1[0])
        hid[cut] = (silu(gate) * upper).astype(BF16)
    shape = (rows, rows)
    earlier = (iota(shape, 1) < iota(shape, 0)).astype(F32)
    across = iota(shape, 1)
    diagonal = iota(shape, 0) == across
    for place in range(hid.shape[0] // rows):
        z = place % (half // rows)
        block = 2 * z + (side if place * rows < half else 1 - side)
        line = notes_ref[block][1:2, :]
        named = (line[:, :rows] == me.astype(F32)) | (line[:, rows : 2 * rows] == me.astype(F32))
        named = named.astype(F32)
        column = jnp.sum(jnp.where(diagonal, named, 0.0), axis=1, keepdims=True)
        position = jnp.sum(earlier * named, axis=1, keepdims=True).astype(jnp.int32)
        pick = jnp.where(position == across, column, 0.0).astype(BF16)
        picked = dot16(pick, hid[place * rows : (place + 1) * rows], ((0,), (0,)))
        out_ref[0, pl.ds(pl.multiple_of(block * rows, rows), rows), :] = picked.astype(BF16)


def experts_by_tokens(copies, notes, w_gate, w_up):
    zs, rows, columns = copies.shape
    ctx = lax.axis_size("ctx")
    groups = [list(range(s, ctx, 2)) for s in range(2)]
    z = lax.all_to_all(
        copies, "ctx", split_axis=0, concat_axis=0, tiled=True, axis_index_groups=groups
    )
    z = z.reshape(zs * rows, columns)
    half = z.shape[0]
    x = swapped(z, "ctx", 1)
    y = swapped(z, "exp", 2)
    cz = swapped(z, "exp", 1)
    d0 = swapped(y[: half // 2], "ctx", 1)
    d1 = swapped(x[half // 2 :], "exp", 2)
    cx = swapped(x, "exp", 1)
    cy = swapped(y, "exp", 1)
    cd0 = swapped(d0, "exp", 1)
    cd1 = swapped(d1, "exp", 1)

    hidden = w_gate.shape[2]
    tile = min(256, hidden)
    place = jnp.stack([lax.axis_index("exp"), lax.axis_index("ctx") % 2]).astype(jnp.int32)

    def weight(bit):
        return pl.BlockSpec((1, columns, tile), lambda n, s: (0, s[0] ^ bit, n))

    def whole(array):
        return pl.BlockSpec(array.shape, lambda n, s: (0,) * array.ndim)

    def partial_sum():
        return pl.BlockSpec((2 * half, tile), lambda n, s: (0, n))

    flops = 2 * 2 * half * 2 * columns * hidden * 2
    sums = jax.ShapeDtypeStruct((2 * half, hidden), F32)
    gate, upper = pl.pallas_call(
        first_body,
        out_shape=[sums, sums],
        grid_spec=pltpu.PrefetchScalarGridSpec(
            num_scalar_prefetch=1,
            grid=(hidden // tile,),
            in_specs=[whole(a) for a in (z, x, cz, cx)]
            + [weight(0), weight(1), weight(0), weight(1)],
            out_specs=[partial_sum(), partial_sum()],
        ),
        compiler_params=pltpu.CompilerParams(vmem_limit_bytes=40 * 2**20),
        cost_estimate=pl.CostEstimate(flops=flops, bytes_accessed=14 * 2**20, transcendentals=0),
        name="first",
    )(place, z, x, cz, cx, w_gate, w_gate, w_up, w_up)
    line = pl.BlockSpec((ctx, NOTES, notes.shape[2]), lambda n, s: (0, STATE // NOTES, 0))
    return pl.pallas_call(
        second_body,
        out_shape=jax.ShapeDtypeStruct((1, 2 * half, hidden), BF16),
        grid_spec=pltpu.PrefetchScalarGridSpec(
            num_scalar_prefetch=1,
            grid=(hidden // tile,),
            in_specs=[whole(a) for a in (y, d0, d1, cy, cd0, cd1)]
            + [partial_sum(), partial_sum()]
            + [weight(2), weight(3), weight(2), weight(3), line],
            out_specs=pl.BlockSpec((1, 2 * half, tile), lambda n, s: (0, 0, n)),
            scratch_shapes=[pltpu.VMEM((2 * half, tile), BF16)],
        ),
        compiler_params=pltpu.CompilerParams(vmem_limit_bytes=40 * 2**20),
        cost_estimate=pl.CostEstimate(flops=flops, bytes_accessed=15 * 2**20, transcendentals=0),
        name="second",
    )(place, y, d0, d1, cy, cd0, cd1, gate, upper, w_gate, w_gate, w_up, w_up, notes)


def slot_matrix(pairs, expert, capacity):
    named = jnp.any(pairs == expert, axis=1).astype(jnp.int32)
    position = jnp.cumsum(named) - named
    hit = position[None, :] == jnp.arange(capacity, dtype=jnp.int32)[:, None]
    return (hit & (named[None, :] > 0)).astype(BF16)


def experts_by_slots(moe_input, pairs, w_gate, w_up):
    experts = lax.axis_size("exp")
    capacity = 4 * moe_input.shape[0] // experts
    pick = jax.vmap(lambda e: slot_matrix(pairs, e, capacity))(jnp.arange(experts))
    slots = jnp.einsum("eqt,td->eqd", pick, moe_input, preferred_element_type=F32)
    routed = lax.all_to_all(slots.astype(BF16), "exp", split_axis=0, concat_axis=2, tiled=True)
    rows = lax.all_gather(routed[0], "ctx", axis=0, tiled=True)
    gate = jnp.dot(rows, w_gate[0], preferred_element_type=F32)
    upper = jnp.dot(rows, w_up[0], preferred_element_type=F32)
    return (jax.nn.silu(gate) * upper).astype(BF16)[None]


def on_device(
    seq_input,
    b_input,
    c_input,
    conv_x,
    conv_bc,
    log_decay,
    skip_gain,
    norm_gain,
    moe_input,
    expert_ids,
    w_gate,
    w_up,
):
    ctx = lax.axis_size("ctx")
    by_tokens = lax.axis_size("exp") == 4 and ctx == 8
    ends, copies = pack(seq_input, b_input, c_input, moe_input, ctx // 2 if by_tokens else 1)
    before = lax.ppermute(ends, "ctx", [(i, i + 1) for i in range(ctx - 1)])
    mixed, notes = mixing(
        seq_input,
        b_input,
        c_input,
        before,
        conv_x,
        conv_bc,
        log_decay,
        skip_gain,
        norm_gain,
        expert_ids,
        by_tokens,
    )
    if by_tokens:
        hidden = experts_by_tokens(copies, notes, w_gate, w_up)
    else:
        hidden = experts_by_slots(moe_input, expert_ids, w_gate, w_up)
    return (mixed, hidden)


def solution(mesh):
    in_specs = (
        P("ctx", "exp"),
        P("ctx", None),
        P("ctx", None),
        P(None, "exp"),
        P(),
        P("exp", "ctx"),
        P("exp"),
        P("exp"),
        P("ctx", "exp"),
        P("ctx", None),
        P("exp", None, "ctx"),
        P("exp", None, "ctx"),
    )
    out_specs = (P("ctx", "exp"), P("exp", None, "ctx"))
    return jax.shard_map(
        on_device, mesh=mesh, in_specs=in_specs, out_specs=out_specs, check_vma=False
    )
```

```python
import functools

import jax
import jax.numpy as jnp
from jax import lax
from jax.experimental import pallas as pl
from jax.experimental.pallas import tpu as pltpu
from jax.sharding import PartitionSpec as P

HDIM = 64
STATE = 128
KCONV = 4
EDGE = 16
NOTES = 8

F32 = jnp.float32
BF16 = jnp.bfloat16


def dot16(a, b, contract=((1,), (0,))):
    return lax.dot_general(a, b, (contract, ((), ())), preferred_element_type=F32)


def halves(value):
    high = value.astype(BF16)
    return high, (value - high.astype(F32)).astype(BF16)


def dot(a, b, contract=((1,), (0,))):
    a_high, a_low = halves(a)
    b_high, b_low = halves(b)
    cross = dot16(a_high, b_low, contract) + dot16(a_low, b_high, contract)
    return dot16(a_high, b_high, contract) + cross


def dot_exact(a, b, contract=((1,), (0,))):
    high, rest = halves(a)
    low = (a - high.astype(F32) - rest.astype(F32)).astype(BF16)
    return dot16(high, b, contract) + (dot16(rest, b, contract) + dot16(low, b, contract))


def dot_left(a, b, contract=((1,), (0,))):
    high, low = halves(a)
    return dot16(high, b, contract) + dot16(low, b, contract)


FIRST = ((0,), (0,))


def iota(shape, axis):
    return lax.broadcasted_iota(jnp.int32, shape, axis)


def head_spread(heads):
    shape = (heads, heads * HDIM)
    return (iota(shape, 1) // HDIM == iota(shape, 0)).astype(BF16)


def upper_ones(length):
    return (iota((length, length), 0) <= iota((length, length), 1)).astype(BF16)


def silu(value):
    return value / (1.0 + jnp.exp(-value))


def one_minus_exp(value):
    series = jnp.ones_like(value)
    for n in range(8, 1, -1):
        series = 1.0 + value * series * (1.0 / n)
    return jnp.where(value > -0.25, -value * series, 1.0 - jnp.exp(value))


def fetched(sources, targets, sems):
    copies = [
        pltpu.make_async_copy(a, b, sems.at[i]) for i, (a, b) in enumerate(zip(sources, targets))
    ]
    for copy in copies:
        copy.start()
    for copy in copies:
        copy.wait()


def call(body, outs, far, near, scratch=(), sems=0, flops=0, name=None):
    moved = sum(a.size * a.dtype.itemsize for a in (*far, *near, *outs))
    scratch = list(scratch) + ([pltpu.SemaphoreType.DMA((sems,))] if sems else [])
    return pl.pallas_call(
        body,
        out_shape=outs,
        in_specs=[pl.BlockSpec(memory_space=pltpu.HBM)] * len(far)
        + [pl.BlockSpec(memory_space=pltpu.VMEM)] * len(near),
        out_specs=[pl.BlockSpec(memory_space=pltpu.VMEM)] * len(outs),
        scratch_shapes=scratch,
        compiler_params=pltpu.CompilerParams(vmem_limit_bytes=24 * 2**20),
        cost_estimate=pl.CostEstimate(flops=flops, bytes_accessed=moved, transcendentals=0),
        name=name,
    )(*(pltpu.with_memory_space_constraint(a, pltpu.HBM) for a in far), *near)


def array(shape, dtype):
    return jax.ShapeDtypeStruct(shape, dtype)


def ends_body(x_ref, b_ref, c_ref, ends_ref, sems):
    tokens, channels = x_ref.shape
    cut = pl.ds(tokens - EDGE, EDGE)
    fetched(
        [x_ref.at[cut, :], b_ref.at[cut, :], c_ref.at[cut, :]],
        [
            ends_ref.at[:, pl.ds(0, channels)],
            ends_ref.at[:, pl.ds(channels, STATE)],
            ends_ref.at[:, pl.ds(channels + STATE, STATE)],
        ],
        sems,
    )


def front_body(
    by_tokens,
    x_hbm,
    b_hbm,
    c_hbm,
    taps_hbm,
    taps_bc_hbm,
    logs_hbm,
    skip_hbm,
    ids_hbm,
    ends_ref,
    drive_ref,
    direct_ref,
    bc_ref,
    row_ref,
    column_ref,
    slab_ref,
    pad_ref,
    x_ref,
    b_ref,
    c_ref,
    taps_ref,
    taps_bc_ref,
    logs_ref,
    skip_ref,
    ids_ref,
    sems,
):
    fetched(
        [x_hbm, b_hbm, c_hbm, taps_hbm, taps_bc_hbm, logs_hbm, skip_hbm, ids_hbm],
        [x_ref, b_ref, c_ref, taps_ref, taps_bc_ref, logs_ref, skip_ref, ids_ref],
        sems,
    )
    tokens, channels = x_ref.shape
    heads = logs_ref.shape[0]
    pad_ref[0:8, :] = ends_ref[...].astype(F32)[EDGE - 8 : EDGE]
    pad_ref[8 : 8 + tokens, :channels] = x_ref[...].astype(F32)
    pad_ref[8 : 8 + tokens, channels : channels + STATE] = b_ref[...].astype(F32)
    pad_ref[8 : 8 + tokens, channels + STATE :] = c_ref[...].astype(F32)

    def conv(taps, start, stop):
        total = jnp.zeros((tokens, stop - start), F32)
        for k in range(KCONV):
            first = 8 - (KCONV - 1) + k
            total = total + taps[k : k + 1] * pad_ref[first : first + tokens, start:stop]
        return silu(total)

    bc = conv(taps_bc_ref[...], channels, channels + 2 * STATE)
    bc_ref[...] = bc
    bmat = bc[:, :STATE]

    logs = logs_ref[...]
    inflow = jnp.sqrt(one_minus_exp(2.0 * logs))
    ones = upper_ones(tokens)
    within = dot_exact(logs, ones)
    row_ref[...] = within
    column_ref[...] = within.T
    total = within[:, tokens - 1 :]
    remain = jnp.exp(total - within)
    spread = head_spread(heads)
    xconv = conv(taps_ref[...], 0, channels)
    drive_ref[...] = xconv * dot_left(inflow, spread, FIRST)
    direct_ref[...] = xconv * dot_exact(skip_ref[...], spread)
    state = dot(bmat, xconv * dot_left(inflow * remain, spread, FIRST), FIRST)
    notes = dot_exact(jnp.exp(jnp.broadcast_to(total, (heads, NOTES))), spread, FIRST)
    if not by_tokens:
        slab_ref[:STATE] = state
        slab_ref[STATE:] = notes
        return
    parts, _, share = slab_ref.shape
    ids = ids_ref[...].astype(F32)
    line = jnp.concatenate([ids[0:1], ids[1:2]], axis=1)
    for i in range(parts):
        cut = slice(i * share, (i + 1) * share)
        slab_ref[i, :STATE] = state[:, cut]
        slab_ref[i, STATE:] = jnp.where(iota((NOTES, share), 0) == 1, line, notes[:, cut])


def weight_copies(w_gate, w_up, held, sems, bits):
    depth = held.shape[2]
    me = lax.axis_index("exp")
    copies = []
    for k, bit in enumerate(bits):
        cut = pl.ds(pl.multiple_of((me ^ bit) * depth, depth), depth)
        for i, w in enumerate((w_gate, w_up)):
            copies.append(
                pltpu.make_async_copy(w.at[0, cut, :], held.at[i, k], sems.at[2 * k + i])
            )
    return copies


def inner_body(
    bits,
    w_gate,
    w_up,
    gain_hbm,
    drive_ref,
    direct_ref,
    bc_ref,
    row_ref,
    column_ref,
    pre_ref,
    decay_ref,
    gain_ref,
    held_ref,
    sems,
):
    copies = [pltpu.make_async_copy(gain_hbm, gain_ref, sems.at[4])]
    copies += weight_copies(w_gate, w_up, held_ref, sems, bits)
    for copy in copies:
        copy.start()
    tokens = drive_ref.shape[0]
    heads = row_ref.shape[0]
    row = row_ref[...]
    column = column_ref[...]
    decay_ref[...] = dot_left(jnp.exp(row), head_spread(heads), FIRST)
    meet = dot(bc_ref[:, STATE:], bc_ref[:, :STATE], ((1,), (1,)))
    lower = iota((tokens, tokens), 0) >= iota((tokens, tokens), 1)
    left = iota((tokens, 2 * HDIM), 1) < HDIM
    for pair in range(heads // 2):
        cut = slice(pair * 2 * HDIM, (pair + 1) * 2 * HDIM)
        d_high, d_low = halves(drive_ref[:, cut])
        both = []
        for h in (2 * pair, 2 * pair + 1):
            gap = column[:, h : h + 1] - row[h : h + 1, :]
            mix = jnp.where(lower, jnp.exp(gap), 0.0) * meet
            m_high, m_low = halves(mix)
            both.append(dot16(m_high, d_high) + dot16(m_high, d_low) + dot16(m_low, d_high))
        pre_ref[:, cut] = direct_ref[:, cut] + jnp.where(left, both[0], both[1])
    for copy in copies:
        copy.wait()


def prefix_body(parts_ref, starts_ref):
    ctx, rows, share = starts_ref.shape
    state = jnp.zeros((rows, share), F32)
    for i in range(ctx):
        starts_ref[i] = state
        if i < ctx - 1:
            state = parts_ref[i, STATE : STATE + 1] * state + parts_ref[i, :STATE]


def back_body(cuts, pre_ref, decay_ref, start_ref, bc_ref, gain_ref, out_ref):
    channels = pre_ref.shape[1]
    width = min(channels, 4 * HDIM)
    group = (iota((width, width), 0) // HDIM == iota((width, width), 1) // HDIM).astype(BF16)
    c_high, c_low = halves(bc_ref[:, STATE:])
    for i in range(channels // width):
        cut = slice(i * width, (i + 1) * width)
        if cuts:
            start = jnp.concatenate([start_ref[2 * i], start_ref[2 * i + 1]], axis=1)
        else:
            start = start_ref[:, cut]
        s_high, s_low = halves(start)
        carried = dot16(c_high, s_high) + dot16(c_high, s_low) + dot16(c_low, s_high)
        pre = pre_ref[:, cut] + carried * decay_ref[:, cut]
        mean = dot_left(pre * pre, group) * (1.0 / HDIM)
        out_ref[:, cut] = (pre * lax.rsqrt(mean + 1e-05) * gain_ref[:, cut]).astype(BF16)


def mixing(
    seq_input, b_input, c_input, before, conv_x, conv_bc, log_decay, skip, gain, ids, w_gate, w_up
):
    tokens, channels = seq_input.shape
    heads = skip.shape[0]
    ctx = lax.axis_size("ctx")
    share = channels // ctx
    cuts = share == 2 * HDIM
    square = array((tokens, channels), F32)
    slabs = (ctx, STATE + NOTES, share) if cuts else (STATE + NOTES, channels)
    outs = [
        square,
        square,
        array((tokens, 2 * STATE), F32),
        array((heads, tokens), F32),
        array((tokens, heads), F32),
        array(slabs, F32),
    ]
    far = (seq_input, b_input, c_input, conv_x, conv_bc, log_decay, skip.reshape(1, heads), ids.T)
    drive, direct, bc, row, column, slab = call(
        functools.partial(front_body, cuts),
        outs,
        far,
        (before,),
        scratch=[pltpu.VMEM((8 + tokens, channels + 2 * STATE), F32)]
        + [pltpu.VMEM(a.shape, a.dtype) for a in far],
        sems=len(far),
        flops=10**9,
        name="front",
    )
    if not cuts:
        slab = slab.reshape(STATE + NOTES, ctx, share).transpose(1, 0, 2)
    parts = lax.all_to_all(slab, "ctx", split_axis=0, concat_axis=0, tiled=True)
    starts = call(
        prefix_body,
        [array((ctx, STATE, share), F32)],
        (),
        (parts,),
        flops=10**6,
        name="prefix",
    )[0]
    start = lax.all_to_all(starts, "ctx", split_axis=0, concat_axis=0, tiled=True)
    if not cuts:
        start = start.transpose(1, 0, 2).reshape(STATE, channels)
    depth = w_gate.shape[1] // lax.axis_size("exp")
    bits = (0, 1) if cuts else ()
    held_shape = (2, max(1, len(bits)), depth if cuts else 8, w_gate.shape[2] if cuts else 128)
    pre, decay, gain, held = call(
        functools.partial(inner_body, bits),
        [square, square, array((1, channels), F32), array(held_shape, BF16)],
        (w_gate, w_up, gain.reshape(1, channels)),
        (drive, direct, bc, row, column),
        sems=5,
        flops=4 * 10**9,
        name="inner",
    )
    mixed = call(
        functools.partial(back_body, cuts),
        [array((tokens, channels), BF16)],
        (),
        (pre, decay, start, bc, gain),
        flops=10**9,
        name="back",
    )[0]
    return mixed, parts, held


def copies_body(moe_ref, copies_ref, sems):
    zs = copies_ref.shape[0]
    fetched([moe_ref] * zs, [copies_ref.at[i] for i in range(zs)], sems)


def swapped(block, axis, bit):
    return lax.ppermute(block, axis, [(i, i ^ bit) for i in range(lax.axis_size(axis))])


TILE = 256


def first_body(w_gate, w_up, held_ref, z, x, cz, cx, gate_ref, up_ref, later_ref, sems):
    copies = weight_copies(w_gate, w_up, later_ref, sems, (2, 3))
    for copy in copies:
        copy.start()
    for start in range(0, gate_ref.shape[1], TILE):
        cut = slice(start, start + TILE)
        for i, out in enumerate((gate_ref, up_ref)):
            here = dot16(jnp.concatenate([z[...], x[...]], 0), held_ref[i, 0, :, cut])
            out[:, cut] = here + dot16(
                jnp.concatenate([cz[...], cx[...]], 0), held_ref[i, 1, :, cut]
            )
    for copy in copies:
        copy.wait()


def second_body(
    y, d0, d1, cy, cd0, cd1, gate_ref, up_ref, held_ref, notes_ref, out_ref, pick_ref, hid_ref
):
    blocks = notes_ref.shape[0]
    length = gate_ref.shape[0]
    rows = length // blocks
    me = lax.axis_index("exp").astype(F32)
    side = lax.axis_index("ctx") % 2
    shape = (rows, rows)
    earlier = (iota(shape, 1) < iota(shape, 0)).astype(F32)
    across = iota(shape, 1)
    diagonal = iota(shape, 0) == across

    def block_at(place):
        z = place % (blocks // 2)
        return 2 * z + (side if place < blocks // 2 else 1 - side)

    for place in range(blocks):
        line = notes_ref[block_at(place), STATE + 1 : STATE + 2, :]
        named = ((line[:, :rows] == me) | (line[:, rows : 2 * rows] == me)).astype(F32)
        column = jnp.sum(jnp.where(diagonal, named, 0.0), axis=1, keepdims=True)
        position = jnp.sum(earlier * named, axis=1, keepdims=True).astype(jnp.int32)
        pick_ref[place] = jnp.where(position == across, column, 0.0).astype(BF16)

    for start in range(0, gate_ref.shape[1], TILE):
        cut = slice(start, start + TILE)
        a = jnp.concatenate([y[...], d0[...], d1[...]], 0)
        b = jnp.concatenate([cy[...], cd0[...], cd1[...]], 0)
        gate = gate_ref[:, cut] + dot16(a, held_ref[0, 0, :, cut]) + dot16(b, held_ref[0, 1, :, cut])
        upper = up_ref[:, cut] + dot16(a, held_ref[1, 0, :, cut]) + dot16(b, held_ref[1, 1, :, cut])
        hid_ref[...] = (silu(gate) * upper).astype(BF16)
        for place in range(blocks):
            picked = dot16(pick_ref[place], hid_ref[place * rows : (place + 1) * rows], FIRST)
            at = pl.ds(pl.multiple_of(block_at(place) * rows, rows), rows)
            out_ref[0, at, cut] = picked.astype(BF16)


def experts_by_tokens(copies, notes, held, w_gate, w_up):
    zs, rows, columns = copies.shape
    ctx = lax.axis_size("ctx")
    groups = [list(range(s, ctx, 2)) for s in range(2)]
    z = lax.all_to_all(
        copies, "ctx", split_axis=0, concat_axis=0, tiled=True, axis_index_groups=groups
    )
    z = z.reshape(zs * rows, columns)
    half = z.shape[0]
    x = swapped(z, "ctx", 1)
    y = swapped(z, "exp", 2)
    cz = swapped(z, "exp", 1)
    d0 = swapped(y[: half // 2], "ctx", 1)
    d1 = swapped(x[half // 2 :], "exp", 2)
    cx = swapped(x, "exp", 1)
    cy = swapped(y, "exp", 1)
    cd0 = swapped(d0, "exp", 1)
    cd1 = swapped(d1, "exp", 1)

    hidden = w_gate.shape[2]
    flops = 2 * 2 * half * 2 * columns * hidden * 2
    sums = array((2 * half, hidden), F32)
    gate, upper, later = call(
        first_body,
        [sums, sums, array(held.shape, BF16)],
        (w_gate, w_up),
        (held, z, x, cz, cx),
        sems=4,
        flops=flops,
        name="first",
    )
    return call(
        second_body,
        [array((1, 2 * half, hidden), BF16)],
        (),
        (y, d0, d1, cy, cd0, cd1, gate, upper, later, notes),
        scratch=[pltpu.VMEM((ctx, rows, rows), BF16), pltpu.VMEM((2 * half, TILE), BF16)],
        flops=flops,
        name="second",
    )[0]


def slot_matrix(pairs, expert, capacity):
    named = jnp.any(pairs == expert, axis=1).astype(jnp.int32)
    position = jnp.cumsum(named) - named
    hit = position[None, :] == jnp.arange(capacity, dtype=jnp.int32)[:, None]
    return (hit & (named[None, :] > 0)).astype(BF16)


def experts_by_slots(moe_input, pairs, w_gate, w_up):
    experts = lax.axis_size("exp")
    capacity = 4 * moe_input.shape[0] // experts
    pick = jax.vmap(lambda e: slot_matrix(pairs, e, capacity))(jnp.arange(experts))
    slots = jnp.einsum("eqt,td->eqd", pick, moe_input, preferred_element_type=F32)
    routed = lax.all_to_all(slots.astype(BF16), "exp", split_axis=0, concat_axis=2, tiled=True)
    rows = lax.all_gather(routed[0], "ctx", axis=0, tiled=True)
    gate = jnp.dot(rows, w_gate[0], preferred_element_type=F32)
    upper = jnp.dot(rows, w_up[0], preferred_element_type=F32)
    return (jax.nn.silu(gate) * upper).astype(BF16)[None]


def on_device(
    seq_input,
    b_input,
    c_input,
    conv_x,
    conv_bc,
    log_decay,
    skip_gain,
    norm_gain,
    moe_input,
    expert_ids,
    w_gate,
    w_up,
):
    ctx = lax.axis_size("ctx")
    by_tokens = lax.axis_size("exp") == 4 and ctx == 8
    tokens, channels = seq_input.shape
    ends = call(
        ends_body,
        [array((EDGE, channels + 2 * STATE), BF16)],
        (seq_input, b_input, c_input),
        (),
        sems=3,
        name="ends",
    )[0]
    before = lax.ppermute(ends, "ctx", [(i, i + 1) for i in range(ctx - 1)])
    mixed, notes, held = mixing(
        seq_input,
        b_input,
        c_input,
        before,
        conv_x,
        conv_bc,
        log_decay,
        skip_gain,
        norm_gain,
        expert_ids,
        w_gate,
        w_up,
    )
    if by_tokens:
        zs = ctx // 2
        copies = call(
            copies_body,
            [array((zs,) + moe_input.shape, BF16)],
            (moe_input,),
            (),
            sems=zs,
            name="copies",
        )[0]
        hidden = experts_by_tokens(copies, notes, held, w_gate, w_up)
    else:
        hidden = experts_by_slots(moe_input, expert_ids, w_gate, w_up)
    return (mixed, hidden)


def solution(mesh):
    in_specs = (
        P("ctx", "exp"),
        P("ctx", None),
        P("ctx", None),
        P(None, "exp"),
        P(),
        P("exp", "ctx"),
        P("exp"),
        P("exp"),
        P("ctx", "exp"),
        P("ctx", None),
        P("exp", None, "ctx"),
        P("exp", None, "ctx"),
    )
    out_specs = (P("ctx", "exp"), P("exp", None, "ctx"))
    return jax.shard_map(
        on_device, mesh=mesh, in_specs=in_specs, out_specs=out_specs, check_vma=False
    )
```

```python
import functools

import jax
import jax.numpy as jnp
from jax import lax
from jax.experimental import pallas as pl
from jax.experimental.pallas import tpu as pltpu
from jax.sharding import PartitionSpec as P

HDIM = 64
STATE = 128
KCONV = 4
EDGE = 16
NOTES = 8

F32 = jnp.float32
BF16 = jnp.bfloat16


def dot16(a, b, contract=((1,), (0,))):
    return lax.dot_general(a, b, (contract, ((), ())), preferred_element_type=F32)


def halves(value):
    high = value.astype(BF16)
    return high, (value - high.astype(F32)).astype(BF16)


def dot(a, b, contract=((1,), (0,))):
    a_high, a_low = halves(a)
    b_high, b_low = halves(b)
    cross = dot16(a_high, b_low, contract) + dot16(a_low, b_high, contract)
    return dot16(a_high, b_high, contract) + cross


def dot_exact(a, b, contract=((1,), (0,))):
    high, rest = halves(a)
    low = (a - high.astype(F32) - rest.astype(F32)).astype(BF16)
    return dot16(high, b, contract) + (dot16(rest, b, contract) + dot16(low, b, contract))


def dot_left(a, b, contract=((1,), (0,))):
    high, low = halves(a)
    return dot16(high, b, contract) + dot16(low, b, contract)


FIRST = ((0,), (0,))


def iota(shape, axis):
    return lax.broadcasted_iota(jnp.int32, shape, axis)


def head_spread(heads):
    shape = (heads, heads * HDIM)
    return (iota(shape, 1) // HDIM == iota(shape, 0)).astype(BF16)


def upper_ones(length):
    return (iota((length, length), 0) <= iota((length, length), 1)).astype(BF16)


def silu(value):
    return value / (1.0 + jnp.exp(-value))


def one_minus_exp(value):
    series = jnp.ones_like(value)
    for n in range(8, 1, -1):
        series = 1.0 + value * series * (1.0 / n)
    return jnp.where(value > -0.25, -value * series, 1.0 - jnp.exp(value))


def started(sources, targets, sems, first=0):
    copies = []
    for i, (source, target) in enumerate(zip(sources, targets)):
        copies.append(pltpu.make_async_copy(source, target, sems.at[first + i]))
        copies[-1].start()
    return copies


def finished(copies):
    for copy in copies:
        copy.wait()


def call(body, outs, args, fixed=0, scratch=(), sems=0, flops=0, grant=8, near=False, name=None):
    moved = sum(a.size * a.dtype.itemsize for a in (*args, *outs))
    scratch = list(scratch) + ([pltpu.SemaphoreType.DMA((sems,))] if sems else [])
    space = pltpu.VMEM if near else pl.ANY
    args = [
        pltpu.with_memory_space_constraint(a, pltpu.HBM) if i < fixed else a
        for i, a in enumerate(args)
    ]
    spaces = [pltpu.HBM if i < fixed else space for i in range(len(args))]
    return pl.pallas_call(
        body,
        out_shape=outs,
        in_specs=[pl.BlockSpec(memory_space=s) for s in spaces],
        out_specs=[pl.BlockSpec(memory_space=space)] * len(outs),
        scratch_shapes=scratch,
        compiler_params=pltpu.CompilerParams(vmem_limit_bytes=grant * 2**20),
        cost_estimate=pl.CostEstimate(flops=flops, bytes_accessed=moved, transcendentals=0),
        name=name,
    )(*args)


def room(arrays):
    return [pltpu.VMEM(a.shape, a.dtype) for a in arrays]


def array(shape, dtype):
    return jax.ShapeDtypeStruct(shape, dtype)


def ends_body(x_ref, b_ref, c_ref, ends_ref, sems):
    tokens, channels = x_ref.shape
    cut = pl.ds(tokens - EDGE, EDGE)
    finished(
        started(
            [x_ref.at[cut, :], b_ref.at[cut, :], c_ref.at[cut, :]],
            [
                ends_ref.at[:, pl.ds(0, channels)],
                ends_ref.at[:, pl.ds(channels, STATE)],
                ends_ref.at[:, pl.ds(channels + STATE, STATE)],
            ],
            sems,
        )
    )


def front_body(by_tokens, count, *refs):
    far, outs, rest = refs[:count], refs[count : count + 4], refs[count + 4 :]
    near, scratch, pad_ref, sems = rest[:count], rest[count : count + 4], rest[-2], rest[-1]
    copies = started(far, near, sems)
    x_ref, b_ref, c_ref, taps_ref, taps_bc_ref, logs_ref, skip_ref, ids_ref, ends_ref = near
    xconv_ref, bc_ref, lines_ref, slab_ref = scratch
    tokens, channels = x_ref.shape
    heads = logs_ref.shape[0]
    finished(copies)
    pad_ref[0:8, :] = ends_ref[...].astype(F32)[EDGE - 8 : EDGE]
    pad_ref[8 : 8 + tokens, :channels] = x_ref[...].astype(F32)
    pad_ref[8 : 8 + tokens, channels : channels + STATE] = b_ref[...].astype(F32)
    pad_ref[8 : 8 + tokens, channels + STATE :] = c_ref[...].astype(F32)

    def conv(taps, start, stop):
        total = jnp.zeros((tokens, stop - start), F32)
        for k in range(KCONV):
            first = 8 - (KCONV - 1) + k
            total = total + taps[k : k + 1] * pad_ref[first : first + tokens, start:stop]
        return silu(total)

    bc = conv(taps_bc_ref[...], channels, channels + 2 * STATE)
    bc_ref[...] = bc
    xconv = conv(taps_ref[...], 0, channels)
    xconv_ref[...] = xconv
    logs = logs_ref[...]
    inflow = jnp.sqrt(one_minus_exp(2.0 * logs))
    within = dot_exact(logs, upper_ones(tokens))
    lines_ref[0] = within
    lines_ref[1] = inflow
    out_copies = started(scratch[:3], outs[:3], sems)
    total = within[:, tokens - 1 :]
    remain = jnp.exp(total - within)
    spread = head_spread(heads)
    state = dot(bc[:, :STATE], xconv * dot_left(inflow * remain, spread, FIRST), FIRST)
    notes = dot_exact(jnp.exp(jnp.broadcast_to(total, (heads, NOTES))), spread, FIRST)
    if by_tokens:
        parts, _, share = slab_ref.shape
        ids = ids_ref[...].astype(F32)
        line = jnp.concatenate([ids[0:1], ids[1:2]], axis=1)
        for i in range(parts):
            cut = slice(i * share, (i + 1) * share)
            slab_ref[i, :STATE] = state[:, cut]
            slab_ref[i, STATE:] = jnp.where(iota((NOTES, share), 0) == 1, line, notes[:, cut])
    else:
        slab_ref[:STATE] = state
        slab_ref[STATE:] = notes
    finished(out_copies + started(scratch[3:], outs[3:], sems, 3))


def inner_body(skip_far, xconv_far, bc_far, lines_far, pre_far, decay_far, *rest):
    far = (skip_far, xconv_far, bc_far, lines_far)
    skip_ref, xconv_ref, bc_ref, lines_ref, pre_ref, decay_ref, sems = rest
    finished(started(far, rest[:4], sems))
    tokens, channels = xconv_ref.shape
    heads = channels // HDIM
    row = lines_ref[0]
    column = row.T
    spread = head_spread(heads)
    decay_ref[...] = dot_left(jnp.exp(row), spread, FIRST)
    copies = started([decay_ref], [decay_far], sems)
    inflow = dot_left(lines_ref[1], spread, FIRST)
    skip = dot_exact(skip_ref[...], spread)
    meet = dot(bc_ref[:, STATE:], bc_ref[:, :STATE], ((1,), (1,)))
    lower = iota((tokens, tokens), 0) >= iota((tokens, tokens), 1)
    left = iota((tokens, 2 * HDIM), 1) < HDIM
    for pair in range(heads // 2):
        cut = slice(pair * 2 * HDIM, (pair + 1) * 2 * HDIM)
        xconv = xconv_ref[:, cut]
        d_high, d_low = halves(xconv * inflow[:, cut])
        both = []
        for h in (2 * pair, 2 * pair + 1):
            gap = column[:, h : h + 1] - row[h : h + 1, :]
            mix = jnp.where(lower, jnp.exp(gap), 0.0) * meet
            m_high, m_low = halves(mix)
            both.append(dot16(m_high, d_high) + dot16(m_high, d_low) + dot16(m_low, d_high))
        pre_ref[:, cut] = skip[:, cut] * xconv + jnp.where(left, both[0], both[1])
    finished(copies + started([pre_ref], [pre_far], sems, 1))


def prefix_body(parts_ref, starts_ref):
    ctx, rows, share = starts_ref.shape
    state = jnp.zeros((rows, share), F32)
    for i in range(ctx):
        starts_ref[i] = state
        if i < ctx - 1:
            state = parts_ref[i, STATE : STATE + 1] * state + parts_ref[i, :STATE]


def back_body(cuts, gain_far, pre_far, decay_far, start_far, bc_far, out_far, *rest):
    far = (start_far, bc_far, pre_far, decay_far, gain_far)
    start_ref, bc_ref, pre_ref, decay_ref, gain_ref, out_ref, sems = rest
    copies = started(far, rest[:5], sems)
    channels = pre_ref.shape[1]
    width = min(channels, 4 * HDIM)
    group = (iota((width, width), 0) // HDIM == iota((width, width), 1) // HDIM).astype(BF16)
    finished(copies)
    c_high, c_low = halves(bc_ref[:, STATE:])
    copies = []
    for i in range(channels // width):
        cut = slice(i * width, (i + 1) * width)
        if cuts:
            start = jnp.concatenate([start_ref[2 * i], start_ref[2 * i + 1]], axis=1)
        else:
            start = start_ref[:, cut]
        s_high, s_low = halves(start)
        carried = dot16(c_high, s_high) + dot16(c_high, s_low) + dot16(c_low, s_high)
        pre = pre_ref[:, cut] + carried * decay_ref[:, cut]
        mean = dot_left(pre * pre, group) * (1.0 / HDIM)
        out_ref[:, cut] = (pre * lax.rsqrt(mean + 1e-05) * gain_ref[:, cut]).astype(BF16)
        copies += started([out_ref.at[:, cut]], [out_far.at[:, cut]], sems, i)
    finished(copies)


def mixing(seq_input, b_input, c_input, before, conv_x, conv_bc, log_decay, skip, gain, ids):
    tokens, channels = seq_input.shape
    heads = skip.shape[0]
    ctx = lax.axis_size("ctx")
    share = channels // ctx
    cuts = share == 2 * HDIM
    skip = skip.reshape(1, heads)
    square = array((tokens, channels), F32)
    slabs = (ctx, STATE + NOTES, share) if cuts else (STATE + NOTES, channels)
    outs = [
        square,
        array((tokens, 2 * STATE), F32),
        array((2, heads, tokens), F32),
        array(slabs, F32),
    ]
    args = (seq_input, b_input, c_input, conv_x, conv_bc, log_decay, skip, ids.T, before)
    xconv, bc, lines, slab = call(
        functools.partial(front_body, cuts, len(args)),
        outs,
        args,
        fixed=len(args) - 1,
        scratch=room(args)
        + room(outs)
        + [pltpu.VMEM((8 + tokens, channels + 2 * STATE), F32)],
        sems=len(args),
        flops=10**9,
        grant=16,
        name="front",
    )
    if not cuts:
        slab = slab.reshape(STATE + NOTES, ctx, share).transpose(1, 0, 2)
    parts = lax.all_to_all(slab, "ctx", split_axis=0, concat_axis=0, tiled=True)
    starts = call(
        prefix_body,
        [array((ctx, STATE, share), F32)],
        (parts,),
        flops=10**6,
        near=True,
        name="prefix",
    )[0]
    start = lax.all_to_all(starts, "ctx", split_axis=0, concat_axis=0, tiled=True)
    if not cuts:
        start = start.transpose(1, 0, 2).reshape(STATE, channels)
    args = (skip, xconv, bc, lines)
    outs = [square, square]
    pre, decay = call(
        inner_body,
        outs,
        args,
        fixed=1,
        scratch=room(args) + room(outs),
        sems=4,
        flops=4 * 10**9,
        grant=16,
        name="inner",
    )
    args = (gain.reshape(1, channels), pre, decay, start, bc)
    outs = [array((tokens, channels), BF16)]
    mixed = call(
        functools.partial(back_body, cuts),
        outs,
        args,
        fixed=1,
        scratch=room([start, bc, pre, decay, args[0]]) + room(outs),
        sems=5,
        flops=10**9,
        grant=16,
        name="back",
    )[0]
    return mixed, parts


TILE = 256


def join_body(a_ref, b_ref, out_ref, sems):
    rows = a_ref.shape[0]
    finished(
        started([a_ref, b_ref], [out_ref.at[pl.ds(0, rows), :], out_ref.at[pl.ds(rows, rows), :]], sems)
    )


def swapped(block, axis, bit):
    return lax.ppermute(block, axis, [(i, i ^ bit) for i in range(lax.axis_size(axis))])


def expert_body(pieces, *refs):
    (w_gate, w_up), far, (notes_far, out_far) = refs[:2], refs[2 : pieces + 2], refs[pieces + 2 : pieces + 4]
    rows_ref, held_ref, notes_ref, pick_ref, hid_ref, out_ref, sems, w_sems = refs[pieces + 4 :]
    length, width = rows_ref.shape
    depth = width // 4
    step = length // 4
    tiles = out_ref.shape[1] // TILE
    blocks = notes_ref.shape[0]
    rows = length // blocks
    me = lax.axis_index("exp")
    here = lax.axis_index("ctx")

    def piece_copies(k):
        cut = pl.ds(k * depth, depth)
        targets = [rows_ref.at[pl.ds(i * step, step), cut] for i in range(4)]
        return [
            pltpu.make_async_copy(far[4 * k + i], targets[i], sems.at[4 * k + i]) for i in range(4)
        ]

    def weight_copies(n, k):
        down = pl.ds(pl.multiple_of((me ^ k) * depth, depth), depth)
        across = pl.ds(n * TILE, TILE)
        return [
            pltpu.make_async_copy(
                w.at[0, down, across], held_ref.at[i, n, k], w_sems.at[i, n, k]
            )
            for i, w in enumerate((w_gate, w_up))
        ]

    for k in range(4):
        for copy in piece_copies(k) + weight_copies(0, k):
            copy.start()
    notes = pltpu.make_async_copy(
        notes_far.at[:, pl.ds(STATE, NOTES), :], notes_ref, sems.at[pieces]
    )
    notes.start()
    for n in range(1, tiles):
        for k in range(4):
            for copy in weight_copies(n, k):
                copy.start()

    shape = (rows, rows)
    earlier = (iota(shape, 1) < iota(shape, 0)).astype(F32)
    across = iota(shape, 1)
    diagonal = iota(shape, 0) == across
    out_copies = []
    for n in range(tiles):
        cut = slice(n * TILE, (n + 1) * TILE)
        gate = upper = None
        for k in range(4):
            if n == 0:
                finished(piece_copies(k))
            finished(weight_copies(n, k))
            block = rows_ref[:, k * depth : (k + 1) * depth]
            more = dot16(block, held_ref[0, n, k])
            gate = more if k == 0 else gate + more
            more = dot16(block, held_ref[1, n, k])
            upper = more if k == 0 else upper + more
        hid_ref[...] = (silu(gate) * upper).astype(BF16)
        if n == 0:
            notes.wait()
        for place in range(blocks):
            side, turn = place // 4, place % 4
            block = here ^ (2 * turn + side)
            if n == 0:
                line = notes_ref[block][1:2, :]
                mine = me.astype(F32)
                named = ((line[:, :rows] == mine) | (line[:, rows : 2 * rows] == mine)).astype(F32)
                column = jnp.sum(jnp.where(diagonal, named, 0.0), axis=1, keepdims=True)
                position = jnp.sum(earlier * named, axis=1, keepdims=True).astype(jnp.int32)
                pick_ref[place] = jnp.where(position == across, column, 0.0).astype(BF16)
            picked = dot16(pick_ref[place], hid_ref[place * rows : (place + 1) * rows], FIRST)
            at = pl.ds(pl.multiple_of(block * rows, rows), rows)
            out_ref[at, cut] = picked.astype(BF16)
        out_copies += started([out_ref.at[:, cut]], [out_far.at[0, :, cut]], sems, n)
    finished(out_copies)


def experts_by_tokens(moe_input, notes, w_gate, w_up):
    rows, columns = moe_input.shape
    ctx = lax.axis_size("ctx")
    joined = call(
        join_body,
        [array((2 * rows, columns), BF16)],
        (moe_input, swapped(moe_input, "ctx", 2)),
        fixed=1,
        sems=2,
        name="join",
    )[0]
    z = (joined, swapped(joined, "ctx", 4))
    x = [swapped(a, "ctx", 1) for a in z]
    y = [swapped(a, "exp", 2) for a in z]
    d = (swapped(y[0], "ctx", 1), swapped(x[1], "exp", 2))
    here = [*z, *x]
    there = [*y, *d]
    beside = [swapped(a, "exp", 1) for a in here]
    corner = [swapped(a, "exp", 1) for a in there]
    pieces = here + beside + there + corner
    hidden = w_gate.shape[2]
    length = ctx * rows
    return call(
        functools.partial(expert_body, len(pieces)),
        [array((1, length, hidden), BF16)],
        (w_gate, w_up, *pieces, notes),
        fixed=2,
        scratch=[
            pltpu.VMEM((length, 4 * columns), BF16),
            pltpu.VMEM((2, hidden // TILE, 4, columns, TILE), BF16),
            pltpu.VMEM((ctx, NOTES, notes.shape[2]), F32),
            pltpu.VMEM((ctx, rows, rows), BF16),
            pltpu.VMEM((length, TILE), BF16),
            pltpu.VMEM((length, hidden), BF16),
            pltpu.SemaphoreType.DMA((len(pieces) + 1,)),
            pltpu.SemaphoreType.DMA((2, hidden // TILE, 4)),
        ],
        flops=4 * length * 4 * columns * hidden,
        grant=36,
        name="experts",
    )[0]


def slot_matrix(pairs, expert, capacity):
    named = jnp.any(pairs == expert, axis=1).astype(jnp.int32)
    position = jnp.cumsum(named) - named
    hit = position[None, :] == jnp.arange(capacity, dtype=jnp.int32)[:, None]
    return (hit & (named[None, :] > 0)).astype(BF16)


def experts_by_slots(moe_input, pairs, w_gate, w_up):
    experts = lax.axis_size("exp")
    capacity = 4 * moe_input.shape[0] // experts
    pick = jax.vmap(lambda e: slot_matrix(pairs, e, capacity))(jnp.arange(experts))
    slots = jnp.einsum("eqt,td->eqd", pick, moe_input, preferred_element_type=F32)
    routed = lax.all_to_all(slots.astype(BF16), "exp", split_axis=0, concat_axis=2, tiled=True)
    rows = lax.all_gather(routed[0], "ctx", axis=0, tiled=True)
    gate = jnp.dot(rows, w_gate[0], preferred_element_type=F32)
    upper = jnp.dot(rows, w_up[0], preferred_element_type=F32)
    return (jax.nn.silu(gate) * upper).astype(BF16)[None]


def on_device(
    seq_input,
    b_input,
    c_input,
    conv_x,
    conv_bc,
    log_decay,
    skip_gain,
    norm_gain,
    moe_input,
    expert_ids,
    w_gate,
    w_up,
):
    ctx = lax.axis_size("ctx")
    by_tokens = lax.axis_size("exp") == 4 and ctx == 8
    tokens, channels = seq_input.shape
    ends = call(
        ends_body,
        [array((EDGE, channels + 2 * STATE), BF16)],
        (seq_input, b_input, c_input),
        fixed=3,
        sems=3,
        name="ends",
    )[0]
    before = lax.ppermute(ends, "ctx", [(i, i + 1) for i in range(ctx - 1)])
    mixed, notes = mixing(
        seq_input,
        b_input,
        c_input,
        before,
        conv_x,
        conv_bc,
        log_decay,
        skip_gain,
        norm_gain,
        expert_ids,
    )
    if by_tokens:
        hidden = experts_by_tokens(moe_input, notes, w_gate, w_up)
    else:
        hidden = experts_by_slots(moe_input, expert_ids, w_gate, w_up)
    return (mixed, hidden)


def solution(mesh):
    in_specs = (
        P("ctx", "exp"),
        P("ctx", None),
        P("ctx", None),
        P(None, "exp"),
        P(),
        P("exp", "ctx"),
        P("exp"),
        P("exp"),
        P("ctx", "exp"),
        P("ctx", None),
        P("exp", None, "ctx"),
        P("exp", None, "ctx"),
    )
    out_specs = (P("ctx", "exp"), P("exp", None, "ctx"))
    return jax.shard_map(
        on_device, mesh=mesh, in_specs=in_specs, out_specs=out_specs, check_vma=False
    )
```

```python
import functools
import math

import jax
import jax.numpy as jnp
from jax import lax
from jax.experimental import pallas as pl
from jax.experimental.pallas import tpu as pltpu
from jax.sharding import PartitionSpec as P

HDIM = 64
STATE = 128
KCONV = 4
EDGE = 16
NOTES = 8

F32 = jnp.float32
BF16 = jnp.bfloat16


def dot16(a, b, contract=((1,), (0,))):
    return lax.dot_general(a, b, (contract, ((), ())), preferred_element_type=F32)


def halves(value):
    high = value.astype(BF16)
    return high, (value - high.astype(F32)).astype(BF16)


def dot(a, b, contract=((1,), (0,))):
    a_high, a_low = halves(a)
    b_high, b_low = halves(b)
    cross = dot16(a_high, b_low, contract) + dot16(a_low, b_high, contract)
    return dot16(a_high, b_high, contract) + cross


def dot_exact(a, b, contract=((1,), (0,))):
    high, rest = halves(a)
    low = (a - high.astype(F32) - rest.astype(F32)).astype(BF16)
    return dot16(high, b, contract) + (dot16(rest, b, contract) + dot16(low, b, contract))


def dot_left(a, b, contract=((1,), (0,))):
    high, low = halves(a)
    return dot16(high, b, contract) + dot16(low, b, contract)


FIRST = ((0,), (0,))


def iota(shape, axis):
    return lax.broadcasted_iota(jnp.int32, shape, axis)


def head_spread(heads):
    shape = (heads, heads * HDIM)
    return (iota(shape, 1) // HDIM == iota(shape, 0)).astype(BF16)


def upper_ones(length):
    return (iota((length, length), 0) <= iota((length, length), 1)).astype(BF16)


def silu(value):
    return value / (1.0 + jnp.exp(-value))


def one_minus_exp(value):
    series = jnp.ones_like(value)
    for n in range(8, 1, -1):
        series = 1.0 + value * series * (1.0 / n)
    return jnp.where(value > -0.25, -value * series, 1.0 - jnp.exp(value))


def started(sources, targets, sems, first=0):
    copies = []
    for i, (source, target) in enumerate(zip(sources, targets)):
        copies.append(pltpu.make_async_copy(source, target, sems.at[first + i]))
        copies[-1].start()
    return copies


def finished(copies):
    for copy in copies:
        copy.wait()


def call(body, outs, args, fixed=0, scratch=(), sems=0, flops=0, grant=8, near=False, name=None):
    moved = sum(math.prod(a.shape) * a.dtype.itemsize for a in (*args, *outs))
    scratch = list(scratch) + ([pltpu.SemaphoreType.DMA((sems,))] if sems else [])
    space = pltpu.VMEM if near else pl.ANY
    args = [
        pltpu.with_memory_space_constraint(a, pltpu.HBM) if i < fixed else a
        for i, a in enumerate(args)
    ]
    spaces = [pltpu.HBM if i < fixed else space for i in range(len(args))]
    return pl.pallas_call(
        body,
        out_shape=outs,
        in_specs=[pl.BlockSpec(memory_space=s) for s in spaces],
        out_specs=[pl.BlockSpec(memory_space=space)] * len(outs),
        scratch_shapes=scratch,
        compiler_params=pltpu.CompilerParams(vmem_limit_bytes=grant * 2**20),
        cost_estimate=pl.CostEstimate(flops=flops, bytes_accessed=moved, transcendentals=0),
        name=name,
    )(*args)


def room(arrays):
    return [pltpu.VMEM(a.shape, a.dtype) for a in arrays]


def array(shape, dtype):
    return jax.ShapeDtypeStruct(shape, dtype)


def ends_body(x_ref, b_ref, c_ref, ends_ref, sems):
    tokens, channels = x_ref.shape
    cut = pl.ds(tokens - EDGE, EDGE)
    finished(
        started(
            [x_ref.at[cut, :], b_ref.at[cut, :], c_ref.at[cut, :]],
            [
                ends_ref.at[:, pl.ds(0, channels)],
                ends_ref.at[:, pl.ds(channels, STATE)],
                ends_ref.at[:, pl.ds(channels + STATE, STATE)],
            ],
            sems,
        )
    )


def local_body(by_tokens, count, *refs):
    far, outs, rest = refs[:count], refs[count : count + 4], refs[count + 4 :]
    near, scratch, pad_ref, sems = rest[:count], rest[count : count + 4], rest[-2], rest[-1]
    copies = started(far, near, sems)
    x_ref, b_ref, c_ref, taps_ref, taps_bc_ref, logs_ref, skip_ref, ids_ref, ends_ref = near
    pre_ref, decay_ref, c_out_ref, state_ref = scratch
    tokens, channels = x_ref.shape
    heads = logs_ref.shape[0]
    finished(copies)
    pad_ref[0:8, :] = ends_ref[...].astype(F32)[EDGE - 8 : EDGE]
    pad_ref[8 : 8 + tokens, :channels] = x_ref[...].astype(F32)
    pad_ref[8 : 8 + tokens, channels : channels + STATE] = b_ref[...].astype(F32)
    pad_ref[8 : 8 + tokens, channels + STATE :] = c_ref[...].astype(F32)

    def conv(taps, start, stop):
        total = jnp.zeros((tokens, stop - start), F32)
        for k in range(KCONV):
            first = 8 - (KCONV - 1) + k
            total = total + taps[k : k + 1] * pad_ref[first : first + tokens, start:stop]
        return silu(total)

    bc = conv(taps_bc_ref[...], channels, channels + 2 * STATE)
    bmat, cmat = bc[:, :STATE], bc[:, STATE:]
    c_out_ref[...] = cmat
    logs = logs_ref[...]
    inflow = jnp.sqrt(one_minus_exp(2.0 * logs))
    row = dot_exact(logs, upper_ones(tokens))
    column = row.T
    total = row[:, tokens - 1 :]
    spread = head_spread(heads)
    decay_ref[...] = dot_left(jnp.exp(row), spread, FIRST)
    copies = started(scratch[1:3], outs[1:3], sems)

    xconv = conv(taps_ref[...], 0, channels)
    pad_ref[:tokens, :channels] = xconv
    drive = xconv * dot_left(inflow, spread, FIRST)
    pre_ref[...] = drive
    fresh = drive * dot_left(jnp.exp(total - row), spread, FIRST)
    state_ref[:STATE] = dot(bmat, fresh, FIRST)
    notes = dot_exact(jnp.exp(jnp.broadcast_to(total, (heads, NOTES))), spread, FIRST)
    if by_tokens:
        ids = ids_ref[...].astype(F32)
        line = jnp.concatenate([ids[0:1], ids[1:2]] * (channels // (2 * ids.shape[1])), axis=1)
        notes = jnp.where(iota(notes.shape, 0) == 1, line, notes)
    state_ref[STATE:] = notes
    copies += started(scratch[3:], outs[3:], sems, 2)

    skip = dot_exact(skip_ref[...], spread)
    meet = dot(cmat, bmat, ((1,), (1,)))
    lower = iota((tokens, tokens), 0) >= iota((tokens, tokens), 1)
    left = iota((tokens, 2 * HDIM), 1) < HDIM
    for pair in range(heads // 2):
        cut = slice(pair * 2 * HDIM, (pair + 1) * 2 * HDIM)
        d_high, d_low = halves(pre_ref[:, cut])
        both = []
        for h in (2 * pair, 2 * pair + 1):
            gap = column[:, h : h + 1] - row[h : h + 1, :]
            mix = jnp.where(lower, jnp.exp(gap), 0.0) * meet
            m_high, m_low = halves(mix)
            both.append(dot16(m_high, d_high) + dot16(m_high, d_low) + dot16(m_low, d_high))
        direct = skip[:, cut] * pad_ref[:tokens, cut]
        pre_ref[:, cut] = direct + jnp.where(left, both[0], both[1])
    finished(copies + started(scratch[:1], outs[:1], sems, 3))


def slabs_body(state_ref, after_ref, slabs_ref, sems):
    parts, _, share = slabs_ref.shape
    cuts = [state_ref.at[:, pl.ds(i * share, share)] for i in range(parts)]
    finished(started(cuts, [slabs_ref.at[i] for i in range(parts)], sems))


def prefix_body(parts_ref, starts_ref):
    ctx, rows, share = starts_ref.shape
    state = jnp.zeros((rows, share), F32)
    for i in range(ctx):
        starts_ref[i] = state
        if i < ctx - 1:
            state = parts_ref[i, STATE : STATE + 1] * state + parts_ref[i, :STATE]


def back_body(cuts, gain_far, pre_far, decay_far, c_far, start_far, out_far, *rest):
    far = (start_far, c_far, pre_far, decay_far, gain_far)
    start_ref, c_ref, pre_ref, decay_ref, gain_ref, out_ref, sems = rest
    copies = started(far, rest[:5], sems)
    channels = pre_ref.shape[1]
    width = min(channels, 4 * HDIM)
    group = (iota((width, width), 0) // HDIM == iota((width, width), 1) // HDIM).astype(BF16)
    finished(copies)
    c_high, c_low = halves(c_ref[...])
    copies = []
    for i in range(channels // width):
        cut = slice(i * width, (i + 1) * width)
        if cuts:
            start = jnp.concatenate([start_ref[2 * i], start_ref[2 * i + 1]], axis=1)
        else:
            start = start_ref[:, cut]
        s_high, s_low = halves(start)
        carried = dot16(c_high, s_high) + dot16(c_high, s_low) + dot16(c_low, s_high)
        pre = pre_ref[:, cut] + carried * decay_ref[:, cut]
        mean = dot_left(pre * pre, group) * (1.0 / HDIM)
        out_ref[:, cut] = (pre * lax.rsqrt(mean + 1e-05) * gain_ref[:, cut]).astype(BF16)
        copies += started([out_ref.at[:, cut]], [out_far.at[:, cut]], sems, i)
    finished(copies)


def mixing(
    seq_input, b_input, c_input, before, conv_x, conv_bc, log_decay, skip, gain, ids, after
):
    tokens, channels = seq_input.shape
    heads = skip.shape[0]
    ctx = lax.axis_size("ctx")
    share = channels // ctx
    cuts = after is not None
    outs = [
        pltpu.HBM((tokens, channels), F32),
        pltpu.HBM((tokens, channels), F32),
        pltpu.HBM((tokens, STATE), F32),
        array((STATE + NOTES, channels), F32),
    ]
    args = (seq_input, b_input, c_input, conv_x, conv_bc, log_decay)
    args = (*args, skip.reshape(1, heads), ids.T, before)
    pre, decay, cmat, state = call(
        functools.partial(local_body, cuts, len(args)),
        outs,
        args,
        fixed=len(args) - 1,
        scratch=room(args) + room(outs) + [pltpu.VMEM((8 + tokens, channels + 2 * STATE), F32)],
        sems=len(args),
        flops=10**10,
        grant=20,
        name="local",
    )
    if cuts:
        slabs = call(
            slabs_body,
            [array((ctx, STATE + NOTES, share), F32)],
            (state, after),
            sems=ctx,
            name="slabs",
        )[0]
    else:
        slabs = state.reshape(STATE + NOTES, ctx, share).transpose(1, 0, 2)
    parts = lax.all_to_all(slabs, "ctx", split_axis=0, concat_axis=0, tiled=True)
    starts = call(
        prefix_body,
        [array((ctx, STATE, share), F32)],
        (parts,),
        near=True,
        name="prefix",
    )[0]
    start = lax.all_to_all(starts, "ctx", split_axis=0, concat_axis=0, tiled=True)
    if not cuts:
        start = start.transpose(1, 0, 2).reshape(STATE, channels)
    args = (gain.reshape(1, channels), pre, decay, cmat, start)
    outs = [array((tokens, channels), BF16)]
    mixed = call(
        functools.partial(back_body, cuts),
        outs,
        args,
        fixed=4,
        scratch=room([start, cmat, pre, decay, args[0]]) + room(outs),
        sems=5,
        flops=10**9,
        grant=16,
        name="back",
    )[0]
    return mixed, parts


TILE = 256


def join_body(a_ref, b_ref, out_ref, sems):
    rows = a_ref.shape[0]
    finished(
        started([a_ref, b_ref], [out_ref.at[pl.ds(0, rows), :], out_ref.at[pl.ds(rows, rows), :]], sems)
    )


def swapped(block, axis, bit):
    return lax.ppermute(block, axis, [(i, i ^ bit) for i in range(lax.axis_size(axis))])


def expert_body(pieces, *refs):
    (w_gate, w_up), far, (notes_far, out_far) = refs[:2], refs[2 : pieces + 2], refs[pieces + 2 : pieces + 4]
    rows_ref, held_ref, notes_ref, pick_ref, hid_ref, out_ref, sems, w_sems = refs[pieces + 4 :]
    length, width = rows_ref.shape
    depth = width // 4
    step = length // 4
    tiles = out_ref.shape[1] // TILE
    blocks = notes_ref.shape[0]
    rows = length // blocks
    me = lax.axis_index("exp")
    here = lax.axis_index("ctx")

    def piece_copies(k):
        cut = pl.ds(pl.multiple_of((me ^ k) * depth, depth), depth)
        targets = [rows_ref.at[pl.ds(i * step, step), cut] for i in range(4)]
        return [
            pltpu.make_async_copy(far[4 * k + i], targets[i], sems.at[4 * k + i]) for i in range(4)
        ]

    def weight_copies(n, i):
        w = (w_gate, w_up)[i]
        across = pl.ds(n * TILE, TILE)
        cuts = [pl.ds(k * depth, depth) for k in range(4)]
        return [
            pltpu.make_async_copy(
                w.at[0, cut, across], held_ref.at[i, n, cut, :], w_sems.at[i, n, k]
            )
            for k, cut in enumerate(cuts)
        ]

    for k in range(4):
        for copy in piece_copies(k):
            copy.start()
    notes = pltpu.make_async_copy(
        notes_far.at[:, pl.ds(STATE, NOTES), :], notes_ref, sems.at[pieces]
    )
    notes.start()
    for n in range(tiles):
        for i in range(2):
            for copy in weight_copies(n, i):
                copy.start()

    shape = (rows, rows)
    earlier = (iota(shape, 1) < iota(shape, 0)).astype(F32)
    across = iota(shape, 1)
    diagonal = iota(shape, 0) == across
    out_copies = []
    for n in range(tiles):
        cut = slice(n * TILE, (n + 1) * TILE)
        if n == 0:
            for k in range(4):
                finished(piece_copies(k))
        finished(weight_copies(n, 0))
        gate = dot16(rows_ref[...], held_ref[0, n])
        finished(weight_copies(n, 1))
        upper = dot16(rows_ref[...], held_ref[1, n])
        hid_ref[...] = (silu(gate) * upper).astype(BF16)
        if n == 0:
            notes.wait()
        for place in range(blocks):
            side, turn = place // 4, place % 4
            block = here ^ (2 * turn + side)
            if n == 0:
                line = notes_ref[block][1:2, :]
                mine = me.astype(F32)
                named = ((line[:, :rows] == mine) | (line[:, rows : 2 * rows] == mine)).astype(F32)
                column = jnp.sum(jnp.where(diagonal, named, 0.0), axis=1, keepdims=True)
                position = jnp.sum(earlier * named, axis=1, keepdims=True).astype(jnp.int32)
                pick_ref[place] = jnp.where(position == across, column, 0.0).astype(BF16)
            picked = dot16(pick_ref[place], hid_ref[place * rows : (place + 1) * rows], FIRST)
            at = pl.ds(pl.multiple_of(block * rows, rows), rows)
            out_ref[at, cut] = picked.astype(BF16)
        out_copies += started([out_ref.at[:, cut]], [out_far.at[0, :, cut]], sems, n)
    finished(out_copies)


def along_z(moe_input):
    rows, columns = moe_input.shape
    joined = call(
        join_body,
        [array((2 * rows, columns), BF16)],
        (moe_input, swapped(moe_input, "ctx", 2)),
        fixed=1,
        sems=2,
        name="join",
    )[0]
    return joined, swapped(joined, "ctx", 4)


def experts_by_tokens(z, notes, w_gate, w_up):
    ctx = lax.axis_size("ctx")
    rows, columns = z[0].shape[0] // 2, z[0].shape[1]
    x = [swapped(a, "ctx", 1) for a in z]
    y = [swapped(a, "exp", 2) for a in z]
    d = (swapped(y[0], "ctx", 1), swapped(x[1], "exp", 2))
    here = [*z, *x]
    there = [*y, *d]
    beside = [swapped(a, "exp", 1) for a in here]
    corner = [swapped(a, "exp", 1) for a in there]
    pieces = here + beside + there + corner
    hidden = w_gate.shape[2]
    length = ctx * rows
    return call(
        functools.partial(expert_body, len(pieces)),
        [array((1, length, hidden), BF16)],
        (w_gate, w_up, *pieces, notes),
        fixed=2,
        scratch=[
            pltpu.VMEM((length, 4 * columns), BF16),
            pltpu.VMEM((2, hidden // TILE, 4 * columns, TILE), BF16),
            pltpu.VMEM((ctx, NOTES, notes.shape[2]), F32),
            pltpu.VMEM((ctx, rows, rows), BF16),
            pltpu.VMEM((length, TILE), BF16),
            pltpu.VMEM((length, hidden), BF16),
            pltpu.SemaphoreType.DMA((len(pieces) + 1,)),
            pltpu.SemaphoreType.DMA((2, hidden // TILE, 4)),
        ],
        flops=4 * length * 4 * columns * hidden,
        grant=36,
        name="experts",
    )[0]


def slot_matrix(pairs, expert, capacity):
    named = jnp.any(pairs == expert, axis=1).astype(jnp.int32)
    position = jnp.cumsum(named) - named
    hit = position[None, :] == jnp.arange(capacity, dtype=jnp.int32)[:, None]
    return (hit & (named[None, :] > 0)).astype(BF16)


def experts_by_slots(moe_input, pairs, w_gate, w_up):
    experts = lax.axis_size("exp")
    capacity = 4 * moe_input.shape[0] // experts
    pick = jax.vmap(lambda e: slot_matrix(pairs, e, capacity))(jnp.arange(experts))
    slots = jnp.einsum("eqt,td->eqd", pick, moe_input, preferred_element_type=F32)
    routed = lax.all_to_all(slots.astype(BF16), "exp", split_axis=0, concat_axis=2, tiled=True)
    rows = lax.all_gather(routed[0], "ctx", axis=0, tiled=True)
    gate = jnp.dot(rows, w_gate[0], preferred_element_type=F32)
    upper = jnp.dot(rows, w_up[0], preferred_element_type=F32)
    return (jax.nn.silu(gate) * upper).astype(BF16)[None]


def on_device(
    seq_input,
    b_input,
    c_input,
    conv_x,
    conv_bc,
    log_decay,
    skip_gain,
    norm_gain,
    moe_input,
    expert_ids,
    w_gate,
    w_up,
):
    ctx = lax.axis_size("ctx")
    by_tokens = lax.axis_size("exp") == 4 and ctx == 8
    tokens, channels = seq_input.shape
    ends = call(
        ends_body,
        [array((EDGE, channels + 2 * STATE), BF16)],
        (seq_input, b_input, c_input),
        fixed=3,
        sems=3,
        name="ends",
    )[0]
    before = lax.ppermute(ends, "ctx", [(i, i + 1) for i in range(ctx - 1)])
    z = along_z(moe_input) if by_tokens else (None, None)
    mixed, notes = mixing(
        seq_input,
        b_input,
        c_input,
        before,
        conv_x,
        conv_bc,
        log_decay,
        skip_gain,
        norm_gain,
        expert_ids,
        z[1],
    )
    if by_tokens:
        hidden = experts_by_tokens(z, notes, w_gate, w_up)
    else:
        hidden = experts_by_slots(moe_input, expert_ids, w_gate, w_up)
    return (mixed, hidden)


def solution(mesh):
    in_specs = (
        P("ctx", "exp"),
        P("ctx", None),
        P("ctx", None),
        P(None, "exp"),
        P(),
        P("exp", "ctx"),
        P("exp"),
        P("exp"),
        P("ctx", "exp"),
        P("ctx", None),
        P("exp", None, "ctx"),
        P("exp", None, "ctx"),
    )
    out_specs = (P("ctx", "exp"), P("exp", None, "ctx"))
    return jax.shard_map(
        on_device, mesh=mesh, in_specs=in_specs, out_specs=out_specs, check_vma=False
    )
```

```python
import functools
import math

import jax
import jax.numpy as jnp
from jax import lax
from jax.experimental import pallas as pl
from jax.experimental.pallas import tpu as pltpu
from jax.sharding import PartitionSpec as P

HDIM = 64
STATE = 128
KCONV = 4
EDGE = 16
NOTES = 8

F32 = jnp.float32
BF16 = jnp.bfloat16


def dot16(a, b, contract=((1,), (0,))):
    return lax.dot_general(a, b, (contract, ((), ())), preferred_element_type=F32)


def halves(value):
    high = value.astype(BF16)
    return high, (value - high.astype(F32)).astype(BF16)


def dot(a, b, contract=((1,), (0,))):
    a_high, a_low = halves(a)
    b_high, b_low = halves(b)
    cross = dot16(a_high, b_low, contract) + dot16(a_low, b_high, contract)
    return dot16(a_high, b_high, contract) + cross


def dot_exact(a, b, contract=((1,), (0,))):
    high, rest = halves(a)
    low = (a - high.astype(F32) - rest.astype(F32)).astype(BF16)
    return dot16(high, b, contract) + (dot16(rest, b, contract) + dot16(low, b, contract))


def dot_left(a, b, contract=((1,), (0,))):
    high, low = halves(a)
    return dot16(high, b, contract) + dot16(low, b, contract)


FIRST = ((0,), (0,))


def iota(shape, axis):
    return lax.broadcasted_iota(jnp.int32, shape, axis)


def head_spread(heads):
    shape = (heads, heads * HDIM)
    return (iota(shape, 1) // HDIM == iota(shape, 0)).astype(BF16)


def upper_ones(length):
    return (iota((length, length), 0) <= iota((length, length), 1)).astype(BF16)


def silu(value):
    return value / (1.0 + jnp.exp(-value))


def one_minus_exp(value):
    series = jnp.ones_like(value)
    for n in range(8, 1, -1):
        series = 1.0 + value * series * (1.0 / n)
    return jnp.where(value > -0.25, -value * series, 1.0 - jnp.exp(value))


def started(sources, targets, sems, first=0):
    copies = []
    for i, (source, target) in enumerate(zip(sources, targets)):
        copies.append(pltpu.make_async_copy(source, target, sems.at[first + i]))
        copies[-1].start()
    return copies


def finished(copies):
    for copy in copies:
        copy.wait()


def call(
    body,
    outs,
    args,
    fixed=0,
    held=0,
    near_args=0,
    near_outs=0,
    scratch=(),
    sems=0,
    flops=0,
    grant=8,
    near=False,
    name=None,
):
    moved = sum(math.prod(a.shape) * a.dtype.itemsize for a in (*args, *outs))
    scratch = list(scratch) + ([pltpu.SemaphoreType.DMA((sems,))] if sems else [])
    space = pltpu.VMEM if near else pl.ANY
    spaces = [pltpu.HBM] * fixed + [pltpu.VMEM] * held
    args = [
        pltpu.with_memory_space_constraint(a, spaces[i]) if i < len(spaces) else a
        for i, a in enumerate(args)
    ]
    spaces += [space] * (len(args) - near_args - len(spaces)) + [pltpu.VMEM] * near_args
    out_spaces = [space] * (len(outs) - near_outs) + [pltpu.VMEM] * near_outs
    return pl.pallas_call(
        body,
        out_shape=outs,
        in_specs=[pl.BlockSpec(memory_space=s) for s in spaces],
        out_specs=[pl.BlockSpec(memory_space=s) for s in out_spaces],
        scratch_shapes=scratch,
        compiler_params=pltpu.CompilerParams(vmem_limit_bytes=grant * 2**20),
        cost_estimate=pl.CostEstimate(flops=flops, bytes_accessed=moved, transcendentals=0),
        name=name,
    )(*args)


def room(arrays):
    return [pltpu.VMEM(a.shape, a.dtype) for a in arrays]


def array(shape, dtype):
    return jax.ShapeDtypeStruct(shape, dtype)


def ends_body(x_ref, b_ref, c_ref, ends_ref, sems):
    tokens, channels = x_ref.shape
    cut = pl.ds(tokens - EDGE, EDGE)
    finished(
        started(
            [x_ref.at[cut, :], b_ref.at[cut, :], c_ref.at[cut, :]],
            [
                ends_ref.at[:, pl.ds(0, channels)],
                ends_ref.at[:, pl.ds(channels, STATE)],
                ends_ref.at[:, pl.ds(channels + STATE, STATE)],
            ],
            sems,
        )
    )


def front_body(paired, count, *refs):
    far, outs, rest = refs[:count], refs[count : count + 3], refs[count + 3 :]
    ends = rest[: 1 + paired]
    rest = rest[1 + paired :]
    near, scratch, pad_ref, sems = rest[:count], rest[count : count + 3], rest[-2], rest[-1]
    copies = started(far, near, sems)
    x_ref, b_ref, c_ref, taps_ref, taps_bc_ref, logs_ref, ids_ref, ends_ref = near
    xconv_ref, bc_ref, lines_ref = scratch
    tokens, channels = x_ref.shape
    heads = logs_ref.shape[0]
    finished(copies)
    pad_ref[0:8, :] = ends_ref[...].astype(F32)[EDGE - 8 : EDGE]
    pad_ref[8 : 8 + tokens, :channels] = x_ref[...].astype(F32)
    pad_ref[8 : 8 + tokens, channels : channels + STATE] = b_ref[...].astype(F32)
    pad_ref[8 : 8 + tokens, channels + STATE :] = c_ref[...].astype(F32)

    def conv(taps, start, stop):
        total = jnp.zeros((tokens, stop - start), F32)
        for k in range(KCONV):
            first = 8 - (KCONV - 1) + k
            total = total + taps[k : k + 1] * pad_ref[first : first + tokens, start:stop]
        return silu(total)

    bc = conv(taps_bc_ref[...], channels, channels + 2 * STATE)
    bc_ref[...] = bc
    xconv = conv(taps_ref[...], 0, channels)
    xconv_ref[...] = xconv
    logs = logs_ref[...]
    inflow = jnp.sqrt(one_minus_exp(2.0 * logs))
    row = dot_exact(logs, upper_ones(tokens))
    lines_ref[0] = row
    lines_ref[1] = inflow
    copies = started(scratch, outs, sems)
    total = row[:, tokens - 1 :]
    spread = head_spread(heads)
    fresh = xconv * dot_left(inflow * jnp.exp(total - row), spread, FIRST)
    state = dot(bc[:, :STATE], fresh, FIRST)
    total = jnp.broadcast_to(total, (heads, NOTES))
    if paired:
        total = dot_exact(total, spread, FIRST)
        half = channels // 2
        side = lax.axis_index("ctx") % 2
        ids = ids_ref[...].astype(F32)
        line = jnp.concatenate([ids[0:1], ids[1:2]], axis=1)
        line = jnp.concatenate([line] * (half // line.shape[1]), axis=1)
        for ref, first in ((ends[0], side == 0), (ends[1], side != 0)):
            mine = jnp.where(first, state[:, :half], state[:, half:])
            logsum = jnp.where(first, total[:1, :half], total[:1, half:])
            if ref is ends[0]:
                put(ref, mine, logsum, line)
            else:
                send(ref, mine, logsum, line)
    else:
        ends[0][:STATE] = state
        ends[0][STATE:] = dot_exact(jnp.exp(total), spread, FIRST)
    finished(copies)


def put(ref, state, logsum, line):
    ref[:STATE] = state
    at = iota((NOTES, state.shape[1]), 0)
    ref[STATE:] = jnp.where(at == 0, logsum, line)


def send(ref, state, logsum, line):
    largest = jnp.max(jnp.abs(state), axis=0, keepdims=True)
    power = jnp.ceil(jnp.log2(jnp.maximum(largest, 1e-30))) - 15.0
    whole = jnp.clip(jnp.round(state * jnp.exp2(-power)), -32767.0, 32767.0)
    ref[:STATE] = whole.astype(jnp.int32).astype(jnp.int16)
    logsum = jnp.round(jnp.maximum(logsum, -128.0) * 2.0**22).astype(jnp.int32)
    at = iota((16, state.shape[1]), 0)
    notes = jnp.where(at == 0, power.astype(jnp.int32), line.astype(jnp.int32))
    notes = jnp.where(at == 1, logsum >> 15, jnp.where(at == 2, logsum & 32767, notes))
    ref[STATE:] = notes.astype(jnp.int16)


def taken(ref):
    return ref[:STATE], ref[STATE : STATE + 1], ref[STATE + 1 : STATE + 2]


def received(ref):
    notes = ref[STATE:].astype(jnp.int32).astype(F32)
    state = ref[:STATE].astype(jnp.int32).astype(F32) * jnp.exp2(notes[0:1])
    return state, notes[1:2] * 2.0**-7 + notes[2:3] * 2.0**-22, notes[3:4]


def ordered(first, own, other):
    return [jnp.where(first, a, b) for a, b in zip(own, other)], [
        jnp.where(first, b, a) for a, b in zip(own, other)
    ]


def together(first, own, other, width):
    (a, a_log, a_line), (b, b_log, b_line) = ordered(first, own, other)
    line = jnp.concatenate([a_line[:, :width], b_line[:, :width]], axis=1)
    line = jnp.concatenate([line] * (a.shape[1] // line.shape[1]), axis=1)
    return jnp.exp(b_log) * a + b, a_log + b_log, line


def place():
    here = lax.axis_index("ctx")
    return here % 2, (here // 2) % 2, here // 4


def pair_body(width, own_ref, got_ref, pair_ref, sent_ref):
    x, _, _ = place()
    pair = together(x == 0, taken(own_ref), received(got_ref), width)
    put(pair_ref, *pair)
    send(sent_ref, *pair)


def four_body(width, pair_ref, got_ref, sent_ref):
    _, z, _ = place()
    send(sent_ref, *together(z == 0, taken(pair_ref), received(got_ref), 2 * width))


def turn_body(
    width, own_ref, got_ref, pair_ref, pair_got_ref, four_got_ref, mine_ref, sent_ref, ids_ref
):
    x, z, zz = place()
    pair, pair_got, four_got = taken(pair_ref), received(pair_got_ref), received(four_got_ref)
    line = together(z == 0, pair, pair_got, 2 * width)[2]
    lines = ordered(zz == 0, [line], [four_got[2]])
    at = iota(ids_ref.shape, 0)
    ids = jnp.zeros(ids_ref.shape, F32)
    for i in range(ids_ref.shape[0]):
        part = lines[i // 4][0][:, i % 4 * width : (i % 4 + 1) * width]
        ids = jnp.where(at == i, part, ids)
    ids_ref[...] = ids

    before = jnp.where(zz == 0, 0.0, four_got[0])
    before = jnp.where(z == 0, before, jnp.exp(pair_got[1]) * before + pair_got[0])
    (first, first_log), _ = ordered(x == 0, taken(own_ref)[:2], received(got_ref)[:2])
    after = jnp.exp(first_log) * before + first
    mine_ref[...] = jnp.where(x == 0, before, after)
    other = jnp.where(x == 0, after, before)
    send(sent_ref, other, jnp.zeros_like(first_log), jnp.zeros_like(first_log))


def inner_body(skip_far, xconv_far, bc_far, lines_far, pre_far, decay_far, *rest):
    far = (skip_far, xconv_far, bc_far, lines_far)
    skip_ref, xconv_ref, bc_ref, lines_ref, pre_ref, decay_ref, sems = rest
    finished(started(far, rest[:4], sems))
    tokens, channels = xconv_ref.shape
    heads = channels // HDIM
    row = lines_ref[0]
    column = row.T
    spread = head_spread(heads)
    decay_ref[...] = dot_left(jnp.exp(row), spread, FIRST)
    copies = started([decay_ref], [decay_far], sems)
    inflow = dot_left(lines_ref[1], spread, FIRST)
    skip = dot_exact(skip_ref[...], spread)
    meet = dot(bc_ref[:, STATE:], bc_ref[:, :STATE], ((1,), (1,)))
    lower = iota((tokens, tokens), 0) >= iota((tokens, tokens), 1)
    left = iota((tokens, 2 * HDIM), 1) < HDIM
    for pair in range(heads // 2):
        cut = slice(pair * 2 * HDIM, (pair + 1) * 2 * HDIM)
        xconv = xconv_ref[:, cut]
        d_high, d_low = halves(xconv * inflow[:, cut])
        both = []
        for h in (2 * pair, 2 * pair + 1):
            gap = column[:, h : h + 1] - row[h : h + 1, :]
            mix = jnp.where(lower, jnp.exp(gap), 0.0) * meet
            m_high, m_low = halves(mix)
            both.append(dot16(m_high, d_high) + dot16(m_high, d_low) + dot16(m_low, d_high))
        pre_ref[:, cut] = skip[:, cut] * xconv + jnp.where(left, both[0], both[1])
    finished(copies + started([pre_ref], [pre_far], sems, 1))


def prefix_body(parts_ref, starts_ref):
    ctx, rows, share = starts_ref.shape
    state = jnp.zeros((rows, share), F32)
    for i in range(ctx):
        starts_ref[i] = state
        if i < ctx - 1:
            state = parts_ref[i, STATE : STATE + 1] * state + parts_ref[i, :STATE]


def back_body(paired, gain_far, pre_far, decay_far, bc_far, *rest):
    starts, (out_far, *rest) = rest[: 1 + paired], rest[1 + paired :]
    far = (gain_far, pre_far, decay_far, bc_far)
    gain_ref, pre_ref, decay_ref, bc_ref, out_ref, sems = rest
    copies = started(far, rest[:4], sems)
    channels = pre_ref.shape[1]
    width = min(channels, 4 * HDIM)
    group = (iota((width, width), 0) // HDIM == iota((width, width), 1) // HDIM).astype(BF16)
    if paired:
        side = lax.axis_index("ctx") % 2
        mine, other = starts[0][...], received(starts[1])[0]
        start = [jnp.where(side == 0, mine, other), jnp.where(side == 0, other, mine)]
        start = jnp.concatenate(start, axis=1)
    else:
        start = starts[0][...]
    finished(copies)
    c_high, c_low = halves(bc_ref[:, STATE:])
    copies = []
    for i in range(channels // width):
        cut = slice(i * width, (i + 1) * width)
        s_high, s_low = halves(start[:, cut])
        carried = dot16(c_high, s_high) + dot16(c_high, s_low) + dot16(c_low, s_high)
        pre = pre_ref[:, cut] + carried * decay_ref[:, cut]
        mean = dot_left(pre * pre, group) * (1.0 / HDIM)
        out_ref[:, cut] = (pre * lax.rsqrt(mean + 1e-05) * gain_ref[:, cut]).astype(BF16)
        copies += started([out_ref.at[:, cut]], [out_far.at[:, cut]], sems, i)
    finished(copies)


def entering_by_pairs(keep, sent, width):
    pair_array, sent_array = array(keep.shape, F32), array(sent.shape, jnp.int16)
    got = swapped(sent, "ctx", 1)
    pair, sent = call(
        functools.partial(pair_body, width),
        [pair_array, sent_array],
        (keep, got),
        near=True,
        name="pair",
    )
    pair_got = swapped(sent, "ctx", 2)
    (sent,) = call(
        functools.partial(four_body, width), [sent_array], (pair, pair_got), near=True, name="four"
    )
    four_got = swapped(sent, "ctx", 4)
    mine, sent, ids = call(
        functools.partial(turn_body, width),
        [array((STATE, keep.shape[1]), F32), sent_array, array((8, width), F32)],
        (keep, got, pair, pair_got, four_got),
        near=True,
        name="turn",
    )
    return (mine, swapped(sent, "ctx", 1)), ids


def entering_by_rows(state):
    ctx = lax.axis_size("ctx")
    rows, channels = state.shape
    slabs = state.reshape(rows, ctx, channels // ctx).transpose(1, 0, 2)
    parts = lax.all_to_all(slabs, "ctx", split_axis=0, concat_axis=0, tiled=True)
    (starts,) = call(
        prefix_body,
        [array((ctx, STATE, channels // ctx), F32)],
        (parts,),
        near=True,
        name="prefix",
    )
    start = lax.all_to_all(starts, "ctx", split_axis=0, concat_axis=0, tiled=True)
    return start.transpose(1, 0, 2).reshape(STATE, channels)


def mixing(
    paired, seq_input, b_input, c_input, before, conv_x, conv_bc, log_decay, skip, gain, ids
):
    tokens, channels = seq_input.shape
    heads = skip.shape[0]
    width = 2 * ids.shape[0]
    outs = [
        array((tokens, channels), F32),
        array((tokens, 2 * STATE), F32),
        array((2, heads, tokens), F32),
    ]
    if paired:
        ends = [array((STATE + NOTES, channels // 2), F32)]
        ends.append(array((STATE + 16, channels // 2), jnp.int16))
    else:
        ends = [array((STATE + NOTES, channels), F32)]
    args = (seq_input, b_input, c_input, conv_x, conv_bc, log_decay, ids.T, before)
    xconv, bc, lines, *ends = call(
        functools.partial(front_body, paired, len(args)),
        outs + ends,
        args,
        fixed=len(args) - 1,
        near_outs=len(ends),
        scratch=room(args) + room(outs) + [pltpu.VMEM((8 + tokens, channels + 2 * STATE), F32)],
        sems=len(args),
        flops=10**9,
        grant=20,
        name="front",
    )
    if paired:
        starts, lines_of_ids = entering_by_pairs(*ends, width)
    else:
        starts, lines_of_ids = (entering_by_rows(ends[0]),), None
    args = (skip.reshape(1, heads), xconv, bc, lines)
    outs = [array((tokens, channels), F32)] * 2
    pre, decay = call(
        inner_body,
        outs,
        args,
        fixed=1,
        scratch=room(args) + room(outs),
        sems=4,
        flops=4 * 10**9,
        grant=16,
        name="inner",
    )
    args = (gain.reshape(1, channels), pre, decay, bc)
    outs = [array((tokens, channels), BF16)]
    (mixed,) = call(
        functools.partial(back_body, paired),
        outs,
        (*args, *starts),
        fixed=1,
        near_args=len(starts),
        scratch=room(args) + room(outs),
        sems=max(4, channels // (4 * HDIM)),
        flops=10**9,
        grant=16,
        name="back",
    )
    return mixed, lines_of_ids


TILE = 512


def join_body(a_ref, b_ref, out_ref, sems):
    rows = a_ref.shape[0]
    finished(
        started([a_ref, b_ref], [out_ref.at[pl.ds(0, rows), :], out_ref.at[pl.ds(rows, rows), :]], sems)
    )


def swapped(block, axis, bit):
    return lax.ppermute(block, axis, [(i, i ^ bit) for i in range(lax.axis_size(axis))])


def expert_body(pieces, w_gate, w_up, *refs):
    far, ids_ref, out_far = refs[:pieces], refs[pieces], refs[pieces + 1]
    pick_ref, hid_ref, out_ref, sems = refs[pieces + 2 :]
    length, hidden = out_ref.shape
    blocks = ids_ref.shape[0]
    rows = length // blocks
    depth = far[0].shape[1]
    me = lax.axis_index("exp")
    here = lax.axis_index("ctx")
    downs = [pl.ds(pl.multiple_of((me ^ k) * depth, depth), depth) for k in range(4)]

    shape = (rows, rows)
    earlier = (iota(shape, 1) < iota(shape, 0)).astype(F32)
    across = iota(shape, 1)
    diagonal = iota(shape, 0) == across
    turns = [here ^ (2 * (i % 4) + i // 4) for i in range(blocks)]
    for i, block in enumerate(turns):
        line = ids_ref[pl.ds(block, 1), :]
        mine = me.astype(F32)
        named = ((line[:, :rows] == mine) | (line[:, rows:] == mine)).astype(F32)
        column = jnp.sum(jnp.where(diagonal, named, 0.0), axis=1, keepdims=True)
        position = jnp.sum(earlier * named, axis=1, keepdims=True).astype(jnp.int32)
        pick_ref[i] = jnp.where(position == across, column, 0.0).astype(BF16)

    out_copies = []
    for n in range(hidden // TILE):
        cut = slice(n * TILE, (n + 1) * TILE)
        gate = upper = None
        for k in range(4):
            block = jnp.concatenate([piece[...] for piece in far[4 * k : 4 * k + 4]], axis=0)
            more = dot16(block, w_gate[0, downs[k], cut])
            gate = more if k == 0 else gate + more
            more = dot16(block, w_up[0, downs[k], cut])
            upper = more if k == 0 else upper + more
        hid_ref[...] = (silu(gate) * upper).astype(BF16)
        for i, block in enumerate(turns):
            picked = dot16(pick_ref[i], hid_ref[i * rows : (i + 1) * rows], FIRST)
            out_ref[pl.ds(pl.multiple_of(block * rows, rows), rows), cut] = picked.astype(BF16)
        out_copies += started([out_ref.at[:, cut]], [out_far.at[0, :, cut]], sems, n)
    finished(out_copies)


def along_z(moe_input):
    rows, columns = moe_input.shape
    joined = call(
        join_body,
        [array((2 * rows, columns), BF16)],
        (moe_input, swapped(moe_input, "ctx", 2)),
        fixed=1,
        sems=2,
        name="join",
    )[0]
    return joined, swapped(joined, "ctx", 4)


def experts_by_tokens(moe_input, ids, w_gate, w_up):
    z = along_z(moe_input)
    x = [swapped(a, "ctx", 1) for a in z]
    y = [swapped(a, "exp", 2) for a in z]
    d = (swapped(y[0], "ctx", 1), swapped(x[1], "exp", 2))
    here = [*z, *x]
    there = [*y, *d]
    beside = [swapped(a, "exp", 1) for a in here]
    corner = [swapped(a, "exp", 1) for a in there]
    pieces = here + beside + there + corner
    rows = moe_input.shape[0]
    length = rows * lax.axis_size("ctx")
    hidden = w_gate.shape[2]
    return call(
        functools.partial(expert_body, len(pieces)),
        [array((1, length, hidden), BF16)],
        (w_gate, w_up, *pieces, ids),
        held=2,
        near_args=len(pieces) + 1,
        scratch=[
            pltpu.VMEM((length // rows, rows, rows), BF16),
            pltpu.VMEM((length, TILE), BF16),
            pltpu.VMEM((length, hidden), BF16),
        ],
        sems=hidden // TILE,
        flops=4 * length * w_gate.shape[1] * hidden,
        grant=16,
        name="experts",
    )[0]


def slot_matrix(pairs, expert, capacity):
    named = jnp.any(pairs == expert, axis=1).astype(jnp.int32)
    position = jnp.cumsum(named) - named
    hit = position[None, :] == jnp.arange(capacity, dtype=jnp.int32)[:, None]
    return (hit & (named[None, :] > 0)).astype(BF16)


def experts_by_slots(moe_input, pairs, w_gate, w_up):
    experts = lax.axis_size("exp")
    capacity = 4 * moe_input.shape[0] // experts
    pick = jax.vmap(lambda e: slot_matrix(pairs, e, capacity))(jnp.arange(experts))
    slots = jnp.einsum("eqt,td->eqd", pick, moe_input, preferred_element_type=F32)
    routed = lax.all_to_all(slots.astype(BF16), "exp", split_axis=0, concat_axis=2, tiled=True)
    rows = lax.all_gather(routed[0], "ctx", axis=0, tiled=True)
    gate = jnp.dot(rows, w_gate[0], preferred_element_type=F32)
    upper = jnp.dot(rows, w_up[0], preferred_element_type=F32)
    return (jax.nn.silu(gate) * upper).astype(BF16)[None]


def on_device(
    seq_input,
    b_input,
    c_input,
    conv_x,
    conv_bc,
    log_decay,
    skip_gain,
    norm_gain,
    moe_input,
    expert_ids,
    w_gate,
    w_up,
):
    ctx = lax.axis_size("ctx")
    by_tokens = lax.axis_size("exp") == 4 and ctx == 8
    tokens, channels = seq_input.shape
    ends = call(
        ends_body,
        [array((EDGE, channels + 2 * STATE), BF16)],
        (seq_input, b_input, c_input),
        fixed=3,
        sems=3,
        name="ends",
    )[0]
    before = lax.ppermute(ends, "ctx", [(i, i + 1) for i in range(ctx - 1)])
    mixed, ids = mixing(
        by_tokens,
        seq_input,
        b_input,
        c_input,
        before,
        conv_x,
        conv_bc,
        log_decay,
        skip_gain,
        norm_gain,
        expert_ids,
    )
    if by_tokens:
        hidden = experts_by_tokens(moe_input, ids, w_gate, w_up)
    else:
        hidden = experts_by_slots(moe_input, expert_ids, w_gate, w_up)
    return (mixed, hidden)


def solution(mesh):
    in_specs = (
        P("ctx", "exp"),
        P("ctx", None),
        P("ctx", None),
        P(None, "exp"),
        P(),
        P("exp", "ctx"),
        P("exp"),
        P("exp"),
        P("ctx", "exp"),
        P("ctx", None),
        P("exp", None, "ctx"),
        P("exp", None, "ctx"),
    )
    out_specs = (P("ctx", "exp"), P("exp", None, "ctx"))
    return jax.shard_map(
        on_device, mesh=mesh, in_specs=in_specs, out_specs=out_specs, check_vma=False
    )
```

```python
import functools
import math

import jax
import jax.numpy as jnp
from jax import lax
from jax.experimental import pallas as pl
from jax.experimental.pallas import tpu as pltpu
from jax.sharding import PartitionSpec as P

HDIM = 64
STATE = 128
KCONV = 4
EDGE = 16
NOTES = 8

F32 = jnp.float32
BF16 = jnp.bfloat16


def dot16(a, b, contract=((1,), (0,))):
    return lax.dot_general(a, b, (contract, ((), ())), preferred_element_type=F32)


def halves(value):
    high = value.astype(BF16)
    return high, (value - high.astype(F32)).astype(BF16)


def dot(a, b, contract=((1,), (0,))):
    a_high, a_low = halves(a)
    b_high, b_low = halves(b)
    cross = dot16(a_high, b_low, contract) + dot16(a_low, b_high, contract)
    return dot16(a_high, b_high, contract) + cross


def dot_exact(a, b, contract=((1,), (0,))):
    high, rest = halves(a)
    low = (a - high.astype(F32) - rest.astype(F32)).astype(BF16)
    return dot16(high, b, contract) + (dot16(rest, b, contract) + dot16(low, b, contract))


def dot_left(a, b, contract=((1,), (0,))):
    high, low = halves(a)
    return dot16(high, b, contract) + dot16(low, b, contract)


FIRST = ((0,), (0,))


def iota(shape, axis):
    return lax.broadcasted_iota(jnp.int32, shape, axis)


def head_spread(heads):
    shape = (heads, heads * HDIM)
    return (iota(shape, 1) // HDIM == iota(shape, 0)).astype(BF16)


def upper_ones(length):
    return (iota((length, length), 0) <= iota((length, length), 1)).astype(BF16)


def silu(value):
    return value / (1.0 + jnp.exp(-value))


def one_minus_exp(value):
    series = jnp.ones_like(value)
    for n in range(8, 1, -1):
        series = 1.0 + value * series * (1.0 / n)
    return jnp.where(value > -0.25, -value * series, 1.0 - jnp.exp(value))


def started(sources, targets, sems, first=0):
    copies = []
    for i, (source, target) in enumerate(zip(sources, targets)):
        copies.append(pltpu.make_async_copy(source, target, sems.at[first + i]))
        copies[-1].start()
    return copies


def finished(copies):
    for copy in copies:
        copy.wait()


def following(body, count, skipped):
    return lambda *refs: body(*refs[:count], *refs[count + skipped :])


def call(
    body,
    outs,
    args,
    fixed=0,
    held=0,
    near_args=0,
    near_outs=0,
    after=(),
    after_far=(),
    aliases=None,
    scratch=(),
    sems=0,
    flops=0,
    grant=8,
    near=False,
    spaces_of=None,
    name=None,
):
    body = following(body, len(args), len(after) + len(after_far))
    moved = sum(math.prod(a.shape) * a.dtype.itemsize for a in (*args, *outs))
    scratch = list(scratch) + ([pltpu.SemaphoreType.DMA((sems,))] if sems else [])
    space = pltpu.VMEM if near else pl.ANY
    spaces = [pltpu.HBM] * fixed + [pltpu.VMEM] * held
    args = [
        pltpu.with_memory_space_constraint(a, spaces[i]) if i < len(spaces) else a
        for i, a in enumerate(args)
    ]
    spaces += [space] * (len(args) - near_args - len(spaces)) + [pltpu.VMEM] * near_args
    spaces = spaces_of or spaces
    args, spaces = [*args, *after], spaces + [pl.ANY] * len(after)
    args += [pltpu.with_memory_space_constraint(a, pltpu.HBM) for a in after_far]
    spaces += [pltpu.HBM] * len(after_far)
    out_spaces = [space] * (len(outs) - near_outs) + [pltpu.VMEM] * near_outs
    return pl.pallas_call(
        body,
        out_shape=outs,
        in_specs=[pl.BlockSpec(memory_space=s) for s in spaces],
        out_specs=[pl.BlockSpec(memory_space=s) for s in out_spaces],
        scratch_shapes=scratch,
        input_output_aliases=aliases or {},
        compiler_params=pltpu.CompilerParams(vmem_limit_bytes=grant * 2**20),
        cost_estimate=pl.CostEstimate(flops=flops, bytes_accessed=moved, transcendentals=0),
        name=name,
    )(*args)


def room(arrays):
    return [pltpu.VMEM(a.shape, a.dtype) for a in arrays]


def array(shape, dtype):
    return jax.ShapeDtypeStruct(shape, dtype)


def ends_body(x_ref, b_ref, c_ref, ends_ref, sems):
    tokens, channels = x_ref.shape
    cut = pl.ds(tokens - EDGE, EDGE)
    finished(
        started(
            [x_ref.at[cut, :], b_ref.at[cut, :], c_ref.at[cut, :]],
            [
                ends_ref.at[:, pl.ds(0, channels)],
                ends_ref.at[:, pl.ds(channels, STATE)],
                ends_ref.at[:, pl.ds(channels + STATE, STATE)],
            ],
            sems,
        )
    )


def front_body(paired, count, *refs):
    far, outs, rest = refs[:count], refs[count : count + 3], refs[count + 3 :]
    ends = rest[: 1 + paired]
    rest = rest[1 + paired :]
    near, scratch, pad_ref, sems = rest[:count], rest[count : count + 3], rest[-2], rest[-1]
    copies = started(far, near, sems)
    x_ref, b_ref, c_ref, taps_ref, taps_bc_ref, logs_ref, ids_ref, ends_ref = near
    xconv_ref, bc_ref, lines_ref = scratch
    tokens, channels = x_ref.shape
    heads = logs_ref.shape[0]
    finished(copies)
    pad_ref[0:8, :] = ends_ref[...].astype(F32)[EDGE - 8 : EDGE]
    pad_ref[8 : 8 + tokens, :channels] = x_ref[...].astype(F32)
    pad_ref[8 : 8 + tokens, channels : channels + STATE] = b_ref[...].astype(F32)
    pad_ref[8 : 8 + tokens, channels + STATE :] = c_ref[...].astype(F32)

    def conv(taps, start, stop):
        total = jnp.zeros((tokens, stop - start), F32)
        for k in range(KCONV):
            first = 8 - (KCONV - 1) + k
            total = total + taps[k : k + 1] * pad_ref[first : first + tokens, start:stop]
        return silu(total)

    bc = conv(taps_bc_ref[...], channels, channels + 2 * STATE)
    bc_ref[...] = bc
    xconv = conv(taps_ref[...], 0, channels)
    xconv_ref[...] = xconv
    logs = logs_ref[...]
    inflow = jnp.sqrt(one_minus_exp(2.0 * logs))
    row = dot_exact(logs, upper_ones(tokens))
    lines_ref[0] = row
    lines_ref[1] = inflow
    copies = started(scratch, outs, sems)
    total = row[:, tokens - 1 :]
    spread = head_spread(heads)
    fresh = xconv * dot_left(inflow * jnp.exp(total - row), spread, FIRST)
    state = dot(bc[:, :STATE], fresh, FIRST)
    total = jnp.broadcast_to(total, (heads, NOTES))
    if paired:
        total = dot_exact(total, spread, FIRST)
        half = channels // 2
        side = lax.axis_index("ctx") % 2
        ids = ids_ref[...].astype(F32)
        line = jnp.concatenate([ids[0:1], ids[1:2]], axis=1)
        line = jnp.concatenate([line] * (half // line.shape[1]), axis=1)
        for ref, first in ((ends[0], side == 0), (ends[1], side != 0)):
            mine = jnp.where(first, state[:, :half], state[:, half:])
            logsum = jnp.where(first, total[:1, :half], total[:1, half:])
            if ref is ends[0]:
                put(ref, mine, logsum, line)
            else:
                send(ref, mine, logsum, line)
    else:
        ends[0][:STATE] = state
        ends[0][STATE:] = dot_exact(jnp.exp(total), spread, FIRST)
    finished(copies)


def put(ref, state, logsum, line):
    ref[:STATE] = state
    at = iota((NOTES, state.shape[1]), 0)
    ref[STATE:] = jnp.where(at == 0, logsum, line)


def send(ref, state, logsum, line):
    largest = jnp.max(jnp.abs(state), axis=0, keepdims=True)
    power = jnp.ceil(jnp.log2(jnp.maximum(largest, 1e-30))) - 15.0
    whole = jnp.clip(jnp.round(state * jnp.exp2(-power)), -32767.0, 32767.0)
    ref[:STATE] = whole.astype(jnp.int32).astype(jnp.int16)
    logsum = jnp.round(jnp.maximum(logsum, -128.0) * 2.0**22).astype(jnp.int32)
    at = iota((16, state.shape[1]), 0)
    notes = jnp.where(at == 0, power.astype(jnp.int32), line.astype(jnp.int32))
    notes = jnp.where(at == 1, logsum >> 15, jnp.where(at == 2, logsum & 32767, notes))
    ref[STATE:] = notes.astype(jnp.int16)


def taken(ref):
    return ref[:STATE], ref[STATE : STATE + 1], ref[STATE + 1 : STATE + 2]


def received(ref):
    notes = ref[STATE:].astype(jnp.int32).astype(F32)
    state = ref[:STATE].astype(jnp.int32).astype(F32) * jnp.exp2(notes[0:1])
    return state, notes[1:2] * 2.0**-7 + notes[2:3] * 2.0**-22, notes[3:4]


def ordered(first, own, other):
    return [jnp.where(first, a, b) for a, b in zip(own, other)], [
        jnp.where(first, b, a) for a, b in zip(own, other)
    ]


def together(first, own, other, width):
    (a, a_log, a_line), (b, b_log, b_line) = ordered(first, own, other)
    line = jnp.concatenate([a_line[:, :width], b_line[:, :width]], axis=1)
    line = jnp.concatenate([line] * (a.shape[1] // line.shape[1]), axis=1)
    return jnp.exp(b_log) * a + b, a_log + b_log, line


def place():
    here = lax.axis_index("ctx")
    return here % 2, (here // 2) % 2, here // 4


def pair_body(width, own_ref, got_ref, pair_ref, sent_ref):
    x, _, _ = place()
    pair = together(x == 0, taken(own_ref), received(got_ref), width)
    put(pair_ref, *pair)
    send(sent_ref, *pair)


def four_body(width, pair_ref, got_ref, sent_ref):
    _, z, _ = place()
    send(sent_ref, *together(z == 0, taken(pair_ref), received(got_ref), 2 * width))


def turn_body(
    width, own_ref, got_ref, pair_ref, pair_got_ref, four_got_ref, mine_ref, sent_ref, ids_ref
):
    x, z, zz = place()
    pair, pair_got, four_got = taken(pair_ref), received(pair_got_ref), received(four_got_ref)
    line = together(z == 0, pair, pair_got, 2 * width)[2]
    lines = ordered(zz == 0, [line], [four_got[2]])
    at = iota(ids_ref.shape, 0)
    ids = jnp.zeros(ids_ref.shape, F32)
    for i in range(ids_ref.shape[0]):
        part = lines[i // 4][0][:, i % 4 * width : (i % 4 + 1) * width]
        ids = jnp.where(at == i, part, ids)
    ids_ref[...] = ids

    before = jnp.where(zz == 0, 0.0, four_got[0])
    before = jnp.where(z == 0, before, jnp.exp(pair_got[1]) * before + pair_got[0])
    (first, first_log), _ = ordered(x == 0, taken(own_ref)[:2], received(got_ref)[:2])
    after = jnp.exp(first_log) * before + first
    mine_ref[...] = jnp.where(x == 0, before, after)
    other = jnp.where(x == 0, after, before)
    send(sent_ref, other, jnp.zeros_like(first_log), jnp.zeros_like(first_log))


def inner_body(skip_far, xconv_far, bc_far, lines_far, pre_far, decay_far, *rest):
    far = (skip_far, xconv_far, bc_far, lines_far)
    skip_ref, xconv_ref, bc_ref, lines_ref, pre_ref, decay_ref, sems = rest
    finished(started(far, rest[:4], sems))
    tokens, channels = xconv_ref.shape
    heads = channels // HDIM
    row = lines_ref[0]
    column = row.T
    spread = head_spread(heads)
    decay_ref[...] = dot_left(jnp.exp(row), spread, FIRST)
    copies = started([decay_ref], [decay_far], sems)
    inflow = dot_left(lines_ref[1], spread, FIRST)
    skip = dot_exact(skip_ref[...], spread)
    meet = dot(bc_ref[:, STATE:], bc_ref[:, :STATE], ((1,), (1,)))
    lower = iota((tokens, tokens), 0) >= iota((tokens, tokens), 1)
    left = iota((tokens, 2 * HDIM), 1) < HDIM
    for pair in range(heads // 2):
        cut = slice(pair * 2 * HDIM, (pair + 1) * 2 * HDIM)
        xconv = xconv_ref[:, cut]
        d_high, d_low = halves(xconv * inflow[:, cut])
        both = []
        for h in (2 * pair, 2 * pair + 1):
            gap = column[:, h : h + 1] - row[h : h + 1, :]
            mix = jnp.where(lower, jnp.exp(gap), 0.0) * meet
            m_high, m_low = halves(mix)
            both.append(dot16(m_high, d_high) + dot16(m_high, d_low) + dot16(m_low, d_high))
        pre_ref[:, cut] = skip[:, cut] * xconv + jnp.where(left, both[0], both[1])
    finished(copies + started([pre_ref], [pre_far], sems, 1))


def prefix_body(parts_ref, starts_ref):
    ctx, rows, share = starts_ref.shape
    state = jnp.zeros((rows, share), F32)
    for i in range(ctx):
        starts_ref[i] = state
        if i < ctx - 1:
            state = parts_ref[i, STATE : STATE + 1] * state + parts_ref[i, :STATE]


def back_body(paired, gain_far, pre_far, decay_far, bc_far, *rest):
    starts, (out_far, *rest) = rest[: 1 + paired], rest[1 + paired :]
    far = (gain_far, pre_far, decay_far, bc_far)
    gain_ref, pre_ref, decay_ref, bc_ref, out_ref, sems = rest
    copies = started(far, rest[:4], sems)
    channels = pre_ref.shape[1]
    width = min(channels, 4 * HDIM)
    group = (iota((width, width), 0) // HDIM == iota((width, width), 1) // HDIM).astype(BF16)
    if paired:
        side = lax.axis_index("ctx") % 2
        mine, other = starts[0][...], received(starts[1])[0]
        start = [jnp.where(side == 0, mine, other), jnp.where(side == 0, other, mine)]
        start = jnp.concatenate(start, axis=1)
    else:
        start = starts[0][...]
    finished(copies)
    c_high, c_low = halves(bc_ref[:, STATE:])
    copies = []
    for i in range(channels // width):
        cut = slice(i * width, (i + 1) * width)
        s_high, s_low = halves(start[:, cut])
        carried = dot16(c_high, s_high) + dot16(c_high, s_low) + dot16(c_low, s_high)
        pre = pre_ref[:, cut] + carried * decay_ref[:, cut]
        mean = dot_left(pre * pre, group) * (1.0 / HDIM)
        out_ref[:, cut] = (pre * lax.rsqrt(mean + 1e-05) * gain_ref[:, cut]).astype(BF16)
        copies += started([out_ref.at[:, cut]], [out_far.at[:, cut]], sems, i)
    finished(copies)


def entering_by_pairs(keep, sent, width, after):
    pair_array, sent_array = array(keep.shape, F32), array(sent.shape, jnp.int16)
    got = swapped(sent, "ctx", 1)
    pair, sent = call(
        functools.partial(pair_body, width),
        [pair_array, sent_array],
        (keep, got),
        near=True,
        after=after[0],
        name="pair",
    )
    pair_got = swapped(sent, "ctx", 2)
    (sent,) = call(
        functools.partial(four_body, width),
        [sent_array],
        (pair, pair_got),
        near=True,
        after=after[1],
        name="four",
    )
    four_got = swapped(sent, "ctx", 4)
    mine, sent, ids = call(
        functools.partial(turn_body, width),
        [array((STATE, keep.shape[1]), F32), sent_array, array((8, width), F32)],
        (keep, got, pair, pair_got, four_got),
        near=True,
        after=after[2],
        name="turn",
    )
    return (mine, swapped(sent, "ctx", 1)), ids


def entering_by_rows(state):
    ctx = lax.axis_size("ctx")
    rows, channels = state.shape
    slabs = state.reshape(rows, ctx, channels // ctx).transpose(1, 0, 2)
    parts = lax.all_to_all(slabs, "ctx", split_axis=0, concat_axis=0, tiled=True)
    (starts,) = call(
        prefix_body,
        [array((ctx, STATE, channels // ctx), F32)],
        (parts,),
        near=True,
        name="prefix",
    )
    start = lax.all_to_all(starts, "ctx", split_axis=0, concat_axis=0, tiled=True)
    return start.transpose(1, 0, 2).reshape(STATE, channels)


def mixing(
    after, seq_input, b_input, c_input, before, conv_x, conv_bc, log_decay, skip, gain, ids
):
    tokens, channels = seq_input.shape
    heads = skip.shape[0]
    width = 2 * ids.shape[0]
    paired = after is not None
    outs = [
        array((tokens, channels), F32),
        array((tokens, 2 * STATE), F32),
        array((2, heads, tokens), F32),
    ]
    if paired:
        ends = [array((STATE + NOTES, channels // 2), F32)]
        ends.append(array((STATE + 16, channels // 2), jnp.int16))
    else:
        ends = [array((STATE + NOTES, channels), F32)]
    args = (seq_input, b_input, c_input, conv_x, conv_bc, log_decay, ids.T, before)
    xconv, bc, lines, *ends = call(
        functools.partial(front_body, paired, len(args)),
        outs + ends,
        args,
        fixed=len(args) - 1,
        near_outs=len(ends),
        after=after[0] if paired else (),
        scratch=room(args) + room(outs) + [pltpu.VMEM((8 + tokens, channels + 2 * STATE), F32)],
        sems=len(args),
        flops=10**9,
        grant=20,
        name="front",
    )
    args = (skip.reshape(1, heads), xconv, bc, lines)
    outs = [array((tokens, channels), F32)] * 2
    pre, decay = call(
        inner_body,
        outs,
        args,
        fixed=1,
        scratch=room(args) + room(outs),
        sems=4,
        flops=4 * 10**9,
        grant=16,
        name="inner",
    )
    if paired:
        first, second, third = after[1:]
        starts, lines_of_ids = entering_by_pairs(*ends, width, (first, (*second, pre), third))
    else:
        starts, lines_of_ids = (entering_by_rows(ends[0]),), None

    def finish(after=()):
        args = (gain.reshape(1, channels), pre, decay, bc)
        outs = [array((tokens, channels), BF16)]
        return call(
            functools.partial(back_body, paired),
            outs,
            (*args, *starts),
            fixed=1,
            near_args=len(starts),
            after_far=after,
            scratch=room(args) + room(outs),
            sems=max(4, channels // (4 * HDIM)),
            flops=10**9,
            grant=16,
            name="back",
        )[0]

    return finish, lines_of_ids


TILE = 512


def join_body(a_ref, b_ref, out_ref, sems):
    rows = a_ref.shape[0]
    finished(
        started([a_ref, b_ref], [out_ref.at[pl.ds(0, rows), :], out_ref.at[pl.ds(rows, rows), :]], sems)
    )


def swapped(block, axis, bit):
    return lax.ppermute(block, axis, [(i, i ^ bit) for i in range(lax.axis_size(axis))])


def expert_body(part, w_gate, w_up, *refs):
    far, ids_ref, out_far = refs[:8], refs[8], refs[9 + part]
    pick_ref, hid_ref, out_ref, sems = refs[10 + part :]
    length, hidden = out_ref.shape
    rows = far[0].shape[0] // 2
    depth = far[0].shape[1]
    me = lax.axis_index("exp")
    here = lax.axis_index("ctx")
    downs = [pl.ds(pl.multiple_of((me ^ k) * depth, depth), depth) for k in range(4)]
    pair = (here // 4) ^ part

    shape = (rows, rows)
    earlier = (iota(shape, 1) < iota(shape, 0)).astype(F32)
    across = iota(shape, 1)
    diagonal = iota(shape, 0) == across
    turns = [(here % 4) ^ (2 * (i % 2) + i // 2) for i in range(length // rows)]
    for i, block in enumerate(turns):
        line = ids_ref[pl.ds(4 * pair + block, 1), :]
        mine = me.astype(F32)
        named = ((line[:, :rows] == mine) | (line[:, rows:] == mine)).astype(F32)
        column = jnp.sum(jnp.where(diagonal, named, 0.0), axis=1, keepdims=True)
        position = jnp.sum(earlier * named, axis=1, keepdims=True).astype(jnp.int32)
        pick_ref[i] = jnp.where(position == across, column, 0.0).astype(BF16)

    out_copies = []
    out_rows = pl.ds(pl.multiple_of(pair * length, length), length)
    for n in range(hidden // TILE):
        cut = slice(n * TILE, (n + 1) * TILE)
        gate = upper = None
        for k in range(4):
            block = jnp.concatenate([piece[...] for piece in far[2 * k : 2 * k + 2]], axis=0)
            more = dot16(block, w_gate[0, downs[k], cut])
            gate = more if k == 0 else gate + more
            more = dot16(block, w_up[0, downs[k], cut])
            upper = more if k == 0 else upper + more
        hid_ref[...] = (silu(gate) * upper).astype(BF16)
        for i, block in enumerate(turns):
            picked = dot16(pick_ref[i], hid_ref[i * rows : (i + 1) * rows], FIRST)
            out_ref[pl.ds(pl.multiple_of(block * rows, rows), rows), cut] = picked.astype(BF16)
        out_copies += started([out_ref.at[:, cut]], [out_far.at[0, out_rows, cut]], sems, n)
    finished(out_copies)


def along_z(moe_input):
    rows, columns = moe_input.shape
    joined = call(
        join_body,
        [array((2 * rows, columns), BF16)],
        (moe_input, swapped(moe_input, "ctx", 2)),
        fixed=1,
        sems=2,
        name="join",
    )[0]
    return joined, swapped(joined, "ctx", 4)


def gathered(moe_input):
    z = along_z(moe_input)
    x = [swapped(a, "ctx", 1) for a in z]
    y = [swapped(a, "exp", 2) for a in z]
    d = (swapped(y[0], "ctx", 1), swapped(x[1], "exp", 2))
    halves_of_rows = []
    for pieces in zip(z, x, y, d):
        beside = [swapped(a, "exp", 1) for a in pieces]
        halves_of_rows.append([*pieces[:2], *beside[:2], *pieces[2:], *beside[2:]])
    return halves_of_rows


def experts_by_tokens(part, pieces, ids, w_gate, w_up, so_far, after):
    rows = pieces[0].shape[0] // 2
    length = 4 * rows
    hidden = w_gate.shape[2]
    args = (w_gate, w_up, *pieces, ids)
    return call(
        functools.partial(expert_body, part),
        [pltpu.HBM((1, 2 * length, hidden), BF16)],
        args + ((so_far,) if part else ()),
        held=2,
        near_args=0,
        aliases={len(args): 0} if part else None,
        after_far=after,
        scratch=[
            pltpu.VMEM((length // rows, rows, rows), BF16),
            pltpu.VMEM((length, TILE), BF16),
            pltpu.VMEM((length, hidden), BF16),
        ],
        sems=hidden // TILE,
        flops=4 * length * w_gate.shape[1] * hidden,
        grant=16,
        spaces_of=[pltpu.VMEM] * len(args) + [pltpu.HBM] * part,
        name="experts",
    )[0]


def slot_matrix(pairs, expert, capacity):
    named = jnp.any(pairs == expert, axis=1).astype(jnp.int32)
    position = jnp.cumsum(named) - named
    hit = position[None, :] == jnp.arange(capacity, dtype=jnp.int32)[:, None]
    return (hit & (named[None, :] > 0)).astype(BF16)


def experts_by_slots(moe_input, pairs, w_gate, w_up):
    experts = lax.axis_size("exp")
    capacity = 4 * moe_input.shape[0] // experts
    pick = jax.vmap(lambda e: slot_matrix(pairs, e, capacity))(jnp.arange(experts))
    slots = jnp.einsum("eqt,td->eqd", pick, moe_input, preferred_element_type=F32)
    routed = lax.all_to_all(slots.astype(BF16), "exp", split_axis=0, concat_axis=2, tiled=True)
    rows = lax.all_gather(routed[0], "ctx", axis=0, tiled=True)
    gate = jnp.dot(rows, w_gate[0], preferred_element_type=F32)
    upper = jnp.dot(rows, w_up[0], preferred_element_type=F32)
    return (jax.nn.silu(gate) * upper).astype(BF16)[None]


def on_device(
    seq_input,
    b_input,
    c_input,
    conv_x,
    conv_bc,
    log_decay,
    skip_gain,
    norm_gain,
    moe_input,
    expert_ids,
    w_gate,
    w_up,
):
    ctx = lax.axis_size("ctx")
    by_tokens = lax.axis_size("exp") == 4 and ctx == 8
    tokens, channels = seq_input.shape
    ends = call(
        ends_body,
        [array((EDGE, channels + 2 * STATE), BF16)],
        (seq_input, b_input, c_input),
        fixed=3,
        sems=3,
        name="ends",
    )[0]
    before = lax.ppermute(ends, "ctx", [(i, i + 1) for i in range(ctx - 1)])
    follow = None
    if by_tokens:
        one, two = gathered(moe_input)
        follow = (one[:1], (one[1], one[4], one[2]), two[:1])
        follow += ((two[1], two[4], two[2], one[5], one[3], one[6]),)
    finish, ids = mixing(
        follow,
        seq_input,
        b_input,
        c_input,
        before,
        conv_x,
        conv_bc,
        log_decay,
        skip_gain,
        norm_gain,
        expert_ids,
    )
    if by_tokens:
        hidden = experts_by_tokens(0, one, ids, w_gate, w_up, None, ())
        mixed = finish((hidden,))
        hidden = experts_by_tokens(1, two, ids, w_gate, w_up, hidden, (mixed,))
    else:
        mixed = finish()
        hidden = experts_by_slots(moe_input, expert_ids, w_gate, w_up)
    return (mixed, hidden)


def solution(mesh):
    in_specs = (
        P("ctx", "exp"),
        P("ctx", None),
        P("ctx", None),
        P(None, "exp"),
        P(),
        P("exp", "ctx"),
        P("exp"),
        P("exp"),
        P("ctx", "exp"),
        P("ctx", None),
        P("exp", None, "ctx"),
        P("exp", None, "ctx"),
    )
    out_specs = (P("ctx", "exp"), P("exp", None, "ctx"))
    return jax.shard_map(
        on_device, mesh=mesh, in_specs=in_specs, out_specs=out_specs, check_vma=False
    )
```

```python
import functools
import math

import jax
import jax.numpy as jnp
from jax import lax
from jax.experimental import pallas as pl
from jax.experimental.pallas import tpu as pltpu
from jax.sharding import PartitionSpec as P

HDIM = 64
STATE = 128
KCONV = 4
EDGE = 16
NOTES = 8

F32 = jnp.float32
BF16 = jnp.bfloat16


def dot16(a, b, contract=((1,), (0,))):
    return lax.dot_general(a, b, (contract, ((), ())), preferred_element_type=F32)


def halves(value):
    high = value.astype(BF16)
    return high, (value - high.astype(F32)).astype(BF16)


def dot(a, b, contract=((1,), (0,))):
    a_high, a_low = halves(a)
    b_high, b_low = halves(b)
    cross = dot16(a_high, b_low, contract) + dot16(a_low, b_high, contract)
    return dot16(a_high, b_high, contract) + cross


def dot_exact(a, b, contract=((1,), (0,))):
    high, rest = halves(a)
    low = (a - high.astype(F32) - rest.astype(F32)).astype(BF16)
    return dot16(high, b, contract) + (dot16(rest, b, contract) + dot16(low, b, contract))


def dot_left(a, b, contract=((1,), (0,))):
    high, low = halves(a)
    return dot16(high, b, contract) + dot16(low, b, contract)


FIRST = ((0,), (0,))


def iota(shape, axis):
    return lax.broadcasted_iota(jnp.int32, shape, axis)


def head_spread(heads):
    shape = (heads, heads * HDIM)
    return (iota(shape, 1) // HDIM == iota(shape, 0)).astype(BF16)


def upper_ones(length):
    return (iota((length, length), 0) <= iota((length, length), 1)).astype(BF16)


def silu(value):
    return value / (1.0 + jnp.exp(-value))


def one_minus_exp(value):
    series = jnp.ones_like(value)
    for n in range(8, 1, -1):
        series = 1.0 + value * series * (1.0 / n)
    return jnp.where(value > -0.25, -value * series, 1.0 - jnp.exp(value))


def started(sources, targets, sems, first=0):
    copies = []
    for i, (source, target) in enumerate(zip(sources, targets)):
        copies.append(pltpu.make_async_copy(source, target, sems.at[first + i]))
        copies[-1].start()
    return copies


def finished(copies):
    for copy in copies:
        copy.wait()


def following(body, count, skipped):
    return lambda *refs: body(*refs[:count], *refs[count + skipped :])


def call(
    body,
    outs,
    args,
    fixed=0,
    held=0,
    near_args=0,
    near_outs=0,
    after=(),
    after_far=(),
    aliases=None,
    scratch=(),
    sems=0,
    flops=0,
    grant=8,
    near=False,
    spaces_of=None,
    name=None,
):
    body = following(body, len(args), len(after) + len(after_far))
    moved = sum(math.prod(a.shape) * a.dtype.itemsize for a in (*args, *outs))
    scratch = list(scratch) + ([pltpu.SemaphoreType.DMA((sems,))] if sems else [])
    space = pltpu.VMEM if near else pl.ANY
    spaces = [pltpu.HBM] * fixed + [pltpu.VMEM] * held
    args = [
        pltpu.with_memory_space_constraint(a, spaces[i]) if i < len(spaces) else a
        for i, a in enumerate(args)
    ]
    spaces += [space] * (len(args) - near_args - len(spaces)) + [pltpu.VMEM] * near_args
    spaces = spaces_of or spaces
    args, spaces = [*args, *after], spaces + [pl.ANY] * len(after)
    args += [pltpu.with_memory_space_constraint(a, pltpu.HBM) for a in after_far]
    spaces += [pltpu.HBM] * len(after_far)
    out_spaces = [space] * (len(outs) - near_outs) + [pltpu.VMEM] * near_outs
    return pl.pallas_call(
        body,
        out_shape=outs,
        in_specs=[pl.BlockSpec(memory_space=s) for s in spaces],
        out_specs=[pl.BlockSpec(memory_space=s) for s in out_spaces],
        scratch_shapes=scratch,
        input_output_aliases=aliases or {},
        compiler_params=pltpu.CompilerParams(vmem_limit_bytes=grant * 2**20),
        cost_estimate=pl.CostEstimate(flops=flops, bytes_accessed=moved, transcendentals=0),
        name=name,
    )(*args)


def room(arrays):
    return [pltpu.VMEM(a.shape, a.dtype) for a in arrays]


def array(shape, dtype):
    return jax.ShapeDtypeStruct(shape, dtype)


def ends_body(x_ref, b_ref, c_ref, ends_ref, sems):
    tokens, channels = x_ref.shape
    cut = pl.ds(tokens - EDGE, EDGE)
    finished(
        started(
            [x_ref.at[cut, :], b_ref.at[cut, :], c_ref.at[cut, :]],
            [
                ends_ref.at[:, pl.ds(0, channels)],
                ends_ref.at[:, pl.ds(channels, STATE)],
                ends_ref.at[:, pl.ds(channels + STATE, STATE)],
            ],
            sems,
        )
    )


def local_body(paired, count, *refs):
    far, outs, rest = refs[:count], refs[count : count + 3], refs[count + 3 :]
    ends = rest[: 1 + paired]
    rest = rest[1 + paired :]
    near, scratch, pad_ref, sems = rest[:count], rest[count : count + 3], rest[-2], rest[-1]
    copies = started(far, near, sems)
    x_ref, b_ref, c_ref, taps_ref, taps_bc_ref, logs_ref, skip_ref, ids_ref, ends_ref = near
    pre_ref, decay_ref, c_out_ref = scratch
    tokens, channels = x_ref.shape
    heads = logs_ref.shape[0]
    finished(copies)
    pad_ref[0:8, :] = ends_ref[...].astype(F32)[EDGE - 8 : EDGE]
    pad_ref[8 : 8 + tokens, :channels] = x_ref[...].astype(F32)
    pad_ref[8 : 8 + tokens, channels : channels + STATE] = b_ref[...].astype(F32)
    pad_ref[8 : 8 + tokens, channels + STATE :] = c_ref[...].astype(F32)

    def conv(taps, start, stop):
        total = jnp.zeros((tokens, stop - start), F32)
        for k in range(KCONV):
            first = 8 - (KCONV - 1) + k
            total = total + taps[k : k + 1] * pad_ref[first : first + tokens, start:stop]
        return silu(total)

    bc = conv(taps_bc_ref[...], channels, channels + 2 * STATE)
    bmat, cmat = bc[:, :STATE], bc[:, STATE:]
    c_out_ref[...] = cmat
    logs = logs_ref[...]
    inflow = jnp.sqrt(one_minus_exp(2.0 * logs))
    row = dot_exact(logs, upper_ones(tokens))
    column = row.T
    total = row[:, tokens - 1 :]
    spread = head_spread(heads)
    decay_ref[...] = dot_left(jnp.exp(row), spread, FIRST)
    copies = started(scratch[1:], outs[1:], sems)

    xconv = conv(taps_ref[...], 0, channels)
    pad_ref[:tokens, :channels] = xconv
    drive = xconv * dot_left(inflow, spread, FIRST)
    pre_ref[...] = drive
    fresh = drive * dot_left(jnp.exp(total - row), spread, FIRST)
    state = dot(bmat, fresh, FIRST)
    total = jnp.broadcast_to(total, (heads, NOTES))
    if paired:
        total = dot_exact(total, spread, FIRST)
        half = channels // 2
        side = lax.axis_index("ctx") % 2
        ids = ids_ref[...].astype(F32)
        line = jnp.concatenate([ids[0:1], ids[1:2]], axis=1)
        line = jnp.concatenate([line] * (half // line.shape[1]), axis=1)
        for ref, first in ((ends[0], side == 0), (ends[1], side != 0)):
            mine = jnp.where(first, state[:, :half], state[:, half:])
            logsum = jnp.where(first, total[:1, :half], total[:1, half:])
            if ref is ends[0]:
                put(ref, mine, logsum, line)
            else:
                send(ref, mine, logsum, line)
    else:
        ends[0][:STATE] = state
        ends[0][STATE:] = dot_exact(jnp.exp(total), spread, FIRST)

    skip = dot_exact(skip_ref[...], spread)
    meet = dot(cmat, bmat, ((1,), (1,)))
    lower = iota((tokens, tokens), 0) >= iota((tokens, tokens), 1)
    left = iota((tokens, 2 * HDIM), 1) < HDIM
    for pair in range(heads // 2):
        cut = slice(pair * 2 * HDIM, (pair + 1) * 2 * HDIM)
        d_high, d_low = halves(pre_ref[:, cut])
        both = []
        for h in (2 * pair, 2 * pair + 1):
            gap = column[:, h : h + 1] - row[h : h + 1, :]
            mix = jnp.where(lower, jnp.exp(gap), 0.0) * meet
            m_high, m_low = halves(mix)
            both.append(dot16(m_high, d_high) + dot16(m_high, d_low) + dot16(m_low, d_high))
        direct = skip[:, cut] * pad_ref[:tokens, cut]
        pre_ref[:, cut] = direct + jnp.where(left, both[0], both[1])
    finished(copies + started(scratch[:1], outs[:1], sems, 2))


def put(ref, state, logsum, line):
    ref[:STATE] = state
    at = iota((NOTES, state.shape[1]), 0)
    ref[STATE:] = jnp.where(at == 0, logsum, line)


def send(ref, state, logsum, line):
    largest = jnp.max(jnp.abs(state), axis=0, keepdims=True)
    power = jnp.ceil(jnp.log2(jnp.maximum(largest, 1e-30))) - 15.0
    whole = jnp.clip(jnp.round(state * jnp.exp2(-power)), -32767.0, 32767.0)
    ref[:STATE] = whole.astype(jnp.int32).astype(jnp.int16)
    logsum = jnp.round(jnp.maximum(logsum, -128.0) * 2.0**22).astype(jnp.int32)
    at = iota((16, state.shape[1]), 0)
    notes = jnp.where(at == 0, power.astype(jnp.int32), line.astype(jnp.int32))
    notes = jnp.where(at == 1, logsum >> 15, jnp.where(at == 2, logsum & 32767, notes))
    ref[STATE:] = notes.astype(jnp.int16)


def taken(ref):
    return ref[:STATE], ref[STATE : STATE + 1], ref[STATE + 1 : STATE + 2]


def received(ref):
    notes = ref[STATE:].astype(jnp.int32).astype(F32)
    state = ref[:STATE].astype(jnp.int32).astype(F32) * jnp.exp2(notes[0:1])
    return state, notes[1:2] * 2.0**-7 + notes[2:3] * 2.0**-22, notes[3:4]


def ordered(first, own, other):
    return [jnp.where(first, a, b) for a, b in zip(own, other)], [
        jnp.where(first, b, a) for a, b in zip(own, other)
    ]


def together(first, own, other, width):
    (a, a_log, a_line), (b, b_log, b_line) = ordered(first, own, other)
    line = jnp.concatenate([a_line[:, :width], b_line[:, :width]], axis=1)
    line = jnp.concatenate([line] * (a.shape[1] // line.shape[1]), axis=1)
    return jnp.exp(b_log) * a + b, a_log + b_log, line


def place():
    here = lax.axis_index("ctx")
    return here % 2, (here // 2) % 2, here // 4


def pair_body(width, own_ref, got_ref, pair_ref, sent_ref):
    x, _, _ = place()
    pair = together(x == 0, taken(own_ref), received(got_ref), width)
    put(pair_ref, *pair)
    send(sent_ref, *pair)


def list_ids(ids_ref, early, late, width):
    at = iota(ids_ref.shape, 0)
    ids = jnp.zeros(ids_ref.shape, F32)
    for i in range(ids_ref.shape[0]):
        line = (early, late)[i // 4]
        ids = jnp.where(at == i, line[:, i % 4 * width : (i % 4 + 1) * width], ids)
    ids_ref[...] = ids


def four_body(width, pair_ref, got_ref, sent_ref, ids_ref):
    _, z, _ = place()
    four = together(z == 0, taken(pair_ref), received(got_ref), 2 * width)
    send(sent_ref, *four)
    list_ids(ids_ref, four[2], four[2], width)


def turn_body(
    width,
    own_ref,
    got_ref,
    pair_ref,
    pair_got_ref,
    four_got_ref,
    rows_ref,
    mine_ref,
    sent_ref,
    ids_ref,
    same_rows_ref,
):
    same_rows_ref[...] = rows_ref[...]
    x, z, zz = place()
    pair, pair_got, four_got = taken(pair_ref), received(pair_got_ref), received(four_got_ref)
    line = together(z == 0, pair, pair_got, 2 * width)[2]
    (early,), (late,) = ordered(zz == 0, [line], [four_got[2]])
    list_ids(ids_ref, early, late, width)

    before = jnp.where(zz == 0, 0.0, four_got[0])
    before = jnp.where(z == 0, before, jnp.exp(pair_got[1]) * before + pair_got[0])
    (first, first_log), _ = ordered(x == 0, taken(own_ref)[:2], received(got_ref)[:2])
    after = jnp.exp(first_log) * before + first
    mine_ref[...] = jnp.where(x == 0, before, after)
    other = jnp.where(x == 0, after, before)
    send(sent_ref, other, jnp.zeros_like(first_log), jnp.zeros_like(first_log))


def prefix_body(parts_ref, starts_ref):
    ctx, rows, share = starts_ref.shape
    state = jnp.zeros((rows, share), F32)
    for i in range(ctx):
        starts_ref[i] = state
        if i < ctx - 1:
            state = parts_ref[i, STATE : STATE + 1] * state + parts_ref[i, :STATE]


def back_body(paired, gain_far, pre_far, decay_far, c_far, *rest):
    starts, (out_far, *rest) = rest[: 1 + paired], rest[1 + paired :]
    far = (gain_far, pre_far, decay_far, c_far)
    gain_ref, pre_ref, decay_ref, c_ref, out_ref, sems = rest
    copies = started(far, rest[:4], sems)
    channels = pre_ref.shape[1]
    width = min(channels, 4 * HDIM)
    group = (iota((width, width), 0) // HDIM == iota((width, width), 1) // HDIM).astype(BF16)
    if paired:
        side = lax.axis_index("ctx") % 2
        mine, other = starts[0][...], received(starts[1])[0]
        start = [jnp.where(side == 0, mine, other), jnp.where(side == 0, other, mine)]
        start = jnp.concatenate(start, axis=1)
    else:
        start = starts[0][...]
    finished(copies)
    c_high, c_low = halves(c_ref[...])
    copies = []
    for i in range(channels // width):
        cut = slice(i * width, (i + 1) * width)
        s_high, s_low = halves(start[:, cut])
        carried = dot16(c_high, s_high) + dot16(c_high, s_low) + dot16(c_low, s_high)
        pre = pre_ref[:, cut] + carried * decay_ref[:, cut]
        mean = dot_left(pre * pre, group) * (1.0 / HDIM)
        out_ref[:, cut] = (pre * lax.rsqrt(mean + 1e-05) * gain_ref[:, cut]).astype(BF16)
        copies += started([out_ref.at[:, cut]], [out_far.at[:, cut]], sems, i)
    finished(copies)


def entering_by_pairs(keep, sent, width, after, meanwhile, late_rows):
    pair_array, sent_array = array(keep.shape, F32), array(sent.shape, jnp.int16)
    ids_array = array((8, width), F32)
    got = swapped(sent, "ctx", 1)
    pair, sent = call(
        functools.partial(pair_body, width),
        [pair_array, sent_array],
        (keep, got),
        near=True,
        after=after[0],
        name="pair",
    )
    pair_got = swapped(sent, "ctx", 2)
    sent, ids = call(
        functools.partial(four_body, width),
        [sent_array, ids_array],
        (pair, pair_got),
        near=True,
        after=after[1],
        name="four",
    )
    four_got = swapped(sent, "ctx", 4)
    done = meanwhile(ids)
    mine, sent, ids, late_rows = call(
        functools.partial(turn_body, width),
        [array((STATE, keep.shape[1]), F32), sent_array, ids_array, late_rows],
        (keep, got, pair, pair_got, four_got, late_rows),
        near=True,
        after=after[2],
        after_far=(done,),
        name="turn",
    )
    return (mine, swapped(sent, "ctx", 1)), ids, (done, late_rows)


def entering_by_rows(state):
    ctx = lax.axis_size("ctx")
    rows, channels = state.shape
    slabs = state.reshape(rows, ctx, channels // ctx).transpose(1, 0, 2)
    parts = lax.all_to_all(slabs, "ctx", split_axis=0, concat_axis=0, tiled=True)
    (starts,) = call(
        prefix_body,
        [array((ctx, STATE, channels // ctx), F32)],
        (parts,),
        near=True,
        name="prefix",
    )
    start = lax.all_to_all(starts, "ctx", split_axis=0, concat_axis=0, tiled=True)
    return start.transpose(1, 0, 2).reshape(STATE, channels)


def mixing(
    after, meanwhile, late_rows, seq_input, b_input, c_input, before, conv_x, conv_bc, log_decay, skip, gain, ids
):
    tokens, channels = seq_input.shape
    heads = skip.shape[0]
    width = 2 * ids.shape[0]
    paired = after is not None
    outs = [
        array((tokens, channels), F32),
        array((tokens, channels), F32),
        array((tokens, STATE), F32),
    ]
    if paired:
        ends = [array((STATE + NOTES, channels // 2), F32)]
        ends.append(array((STATE + 16, channels // 2), jnp.int16))
    else:
        ends = [array((STATE + NOTES, channels), F32)]
    args = (seq_input, b_input, c_input, conv_x, conv_bc, log_decay)
    args = (*args, skip.reshape(1, heads), ids.T, before)
    pre, decay, cmat, *ends = call(
        functools.partial(local_body, paired, len(args)),
        outs + ends,
        args,
        fixed=len(args) - 1,
        near_outs=len(ends),
        after=after[0] if paired else (),
        scratch=room(args) + room(outs) + [pltpu.VMEM((8 + tokens, channels + 2 * STATE), F32)],
        sems=len(args),
        flops=5 * 10**9,
        grant=20,
        name="local",
    )
    done = None
    if paired:
        first, second, third = after[1:]
        after = (first, second, third)
        starts, lines_of_ids, done = entering_by_pairs(
            *ends, width, after, meanwhile, late_rows
        )
    else:
        starts, lines_of_ids = (entering_by_rows(ends[0]),), None

    def finish(after=()):
        args = (gain.reshape(1, channels), pre, decay, cmat)
        outs = [array((tokens, channels), BF16)]
        return call(
            functools.partial(back_body, paired),
            outs,
            (*args, *starts),
            fixed=1,
            near_args=len(starts),
            after_far=after,
            scratch=room(args) + room(outs),
            sems=max(4, channels // (4 * HDIM)),
            flops=10**9,
            grant=16,
            name="back",
        )[0]

    return finish, lines_of_ids, done


TILE = 512


def join_body(a_ref, b_ref, out_ref, sems):
    rows = a_ref.shape[0]
    finished(
        started([a_ref, b_ref], [out_ref.at[pl.ds(0, rows), :], out_ref.at[pl.ds(rows, rows), :]], sems)
    )


def swapped(block, axis, bit):
    return lax.ppermute(block, axis, [(i, i ^ bit) for i in range(lax.axis_size(axis))])


def expert_body(part, w_gate, w_up, *refs):
    far, ids_ref, out_far = refs[:8], refs[8], refs[9 + part]
    pick_ref, hid_ref, out_ref, sems = refs[10 + part :]
    length, hidden = out_ref.shape
    rows = far[0].shape[0] // 2
    depth = far[0].shape[1]
    me = lax.axis_index("exp")
    here = lax.axis_index("ctx")
    downs = [pl.ds(pl.multiple_of((me ^ k) * depth, depth), depth) for k in range(4)]
    pair = (here // 4) ^ part

    shape = (rows, rows)
    earlier = (iota(shape, 1) < iota(shape, 0)).astype(F32)
    across = iota(shape, 1)
    diagonal = iota(shape, 0) == across
    turns = [(here % 4) ^ (2 * (i % 2) + i // 2) for i in range(length // rows)]
    for i, block in enumerate(turns):
        line = ids_ref[pl.ds(4 * pair + block, 1), :]
        mine = me.astype(F32)
        named = ((line[:, :rows] == mine) | (line[:, rows:] == mine)).astype(F32)
        column = jnp.sum(jnp.where(diagonal, named, 0.0), axis=1, keepdims=True)
        position = jnp.sum(earlier * named, axis=1, keepdims=True).astype(jnp.int32)
        pick_ref[i] = jnp.where(position == across, column, 0.0).astype(BF16)

    out_copies = []
    out_rows = pl.ds(pl.multiple_of(pair * length, length), length)
    for n in range(hidden // TILE):
        cut = slice(n * TILE, (n + 1) * TILE)
        gate = upper = None
        for k in range(4):
            block = jnp.concatenate([piece[...] for piece in far[2 * k : 2 * k + 2]], axis=0)
            more = dot16(block, w_gate[0, downs[k], cut])
            gate = more if k == 0 else gate + more
            more = dot16(block, w_up[0, downs[k], cut])
            upper = more if k == 0 else upper + more
        hid_ref[...] = (silu(gate) * upper).astype(BF16)
        for i, block in enumerate(turns):
            picked = dot16(pick_ref[i], hid_ref[i * rows : (i + 1) * rows], FIRST)
            out_ref[pl.ds(pl.multiple_of(block * rows, rows), rows), cut] = picked.astype(BF16)
        out_copies += started([out_ref.at[:, cut]], [out_far.at[0, out_rows, cut]], sems, n)
    finished(out_copies)


def along_z(moe_input, before):
    rows, columns = moe_input.shape
    joined = call(
        join_body,
        [array((2 * rows, columns), BF16)],
        (moe_input, swapped(moe_input, "ctx", 2)),
        fixed=1,
        sems=2,
        after=(before,),
        name="join",
    )[0]
    return joined, swapped(joined, "ctx", 4)


def gathered(moe_input, before):
    z = along_z(moe_input, before)
    x = [swapped(a, "ctx", 1) for a in z]
    y = [swapped(a, "exp", 2) for a in z]
    d = (swapped(y[0], "ctx", 1), swapped(x[1], "exp", 2))
    halves_of_rows = []
    for i, pieces in enumerate(zip(z, x, y, d)):
        beside = [swapped(a, "exp", 1) for a in pieces[: 4 - i]]
        halves_of_rows.append([*pieces[:2], *beside[:2], *pieces[2:], *beside[2:]])
    return halves_of_rows


def experts_by_tokens(part, pieces, ids, w_gate, w_up, so_far):
    rows = pieces[0].shape[0] // 2
    length = 4 * rows
    hidden = w_gate.shape[2]
    args = (w_gate, w_up, *pieces, ids)
    return call(
        functools.partial(expert_body, part),
        [pltpu.HBM((1, 2 * length, hidden), BF16)],
        args + ((so_far,) if part else ()),
        held=2,
        near_args=0,
        aliases={len(args): 0} if part else None,
        scratch=[
            pltpu.VMEM((length // rows, rows, rows), BF16),
            pltpu.VMEM((length, TILE), BF16),
            pltpu.VMEM((length, hidden), BF16),
        ],
        sems=hidden // TILE,
        flops=4 * length * w_gate.shape[1] * hidden,
        grant=16,
        spaces_of=[pltpu.VMEM] * len(args) + [pltpu.HBM] * part,
        name="experts",
    )[0]


def slot_matrix(pairs, expert, capacity):
    named = jnp.any(pairs == expert, axis=1).astype(jnp.int32)
    position = jnp.cumsum(named) - named
    hit = position[None, :] == jnp.arange(capacity, dtype=jnp.int32)[:, None]
    return (hit & (named[None, :] > 0)).astype(BF16)


def experts_by_slots(moe_input, pairs, w_gate, w_up):
    experts = lax.axis_size("exp")
    capacity = 4 * moe_input.shape[0] // experts
    pick = jax.vmap(lambda e: slot_matrix(pairs, e, capacity))(jnp.arange(experts))
    slots = jnp.einsum("eqt,td->eqd", pick, moe_input, preferred_element_type=F32)
    routed = lax.all_to_all(slots.astype(BF16), "exp", split_axis=0, concat_axis=2, tiled=True)
    rows = lax.all_gather(routed[0], "ctx", axis=0, tiled=True)
    gate = jnp.dot(rows, w_gate[0], preferred_element_type=F32)
    upper = jnp.dot(rows, w_up[0], preferred_element_type=F32)
    return (jax.nn.silu(gate) * upper).astype(BF16)[None]


def on_device(
    seq_input,
    b_input,
    c_input,
    conv_x,
    conv_bc,
    log_decay,
    skip_gain,
    norm_gain,
    moe_input,
    expert_ids,
    w_gate,
    w_up,
):
    ctx = lax.axis_size("ctx")
    by_tokens = lax.axis_size("exp") == 4 and ctx == 8
    tokens, channels = seq_input.shape
    ends = call(
        ends_body,
        [array((EDGE, channels + 2 * STATE), BF16)],
        (seq_input, b_input, c_input),
        fixed=3,
        sems=3,
        name="ends",
    )[0]
    before = lax.ppermute(ends, "ctx", [(i, i + 1) for i in range(ctx - 1)])
    follow = meanwhile = late_rows = None
    if by_tokens:
        one, two = gathered(moe_input, before)
        follow = (one[:1], (), (two[0], one[1], one[4], one[2]))
        follow += ((two[1], two[4], two[2]),)
        late_rows = two[5]

        def meanwhile(ids):
            return experts_by_tokens(0, one, ids, w_gate, w_up, None)

    finish, ids, done = mixing(
        follow,
        meanwhile,
        late_rows,
        seq_input,
        b_input,
        c_input,
        before,
        conv_x,
        conv_bc,
        log_decay,
        skip_gain,
        norm_gain,
        expert_ids,
    )
    if by_tokens:
        hidden, late_rows = done
        two.append(swapped(late_rows, "exp", 1))
        hidden = experts_by_tokens(1, two, ids, w_gate, w_up, hidden)
        mixed = finish((hidden,))
    else:
        mixed = finish()
        hidden = experts_by_slots(moe_input, expert_ids, w_gate, w_up)
    return (mixed, hidden)


def solution(mesh):
    in_specs = (
        P("ctx", "exp"),
        P("ctx", None),
        P("ctx", None),
        P(None, "exp"),
        P(),
        P("exp", "ctx"),
        P("exp"),
        P("exp"),
        P("ctx", "exp"),
        P("ctx", None),
        P("exp", None, "ctx"),
        P("exp", None, "ctx"),
    )
    out_specs = (P("ctx", "exp"), P("exp", None, "ctx"))
    return jax.shard_map(
        on_device, mesh=mesh, in_specs=in_specs, out_specs=out_specs, check_vma=False
    )
```

```python
import functools
import math

import jax
import jax.numpy as jnp
from jax import lax
from jax.experimental import pallas as pl
from jax.experimental.pallas import tpu as pltpu
from jax.sharding import PartitionSpec as P

HDIM = 64
STATE = 128
KCONV = 4
EDGE = 16
NOTES = 8

F32 = jnp.float32
BF16 = jnp.bfloat16


def dot16(a, b, contract=((1,), (0,))):
    return lax.dot_general(a, b, (contract, ((), ())), preferred_element_type=F32)


def halves(value):
    high = value.astype(BF16)
    return high, (value - high.astype(F32)).astype(BF16)


def dot(a, b, contract=((1,), (0,))):
    a_high, a_low = halves(a)
    b_high, b_low = halves(b)
    cross = dot16(a_high, b_low, contract) + dot16(a_low, b_high, contract)
    return dot16(a_high, b_high, contract) + cross


def dot_exact(a, b, contract=((1,), (0,))):
    high, rest = halves(a)
    low = (a - high.astype(F32) - rest.astype(F32)).astype(BF16)
    return dot16(high, b, contract) + (dot16(rest, b, contract) + dot16(low, b, contract))


def dot_left(a, b, contract=((1,), (0,))):
    high, low = halves(a)
    return dot16(high, b, contract) + dot16(low, b, contract)


FIRST = ((0,), (0,))


def iota(shape, axis):
    return lax.broadcasted_iota(jnp.int32, shape, axis)


def head_spread(heads):
    shape = (heads, heads * HDIM)
    return (iota(shape, 1) // HDIM == iota(shape, 0)).astype(BF16)


def upper_ones(length):
    return (iota((length, length), 0) <= iota((length, length), 1)).astype(BF16)


def silu(value):
    return value / (1.0 + jnp.exp(-value))


def one_minus_exp(value):
    series = jnp.ones_like(value)
    for n in range(8, 1, -1):
        series = 1.0 + value * series * (1.0 / n)
    return jnp.where(value > -0.25, -value * series, 1.0 - jnp.exp(value))


def started(sources, targets, sems, first=0):
    copies = []
    for i, (source, target) in enumerate(zip(sources, targets)):
        copies.append(pltpu.make_async_copy(source, target, sems.at[first + i]))
        copies[-1].start()
    return copies


def finished(copies):
    for copy in copies:
        copy.wait()


def following(body, count, skipped):
    return lambda *refs: body(*refs[:count], *refs[count + skipped :])


def call(
    body,
    outs,
    args,
    fixed=0,
    held=0,
    near_args=0,
    near_outs=0,
    after=(),
    after_far=(),
    aliases=None,
    scratch=(),
    sems=0,
    flops=0,
    grant=8,
    near=False,
    spaces_of=None,
    name=None,
):
    body = following(body, len(args), len(after) + len(after_far))
    moved = sum(math.prod(a.shape) * a.dtype.itemsize for a in (*args, *outs))
    scratch = list(scratch) + ([pltpu.SemaphoreType.DMA((sems,))] if sems else [])
    space = pltpu.VMEM if near else pl.ANY
    spaces = [pltpu.HBM] * fixed + [pltpu.VMEM] * held
    args = [
        pltpu.with_memory_space_constraint(a, spaces[i]) if i < len(spaces) else a
        for i, a in enumerate(args)
    ]
    spaces += [space] * (len(args) - near_args - len(spaces)) + [pltpu.VMEM] * near_args
    spaces = spaces_of or spaces
    args, spaces = [*args, *after], spaces + [pl.ANY] * len(after)
    args += [pltpu.with_memory_space_constraint(a, pltpu.HBM) for a in after_far]
    spaces += [pltpu.HBM] * len(after_far)
    out_spaces = [space] * (len(outs) - near_outs) + [pltpu.VMEM] * near_outs
    return pl.pallas_call(
        body,
        out_shape=outs,
        in_specs=[pl.BlockSpec(memory_space=s) for s in spaces],
        out_specs=[pl.BlockSpec(memory_space=s) for s in out_spaces],
        scratch_shapes=scratch,
        input_output_aliases=aliases or {},
        compiler_params=pltpu.CompilerParams(vmem_limit_bytes=grant * 2**20),
        cost_estimate=pl.CostEstimate(flops=flops, bytes_accessed=moved, transcendentals=0),
        name=name,
    )(*args)


def room(arrays):
    return [pltpu.VMEM(a.shape, a.dtype) for a in arrays]


def array(shape, dtype):
    return jax.ShapeDtypeStruct(shape, dtype)


def ends_body(x_ref, b_ref, c_ref, ends_ref, sems):
    tokens, channels = x_ref.shape
    cut = pl.ds(tokens - EDGE, EDGE)
    finished(
        started(
            [x_ref.at[cut, :], b_ref.at[cut, :], c_ref.at[cut, :]],
            [
                ends_ref.at[:, pl.ds(0, channels)],
                ends_ref.at[:, pl.ds(channels, STATE)],
                ends_ref.at[:, pl.ds(channels + STATE, STATE)],
            ],
            sems,
        )
    )


def local_body(paired, count, *refs):
    far, outs, rest = refs[:count], refs[count : count + 3], refs[count + 3 :]
    ends = rest[: 1 + paired]
    rest = rest[1 + paired :]
    near, scratch, pad_ref, sems = rest[:count], rest[count : count + 3], rest[-2], rest[-1]
    copies = started(far, near, sems)
    x_ref, b_ref, c_ref, taps_ref, taps_bc_ref, logs_ref, skip_ref, ids_ref, ends_ref = near
    pre_ref, decay_ref, c_out_ref = scratch
    tokens, channels = x_ref.shape
    heads = logs_ref.shape[0]
    finished(copies)
    pad_ref[0:8, :] = ends_ref[...].astype(F32)[EDGE - 8 : EDGE]
    pad_ref[8 : 8 + tokens, :channels] = x_ref[...].astype(F32)
    pad_ref[8 : 8 + tokens, channels : channels + STATE] = b_ref[...].astype(F32)
    pad_ref[8 : 8 + tokens, channels + STATE :] = c_ref[...].astype(F32)

    def conv(taps, start, stop):
        total = jnp.zeros((tokens, stop - start), F32)
        for k in range(KCONV):
            first = 8 - (KCONV - 1) + k
            total = total + taps[k : k + 1] * pad_ref[first : first + tokens, start:stop]
        return silu(total)

    bc = conv(taps_bc_ref[...], channels, channels + 2 * STATE)
    bmat, cmat = bc[:, :STATE], bc[:, STATE:]
    c_out_ref[...] = cmat
    logs = logs_ref[...]
    inflow = jnp.sqrt(one_minus_exp(2.0 * logs))
    row = dot_exact(logs, upper_ones(tokens))
    column = row.T
    total = row[:, tokens - 1 :]
    spread = head_spread(heads)
    decay_ref[...] = dot_left(jnp.exp(row), spread, FIRST)
    copies = started(scratch[1:], outs[1:], sems)

    xconv = conv(taps_ref[...], 0, channels)
    pad_ref[:tokens, :channels] = xconv
    drive = xconv * dot_left(inflow, spread, FIRST)
    pre_ref[...] = drive
    fresh = drive * dot_left(jnp.exp(total - row), spread, FIRST)
    state = dot(bmat, fresh, FIRST)
    total = jnp.broadcast_to(total, (heads, NOTES))
    if paired:
        total = dot_exact(total, spread, FIRST)
        half = channels // 2
        side = lax.axis_index("ctx") % 2
        ids = ids_ref[...].astype(F32)
        line = jnp.concatenate([ids[0:1], ids[1:2]], axis=1)
        line = jnp.concatenate([line] * (half // line.shape[1]), axis=1)
        for ref, first in ((ends[0], side == 0), (ends[1], side != 0)):
            mine = jnp.where(first, state[:, :half], state[:, half:])
            logsum = jnp.where(first, total[:1, :half], total[:1, half:])
            if ref is ends[0]:
                put(ref, mine, logsum, line)
            else:
                send(ref, mine, logsum, line)
    else:
        ends[0][:STATE] = state
        ends[0][STATE:] = dot_exact(jnp.exp(total), spread, FIRST)

    skip = dot_exact(skip_ref[...], spread)
    meet = dot(cmat, bmat, ((1,), (1,)))
    lower = iota((tokens, tokens), 0) >= iota((tokens, tokens), 1)
    left = iota((tokens, 2 * HDIM), 1) < HDIM
    for pair in range(heads // 2):
        cut = slice(pair * 2 * HDIM, (pair + 1) * 2 * HDIM)
        d_high, d_low = halves(pre_ref[:, cut])
        both = []
        for h in (2 * pair, 2 * pair + 1):
            gap = column[:, h : h + 1] - row[h : h + 1, :]
            mix = jnp.where(lower, jnp.exp(gap), 0.0) * meet
            m_high, m_low = halves(mix)
            both.append(dot16(m_high, d_high) + dot16(m_high, d_low) + dot16(m_low, d_high))
        direct = skip[:, cut] * pad_ref[:tokens, cut]
        pre_ref[:, cut] = direct + jnp.where(left, both[0], both[1])
    finished(copies + started(scratch[:1], outs[:1], sems, 2))


def put(ref, state, logsum, line):
    ref[:STATE] = state
    at = iota((NOTES, state.shape[1]), 0)
    ref[STATE:] = jnp.where(at == 0, logsum, line)


def send(ref, state, logsum, line):
    largest = jnp.max(jnp.abs(state), axis=0, keepdims=True)
    power = jnp.ceil(jnp.log2(jnp.maximum(largest, 1e-30))) - 15.0
    whole = jnp.clip(jnp.round(state * jnp.exp2(-power)), -32767.0, 32767.0)
    ref[:STATE] = whole.astype(jnp.int32).astype(jnp.int16)
    logsum = jnp.round(jnp.maximum(logsum, -128.0) * 2.0**22).astype(jnp.int32)
    at = iota((16, state.shape[1]), 0)
    notes = jnp.where(at == 0, power.astype(jnp.int32), line.astype(jnp.int32))
    notes = jnp.where(at == 1, logsum >> 15, jnp.where(at == 2, logsum & 32767, notes))
    ref[STATE:] = notes.astype(jnp.int16)


def taken(ref):
    return ref[:STATE], ref[STATE : STATE + 1], ref[STATE + 1 : STATE + 2]


def received(ref):
    notes = ref[STATE:].astype(jnp.int32).astype(F32)
    state = ref[:STATE].astype(jnp.int32).astype(F32) * jnp.exp2(notes[0:1])
    return state, notes[1:2] * 2.0**-7 + notes[2:3] * 2.0**-22, notes[3:4]


def ordered(first, own, other):
    return [jnp.where(first, a, b) for a, b in zip(own, other)], [
        jnp.where(first, b, a) for a, b in zip(own, other)
    ]


def together(first, own, other, width):
    (a, a_log, a_line), (b, b_log, b_line) = ordered(first, own, other)
    line = jnp.concatenate([a_line[:, :width], b_line[:, :width]], axis=1)
    line = jnp.concatenate([line] * (a.shape[1] // line.shape[1]), axis=1)
    return jnp.exp(b_log) * a + b, a_log + b_log, line


def place():
    here = lax.axis_index("ctx")
    return here % 2, (here // 2) % 2, here // 4


def pair_body(width, own_ref, got_ref, pair_ref, sent_ref):
    x, _, _ = place()
    pair = together(x == 0, taken(own_ref), received(got_ref), width)
    put(pair_ref, *pair)
    send(sent_ref, *pair)


def list_ids(ids_ref, early, late, width):
    at = iota(ids_ref.shape, 0)
    ids = jnp.zeros(ids_ref.shape, F32)
    for i in range(ids_ref.shape[0]):
        line = (early, late)[i // 4]
        ids = jnp.where(at == i, line[:, i % 4 * width : (i % 4 + 1) * width], ids)
    ids_ref[...] = ids


def four_body(width, pair_ref, got_ref, sent_ref, ids_ref):
    _, z, _ = place()
    four = together(z == 0, taken(pair_ref), received(got_ref), 2 * width)
    send(sent_ref, *four)
    list_ids(ids_ref, four[2], four[2], width)


def turn_body(
    width,
    own_ref,
    got_ref,
    pair_ref,
    pair_got_ref,
    four_got_ref,
    rows_ref,
    mine_ref,
    sent_ref,
    ids_ref,
    same_rows_ref,
):
    same_rows_ref[...] = rows_ref[...]
    x, z, zz = place()
    pair, pair_got, four_got = taken(pair_ref), received(pair_got_ref), received(four_got_ref)
    line = together(z == 0, pair, pair_got, 2 * width)[2]
    (early,), (late,) = ordered(zz == 0, [line], [four_got[2]])
    list_ids(ids_ref, early, late, width)

    before = jnp.where(zz == 0, 0.0, four_got[0])
    before = jnp.where(z == 0, before, jnp.exp(pair_got[1]) * before + pair_got[0])
    (first, first_log), _ = ordered(x == 0, taken(own_ref)[:2], received(got_ref)[:2])
    after = jnp.exp(first_log) * before + first
    mine_ref[...] = jnp.where(x == 0, before, after)
    other = jnp.where(x == 0, after, before)
    send(sent_ref, other, jnp.zeros_like(first_log), jnp.zeros_like(first_log))


def prefix_body(parts_ref, starts_ref):
    ctx, rows, share = starts_ref.shape
    state = jnp.zeros((rows, share), F32)
    for i in range(ctx):
        starts_ref[i] = state
        if i < ctx - 1:
            state = parts_ref[i, STATE : STATE + 1] * state + parts_ref[i, :STATE]


def back_body(paired, gain_far, pre_far, decay_far, c_far, *rest):
    starts, (out_far, *rest) = rest[: 1 + paired], rest[1 + paired :]
    far = (gain_far, pre_far, decay_far, c_far)
    gain_ref, pre_ref, decay_ref, c_ref, out_ref, sems = rest
    copies = started(far, rest[:4], sems)
    channels = pre_ref.shape[1]
    width = min(channels, 4 * HDIM)
    group = (iota((width, width), 0) // HDIM == iota((width, width), 1) // HDIM).astype(BF16)
    if paired:
        side = lax.axis_index("ctx") % 2
        mine, other = starts[0][...], received(starts[1])[0]
        start = [jnp.where(side == 0, mine, other), jnp.where(side == 0, other, mine)]
        start = jnp.concatenate(start, axis=1)
    else:
        start = starts[0][...]
    finished(copies)
    c_high, c_low = halves(c_ref[...])
    copies = []
    for i in range(channels // width):
        cut = slice(i * width, (i + 1) * width)
        s_high, s_low = halves(start[:, cut])
        carried = dot16(c_high, s_high) + dot16(c_high, s_low) + dot16(c_low, s_high)
        pre = pre_ref[:, cut] + carried * decay_ref[:, cut]
        mean = dot_left(pre * pre, group) * (1.0 / HDIM)
        out_ref[:, cut] = (pre * lax.rsqrt(mean + 1e-05) * gain_ref[:, cut]).astype(BF16)
        copies += started([out_ref.at[:, cut]], [out_far.at[:, cut]], sems, i)
    finished(copies)


def entering_by_pairs(keep, sent, width, after, meanwhile, late_rows):
    pair_array, sent_array = array(keep.shape, F32), array(sent.shape, jnp.int16)
    ids_array = array((8, width), F32)
    got = swapped(sent, "ctx", 1)
    pair, sent = call(
        functools.partial(pair_body, width),
        [pair_array, sent_array],
        (keep, got),
        near=True,
        after=after[0],
        name="pair",
    )
    pair_got = swapped(sent, "ctx", 2)
    sent, ids = call(
        functools.partial(four_body, width),
        [sent_array, ids_array],
        (pair, pair_got),
        near=True,
        after=after[1],
        name="four",
    )
    four_got = swapped(sent, "ctx", 4)
    done = meanwhile(ids)
    mine, sent, ids, late_rows = call(
        functools.partial(turn_body, width),
        [array((STATE, keep.shape[1]), F32), sent_array, ids_array, late_rows],
        (keep, got, pair, pair_got, four_got, late_rows),
        near=True,
        after=after[2],
        after_far=(done,),
        name="turn",
    )
    return (mine, swapped(sent, "ctx", 1)), ids, (done, late_rows)


def entering_by_rows(state):
    ctx = lax.axis_size("ctx")
    rows, channels = state.shape
    slabs = state.reshape(rows, ctx, channels // ctx).transpose(1, 0, 2)
    parts = lax.all_to_all(slabs, "ctx", split_axis=0, concat_axis=0, tiled=True)
    (starts,) = call(
        prefix_body,
        [array((ctx, STATE, channels // ctx), F32)],
        (parts,),
        near=True,
        name="prefix",
    )
    start = lax.all_to_all(starts, "ctx", split_axis=0, concat_axis=0, tiled=True)
    return start.transpose(1, 0, 2).reshape(STATE, channels)


def mixing(
    after, meanwhile, late_rows, seq_input, b_input, c_input, before, conv_x, conv_bc, log_decay, skip, gain, ids
):
    tokens, channels = seq_input.shape
    heads = skip.shape[0]
    width = 2 * ids.shape[0]
    paired = after is not None
    outs = [
        array((tokens, channels), F32),
        array((tokens, channels), F32),
        array((tokens, STATE), F32),
    ]
    if paired:
        ends = [array((STATE + NOTES, channels // 2), F32)]
        ends.append(array((STATE + 16, channels // 2), jnp.int16))
    else:
        ends = [array((STATE + NOTES, channels), F32)]
    args = (seq_input, b_input, c_input, conv_x, conv_bc, log_decay)
    args = (*args, skip.reshape(1, heads), ids.T, before)
    pre, decay, cmat, *ends = call(
        functools.partial(local_body, paired, len(args)),
        outs + ends,
        args,
        fixed=len(args) - 1,
        near_outs=len(ends),
        after=after[0] if paired else (),
        scratch=room(args) + room(outs) + [pltpu.VMEM((8 + tokens, channels + 2 * STATE), F32)],
        sems=len(args),
        flops=5 * 10**9,
        grant=20,
        name="local",
    )
    done = None
    if paired:
        first, second, third = after[1:]
        after = (first, second, third)
        starts, lines_of_ids, done = entering_by_pairs(
            *ends, width, after, meanwhile, late_rows
        )
    else:
        starts, lines_of_ids = (entering_by_rows(ends[0]),), None

    def finish(after=()):
        args = (gain.reshape(1, channels), pre, decay, cmat)
        outs = [array((tokens, channels), BF16)]
        return call(
            functools.partial(back_body, paired),
            outs,
            (*args, *starts),
            fixed=1,
            near_args=len(starts),
            after_far=after,
            scratch=room(args) + room(outs),
            sems=max(4, channels // (4 * HDIM)),
            flops=10**9,
            grant=16,
            name="back",
        )[0]

    return finish, lines_of_ids, done


TILE = 512


def join_body(a_ref, b_ref, out_ref, sems):
    rows = a_ref.shape[0]
    finished(
        started([a_ref, b_ref], [out_ref.at[pl.ds(0, rows), :], out_ref.at[pl.ds(rows, rows), :]], sems)
    )


def swapped(block, axis, bit):
    return lax.ppermute(block, axis, [(i, i ^ bit) for i in range(lax.axis_size(axis))])


def expert_body(part, w_gate, w_up, *refs):
    far, ids_ref, out_far = refs[:8], refs[8], refs[9 + part]
    pick_ref, hid_ref, out_ref, sems = refs[10 + part :]
    length, hidden = out_ref.shape
    rows = far[0].shape[0] // 2
    depth = far[0].shape[1]
    me = lax.axis_index("exp")
    here = lax.axis_index("ctx")
    downs = [pl.ds(pl.multiple_of((me ^ k) * depth, depth), depth) for k in range(4)]
    pair = (here // 4) ^ part

    shape = (rows, rows)
    earlier = (iota(shape, 1) < iota(shape, 0)).astype(F32)
    across = iota(shape, 1)
    diagonal = iota(shape, 0) == across
    turns = [(here % 4) ^ (2 * (i % 2) + i // 2) for i in range(length // rows)]
    for i, block in enumerate(turns):
        line = ids_ref[pl.ds(4 * pair + block, 1), :]
        mine = me.astype(F32)
        named = ((line[:, :rows] == mine) | (line[:, rows:] == mine)).astype(F32)
        column = jnp.sum(jnp.where(diagonal, named, 0.0), axis=1, keepdims=True)
        position = jnp.sum(earlier * named, axis=1, keepdims=True).astype(jnp.int32)
        pick_ref[i] = jnp.where(position == across, column, 0.0).astype(BF16)

    out_copies = []
    out_rows = pl.ds(pl.multiple_of(pair * length, length), length)
    for n in range(hidden // TILE):
        cut = slice(n * TILE, (n + 1) * TILE)
        gate = upper = None
        for k in range(4):
            block = jnp.concatenate([piece[...] for piece in far[2 * k : 2 * k + 2]], axis=0)
            more = dot16(block, w_gate[0, downs[k], cut])
            gate = more if k == 0 else gate + more
            more = dot16(block, w_up[0, downs[k], cut])
            upper = more if k == 0 else upper + more
        hid_ref[...] = (silu(gate) * upper).astype(BF16)
        for i, block in enumerate(turns):
            picked = dot16(pick_ref[i], hid_ref[i * rows : (i + 1) * rows], FIRST)
            out_ref[pl.ds(pl.multiple_of(block * rows, rows), rows), cut] = picked.astype(BF16)
        out_copies += started([out_ref.at[:, cut]], [out_far.at[0, out_rows, cut]], sems, n)
    finished(out_copies)


def along_z(moe_input):
    rows, columns = moe_input.shape
    joined = call(
        join_body,
        [array((2 * rows, columns), BF16)],
        (moe_input, swapped(moe_input, "ctx", 2)),
        fixed=1,
        sems=2,
        name="join",
    )[0]
    return joined, swapped(joined, "ctx", 4)


def gathered(moe_input):
    z = along_z(moe_input)
    x = [swapped(a, "ctx", 1) for a in z]
    y = [swapped(a, "exp", 2) for a in z]
    d = (swapped(x[0], "exp", 2), swapped(y[1], "ctx", 1))
    halves_of_rows = []
    for i, pieces in enumerate(zip(z, x, y, d)):
        beside = [swapped(a, "exp", 1) for a in pieces[: 4 - i]]
        halves_of_rows.append([*pieces[:2], *beside[:2], *pieces[2:], *beside[2:]])
    return halves_of_rows


def experts_by_tokens(part, pieces, ids, w_gate, w_up, so_far):
    rows = pieces[0].shape[0] // 2
    length = 4 * rows
    hidden = w_gate.shape[2]
    args = (w_gate, w_up, *pieces, ids)
    return call(
        functools.partial(expert_body, part),
        [pltpu.HBM((1, 2 * length, hidden), BF16)],
        args + ((so_far,) if part else ()),
        held=2,
        near_args=0,
        aliases={len(args): 0} if part else None,
        scratch=[
            pltpu.VMEM((length // rows, rows, rows), BF16),
            pltpu.VMEM((length, TILE), BF16),
            pltpu.VMEM((length, hidden), BF16),
        ],
        sems=hidden // TILE,
        flops=4 * length * w_gate.shape[1] * hidden,
        grant=16,
        spaces_of=[pltpu.VMEM] * len(args) + [pltpu.HBM] * part,
        name="experts",
    )[0]


def slot_matrix(pairs, expert, capacity):
    named = jnp.any(pairs == expert, axis=1).astype(jnp.int32)
    position = jnp.cumsum(named) - named
    hit = position[None, :] == jnp.arange(capacity, dtype=jnp.int32)[:, None]
    return (hit & (named[None, :] > 0)).astype(BF16)


def experts_by_slots(moe_input, pairs, w_gate, w_up):
    experts = lax.axis_size("exp")
    capacity = 4 * moe_input.shape[0] // experts
    pick = jax.vmap(lambda e: slot_matrix(pairs, e, capacity))(jnp.arange(experts))
    slots = jnp.einsum("eqt,td->eqd", pick, moe_input, preferred_element_type=F32)
    routed = lax.all_to_all(slots.astype(BF16), "exp", split_axis=0, concat_axis=2, tiled=True)
    rows = lax.all_gather(routed[0], "ctx", axis=0, tiled=True)
    gate = jnp.dot(rows, w_gate[0], preferred_element_type=F32)
    upper = jnp.dot(rows, w_up[0], preferred_element_type=F32)
    return (jax.nn.silu(gate) * upper).astype(BF16)[None]


def on_device(
    seq_input,
    b_input,
    c_input,
    conv_x,
    conv_bc,
    log_decay,
    skip_gain,
    norm_gain,
    moe_input,
    expert_ids,
    w_gate,
    w_up,
):
    ctx = lax.axis_size("ctx")
    by_tokens = lax.axis_size("exp") == 4 and ctx == 8
    tokens, channels = seq_input.shape
    ends = call(
        ends_body,
        [array((EDGE, channels + 2 * STATE), BF16)],
        (seq_input, b_input, c_input),
        fixed=3,
        sems=3,
        name="ends",
    )[0]
    before = lax.ppermute(ends, "ctx", [(i, i + 1) for i in range(ctx - 1)])
    follow = meanwhile = late_rows = None
    if by_tokens:
        one, two = gathered(moe_input)
        follow = (one[:1], (one[1], one[4], one[2], two[0]), ())
        follow += ((two[1], two[4], two[2]),)
        late_rows = two[5]

        def meanwhile(ids):
            return experts_by_tokens(0, one, ids, w_gate, w_up, None)

    finish, ids, done = mixing(
        follow,
        meanwhile,
        late_rows,
        seq_input,
        b_input,
        c_input,
        before,
        conv_x,
        conv_bc,
        log_decay,
        skip_gain,
        norm_gain,
        expert_ids,
    )
    if by_tokens:
        hidden, late_rows = done
        two.append(swapped(late_rows, "exp", 1))
        hidden = experts_by_tokens(1, two, ids, w_gate, w_up, hidden)
        mixed = finish((hidden,))
    else:
        mixed = finish()
        hidden = experts_by_slots(moe_input, expert_ids, w_gate, w_up)
    return (mixed, hidden)


def solution(mesh):
    in_specs = (
        P("ctx", "exp"),
        P("ctx", None),
        P("ctx", None),
        P(None, "exp"),
        P(),
        P("exp", "ctx"),
        P("exp"),
        P("exp"),
        P("ctx", "exp"),
        P("ctx", None),
        P("exp", None, "ctx"),
        P("exp", None, "ctx"),
    )
    out_specs = (P("ctx", "exp"), P("exp", None, "ctx"))
    return jax.shard_map(
        on_device, mesh=mesh, in_specs=in_specs, out_specs=out_specs, check_vma=False
    )
```

```python
import functools
import math

import jax
import jax.numpy as jnp
from jax import lax
from jax.experimental import pallas as pl
from jax.experimental.pallas import tpu as pltpu
from jax.sharding import PartitionSpec as P

HDIM = 64
STATE = 128
KCONV = 4
EDGE = 16
NOTES = 8

F32 = jnp.float32
BF16 = jnp.bfloat16


def dot16(a, b, contract=((1,), (0,))):
    return lax.dot_general(a, b, (contract, ((), ())), preferred_element_type=F32)


def halves(value):
    high = value.astype(BF16)
    return high, (value - high.astype(F32)).astype(BF16)


def dot(a, b, contract=((1,), (0,))):
    a_high, a_low = halves(a)
    b_high, b_low = halves(b)
    cross = dot16(a_high, b_low, contract) + dot16(a_low, b_high, contract)
    return dot16(a_high, b_high, contract) + cross


def dot_exact(a, b, contract=((1,), (0,))):
    high, rest = halves(a)
    low = (a - high.astype(F32) - rest.astype(F32)).astype(BF16)
    return dot16(high, b, contract) + (dot16(rest, b, contract) + dot16(low, b, contract))


def dot_left(a, b, contract=((1,), (0,))):
    high, low = halves(a)
    return dot16(high, b, contract) + dot16(low, b, contract)


FIRST = ((0,), (0,))


def iota(shape, axis):
    return lax.broadcasted_iota(jnp.int32, shape, axis)


def head_spread(heads):
    shape = (heads, heads * HDIM)
    return (iota(shape, 1) // HDIM == iota(shape, 0)).astype(BF16)


def upper_ones(length):
    return (iota((length, length), 0) <= iota((length, length), 1)).astype(BF16)


def silu(value):
    return value / (1.0 + jnp.exp(-value))


def one_minus_exp(value):
    series = jnp.ones_like(value)
    for n in range(8, 1, -1):
        series = 1.0 + value * series * (1.0 / n)
    return jnp.where(value > -0.25, -value * series, 1.0 - jnp.exp(value))


def started(sources, targets, sems, first=0):
    copies = []
    for i, (source, target) in enumerate(zip(sources, targets)):
        copies.append(pltpu.make_async_copy(source, target, sems.at[first + i]))
        copies[-1].start()
    return copies


def finished(copies):
    for copy in copies:
        copy.wait()


def following(body, count, skipped):
    return lambda *refs: body(*refs[:count], *refs[count + skipped :])


def call(
    body,
    outs,
    args,
    fixed=0,
    held=0,
    near_args=0,
    near_outs=0,
    after=(),
    after_far=(),
    aliases=None,
    scratch=(),
    sems=0,
    flops=0,
    grant=8,
    near=False,
    spaces_of=None,
    name=None,
):
    body = following(body, len(args), len(after) + len(after_far))
    moved = sum(math.prod(a.shape) * a.dtype.itemsize for a in (*args, *outs))
    scratch = list(scratch) + ([pltpu.SemaphoreType.DMA((sems,))] if sems else [])
    space = pltpu.VMEM if near else pl.ANY
    spaces = [pltpu.HBM] * fixed + [pltpu.VMEM] * held
    args = [
        pltpu.with_memory_space_constraint(a, spaces[i]) if i < len(spaces) else a
        for i, a in enumerate(args)
    ]
    spaces += [space] * (len(args) - near_args - len(spaces)) + [pltpu.VMEM] * near_args
    spaces = spaces_of or spaces
    args, spaces = [*args, *after], spaces + [pl.ANY] * len(after)
    args += [pltpu.with_memory_space_constraint(a, pltpu.HBM) for a in after_far]
    spaces += [pltpu.HBM] * len(after_far)
    out_spaces = [space] * (len(outs) - near_outs) + [pltpu.VMEM] * near_outs
    return pl.pallas_call(
        body,
        out_shape=outs,
        in_specs=[pl.BlockSpec(memory_space=s) for s in spaces],
        out_specs=[pl.BlockSpec(memory_space=s) for s in out_spaces],
        scratch_shapes=scratch,
        input_output_aliases=aliases or {},
        compiler_params=pltpu.CompilerParams(vmem_limit_bytes=grant * 2**20),
        cost_estimate=pl.CostEstimate(flops=flops, bytes_accessed=moved, transcendentals=0),
        name=name,
    )(*args)


def room(arrays):
    return [pltpu.VMEM(a.shape, a.dtype) for a in arrays]


def array(shape, dtype):
    return jax.ShapeDtypeStruct(shape, dtype)


def ends_body(x_ref, b_ref, c_ref, ends_ref, sems):
    tokens, channels = x_ref.shape
    cut = pl.ds(tokens - EDGE, EDGE)
    finished(
        started(
            [x_ref.at[cut, :], b_ref.at[cut, :], c_ref.at[cut, :]],
            [
                ends_ref.at[:, pl.ds(0, channels)],
                ends_ref.at[:, pl.ds(channels, STATE)],
                ends_ref.at[:, pl.ds(channels + STATE, STATE)],
            ],
            sems,
        )
    )


def local_body(paired, count, *refs):
    far, outs, rest = refs[:count], refs[count : count + 3], refs[count + 3 :]
    ends = rest[: 1 + paired]
    rest = rest[1 + paired :]
    near, scratch, pad_ref, sems = rest[:count], rest[count : count + 3], rest[-2], rest[-1]
    copies = started(far, near, sems)
    x_ref, b_ref, c_ref, taps_ref, taps_bc_ref, logs_ref, skip_ref, ids_ref, ends_ref = near
    pre_ref, decay_ref, c_out_ref = scratch
    tokens, channels = x_ref.shape
    heads = logs_ref.shape[0]
    finished(copies)
    pad_ref[0:8, :] = ends_ref[...].astype(F32)[EDGE - 8 : EDGE]
    pad_ref[8 : 8 + tokens, :channels] = x_ref[...].astype(F32)
    pad_ref[8 : 8 + tokens, channels : channels + STATE] = b_ref[...].astype(F32)
    pad_ref[8 : 8 + tokens, channels + STATE :] = c_ref[...].astype(F32)

    def conv(taps, start, stop):
        total = jnp.zeros((tokens, stop - start), F32)
        for k in range(KCONV):
            first = 8 - (KCONV - 1) + k
            total = total + taps[k : k + 1] * pad_ref[first : first + tokens, start:stop]
        return silu(total)

    bc = conv(taps_bc_ref[...], channels, channels + 2 * STATE)
    bmat, cmat = bc[:, :STATE], bc[:, STATE:]
    c_out_ref[...] = cmat
    logs = logs_ref[...]
    inflow = jnp.sqrt(one_minus_exp(2.0 * logs))
    row = dot_exact(logs, upper_ones(tokens))
    column = row.T
    total = row[:, tokens - 1 :]
    spread = head_spread(heads)
    decay_ref[...] = dot_left(jnp.exp(row), spread, FIRST)
    copies = started(scratch[1:], outs[1:], sems)

    xconv = conv(taps_ref[...], 0, channels)
    pad_ref[:tokens, :channels] = xconv
    drive = xconv * dot_left(inflow, spread, FIRST)
    pre_ref[...] = drive
    fresh = drive * dot_left(jnp.exp(total - row), spread, FIRST)
    state = dot(bmat, fresh, FIRST)
    total = jnp.broadcast_to(total, (heads, NOTES))
    if paired:
        total = dot_exact(total, spread, FIRST)
        half = channels // 2
        side = lax.axis_index("ctx") % 2
        ids = ids_ref[...].astype(F32)
        line = jnp.concatenate([ids[0:1], ids[1:2]], axis=1)
        line = jnp.concatenate([line] * (half // line.shape[1]), axis=1)
        for ref, first in ((ends[0], side == 0), (ends[1], side != 0)):
            mine = jnp.where(first, state[:, :half], state[:, half:])
            logsum = jnp.where(first, total[:1, :half], total[:1, half:])
            if ref is ends[0]:
                put(ref, mine, logsum, line)
            else:
                send(ref, mine, logsum, line)
    else:
        ends[0][:STATE] = state
        ends[0][STATE:] = dot_exact(jnp.exp(total), spread, FIRST)

    skip = dot_exact(skip_ref[...], spread)
    meet = dot(cmat, bmat, ((1,), (1,)))
    lower = iota((tokens, tokens), 0) >= iota((tokens, tokens), 1)
    left = iota((tokens, 2 * HDIM), 1) < HDIM
    for pair in range(heads // 2):
        cut = slice(pair * 2 * HDIM, (pair + 1) * 2 * HDIM)
        d_high, d_low = halves(pre_ref[:, cut])
        both = []
        for h in (2 * pair, 2 * pair + 1):
            gap = column[:, h : h + 1] - row[h : h + 1, :]
            mix = jnp.where(lower, jnp.exp(gap), 0.0) * meet
            m_high, m_low = halves(mix)
            both.append(dot16(m_high, d_high) + dot16(m_high, d_low) + dot16(m_low, d_high))
        direct = skip[:, cut] * pad_ref[:tokens, cut]
        pre_ref[:, cut] = direct + jnp.where(left, both[0], both[1])
    finished(copies + started(scratch[:1], outs[:1], sems, 2))


def put(ref, state, logsum, line):
    ref[:STATE] = state
    at = iota((NOTES, state.shape[1]), 0)
    ref[STATE:] = jnp.where(at == 0, logsum, line)


def send(ref, state, logsum, line):
    largest = jnp.max(jnp.abs(state), axis=0, keepdims=True)
    power = jnp.ceil(jnp.log2(jnp.maximum(largest, 1e-30))) - 15.0
    whole = jnp.clip(jnp.round(state * jnp.exp2(-power)), -32767.0, 32767.0)
    ref[:STATE] = whole.astype(jnp.int32).astype(jnp.int16)
    logsum = jnp.round(jnp.maximum(logsum, -128.0) * 2.0**22).astype(jnp.int32)
    at = iota((16, state.shape[1]), 0)
    notes = jnp.where(at == 0, power.astype(jnp.int32), line.astype(jnp.int32))
    notes = jnp.where(at == 1, logsum >> 15, jnp.where(at == 2, logsum & 32767, notes))
    ref[STATE:] = notes.astype(jnp.int16)


def taken(ref):
    return ref[:STATE], ref[STATE : STATE + 1], ref[STATE + 1 : STATE + 2]


def received(ref):
    notes = ref[STATE:].astype(jnp.int32).astype(F32)
    state = ref[:STATE].astype(jnp.int32).astype(F32) * jnp.exp2(notes[0:1])
    return state, notes[1:2] * 2.0**-7 + notes[2:3] * 2.0**-22, notes[3:4]


def ordered(first, own, other):
    return [jnp.where(first, a, b) for a, b in zip(own, other)], [
        jnp.where(first, b, a) for a, b in zip(own, other)
    ]


def together(first, own, other, width):
    (a, a_log, a_line), (b, b_log, b_line) = ordered(first, own, other)
    line = jnp.concatenate([a_line[:, :width], b_line[:, :width]], axis=1)
    line = jnp.concatenate([line] * (a.shape[1] // line.shape[1]), axis=1)
    return jnp.exp(b_log) * a + b, a_log + b_log, line


def place():
    here = lax.axis_index("ctx")
    return here % 2, (here // 2) % 2, here // 4


def pair_body(width, own_ref, got_ref, pair_ref, sent_ref):
    x, _, _ = place()
    pair = together(x == 0, taken(own_ref), received(got_ref), width)
    put(pair_ref, *pair)
    send(sent_ref, *pair)


def list_ids(ids_ref, early, late, width):
    at = iota(ids_ref.shape, 0)
    ids = jnp.zeros(ids_ref.shape, F32)
    for i in range(ids_ref.shape[0]):
        line = (early, late)[i // 4]
        ids = jnp.where(at == i, line[:, i % 4 * width : (i % 4 + 1) * width], ids)
    ids_ref[...] = ids


def join_rows(pieces, joined_ref):
    rows = pieces[0].shape[0]
    for i, piece in enumerate(pieces):
        joined_ref[i * rows : (i + 1) * rows] = piece[...]


def four_body(width, pair_ref, got_ref, a, b, c, d, sent_ref, ids_ref, joined_ref):
    join_rows((a, b, c, d), joined_ref)
    _, z, _ = place()
    four = together(z == 0, taken(pair_ref), received(got_ref), 2 * width)
    send(sent_ref, *four)
    list_ids(ids_ref, four[2], four[2], width)


def turn_body(
    width,
    own_ref,
    got_ref,
    pair_ref,
    pair_got_ref,
    four_got_ref,
    a,
    b,
    c,
    d,
    mine_ref,
    sent_ref,
    ids_ref,
    joined_ref,
):
    join_rows((a, b, c, d), joined_ref)
    x, z, zz = place()
    pair, pair_got, four_got = taken(pair_ref), received(pair_got_ref), received(four_got_ref)
    line = together(z == 0, pair, pair_got, 2 * width)[2]
    (early,), (late,) = ordered(zz == 0, [line], [four_got[2]])
    list_ids(ids_ref, early, late, width)

    before = jnp.where(zz == 0, 0.0, four_got[0])
    before = jnp.where(z == 0, before, jnp.exp(pair_got[1]) * before + pair_got[0])
    (first, first_log), _ = ordered(x == 0, taken(own_ref)[:2], received(got_ref)[:2])
    after = jnp.exp(first_log) * before + first
    mine_ref[...] = jnp.where(x == 0, before, after)
    other = jnp.where(x == 0, after, before)
    send(sent_ref, other, jnp.zeros_like(first_log), jnp.zeros_like(first_log))


def prefix_body(parts_ref, starts_ref):
    ctx, rows, share = starts_ref.shape
    state = jnp.zeros((rows, share), F32)
    for i in range(ctx):
        starts_ref[i] = state
        if i < ctx - 1:
            state = parts_ref[i, STATE : STATE + 1] * state + parts_ref[i, :STATE]


def back_body(paired, gain_far, pre_far, decay_far, c_far, *rest):
    starts, (out_far, *rest) = rest[: 1 + paired], rest[1 + paired :]
    far = (gain_far, pre_far, decay_far, c_far)
    gain_ref, pre_ref, decay_ref, c_ref, out_ref, sems = rest
    copies = started(far, rest[:4], sems)
    channels = pre_ref.shape[1]
    width = min(channels, 4 * HDIM)
    group = (iota((width, width), 0) // HDIM == iota((width, width), 1) // HDIM).astype(BF16)
    if paired:
        side = lax.axis_index("ctx") % 2
        mine, other = starts[0][...], received(starts[1])[0]
        start = [jnp.where(side == 0, mine, other), jnp.where(side == 0, other, mine)]
        start = jnp.concatenate(start, axis=1)
    else:
        start = starts[0][...]
    finished(copies)
    c_high, c_low = halves(c_ref[...])
    copies = []
    for i in range(channels // width):
        cut = slice(i * width, (i + 1) * width)
        s_high, s_low = halves(start[:, cut])
        carried = dot16(c_high, s_high) + dot16(c_high, s_low) + dot16(c_low, s_high)
        pre = pre_ref[:, cut] + carried * decay_ref[:, cut]
        mean = dot_left(pre * pre, group) * (1.0 / HDIM)
        out_ref[:, cut] = (pre * lax.rsqrt(mean + 1e-05) * gain_ref[:, cut]).astype(BF16)
        copies += started([out_ref.at[:, cut]], [out_far.at[:, cut]], sems, i)
    finished(copies)


def entering_by_pairs(keep, sent, width, follow, pieces, meanwhile):
    pair_array, sent_array = array(keep.shape, F32), array(sent.shape, jnp.int16)
    ids_array = array((8, width), F32)
    joined_array = [array((4 * p[0].shape[0], p[0].shape[1]), BF16) for p in pieces]
    got = swapped(sent, "ctx", 1)
    pair, sent = call(
        functools.partial(pair_body, width),
        [pair_array, sent_array],
        (keep, got),
        near=True,
        after=follow,
        name="pair",
    )
    pair_got = swapped(sent, "ctx", 2)
    sent, ids, joined = call(
        functools.partial(four_body, width),
        [sent_array, ids_array, joined_array[0]],
        (pair, pair_got, *pieces[0]),
        near=True,
        after=pieces[1][1:3],
        name="four",
    )
    four_got = swapped(sent, "ctx", 4)
    done = meanwhile(ids, joined)
    mine, sent, ids, joined = call(
        functools.partial(turn_body, width),
        [array((STATE, keep.shape[1]), F32), sent_array, ids_array, joined_array[1]],
        (keep, got, pair, pair_got, four_got, *pieces[1]),
        near=True,
        after_far=(done,),
        name="turn",
    )
    return (mine, swapped(sent, "ctx", 1)), ids, joined, done


def entering_by_rows(state):
    ctx = lax.axis_size("ctx")
    rows, channels = state.shape
    slabs = state.reshape(rows, ctx, channels // ctx).transpose(1, 0, 2)
    parts = lax.all_to_all(slabs, "ctx", split_axis=0, concat_axis=0, tiled=True)
    (starts,) = call(
        prefix_body,
        [array((ctx, STATE, channels // ctx), F32)],
        (parts,),
        near=True,
        name="prefix",
    )
    start = lax.all_to_all(starts, "ctx", split_axis=0, concat_axis=0, tiled=True)
    return start.transpose(1, 0, 2).reshape(STATE, channels)


def mixing(
    pieces, meanwhile, seq_input, b_input, c_input, before, conv_x, conv_bc, log_decay, skip, gain, ids
):
    tokens, channels = seq_input.shape
    heads = skip.shape[0]
    width = 2 * ids.shape[0]
    paired = pieces is not None
    outs = [
        array((tokens, channels), F32),
        array((tokens, channels), F32),
        array((tokens, STATE), F32),
    ]
    if paired:
        ends = [array((STATE + NOTES, channels // 2), F32)]
        ends.append(array((STATE + 16, channels // 2), jnp.int16))
    else:
        ends = [array((STATE + NOTES, channels), F32)]
    args = (seq_input, b_input, c_input, conv_x, conv_bc, log_decay)
    args = (*args, skip.reshape(1, heads), ids.T, before)
    pre, decay, cmat, *ends = call(
        functools.partial(local_body, paired, len(args)),
        outs + ends,
        args,
        fixed=len(args) - 1,
        near_outs=len(ends),
        after=pieces[0][:1] if paired else (),
        scratch=room(args) + room(outs) + [pltpu.VMEM((8 + tokens, channels + 2 * STATE), F32)],
        sems=len(args),
        flops=5 * 10**9,
        grant=20,
        name="local",
    )
    late = None
    if paired:
        follow = (*pieces[0][1:3], pieces[1][0])
        starts, *late = entering_by_pairs(*ends, width, follow, pieces, meanwhile)
    else:
        starts = (entering_by_rows(ends[0]),)

    def finish(after=()):
        args = (gain.reshape(1, channels), pre, decay, cmat)
        outs = [array((tokens, channels), BF16)]
        return call(
            functools.partial(back_body, paired),
            outs,
            (*args, *starts),
            fixed=1,
            near_args=len(starts),
            after_far=after,
            scratch=room(args) + room(outs),
            sems=max(4, channels // (4 * HDIM)),
            flops=10**9,
            grant=16,
            name="back",
        )[0]

    return finish, late


TILE = 512


def join_body(a_ref, b_ref, out_ref, sems):
    rows = a_ref.shape[0]
    finished(
        started([a_ref, b_ref], [out_ref.at[pl.ds(0, rows), :], out_ref.at[pl.ds(rows, rows), :]], sems)
    )


def swapped(block, axis, bit):
    return lax.ppermute(block, axis, [(i, i ^ bit) for i in range(lax.axis_size(axis))])


def expert_body(part, w_gate, w_up, *refs):
    pieces, joined_ref, ids_ref, out_far = refs[:4], refs[4], refs[5], refs[6 + part]
    pick_ref, hid_ref, out_ref, sems = refs[7 + part :]
    length, hidden = out_ref.shape
    rows = pieces[0].shape[0] // 2
    depth = pieces[0].shape[1]
    me = lax.axis_index("exp")
    here = lax.axis_index("ctx")
    downs = [pl.ds(pl.multiple_of((me ^ k) * depth, depth), depth) for k in range(4)]
    pair = (here // 4) ^ part

    shape = (rows, rows)
    earlier = (iota(shape, 1) < iota(shape, 0)).astype(F32)
    across = iota(shape, 1)
    diagonal = iota(shape, 0) == across
    turns = [(here % 4) ^ (2 * (i % 2) + i // 2) for i in range(length // rows)]
    for i, block in enumerate(turns):
        line = ids_ref[pl.ds(4 * pair + block, 1), :]
        mine = me.astype(F32)
        named = ((line[:, :rows] == mine) | (line[:, rows:] == mine)).astype(F32)
        column = jnp.sum(jnp.where(diagonal, named, 0.0), axis=1, keepdims=True)
        position = jnp.sum(earlier * named, axis=1, keepdims=True).astype(jnp.int32)
        pick_ref[i] = jnp.where(position == across, column, 0.0).astype(BF16)

    out_copies = []
    out_rows = pl.ds(pl.multiple_of(pair * length, length), length)
    for n in range(hidden // TILE):
        cut = slice(n * TILE, (n + 1) * TILE)
        gate = upper = None
        for k in range(4):
            if k % 2 == 0:
                block = jnp.concatenate([piece[...] for piece in pieces[k : k + 2]], axis=0)
            else:
                block = joined_ref[k // 2 * length : (k // 2 + 1) * length]
            more = dot16(block, w_gate[0, downs[k], cut])
            gate = more if k == 0 else gate + more
            more = dot16(block, w_up[0, downs[k], cut])
            upper = more if k == 0 else upper + more
        hid_ref[...] = (silu(gate) * upper).astype(BF16)
        for i, block in enumerate(turns):
            picked = dot16(pick_ref[i], hid_ref[i * rows : (i + 1) * rows], FIRST)
            out_ref[pl.ds(pl.multiple_of(block * rows, rows), rows), cut] = picked.astype(BF16)
        out_copies += started([out_ref.at[:, cut]], [out_far.at[0, out_rows, cut]], sems, n)
    finished(out_copies)


def along_z(moe_input):
    rows, columns = moe_input.shape
    joined = call(
        join_body,
        [array((2 * rows, columns), BF16)],
        (moe_input, swapped(moe_input, "ctx", 2)),
        fixed=1,
        sems=2,
        name="join",
    )[0]
    return joined, swapped(joined, "ctx", 4)


def gathered(moe_input):
    z = along_z(moe_input)
    x = [swapped(a, "ctx", 1) for a in z]
    y = [swapped(a, "exp", 2) for a in z]
    d = (swapped(x[0], "exp", 2), swapped(y[1], "ctx", 1))
    return list(zip(z, x, y, d))


def experts_by_tokens(part, pieces, joined, ids, w_gate, w_up, so_far):
    rows = pieces[0].shape[0] // 2
    length = 4 * rows
    hidden = w_gate.shape[2]
    args = (w_gate, w_up, *pieces, swapped(joined, "exp", 1), ids)
    return call(
        functools.partial(expert_body, part),
        [pltpu.HBM((1, 2 * length, hidden), BF16)],
        args + ((so_far,) if part else ()),
        held=2,
        near_args=0,
        aliases={len(args): 0} if part else None,
        scratch=[
            pltpu.VMEM((length // rows, rows, rows), BF16),
            pltpu.VMEM((length, TILE), BF16),
            pltpu.VMEM((length, hidden), BF16),
        ],
        sems=hidden // TILE,
        flops=4 * length * w_gate.shape[1] * hidden,
        grant=16,
        spaces_of=[pltpu.VMEM] * len(args) + [pltpu.HBM] * part,
        name="experts",
    )[0]


def slot_matrix(pairs, expert, capacity):
    named = jnp.any(pairs == expert, axis=1).astype(jnp.int32)
    position = jnp.cumsum(named) - named
    hit = position[None, :] == jnp.arange(capacity, dtype=jnp.int32)[:, None]
    return (hit & (named[None, :] > 0)).astype(BF16)


def experts_by_slots(moe_input, pairs, w_gate, w_up):
    experts = lax.axis_size("exp")
    capacity = 4 * moe_input.shape[0] // experts
    pick = jax.vmap(lambda e: slot_matrix(pairs, e, capacity))(jnp.arange(experts))
    slots = jnp.einsum("eqt,td->eqd", pick, moe_input, preferred_element_type=F32)
    routed = lax.all_to_all(slots.astype(BF16), "exp", split_axis=0, concat_axis=2, tiled=True)
    rows = lax.all_gather(routed[0], "ctx", axis=0, tiled=True)
    gate = jnp.dot(rows, w_gate[0], preferred_element_type=F32)
    upper = jnp.dot(rows, w_up[0], preferred_element_type=F32)
    return (jax.nn.silu(gate) * upper).astype(BF16)[None]


def on_device(
    seq_input,
    b_input,
    c_input,
    conv_x,
    conv_bc,
    log_decay,
    skip_gain,
    norm_gain,
    moe_input,
    expert_ids,
    w_gate,
    w_up,
):
    ctx = lax.axis_size("ctx")
    by_tokens = lax.axis_size("exp") == 4 and ctx == 8
    tokens, channels = seq_input.shape
    ends = call(
        ends_body,
        [array((EDGE, channels + 2 * STATE), BF16)],
        (seq_input, b_input, c_input),
        fixed=3,
        sems=3,
        name="ends",
    )[0]
    before = lax.ppermute(ends, "ctx", [(i, i + 1) for i in range(ctx - 1)])
    pieces = meanwhile = None
    if by_tokens:
        pieces = gathered(moe_input)

        def meanwhile(ids, joined):
            return experts_by_tokens(0, pieces[0], joined, ids, w_gate, w_up, None)

    finish, late = mixing(
        pieces,
        meanwhile,
        seq_input,
        b_input,
        c_input,
        before,
        conv_x,
        conv_bc,
        log_decay,
        skip_gain,
        norm_gain,
        expert_ids,
    )
    if by_tokens:
        ids, joined, hidden = late
        hidden = experts_by_tokens(1, pieces[1], joined, ids, w_gate, w_up, hidden)
        mixed = finish((hidden,))
    else:
        mixed = finish()
        hidden = experts_by_slots(moe_input, expert_ids, w_gate, w_up)
    return (mixed, hidden)


def solution(mesh):
    in_specs = (
        P("ctx", "exp"),
        P("ctx", None),
        P("ctx", None),
        P(None, "exp"),
        P(),
        P("exp", "ctx"),
        P("exp"),
        P("exp"),
        P("ctx", "exp"),
        P("ctx", None),
        P("exp", None, "ctx"),
        P("exp", None, "ctx"),
    )
    out_specs = (P("ctx", "exp"), P("exp", None, "ctx"))
    return jax.shard_map(
        on_device, mesh=mesh, in_specs=in_specs, out_specs=out_specs, check_vma=False
    )
```

```python
import functools
import math

import jax
import jax.numpy as jnp
from jax import lax
from jax.experimental import pallas as pl
from jax.experimental.pallas import tpu as pltpu
from jax.sharding import PartitionSpec as P

HDIM = 64
STATE = 128
KCONV = 4
EDGE = 16
NOTES = 8

F32 = jnp.float32
BF16 = jnp.bfloat16


def dot16(a, b, contract=((1,), (0,))):
    return lax.dot_general(a, b, (contract, ((), ())), preferred_element_type=F32)


def halves(value):
    high = value.astype(BF16)
    return high, (value - high.astype(F32)).astype(BF16)


def dot(a, b, contract=((1,), (0,))):
    a_high, a_low = halves(a)
    b_high, b_low = halves(b)
    cross = dot16(a_high, b_low, contract) + dot16(a_low, b_high, contract)
    return dot16(a_high, b_high, contract) + cross


def dot_exact(a, b, contract=((1,), (0,))):
    high, rest = halves(a)
    low = (a - high.astype(F32) - rest.astype(F32)).astype(BF16)
    return dot16(high, b, contract) + (dot16(rest, b, contract) + dot16(low, b, contract))


def dot_left(a, b, contract=((1,), (0,))):
    high, low = halves(a)
    return dot16(high, b, contract) + dot16(low, b, contract)


FIRST = ((0,), (0,))


def iota(shape, axis):
    return lax.broadcasted_iota(jnp.int32, shape, axis)


def head_spread(heads):
    shape = (heads, heads * HDIM)
    return (iota(shape, 1) // HDIM == iota(shape, 0)).astype(BF16)


def upper_ones(length):
    return (iota((length, length), 0) <= iota((length, length), 1)).astype(BF16)


def silu(value):
    return value / (1.0 + jnp.exp(-value))


def one_minus_exp(value):
    series = jnp.ones_like(value)
    for n in range(8, 1, -1):
        series = 1.0 + value * series * (1.0 / n)
    return jnp.where(value > -0.25, -value * series, 1.0 - jnp.exp(value))


def started(sources, targets, sems, first=0):
    copies = []
    for i, (source, target) in enumerate(zip(sources, targets)):
        copies.append(pltpu.make_async_copy(source, target, sems.at[first + i]))
        copies[-1].start()
    return copies


def finished(copies):
    for copy in copies:
        copy.wait()


def following(body, count, skipped):
    return lambda *refs: body(*refs[:count], *refs[count + skipped :])


def call(
    body,
    outs,
    args,
    fixed=0,
    held=0,
    near_args=0,
    near_outs=0,
    after=(),
    after_far=(),
    aliases=None,
    scratch=(),
    sems=0,
    flops=0,
    grant=8,
    near=False,
    spaces_of=None,
    name=None,
):
    body = following(body, len(args), len(after) + len(after_far))
    moved = sum(math.prod(a.shape) * a.dtype.itemsize for a in (*args, *outs))
    scratch = list(scratch) + ([pltpu.SemaphoreType.DMA((sems,))] if sems else [])
    space = pltpu.VMEM if near else pl.ANY
    spaces = [pltpu.HBM] * fixed + [pltpu.VMEM] * held
    args = [
        pltpu.with_memory_space_constraint(a, spaces[i]) if i < len(spaces) else a
        for i, a in enumerate(args)
    ]
    spaces += [space] * (len(args) - near_args - len(spaces)) + [pltpu.VMEM] * near_args
    spaces = spaces_of or spaces
    args, spaces = [*args, *after], spaces + [pl.ANY] * len(after)
    args += [pltpu.with_memory_space_constraint(a, pltpu.HBM) for a in after_far]
    spaces += [pltpu.HBM] * len(after_far)
    out_spaces = [space] * (len(outs) - near_outs) + [pltpu.VMEM] * near_outs
    return pl.pallas_call(
        body,
        out_shape=outs,
        in_specs=[pl.BlockSpec(memory_space=s) for s in spaces],
        out_specs=[pl.BlockSpec(memory_space=s) for s in out_spaces],
        scratch_shapes=scratch,
        input_output_aliases=aliases or {},
        compiler_params=pltpu.CompilerParams(vmem_limit_bytes=grant * 2**20),
        cost_estimate=pl.CostEstimate(flops=flops, bytes_accessed=moved, transcendentals=0),
        name=name,
    )(*args)


def room(arrays):
    return [pltpu.VMEM(a.shape, a.dtype) for a in arrays]


def array(shape, dtype):
    return jax.ShapeDtypeStruct(shape, dtype)


def ends_body(x_ref, b_ref, c_ref, ends_ref, sems):
    tokens, channels = x_ref.shape
    cut = pl.ds(tokens - EDGE, EDGE)
    finished(
        started(
            [x_ref.at[cut, :], b_ref.at[cut, :], c_ref.at[cut, :]],
            [
                ends_ref.at[:, pl.ds(0, channels)],
                ends_ref.at[:, pl.ds(channels, STATE)],
                ends_ref.at[:, pl.ds(channels + STATE, STATE)],
            ],
            sems,
        )
    )


def local_body(paired, count, *refs):
    far, outs, rest = refs[:count], refs[count : count + 3], refs[count + 3 :]
    ends = rest[: 1 + paired]
    rest = rest[1 + paired :]
    near, scratch, pad_ref, sems = rest[:count], rest[count : count + 3], rest[-2], rest[-1]
    copies = started(far, near, sems)
    x_ref, b_ref, c_ref, taps_ref, taps_bc_ref, logs_ref, skip_ref, ids_ref, ends_ref = near
    pre_ref, decay_ref, c_out_ref = scratch
    tokens, channels = x_ref.shape
    heads = logs_ref.shape[0]
    finished(copies)
    pad_ref[0:8, :] = ends_ref[...].astype(F32)[EDGE - 8 : EDGE]
    pad_ref[8 : 8 + tokens, :channels] = x_ref[...].astype(F32)
    pad_ref[8 : 8 + tokens, channels : channels + STATE] = b_ref[...].astype(F32)
    pad_ref[8 : 8 + tokens, channels + STATE :] = c_ref[...].astype(F32)

    def conv(taps, start, stop):
        total = jnp.zeros((tokens, stop - start), F32)
        for k in range(KCONV):
            first = 8 - (KCONV - 1) + k
            total = total + taps[k : k + 1] * pad_ref[first : first + tokens, start:stop]
        return silu(total)

    bc = conv(taps_bc_ref[...], channels, channels + 2 * STATE)
    bmat, cmat = bc[:, :STATE], bc[:, STATE:]
    c_out_ref[...] = cmat
    logs = logs_ref[...]
    inflow = jnp.sqrt(one_minus_exp(2.0 * logs))
    row = dot_exact(logs, upper_ones(tokens))
    column = row.T
    total = row[:, tokens - 1 :]
    spread = head_spread(heads)
    decay_ref[...] = dot_left(jnp.exp(row), spread, FIRST)
    copies = started(scratch[1:], outs[1:], sems)

    xconv = conv(taps_ref[...], 0, channels)
    pad_ref[:tokens, :channels] = xconv
    drive = xconv * dot_left(inflow, spread, FIRST)
    pre_ref[...] = drive
    fresh = drive * dot_left(jnp.exp(total - row), spread, FIRST)
    state = dot(bmat, fresh, FIRST)
    total = jnp.broadcast_to(total, (heads, NOTES))
    if paired:
        total = dot_exact(total, spread, FIRST)
        half = channels // 2
        side = lax.axis_index("ctx") % 2
        ids = ids_ref[...].astype(F32)
        line = jnp.concatenate([ids[0:1], ids[1:2]], axis=1)
        line = jnp.concatenate([line] * (half // line.shape[1]), axis=1)
        for ref, first in ((ends[0], side == 0), (ends[1], side != 0)):
            mine = jnp.where(first, state[:, :half], state[:, half:])
            logsum = jnp.where(first, total[:1, :half], total[:1, half:])
            if ref is ends[0]:
                put(ref, mine, logsum, line)
            else:
                send(ref, mine, logsum, line)
    else:
        ends[0][:STATE] = state
        ends[0][STATE:] = dot_exact(jnp.exp(total), spread, FIRST)

    skip = dot_exact(skip_ref[...], spread)
    meet = dot(cmat, bmat, ((1,), (1,)))
    lower = iota((tokens, tokens), 0) >= iota((tokens, tokens), 1)
    left = iota((tokens, 2 * HDIM), 1) < HDIM
    for pair in range(heads // 2):
        cut = slice(pair * 2 * HDIM, (pair + 1) * 2 * HDIM)
        d_high, d_low = halves(pre_ref[:, cut])
        both = []
        for h in (2 * pair, 2 * pair + 1):
            gap = column[:, h : h + 1] - row[h : h + 1, :]
            mix = jnp.where(lower, jnp.exp(gap), 0.0) * meet
            m_high, m_low = halves(mix)
            both.append(dot16(m_high, d_high) + dot16(m_high, d_low) + dot16(m_low, d_high))
        direct = skip[:, cut] * pad_ref[:tokens, cut]
        pre_ref[:, cut] = direct + jnp.where(left, both[0], both[1])
    finished(copies + started(scratch[:1], outs[:1], sems, 2))


def put(ref, state, logsum, line):
    ref[:STATE] = state
    at = iota((NOTES, state.shape[1]), 0)
    ref[STATE:] = jnp.where(at == 0, logsum, line)


def send(ref, state, logsum, line):
    largest = jnp.max(jnp.abs(state), axis=0, keepdims=True)
    power = jnp.ceil(jnp.log2(jnp.maximum(largest, 1e-30))) - 15.0
    whole = jnp.clip(jnp.round(state * jnp.exp2(-power)), -32767.0, 32767.0)
    ref[:STATE] = whole.astype(jnp.int32).astype(jnp.int16)
    logsum = jnp.round(jnp.maximum(logsum, -128.0) * 2.0**22).astype(jnp.int32)
    at = iota((16, state.shape[1]), 0)
    notes = jnp.where(at == 0, power.astype(jnp.int32), line.astype(jnp.int32))
    notes = jnp.where(at == 1, logsum >> 15, jnp.where(at == 2, logsum & 32767, notes))
    ref[STATE:] = notes.astype(jnp.int16)


def taken(ref):
    return ref[:STATE], ref[STATE : STATE + 1], ref[STATE + 1 : STATE + 2]


def received(ref):
    notes = ref[STATE:].astype(jnp.int32).astype(F32)
    state = ref[:STATE].astype(jnp.int32).astype(F32) * jnp.exp2(notes[0:1])
    return state, notes[1:2] * 2.0**-7 + notes[2:3] * 2.0**-22, notes[3:4]


def ordered(first, own, other):
    return [jnp.where(first, a, b) for a, b in zip(own, other)], [
        jnp.where(first, b, a) for a, b in zip(own, other)
    ]


def together(first, own, other, width):
    (a, a_log, a_line), (b, b_log, b_line) = ordered(first, own, other)
    line = jnp.concatenate([a_line[:, :width], b_line[:, :width]], axis=1)
    line = jnp.concatenate([line] * (a.shape[1] // line.shape[1]), axis=1)
    return jnp.exp(b_log) * a + b, a_log + b_log, line


def place():
    here = lax.axis_index("ctx")
    return here % 2, (here // 2) % 2, here // 4


def pair_body(width, own_ref, got_ref, pair_ref, sent_ref):
    x, _, _ = place()
    pair = together(x == 0, taken(own_ref), received(got_ref), width)
    put(pair_ref, *pair)
    send(sent_ref, *pair)


def list_ids(ids_ref, early, late, width):
    at = iota(ids_ref.shape, 0)
    ids = jnp.zeros(ids_ref.shape, F32)
    for i in range(ids_ref.shape[0]):
        line = (early, late)[i // 4]
        ids = jnp.where(at == i, line[:, i % 4 * width : (i % 4 + 1) * width], ids)
    ids_ref[...] = ids


def join_rows(pieces, joined_ref):
    rows = pieces[0].shape[0]
    for i, piece in enumerate(pieces):
        joined_ref[i * rows : (i + 1) * rows] = piece[...]


def four_body(width, pair_ref, got_ref, a, b, c, d, sent_ref, ids_ref, joined_ref):
    join_rows((a, b, c, d), joined_ref)
    _, z, _ = place()
    four = together(z == 0, taken(pair_ref), received(got_ref), 2 * width)
    send(sent_ref, *four)
    list_ids(ids_ref, four[2], four[2], width)


def turn_body(
    width,
    own_ref,
    got_ref,
    pair_ref,
    pair_got_ref,
    four_got_ref,
    a,
    b,
    c,
    d,
    mine_ref,
    sent_ref,
    ids_ref,
    joined_ref,
):
    join_rows((a, b, c, d), joined_ref)
    x, z, zz = place()
    pair, pair_got, four_got = taken(pair_ref), received(pair_got_ref), received(four_got_ref)
    line = together(z == 0, pair, pair_got, 2 * width)[2]
    (early,), (late,) = ordered(zz == 0, [line], [four_got[2]])
    list_ids(ids_ref, early, late, width)

    before = jnp.where(zz == 0, 0.0, four_got[0])
    before = jnp.where(z == 0, before, jnp.exp(pair_got[1]) * before + pair_got[0])
    (first, first_log), _ = ordered(x == 0, taken(own_ref)[:2], received(got_ref)[:2])
    after = jnp.exp(first_log) * before + first
    mine_ref[...] = jnp.where(x == 0, before, after)
    other = jnp.where(x == 0, after, before)
    send(sent_ref, other, jnp.zeros_like(first_log), jnp.zeros_like(first_log))


def prefix_body(parts_ref, starts_ref):
    ctx, rows, share = starts_ref.shape
    state = jnp.zeros((rows, share), F32)
    for i in range(ctx):
        starts_ref[i] = state
        if i < ctx - 1:
            state = parts_ref[i, STATE : STATE + 1] * state + parts_ref[i, :STATE]


def back_body(paired, gain_far, pre_far, decay_far, c_far, *rest):
    starts, (out_far, *rest) = rest[: 1 + paired], rest[1 + paired :]
    far = (gain_far, pre_far, decay_far, c_far)
    gain_ref, pre_ref, decay_ref, c_ref, out_ref, sems = rest
    copies = started(far, rest[:4], sems)
    channels = pre_ref.shape[1]
    width = min(channels, 4 * HDIM)
    group = (iota((width, width), 0) // HDIM == iota((width, width), 1) // HDIM).astype(BF16)
    if paired:
        side = lax.axis_index("ctx") % 2
        mine, other = starts[0][...], received(starts[1])[0]
        start = [jnp.where(side == 0, mine, other), jnp.where(side == 0, other, mine)]
        start = jnp.concatenate(start, axis=1)
    else:
        start = starts[0][...]
    finished(copies)
    c_high, c_low = halves(c_ref[...])
    copies = []
    for i in range(channels // width):
        cut = slice(i * width, (i + 1) * width)
        s_high, s_low = halves(start[:, cut])
        carried = dot16(c_high, s_high) + dot16(c_high, s_low) + dot16(c_low, s_high)
        pre = pre_ref[:, cut] + carried * decay_ref[:, cut]
        mean = dot_left(pre * pre, group) * (1.0 / HDIM)
        out_ref[:, cut] = (pre * lax.rsqrt(mean + 1e-05) * gain_ref[:, cut]).astype(BF16)
        copies += started([out_ref.at[:, cut]], [out_far.at[:, cut]], sems, i)
    finished(copies)


def entering_by_pairs(keep, sent, width, follow, pieces, meanwhile):
    pair_array, sent_array = array(keep.shape, F32), array(sent.shape, jnp.int16)
    ids_array = array((8, width), F32)
    joined_array = [array((4 * p[0].shape[0], p[0].shape[1]), BF16) for p in pieces]
    got = swapped(sent, "ctx", 1)
    pair, sent = call(
        functools.partial(pair_body, width),
        [pair_array, sent_array],
        (keep, got),
        near=True,
        after=follow,
        name="pair",
    )
    pair_got = swapped(sent, "ctx", 2)
    sent, ids, joined = call(
        functools.partial(four_body, width),
        [sent_array, ids_array, joined_array[0]],
        (pair, pair_got, *pieces[0]),
        near=True,
        after=pieces[1][1:3],
        name="four",
    )
    four_got = swapped(sent, "ctx", 4)
    done = meanwhile(ids, joined)
    mine, sent, ids, joined = call(
        functools.partial(turn_body, width),
        [array((STATE, keep.shape[1]), F32), sent_array, ids_array, joined_array[1]],
        (keep, got, pair, pair_got, four_got, *pieces[1]),
        near=True,
        after_far=(done,),
        name="turn",
    )
    return (mine, swapped(sent, "ctx", 1)), ids, joined, done


def entering_by_rows(state):
    ctx = lax.axis_size("ctx")
    rows, channels = state.shape
    slabs = state.reshape(rows, ctx, channels // ctx).transpose(1, 0, 2)
    parts = lax.all_to_all(slabs, "ctx", split_axis=0, concat_axis=0, tiled=True)
    (starts,) = call(
        prefix_body,
        [array((ctx, STATE, channels // ctx), F32)],
        (parts,),
        near=True,
        name="prefix",
    )
    start = lax.all_to_all(starts, "ctx", split_axis=0, concat_axis=0, tiled=True)
    return start.transpose(1, 0, 2).reshape(STATE, channels)


def mixing(
    pieces, meanwhile, seq_input, b_input, c_input, before, conv_x, conv_bc, log_decay, skip, gain, ids
):
    tokens, channels = seq_input.shape
    heads = skip.shape[0]
    width = 2 * ids.shape[0]
    paired = pieces is not None
    outs = [
        array((tokens, channels), F32),
        array((tokens, channels), F32),
        array((tokens, STATE), F32),
    ]
    if paired:
        ends = [array((STATE + NOTES, channels // 2), F32)]
        ends.append(array((STATE + 16, channels // 2), jnp.int16))
    else:
        ends = [array((STATE + NOTES, channels), F32)]
    args = (seq_input, b_input, c_input, conv_x, conv_bc, log_decay)
    args = (*args, skip.reshape(1, heads), ids.T, before)
    pre, decay, cmat, *ends = call(
        functools.partial(local_body, paired, len(args)),
        outs + ends,
        args,
        fixed=len(args) - 1,
        near_outs=len(ends),
        after=pieces[0][:1] if paired else (),
        scratch=room(args) + room(outs) + [pltpu.VMEM((8 + tokens, channels + 2 * STATE), F32)],
        sems=len(args),
        flops=5 * 10**9,
        grant=20,
        name="local",
    )
    late = None
    if paired:
        follow = (*pieces[0][1:], pieces[1][0])
        starts, *late = entering_by_pairs(*ends, width, follow, pieces, meanwhile)
    else:
        starts = (entering_by_rows(ends[0]),)

    def finish(after=()):
        args = (gain.reshape(1, channels), pre, decay, cmat)
        outs = [array((tokens, channels), BF16)]
        return call(
            functools.partial(back_body, paired),
            outs,
            (*args, *starts),
            fixed=1,
            near_args=len(starts),
            after_far=after,
            scratch=room(args) + room(outs),
            sems=max(4, channels // (4 * HDIM)),
            flops=10**9,
            grant=16,
            name="back",
        )[0]

    return finish, late


TILE = 512


def join_body(a_ref, b_ref, out_ref, sems):
    rows = a_ref.shape[0]
    finished(
        started([a_ref, b_ref], [out_ref.at[pl.ds(0, rows), :], out_ref.at[pl.ds(rows, rows), :]], sems)
    )


def swapped(block, axis, bit):
    return lax.ppermute(block, axis, [(i, i ^ bit) for i in range(lax.axis_size(axis))])


def expert_body(part, w_gate, w_up, *refs):
    pieces, joined_ref, ids_ref, out_far = refs[:4], refs[4], refs[5], refs[6 + part]
    pick_ref, hid_ref, out_ref, sems = refs[7 + part :]
    length, hidden = out_ref.shape
    rows = pieces[0].shape[0] // 2
    depth = pieces[0].shape[1]
    me = lax.axis_index("exp")
    here = lax.axis_index("ctx")
    downs = [pl.ds(pl.multiple_of((me ^ k) * depth, depth), depth) for k in range(4)]
    pair = (here // 4) ^ part

    shape = (rows, rows)
    earlier = (iota(shape, 1) < iota(shape, 0)).astype(F32)
    across = iota(shape, 1)
    diagonal = iota(shape, 0) == across
    turns = [(here % 4) ^ (2 * (i % 2) + i // 2) for i in range(length // rows)]
    for i, block in enumerate(turns):
        line = ids_ref[pl.ds(4 * pair + block, 1), :]
        mine = me.astype(F32)
        named = ((line[:, :rows] == mine) | (line[:, rows:] == mine)).astype(F32)
        column = jnp.sum(jnp.where(diagonal, named, 0.0), axis=1, keepdims=True)
        position = jnp.sum(earlier * named, axis=1, keepdims=True).astype(jnp.int32)
        pick_ref[i] = jnp.where(position == across, column, 0.0).astype(BF16)

    out_copies = []
    out_rows = pl.ds(pl.multiple_of(pair * length, length), length)
    for n in range(hidden // TILE):
        cut = slice(n * TILE, (n + 1) * TILE)
        gate = upper = None
        for k in range(4):
            if k % 2 == 0:
                block = jnp.concatenate([piece[...] for piece in pieces[k : k + 2]], axis=0)
            else:
                block = joined_ref[k // 2 * length : (k // 2 + 1) * length]
            more = dot16(block, w_gate[0, downs[k], cut])
            gate = more if k == 0 else gate + more
            more = dot16(block, w_up[0, downs[k], cut])
            upper = more if k == 0 else upper + more
        hid_ref[...] = (silu(gate) * upper).astype(BF16)
        for i, block in enumerate(turns):
            picked = dot16(pick_ref[i], hid_ref[i * rows : (i + 1) * rows], FIRST)
            out_ref[pl.ds(pl.multiple_of(block * rows, rows), rows), cut] = picked.astype(BF16)
        out_copies += started([out_ref.at[:, cut]], [out_far.at[0, out_rows, cut]], sems, n)
    finished(out_copies)


def along_z(moe_input):
    rows, columns = moe_input.shape
    joined = call(
        join_body,
        [array((2 * rows, columns), BF16)],
        (moe_input, swapped(moe_input, "ctx", 2)),
        fixed=1,
        sems=2,
        name="join",
    )[0]
    return joined, swapped(joined, "ctx", 4)


def gathered(moe_input):
    z = along_z(moe_input)
    x = [swapped(a, "ctx", 1) for a in z]
    y = [swapped(a, "exp", 2) for a in z]
    corner = lax.axis_size("exp") | 2
    d = [swapped(a, ("ctx", "exp"), corner) for a in z]
    return list(zip(z, x, y, d))


def experts_by_tokens(part, pieces, joined, ids, w_gate, w_up, so_far):
    rows = pieces[0].shape[0] // 2
    length = 4 * rows
    hidden = w_gate.shape[2]
    args = (w_gate, w_up, *pieces, swapped(joined, "exp", 1), ids)
    return call(
        functools.partial(expert_body, part),
        [pltpu.HBM((1, 2 * length, hidden), BF16)],
        args + ((so_far,) if part else ()),
        held=2,
        near_args=0,
        aliases={len(args): 0} if part else None,
        scratch=[
            pltpu.VMEM((length // rows, rows, rows), BF16),
            pltpu.VMEM((length, TILE), BF16),
            pltpu.VMEM((length, hidden), BF16),
        ],
        sems=hidden // TILE,
        flops=4 * length * w_gate.shape[1] * hidden,
        grant=16,
        spaces_of=[pltpu.VMEM] * len(args) + [pltpu.HBM] * part,
        name="experts",
    )[0]


def slot_matrix(pairs, expert, capacity):
    named = jnp.any(pairs == expert, axis=1).astype(jnp.int32)
    position = jnp.cumsum(named) - named
    hit = position[None, :] == jnp.arange(capacity, dtype=jnp.int32)[:, None]
    return (hit & (named[None, :] > 0)).astype(BF16)


def experts_by_slots(moe_input, pairs, w_gate, w_up):
    experts = lax.axis_size("exp")
    capacity = 4 * moe_input.shape[0] // experts
    pick = jax.vmap(lambda e: slot_matrix(pairs, e, capacity))(jnp.arange(experts))
    slots = jnp.einsum("eqt,td->eqd", pick, moe_input, preferred_element_type=F32)
    routed = lax.all_to_all(slots.astype(BF16), "exp", split_axis=0, concat_axis=2, tiled=True)
    rows = lax.all_gather(routed[0], "ctx", axis=0, tiled=True)
    gate = jnp.dot(rows, w_gate[0], preferred_element_type=F32)
    upper = jnp.dot(rows, w_up[0], preferred_element_type=F32)
    return (jax.nn.silu(gate) * upper).astype(BF16)[None]


def on_device(
    seq_input,
    b_input,
    c_input,
    conv_x,
    conv_bc,
    log_decay,
    skip_gain,
    norm_gain,
    moe_input,
    expert_ids,
    w_gate,
    w_up,
):
    ctx = lax.axis_size("ctx")
    by_tokens = lax.axis_size("exp") == 4 and ctx == 8
    tokens, channels = seq_input.shape
    ends = call(
        ends_body,
        [array((EDGE, channels + 2 * STATE), BF16)],
        (seq_input, b_input, c_input),
        fixed=3,
        sems=3,
        name="ends",
    )[0]
    before = lax.ppermute(ends, "ctx", [(i, i + 1) for i in range(ctx - 1)])
    pieces = meanwhile = None
    if by_tokens:
        pieces = gathered(moe_input)

        def meanwhile(ids, joined):
            return experts_by_tokens(0, pieces[0], joined, ids, w_gate, w_up, None)

    finish, late = mixing(
        pieces,
        meanwhile,
        seq_input,
        b_input,
        c_input,
        before,
        conv_x,
        conv_bc,
        log_decay,
        skip_gain,
        norm_gain,
        expert_ids,
    )
    if by_tokens:
        ids, joined, hidden = late
        hidden = experts_by_tokens(1, pieces[1], joined, ids, w_gate, w_up, hidden)
        mixed = finish((hidden,))
    else:
        mixed = finish()
        hidden = experts_by_slots(moe_input, expert_ids, w_gate, w_up)
    return (mixed, hidden)


def solution(mesh):
    in_specs = (
        P("ctx", "exp"),
        P("ctx", None),
        P("ctx", None),
        P(None, "exp"),
        P(),
        P("exp", "ctx"),
        P("exp"),
        P("exp"),
        P("ctx", "exp"),
        P("ctx", None),
        P("exp", None, "ctx"),
        P("exp", None, "ctx"),
    )
    out_specs = (P("ctx", "exp"), P("exp", None, "ctx"))
    return jax.shard_map(
        on_device, mesh=mesh, in_specs=in_specs, out_specs=out_specs, check_vma=False
    )
```

```python
import functools
import math

import jax
import jax.numpy as jnp
from jax import lax
from jax.experimental import pallas as pl
from jax.experimental.pallas import tpu as pltpu
from jax.sharding import PartitionSpec as P

HDIM = 64
STATE = 128
KCONV = 4
EDGE = 16
NOTES = 8

F32 = jnp.float32
BF16 = jnp.bfloat16


def dot16(a, b, contract=((1,), (0,))):
    return lax.dot_general(a, b, (contract, ((), ())), preferred_element_type=F32)


def halves(value):
    high = value.astype(BF16)
    return high, (value - high.astype(F32)).astype(BF16)


def dot(a, b, contract=((1,), (0,))):
    a_high, a_low = halves(a)
    b_high, b_low = halves(b)
    cross = dot16(a_high, b_low, contract) + dot16(a_low, b_high, contract)
    return dot16(a_high, b_high, contract) + cross


def dot_exact(a, b, contract=((1,), (0,))):
    high, rest = halves(a)
    low = (a - high.astype(F32) - rest.astype(F32)).astype(BF16)
    return dot16(high, b, contract) + (dot16(rest, b, contract) + dot16(low, b, contract))


def dot_left(a, b, contract=((1,), (0,))):
    high, low = halves(a)
    return dot16(high, b, contract) + dot16(low, b, contract)


FIRST = ((0,), (0,))


def iota(shape, axis):
    return lax.broadcasted_iota(jnp.int32, shape, axis)


def head_spread(heads):
    shape = (heads, heads * HDIM)
    return (iota(shape, 1) // HDIM == iota(shape, 0)).astype(BF16)


def upper_ones(length):
    return (iota((length, length), 0) <= iota((length, length), 1)).astype(BF16)


def silu(value):
    return value / (1.0 + jnp.exp(-value))


def one_minus_exp(value):
    series = jnp.ones_like(value)
    for n in range(8, 1, -1):
        series = 1.0 + value * series * (1.0 / n)
    return jnp.where(value > -0.25, -value * series, 1.0 - jnp.exp(value))


def started(sources, targets, sems, first=0):
    copies = []
    for i, (source, target) in enumerate(zip(sources, targets)):
        copies.append(pltpu.make_async_copy(source, target, sems.at[first + i]))
        copies[-1].start()
    return copies


def finished(copies):
    for copy in copies:
        copy.wait()


def following(body, count, skipped):
    return lambda *refs: body(*refs[:count], *refs[count + skipped :])


def call(
    body,
    outs,
    args,
    fixed=0,
    held=0,
    near_args=0,
    near_outs=0,
    after=(),
    after_far=(),
    aliases=None,
    scratch=(),
    sems=0,
    flops=0,
    grant=8,
    near=False,
    spaces_of=None,
    name=None,
):
    body = following(body, len(args), len(after) + len(after_far))
    moved = sum(math.prod(a.shape) * a.dtype.itemsize for a in (*args, *outs))
    scratch = list(scratch) + ([pltpu.SemaphoreType.DMA((sems,))] if sems else [])
    space = pltpu.VMEM if near else pl.ANY
    spaces = [pltpu.HBM] * fixed + [pltpu.VMEM] * held
    args = [
        pltpu.with_memory_space_constraint(a, spaces[i]) if i < len(spaces) else a
        for i, a in enumerate(args)
    ]
    spaces += [space] * (len(args) - near_args - len(spaces)) + [pltpu.VMEM] * near_args
    spaces = spaces_of or spaces
    args, spaces = [*args, *after], spaces + [pl.ANY] * len(after)
    args += [pltpu.with_memory_space_constraint(a, pltpu.HBM) for a in after_far]
    spaces += [pltpu.HBM] * len(after_far)
    out_spaces = [space] * (len(outs) - near_outs) + [pltpu.VMEM] * near_outs
    return pl.pallas_call(
        body,
        out_shape=outs,
        in_specs=[pl.BlockSpec(memory_space=s) for s in spaces],
        out_specs=[pl.BlockSpec(memory_space=s) for s in out_spaces],
        scratch_shapes=scratch,
        input_output_aliases=aliases or {},
        compiler_params=pltpu.CompilerParams(vmem_limit_bytes=grant * 2**20),
        cost_estimate=pl.CostEstimate(flops=flops, bytes_accessed=moved, transcendentals=0),
        name=name,
    )(*args)


def room(arrays):
    return [pltpu.VMEM(a.shape, a.dtype) for a in arrays]


def array(shape, dtype):
    return jax.ShapeDtypeStruct(shape, dtype)


def ends_body(x_ref, b_ref, c_ref, ends_ref, sems):
    tokens, channels = x_ref.shape
    cut = pl.ds(tokens - EDGE, EDGE)
    finished(
        started(
            [x_ref.at[cut, :], b_ref.at[cut, :], c_ref.at[cut, :]],
            [
                ends_ref.at[:, pl.ds(0, channels)],
                ends_ref.at[:, pl.ds(channels, STATE)],
                ends_ref.at[:, pl.ds(channels + STATE, STATE)],
            ],
            sems,
        )
    )


def local_body(paired, count, *refs):
    far, outs, rest = refs[:count], refs[count : count + 3], refs[count + 3 :]
    ends = rest[: 1 + paired]
    rest = rest[1 + paired :]
    near, scratch, pad_ref, sems = rest[:count], rest[count : count + 3], rest[-2], rest[-1]
    copies = started(far, near, sems)
    x_ref, b_ref, c_ref, taps_ref, taps_bc_ref, logs_ref, skip_ref, ids_ref, ends_ref = near
    pre_ref, decay_ref, c_out_ref = scratch
    tokens, channels = x_ref.shape
    heads = logs_ref.shape[0]
    finished(copies)
    pad_ref[0:8, :] = ends_ref[...].astype(F32)[EDGE - 8 : EDGE]
    pad_ref[8 : 8 + tokens, :channels] = x_ref[...].astype(F32)
    pad_ref[8 : 8 + tokens, channels : channels + STATE] = b_ref[...].astype(F32)
    pad_ref[8 : 8 + tokens, channels + STATE :] = c_ref[...].astype(F32)

    def conv(taps, start, stop):
        total = jnp.zeros((tokens, stop - start), F32)
        for k in range(KCONV):
            first = 8 - (KCONV - 1) + k
            total = total + taps[k : k + 1] * pad_ref[first : first + tokens, start:stop]
        return silu(total)

    bc = conv(taps_bc_ref[...], channels, channels + 2 * STATE)
    bmat, cmat = bc[:, :STATE], bc[:, STATE:]
    c_out_ref[...] = cmat
    logs = logs_ref[...]
    inflow = jnp.sqrt(one_minus_exp(2.0 * logs))
    row = dot_exact(logs, upper_ones(tokens))
    column = row.T
    total = row[:, tokens - 1 :]
    spread = head_spread(heads)
    decay_ref[...] = dot_left(jnp.exp(row), spread, FIRST)
    copies = started(scratch[1:], outs[1:], sems)

    xconv = conv(taps_ref[...], 0, channels)
    pad_ref[:tokens, :channels] = xconv
    drive = xconv * dot_left(inflow, spread, FIRST)
    pre_ref[...] = drive
    fresh = drive * dot_left(jnp.exp(total - row), spread, FIRST)
    state = dot(bmat, fresh, FIRST)
    total = jnp.broadcast_to(total, (heads, NOTES))
    if paired:
        total = dot_exact(total, spread, FIRST)
        half = channels // 2
        side = lax.axis_index("ctx") % 2
        ids = ids_ref[...].astype(F32)
        line = jnp.concatenate([ids[0:1], ids[1:2]], axis=1)
        line = jnp.concatenate([line] * (half // line.shape[1]), axis=1)
        for ref, first in ((ends[0], side == 0), (ends[1], side != 0)):
            mine = jnp.where(first, state[:, :half], state[:, half:])
            logsum = jnp.where(first, total[:1, :half], total[:1, half:])
            if ref is ends[0]:
                put(ref, mine, logsum, line)
            else:
                send(ref, mine, logsum, line)
    else:
        ends[0][:STATE] = state
        ends[0][STATE:] = dot_exact(jnp.exp(total), spread, FIRST)

    skip = dot_exact(skip_ref[...], spread)
    meet = dot(cmat, bmat, ((1,), (1,)))
    lower = iota((tokens, tokens), 0) >= iota((tokens, tokens), 1)
    left = iota((tokens, 2 * HDIM), 1) < HDIM
    for pair in range(heads // 2):
        cut = slice(pair * 2 * HDIM, (pair + 1) * 2 * HDIM)
        d_high, d_low = halves(pre_ref[:, cut])
        both = []
        for h in (2 * pair, 2 * pair + 1):
            gap = column[:, h : h + 1] - row[h : h + 1, :]
            mix = jnp.where(lower, jnp.exp(gap), 0.0) * meet
            m_high, m_low = halves(mix)
            both.append(dot16(m_high, d_high) + dot16(m_high, d_low) + dot16(m_low, d_high))
        direct = skip[:, cut] * pad_ref[:tokens, cut]
        pre_ref[:, cut] = direct + jnp.where(left, both[0], both[1])
    finished(copies + started(scratch[:1], outs[:1], sems, 2))


def put(ref, state, logsum, line):
    ref[:STATE] = state
    at = iota((NOTES, state.shape[1]), 0)
    ref[STATE:] = jnp.where(at == 0, logsum, line)


def send(ref, state, logsum, line):
    largest = jnp.max(jnp.abs(state), axis=0, keepdims=True)
    power = jnp.ceil(jnp.log2(jnp.maximum(largest, 1e-30))) - 15.0
    whole = jnp.clip(jnp.round(state * jnp.exp2(-power)), -32767.0, 32767.0)
    ref[:STATE] = whole.astype(jnp.int32).astype(jnp.int16)
    logsum = jnp.round(jnp.maximum(logsum, -128.0) * 2.0**22).astype(jnp.int32)
    at = iota((16, state.shape[1]), 0)
    notes = jnp.where(at == 0, power.astype(jnp.int32), line.astype(jnp.int32))
    notes = jnp.where(at == 1, logsum >> 15, jnp.where(at == 2, logsum & 32767, notes))
    ref[STATE:] = notes.astype(jnp.int16)


def taken(ref):
    return ref[:STATE], ref[STATE : STATE + 1], ref[STATE + 1 : STATE + 2]


def received(ref):
    notes = ref[STATE:].astype(jnp.int32).astype(F32)
    state = ref[:STATE].astype(jnp.int32).astype(F32) * jnp.exp2(notes[0:1])
    return state, notes[1:2] * 2.0**-7 + notes[2:3] * 2.0**-22, notes[3:4]


def ordered(first, own, other):
    return [jnp.where(first, a, b) for a, b in zip(own, other)], [
        jnp.where(first, b, a) for a, b in zip(own, other)
    ]


def together(first, own, other, width):
    (a, a_log, a_line), (b, b_log, b_line) = ordered(first, own, other)
    line = jnp.concatenate([a_line[:, :width], b_line[:, :width]], axis=1)
    line = jnp.concatenate([line] * (a.shape[1] // line.shape[1]), axis=1)
    return jnp.exp(b_log) * a + b, a_log + b_log, line


def place():
    here = lax.axis_index("ctx")
    return here % 2, (here // 2) % 2, here // 4


def pair_body(width, own_ref, got_ref, pair_ref, sent_ref):
    x, _, _ = place()
    pair = together(x == 0, taken(own_ref), received(got_ref), width)
    put(pair_ref, *pair)
    send(sent_ref, *pair)


def list_ids(ids_ref, early, late, width):
    at = iota(ids_ref.shape, 0)
    ids = jnp.zeros(ids_ref.shape, F32)
    for i in range(ids_ref.shape[0]):
        line = (early, late)[i // 4]
        ids = jnp.where(at == i, line[:, i % 4 * width : (i % 4 + 1) * width], ids)
    ids_ref[...] = ids


def join_rows(pieces, joined_ref):
    rows = pieces[0].shape[0]
    for i, piece in enumerate(pieces):
        joined_ref[i * rows : (i + 1) * rows] = piece[...]


def four_body(width, pair_ref, got_ref, sent_ref, ids_ref):
    _, z, _ = place()
    four = together(z == 0, taken(pair_ref), received(got_ref), 2 * width)
    send(sent_ref, *four)
    list_ids(ids_ref, four[2], four[2], width)


def turn_body(
    width,
    own_ref,
    got_ref,
    pair_ref,
    pair_got_ref,
    four_got_ref,
    a,
    b,
    c,
    d,
    mine_ref,
    sent_ref,
    ids_ref,
    joined_ref,
):
    join_rows((a, b, c, d), joined_ref)
    x, z, zz = place()
    pair, pair_got, four_got = taken(pair_ref), received(pair_got_ref), received(four_got_ref)
    line = together(z == 0, pair, pair_got, 2 * width)[2]
    (early,), (late,) = ordered(zz == 0, [line], [four_got[2]])
    list_ids(ids_ref, early, late, width)

    before = jnp.where(zz == 0, 0.0, four_got[0])
    before = jnp.where(z == 0, before, jnp.exp(pair_got[1]) * before + pair_got[0])
    (first, first_log), _ = ordered(x == 0, taken(own_ref)[:2], received(got_ref)[:2])
    after = jnp.exp(first_log) * before + first
    mine_ref[...] = jnp.where(x == 0, before, after)
    other = jnp.where(x == 0, after, before)
    send(sent_ref, other, jnp.zeros_like(first_log), jnp.zeros_like(first_log))


def prefix_body(parts_ref, starts_ref):
    ctx, rows, share = starts_ref.shape
    state = jnp.zeros((rows, share), F32)
    for i in range(ctx):
        starts_ref[i] = state
        if i < ctx - 1:
            state = parts_ref[i, STATE : STATE + 1] * state + parts_ref[i, :STATE]


def back_body(paired, gain_far, pre_far, decay_far, c_far, *rest):
    starts, (out_far, *rest) = rest[: 1 + paired], rest[1 + paired :]
    far = (gain_far, pre_far, decay_far, c_far)
    gain_ref, pre_ref, decay_ref, c_ref, out_ref, sems = rest
    copies = started(far, rest[:4], sems)
    channels = pre_ref.shape[1]
    width = min(channels, 4 * HDIM)
    group = (iota((width, width), 0) // HDIM == iota((width, width), 1) // HDIM).astype(BF16)
    if paired:
        side = lax.axis_index("ctx") % 2
        mine, other = starts[0][...], received(starts[1])[0]
        start = [jnp.where(side == 0, mine, other), jnp.where(side == 0, other, mine)]
        start = jnp.concatenate(start, axis=1)
    else:
        start = starts[0][...]
    finished(copies)
    c_high, c_low = halves(c_ref[...])
    copies = []
    for i in range(channels // width):
        cut = slice(i * width, (i + 1) * width)
        s_high, s_low = halves(start[:, cut])
        carried = dot16(c_high, s_high) + dot16(c_high, s_low) + dot16(c_low, s_high)
        pre = pre_ref[:, cut] + carried * decay_ref[:, cut]
        mean = dot_left(pre * pre, group) * (1.0 / HDIM)
        out_ref[:, cut] = (pre * lax.rsqrt(mean + 1e-05) * gain_ref[:, cut]).astype(BF16)
        copies += started([out_ref.at[:, cut]], [out_far.at[:, cut]], sems, i)
    finished(copies)


def entering_by_pairs(keep, sent, width, follow, pieces, meanwhile):
    pair_array, sent_array = array(keep.shape, F32), array(sent.shape, jnp.int16)
    ids_array = array((8, width), F32)
    joined_array = array((4 * pieces[0].shape[0], pieces[0].shape[1]), BF16)
    got = swapped(sent, "ctx", 1)
    pair, sent = call(
        functools.partial(pair_body, width),
        [pair_array, sent_array],
        (keep, got),
        near=True,
        after=follow,
        name="pair",
    )
    pair_got = swapped(sent, "ctx", 2)
    sent, ids = call(
        functools.partial(four_body, width),
        [sent_array, ids_array],
        (pair, pair_got),
        near=True,
        name="four",
    )
    four_got = swapped(sent, "ctx", 4)
    done = meanwhile(ids)
    mine, sent, ids, joined = call(
        functools.partial(turn_body, width),
        [array((STATE, keep.shape[1]), F32), sent_array, ids_array, joined_array],
        (keep, got, pair, pair_got, four_got, *pieces),
        near=True,
        after_far=(done,),
        name="turn",
    )
    return (mine, swapped(sent, "ctx", 1)), ids, joined, done


def entering_by_rows(state):
    ctx = lax.axis_size("ctx")
    rows, channels = state.shape
    slabs = state.reshape(rows, ctx, channels // ctx).transpose(1, 0, 2)
    parts = lax.all_to_all(slabs, "ctx", split_axis=0, concat_axis=0, tiled=True)
    (starts,) = call(
        prefix_body,
        [array((ctx, STATE, channels // ctx), F32)],
        (parts,),
        near=True,
        name="prefix",
    )
    start = lax.all_to_all(starts, "ctx", split_axis=0, concat_axis=0, tiled=True)
    return start.transpose(1, 0, 2).reshape(STATE, channels)


def mixing(
    pieces, meanwhile, seq_input, b_input, c_input, before, conv_x, conv_bc, log_decay, skip, gain, ids
):
    tokens, channels = seq_input.shape
    heads = skip.shape[0]
    width = 2 * ids.shape[0]
    paired = pieces is not None
    outs = [
        array((tokens, channels), F32),
        array((tokens, channels), F32),
        array((tokens, STATE), F32),
    ]
    if paired:
        ends = [array((STATE + NOTES, channels // 2), F32)]
        ends.append(array((STATE + 16, channels // 2), jnp.int16))
    else:
        ends = [array((STATE + NOTES, channels), F32)]
    args = (seq_input, b_input, c_input, conv_x, conv_bc, log_decay)
    args = (*args, skip.reshape(1, heads), ids.T, before)
    pre, decay, cmat, *ends = call(
        functools.partial(local_body, paired, len(args)),
        outs + ends,
        args,
        fixed=len(args) - 1,
        near_outs=len(ends),
        after=pieces[0][:1] if paired else (),
        scratch=room(args) + room(outs) + [pltpu.VMEM((8 + tokens, channels + 2 * STATE), F32)],
        sems=len(args),
        flops=5 * 10**9,
        grant=20,
        name="local",
    )
    late = None
    if paired:
        follow = (*pieces[0][1:3], pieces[1][0])
        starts, *late = entering_by_pairs(*ends, width, follow, pieces[1], meanwhile)
    else:
        starts = (entering_by_rows(ends[0]),)

    def finish(after=()):
        args = (gain.reshape(1, channels), pre, decay, cmat)
        outs = [array((tokens, channels), BF16)]
        return call(
            functools.partial(back_body, paired),
            outs,
            (*args, *starts),
            fixed=1,
            near_args=len(starts),
            after_far=after,
            scratch=room(args) + room(outs),
            sems=max(4, channels // (4 * HDIM)),
            flops=10**9,
            grant=16,
            name="back",
        )[0]

    return finish, late


TILE = 512


def join_body(a_ref, b_ref, out_ref, sems):
    rows = a_ref.shape[0]
    finished(
        started([a_ref, b_ref], [out_ref.at[pl.ds(0, rows), :], out_ref.at[pl.ds(rows, rows), :]], sems)
    )


def swapped(block, axis, bit):
    return lax.ppermute(block, axis, [(i, i ^ bit) for i in range(lax.axis_size(axis))])


def expert_body(part, w_gate, w_up, *refs):
    count = 1 if part else 4
    pieces, beside, refs = refs[:4], refs[4 : 4 + count], refs[4 + count :]
    ids_ref, out_far = refs[0], refs[1 + part]
    pick_ref, hid_ref, out_ref, sems = refs[2 + part :]
    length, hidden = out_ref.shape
    rows = pieces[0].shape[0] // 2
    depth = pieces[0].shape[1]
    me = lax.axis_index("exp")
    here = lax.axis_index("ctx")
    downs = [pl.ds(pl.multiple_of((me ^ k) * depth, depth), depth) for k in range(4)]
    pair = (here // 4) ^ part

    shape = (rows, rows)
    earlier = (iota(shape, 1) < iota(shape, 0)).astype(F32)
    across = iota(shape, 1)
    diagonal = iota(shape, 0) == across
    turns = [(here % 4) ^ (2 * (i % 2) + i // 2) for i in range(length // rows)]
    for i, block in enumerate(turns):
        line = ids_ref[pl.ds(4 * pair + block, 1), :]
        mine = me.astype(F32)
        named = ((line[:, :rows] == mine) | (line[:, rows:] == mine)).astype(F32)
        column = jnp.sum(jnp.where(diagonal, named, 0.0), axis=1, keepdims=True)
        position = jnp.sum(earlier * named, axis=1, keepdims=True).astype(jnp.int32)
        pick_ref[i] = jnp.where(position == across, column, 0.0).astype(BF16)

    out_copies = []
    out_rows = pl.ds(pl.multiple_of(pair * length, length), length)
    for n in range(hidden // TILE):
        cut = slice(n * TILE, (n + 1) * TILE)
        gate = upper = None
        for k in range(4):
            first = k // 2 * 2
            if k % 2 == 1 and part:
                block = beside[0][k // 2 * length : (k // 2 + 1) * length]
            else:
                block = (beside if k % 2 else pieces)[first : first + 2]
                block = jnp.concatenate([piece[...] for piece in block], axis=0)
            more = dot16(block, w_gate[0, downs[k], cut])
            gate = more if k == 0 else gate + more
            more = dot16(block, w_up[0, downs[k], cut])
            upper = more if k == 0 else upper + more
        hid_ref[...] = (silu(gate) * upper).astype(BF16)
        for i, block in enumerate(turns):
            picked = dot16(pick_ref[i], hid_ref[i * rows : (i + 1) * rows], FIRST)
            out_ref[pl.ds(pl.multiple_of(block * rows, rows), rows), cut] = picked.astype(BF16)
        out_copies += started([out_ref.at[:, cut]], [out_far.at[0, out_rows, cut]], sems, n)
    finished(out_copies)


def along_z(moe_input):
    rows, columns = moe_input.shape
    joined = call(
        join_body,
        [array((2 * rows, columns), BF16)],
        (moe_input, swapped(moe_input, "ctx", 2)),
        fixed=1,
        sems=2,
        name="join",
    )[0]
    return joined, swapped(joined, "ctx", 4)


def gathered(moe_input):
    z = along_z(moe_input)
    x = [swapped(a, "ctx", 1) for a in z]
    y = [swapped(a, "exp", 2) for a in z]
    d = (swapped(x[0], "exp", 2), swapped(y[1], "ctx", 1))
    return list(zip(z, x, y, d))


def experts_by_tokens(part, pieces, sent, ids, w_gate, w_up, so_far):
    rows = pieces[0].shape[0] // 2
    length = 4 * rows
    hidden = w_gate.shape[2]
    args = (w_gate, w_up, *pieces, *(swapped(a, "exp", 1) for a in sent), ids)
    return call(
        functools.partial(expert_body, part),
        [pltpu.HBM((1, 2 * length, hidden), BF16)],
        args + ((so_far,) if part else ()),
        held=2,
        near_args=0,
        aliases={len(args): 0} if part else None,
        scratch=[
            pltpu.VMEM((length // rows, rows, rows), BF16),
            pltpu.VMEM((length, TILE), BF16),
            pltpu.VMEM((length, hidden), BF16),
        ],
        sems=hidden // TILE,
        flops=4 * length * w_gate.shape[1] * hidden,
        grant=16,
        spaces_of=[pltpu.VMEM] * len(args) + [pltpu.HBM] * part,
        name="experts",
    )[0]


def slot_matrix(pairs, expert, capacity):
    named = jnp.any(pairs == expert, axis=1).astype(jnp.int32)
    position = jnp.cumsum(named) - named
    hit = position[None, :] == jnp.arange(capacity, dtype=jnp.int32)[:, None]
    return (hit & (named[None, :] > 0)).astype(BF16)


def experts_by_slots(moe_input, pairs, w_gate, w_up):
    experts = lax.axis_size("exp")
    capacity = 4 * moe_input.shape[0] // experts
    pick = jax.vmap(lambda e: slot_matrix(pairs, e, capacity))(jnp.arange(experts))
    slots = jnp.einsum("eqt,td->eqd", pick, moe_input, preferred_element_type=F32)
    routed = lax.all_to_all(slots.astype(BF16), "exp", split_axis=0, concat_axis=2, tiled=True)
    rows = lax.all_gather(routed[0], "ctx", axis=0, tiled=True)
    gate = jnp.dot(rows, w_gate[0], preferred_element_type=F32)
    upper = jnp.dot(rows, w_up[0], preferred_element_type=F32)
    return (jax.nn.silu(gate) * upper).astype(BF16)[None]


def on_device(
    seq_input,
    b_input,
    c_input,
    conv_x,
    conv_bc,
    log_decay,
    skip_gain,
    norm_gain,
    moe_input,
    expert_ids,
    w_gate,
    w_up,
):
    ctx = lax.axis_size("ctx")
    by_tokens = lax.axis_size("exp") == 4 and ctx == 8
    tokens, channels = seq_input.shape
    ends = call(
        ends_body,
        [array((EDGE, channels + 2 * STATE), BF16)],
        (seq_input, b_input, c_input),
        fixed=3,
        sems=3,
        name="ends",
    )[0]
    before = lax.ppermute(ends, "ctx", [(i, i + 1) for i in range(ctx - 1)])
    pieces = meanwhile = None
    if by_tokens:
        pieces = gathered(moe_input)

        def meanwhile(ids):
            return experts_by_tokens(0, pieces[0], pieces[0], ids, w_gate, w_up, None)

    finish, late = mixing(
        pieces,
        meanwhile,
        seq_input,
        b_input,
        c_input,
        before,
        conv_x,
        conv_bc,
        log_decay,
        skip_gain,
        norm_gain,
        expert_ids,
    )
    if by_tokens:
        ids, joined, hidden = late
        hidden = experts_by_tokens(1, pieces[1], [joined], ids, w_gate, w_up, hidden)
        mixed = finish((hidden,))
    else:
        mixed = finish()
        hidden = experts_by_slots(moe_input, expert_ids, w_gate, w_up)
    return (mixed, hidden)


def solution(mesh):
    in_specs = (
        P("ctx", "exp"),
        P("ctx", None),
        P("ctx", None),
        P(None, "exp"),
        P(),
        P("exp", "ctx"),
        P("exp"),
        P("exp"),
        P("ctx", "exp"),
        P("ctx", None),
        P("exp", None, "ctx"),
        P("exp", None, "ctx"),
    )
    out_specs = (P("ctx", "exp"), P("exp", None, "ctx"))
    return jax.shard_map(
        on_device, mesh=mesh, in_specs=in_specs, out_specs=out_specs, check_vma=False
    )
```

```python
import functools
import math

import jax
import jax.numpy as jnp
from jax import lax
from jax.experimental import pallas as pl
from jax.experimental.pallas import tpu as pltpu
from jax.sharding import PartitionSpec as P

HDIM = 64
STATE = 128
KCONV = 4
EDGE = 16
NOTES = 8

F32 = jnp.float32
BF16 = jnp.bfloat16


def dot16(a, b, contract=((1,), (0,))):
    return lax.dot_general(a, b, (contract, ((), ())), preferred_element_type=F32)


def halves(value):
    high = value.astype(BF16)
    return high, (value - high.astype(F32)).astype(BF16)


def dot(a, b, contract=((1,), (0,))):
    a_high, a_low = halves(a)
    b_high, b_low = halves(b)
    cross = dot16(a_high, b_low, contract) + dot16(a_low, b_high, contract)
    return dot16(a_high, b_high, contract) + cross


def dot_exact(a, b, contract=((1,), (0,))):
    high, rest = halves(a)
    low = (a - high.astype(F32) - rest.astype(F32)).astype(BF16)
    return dot16(high, b, contract) + (dot16(rest, b, contract) + dot16(low, b, contract))


def dot_left(a, b, contract=((1,), (0,))):
    high, low = halves(a)
    return dot16(high, b, contract) + dot16(low, b, contract)


FIRST = ((0,), (0,))


def iota(shape, axis):
    return lax.broadcasted_iota(jnp.int32, shape, axis)


def head_spread(heads):
    shape = (heads, heads * HDIM)
    return (iota(shape, 1) // HDIM == iota(shape, 0)).astype(BF16)


def upper_ones(length):
    return (iota((length, length), 0) <= iota((length, length), 1)).astype(BF16)


def silu(value):
    return value / (1.0 + jnp.exp(-value))


def one_minus_exp(value):
    series = jnp.ones_like(value)
    for n in range(8, 1, -1):
        series = 1.0 + value * series * (1.0 / n)
    return jnp.where(value > -0.25, -value * series, 1.0 - jnp.exp(value))


def started(sources, targets, sems, first=0):
    copies = []
    for i, (source, target) in enumerate(zip(sources, targets)):
        copies.append(pltpu.make_async_copy(source, target, sems.at[first + i]))
        copies[-1].start()
    return copies


def finished(copies):
    for copy in copies:
        copy.wait()


def following(body, count, skipped):
    return lambda *refs: body(*refs[:count], *refs[count + skipped :])


def call(
    body,
    outs,
    args,
    fixed=0,
    held=0,
    near_args=0,
    near_outs=0,
    after=(),
    after_far=(),
    aliases=None,
    scratch=(),
    sems=0,
    flops=0,
    grant=8,
    near=False,
    spaces_of=None,
    name=None,
):
    body = following(body, len(args), len(after) + len(after_far))
    moved = sum(math.prod(a.shape) * a.dtype.itemsize for a in (*args, *outs))
    scratch = list(scratch) + ([pltpu.SemaphoreType.DMA((sems,))] if sems else [])
    space = pltpu.VMEM if near else pl.ANY
    spaces = [pltpu.HBM] * fixed + [pltpu.VMEM] * held
    args = [
        pltpu.with_memory_space_constraint(a, spaces[i]) if i < len(spaces) else a
        for i, a in enumerate(args)
    ]
    spaces += [space] * (len(args) - near_args - len(spaces)) + [pltpu.VMEM] * near_args
    spaces = spaces_of or spaces
    args, spaces = [*args, *after], spaces + [pl.ANY] * len(after)
    args += [pltpu.with_memory_space_constraint(a, pltpu.HBM) for a in after_far]
    spaces += [pltpu.HBM] * len(after_far)
    out_spaces = [space] * (len(outs) - near_outs) + [pltpu.VMEM] * near_outs
    return pl.pallas_call(
        body,
        out_shape=outs,
        in_specs=[pl.BlockSpec(memory_space=s) for s in spaces],
        out_specs=[pl.BlockSpec(memory_space=s) for s in out_spaces],
        scratch_shapes=scratch,
        input_output_aliases=aliases or {},
        compiler_params=pltpu.CompilerParams(vmem_limit_bytes=grant * 2**20),
        cost_estimate=pl.CostEstimate(flops=flops, bytes_accessed=moved, transcendentals=0),
        name=name,
    )(*args)


def room(arrays):
    return [pltpu.VMEM(a.shape, a.dtype) for a in arrays]


def array(shape, dtype):
    return jax.ShapeDtypeStruct(shape, dtype)


def ends_body(x_ref, b_ref, c_ref, ends_ref, sems):
    tokens, channels = x_ref.shape
    cut = pl.ds(tokens - EDGE, EDGE)
    finished(
        started(
            [x_ref.at[cut, :], b_ref.at[cut, :], c_ref.at[cut, :]],
            [
                ends_ref.at[:, pl.ds(0, channels)],
                ends_ref.at[:, pl.ds(channels, STATE)],
                ends_ref.at[:, pl.ds(channels + STATE, STATE)],
            ],
            sems,
        )
    )


def front_body(paired, count, *refs):
    far, outs, rest = refs[:count], refs[count : count + 3], refs[count + 3 :]
    ends = rest[: 1 + paired]
    rest = rest[1 + paired :]
    near, scratch, pad_ref, sems = rest[:count], rest[count : count + 3], rest[-2], rest[-1]
    copies = started(far, near, sems)
    x_ref, b_ref, c_ref, taps_ref, taps_bc_ref, logs_ref, ids_ref, ends_ref = near
    xconv_ref, bc_ref, lines_ref = scratch
    tokens, channels = x_ref.shape
    heads = logs_ref.shape[0]
    finished(copies)
    pad_ref[0:8, :] = ends_ref[...].astype(F32)[EDGE - 8 : EDGE]
    pad_ref[8 : 8 + tokens, :channels] = x_ref[...].astype(F32)
    pad_ref[8 : 8 + tokens, channels : channels + STATE] = b_ref[...].astype(F32)
    pad_ref[8 : 8 + tokens, channels + STATE :] = c_ref[...].astype(F32)

    def conv(taps, start, stop):
        total = jnp.zeros((tokens, stop - start), F32)
        for k in range(KCONV):
            first = 8 - (KCONV - 1) + k
            total = total + taps[k : k + 1] * pad_ref[first : first + tokens, start:stop]
        return silu(total)

    bc = conv(taps_bc_ref[...], channels, channels + 2 * STATE)
    bc_ref[...] = bc
    xconv = conv(taps_ref[...], 0, channels)
    xconv_ref[...] = xconv
    logs = logs_ref[...]
    inflow = jnp.sqrt(one_minus_exp(2.0 * logs))
    row = dot_exact(logs, upper_ones(tokens))
    lines_ref[0] = row
    lines_ref[1] = inflow
    copies = started(scratch, outs, sems)
    total = row[:, tokens - 1 :]
    spread = head_spread(heads)
    fresh = xconv * dot_left(inflow * jnp.exp(total - row), spread, FIRST)
    state = dot(bc[:, :STATE], fresh, FIRST)
    total = jnp.broadcast_to(total, (heads, NOTES))
    if paired:
        total = dot_exact(total, spread, FIRST)
        half = channels // 2
        side = lax.axis_index("ctx") % 2
        ids = ids_ref[...].astype(F32)
        line = jnp.concatenate([ids[0:1], ids[1:2]], axis=1)
        line = jnp.concatenate([line] * (half // line.shape[1]), axis=1)
        for ref, first in ((ends[0], side == 0), (ends[1], side != 0)):
            mine = jnp.where(first, state[:, :half], state[:, half:])
            logsum = jnp.where(first, total[:1, :half], total[:1, half:])
            if ref is ends[0]:
                put(ref, mine, logsum, line)
            else:
                send(ref, mine, logsum, line)
    else:
        ends[0][:STATE] = state
        ends[0][STATE:] = dot_exact(jnp.exp(total), spread, FIRST)
    finished(copies)


def inner_body(skip_far, xconv_far, bc_far, lines_far, pre_far, decay_far, *rest):
    far = (skip_far, xconv_far, bc_far, lines_far)
    skip_ref, xconv_ref, bc_ref, lines_ref, pre_ref, decay_ref, sems = rest
    finished(started(far, rest[:4], sems))
    tokens, channels = xconv_ref.shape
    heads = channels // HDIM
    row = lines_ref[0]
    column = row.T
    spread = head_spread(heads)
    decay_ref[...] = dot_left(jnp.exp(row), spread, FIRST)
    copies = started([decay_ref], [decay_far], sems)
    inflow = dot_left(lines_ref[1], spread, FIRST)
    skip = dot_exact(skip_ref[...], spread)
    meet = dot(bc_ref[:, STATE:], bc_ref[:, :STATE], ((1,), (1,)))
    lower = iota((tokens, tokens), 0) >= iota((tokens, tokens), 1)
    left = iota((tokens, 2 * HDIM), 1) < HDIM
    for pair in range(heads // 2):
        cut = slice(pair * 2 * HDIM, (pair + 1) * 2 * HDIM)
        xconv = xconv_ref[:, cut]
        d_high, d_low = halves(xconv * inflow[:, cut])
        both = []
        for h in (2 * pair, 2 * pair + 1):
            gap = column[:, h : h + 1] - row[h : h + 1, :]
            mix = jnp.where(lower, jnp.exp(gap), 0.0) * meet
            m_high, m_low = halves(mix)
            both.append(dot16(m_high, d_high) + dot16(m_high, d_low) + dot16(m_low, d_high))
        pre_ref[:, cut] = skip[:, cut] * xconv + jnp.where(left, both[0], both[1])
    finished(copies + started([pre_ref], [pre_far], sems, 1))


def put(ref, state, logsum, line):
    ref[:STATE] = state
    at = iota((NOTES, state.shape[1]), 0)
    ref[STATE:] = jnp.where(at == 0, logsum, line)


def send(ref, state, logsum, line):
    largest = jnp.max(jnp.abs(state), axis=0, keepdims=True)
    power = jnp.ceil(jnp.log2(jnp.maximum(largest, 1e-30))) - 15.0
    whole = jnp.clip(jnp.round(state * jnp.exp2(-power)), -32767.0, 32767.0)
    ref[:STATE] = whole.astype(jnp.int32).astype(jnp.int16)
    logsum = jnp.round(jnp.maximum(logsum, -128.0) * 2.0**22).astype(jnp.int32)
    at = iota((16, state.shape[1]), 0)
    notes = jnp.where(at == 0, power.astype(jnp.int32), line.astype(jnp.int32))
    notes = jnp.where(at == 1, logsum >> 15, jnp.where(at == 2, logsum & 32767, notes))
    ref[STATE:] = notes.astype(jnp.int16)


def taken(ref):
    return ref[:STATE], ref[STATE : STATE + 1], ref[STATE + 1 : STATE + 2]


def received(ref):
    notes = ref[STATE:].astype(jnp.int32).astype(F32)
    state = ref[:STATE].astype(jnp.int32).astype(F32) * jnp.exp2(notes[0:1])
    return state, notes[1:2] * 2.0**-7 + notes[2:3] * 2.0**-22, notes[3:4]


def ordered(first, own, other):
    return [jnp.where(first, a, b) for a, b in zip(own, other)], [
        jnp.where(first, b, a) for a, b in zip(own, other)
    ]


def together(first, own, other, width):
    (a, a_log, a_line), (b, b_log, b_line) = ordered(first, own, other)
    line = jnp.concatenate([a_line[:, :width], b_line[:, :width]], axis=1)
    line = jnp.concatenate([line] * (a.shape[1] // line.shape[1]), axis=1)
    return jnp.exp(b_log) * a + b, a_log + b_log, line


def place():
    here = lax.axis_index("ctx")
    return here % 2, (here // 2) % 2, here // 4


def pair_body(width, own_ref, got_ref, rows_ref, pair_ref, sent_ref, same_rows_ref):
    same_rows_ref[...] = rows_ref[...]
    x, _, _ = place()
    pair = together(x == 0, taken(own_ref), received(got_ref), width)
    put(pair_ref, *pair)
    send(sent_ref, *pair)


def list_ids(ids_ref, early, late, width):
    at = iota(ids_ref.shape, 0)
    ids = jnp.zeros(ids_ref.shape, F32)
    for i in range(ids_ref.shape[0]):
        line = (early, late)[i // 4]
        ids = jnp.where(at == i, line[:, i % 4 * width : (i % 4 + 1) * width], ids)
    ids_ref[...] = ids


def join_rows(pieces, joined_ref):
    rows = pieces[0].shape[0]
    for i, piece in enumerate(pieces):
        joined_ref[i * rows : (i + 1) * rows] = piece[...]


def four_body(width, pair_ref, got_ref, a, b, c, d, sent_ref, ids_ref, joined_ref):
    join_rows((a, b, c, d), joined_ref)
    _, z, _ = place()
    four = together(z == 0, taken(pair_ref), received(got_ref), 2 * width)
    send(sent_ref, *four)
    list_ids(ids_ref, four[2], four[2], width)


def turn_body(
    width,
    own_ref,
    got_ref,
    pair_ref,
    pair_got_ref,
    four_got_ref,
    a,
    b,
    c,
    d,
    mine_ref,
    sent_ref,
    ids_ref,
    joined_ref,
):
    join_rows((a, b, c, d), joined_ref)
    x, z, zz = place()
    pair, pair_got, four_got = taken(pair_ref), received(pair_got_ref), received(four_got_ref)
    line = together(z == 0, pair, pair_got, 2 * width)[2]
    (early,), (late,) = ordered(zz == 0, [line], [four_got[2]])
    list_ids(ids_ref, early, late, width)

    before = jnp.where(zz == 0, 0.0, four_got[0])
    before = jnp.where(z == 0, before, jnp.exp(pair_got[1]) * before + pair_got[0])
    (first, first_log), _ = ordered(x == 0, taken(own_ref)[:2], received(got_ref)[:2])
    after = jnp.exp(first_log) * before + first
    mine_ref[...] = jnp.where(x == 0, before, after)
    other = jnp.where(x == 0, after, before)
    send(sent_ref, other, jnp.zeros_like(first_log), jnp.zeros_like(first_log))


def prefix_body(parts_ref, starts_ref):
    ctx, rows, share = starts_ref.shape
    state = jnp.zeros((rows, share), F32)
    for i in range(ctx):
        starts_ref[i] = state
        if i < ctx - 1:
            state = parts_ref[i, STATE : STATE + 1] * state + parts_ref[i, :STATE]


def back_body(paired, gain_far, pre_far, decay_far, bc_far, *rest):
    starts, (out_far, *rest) = rest[: 1 + paired], rest[1 + paired :]
    far = (gain_far, pre_far, decay_far, bc_far)
    gain_ref, pre_ref, decay_ref, bc_ref, out_ref, sems = rest
    copies = started(far, rest[:4], sems)
    channels = pre_ref.shape[1]
    width = min(channels, 4 * HDIM)
    group = (iota((width, width), 0) // HDIM == iota((width, width), 1) // HDIM).astype(BF16)
    if paired:
        side = lax.axis_index("ctx") % 2
        mine, other = starts[0][...], received(starts[1])[0]
        start = [jnp.where(side == 0, mine, other), jnp.where(side == 0, other, mine)]
        start = jnp.concatenate(start, axis=1)
    else:
        start = starts[0][...]
    finished(copies)
    c_high, c_low = halves(bc_ref[:, STATE:])
    copies = []
    for i in range(channels // width):
        cut = slice(i * width, (i + 1) * width)
        s_high, s_low = halves(start[:, cut])
        carried = dot16(c_high, s_high) + dot16(c_high, s_low) + dot16(c_low, s_high)
        pre = pre_ref[:, cut] + carried * decay_ref[:, cut]
        mean = dot_left(pre * pre, group) * (1.0 / HDIM)
        out_ref[:, cut] = (pre * lax.rsqrt(mean + 1e-05) * gain_ref[:, cut]).astype(BF16)
        copies += started([out_ref.at[:, cut]], [out_far.at[:, cut]], sems, i)
    finished(copies)


def entering_by_pairs(keep, sent, width, pre, near_pieces, far_rows, meanwhile):
    pair_array, sent_array = array(keep.shape, F32), array(sent.shape, jnp.int16)
    ids_array = array((8, width), F32)
    joined_array = array((4 * far_rows.shape[0], far_rows.shape[1]), BF16)
    got = swapped(sent, "ctx", 1)
    pair, sent, rows = call(
        functools.partial(pair_body, width),
        [pair_array, sent_array, array(far_rows.shape, BF16)],
        (keep, got, far_rows),
        near=True,
        after=(*near_pieces[2:], pre),
        name="pair",
    )
    far_pieces = spread_rows(rows, 1)
    pair_got = swapped(sent, "ctx", 2)
    sent, ids, joined = call(
        functools.partial(four_body, width),
        [sent_array, ids_array, joined_array],
        (pair, pair_got, *near_pieces),
        near=True,
        after=far_pieces[1:3],
        name="four",
    )
    four_got = swapped(sent, "ctx", 4)
    done = meanwhile(ids, joined)
    mine, sent, ids, joined = call(
        functools.partial(turn_body, width),
        [array((STATE, keep.shape[1]), F32), sent_array, ids_array, joined_array],
        (keep, got, pair, pair_got, four_got, *far_pieces),
        near=True,
        after_far=(done,),
        name="turn",
    )
    return (mine, swapped(sent, "ctx", 1)), far_pieces, ids, joined, done


def entering_by_rows(state):
    ctx = lax.axis_size("ctx")
    rows, channels = state.shape
    slabs = state.reshape(rows, ctx, channels // ctx).transpose(1, 0, 2)
    parts = lax.all_to_all(slabs, "ctx", split_axis=0, concat_axis=0, tiled=True)
    (starts,) = call(
        prefix_body,
        [array((ctx, STATE, channels // ctx), F32)],
        (parts,),
        near=True,
        name="prefix",
    )
    start = lax.all_to_all(starts, "ctx", split_axis=0, concat_axis=0, tiled=True)
    return start.transpose(1, 0, 2).reshape(STATE, channels)


def mixing(
    rows, meanwhile, seq_input, b_input, c_input, before, conv_x, conv_bc, log_decay, skip, gain, ids
):
    tokens, channels = seq_input.shape
    heads = skip.shape[0]
    width = 2 * ids.shape[0]
    paired = rows is not None
    outs = [
        array((tokens, channels), F32),
        array((tokens, 2 * STATE), F32),
        array((2, heads, tokens), F32),
    ]
    if paired:
        ends = [array((STATE + NOTES, channels // 2), F32)]
        ends.append(array((STATE + 16, channels // 2), jnp.int16))
    else:
        ends = [array((STATE + NOTES, channels), F32)]
    args = (seq_input, b_input, c_input, conv_x, conv_bc, log_decay, ids.T, before)
    xconv, bc, lines, *ends = call(
        functools.partial(front_body, paired, len(args)),
        outs + ends,
        args,
        fixed=len(args) - 1,
        near_outs=len(ends),
        after=rows[0][:1] if paired else (),
        scratch=room(args) + room(outs) + [pltpu.VMEM((8 + tokens, channels + 2 * STATE), F32)],
        sems=len(args),
        flops=5 * 10**9,
        grant=20,
        name="front",
    )
    args = (skip.reshape(1, heads), xconv, bc, lines)
    outs = [array((tokens, channels), F32)] * 2
    pre, decay = call(
        inner_body,
        outs,
        args,
        fixed=1,
        scratch=room(args) + room(outs),
        sems=4,
        flops=4 * 10**9,
        grant=16,
        name="inner",
    )
    late = None
    if paired:
        starts, *late = entering_by_pairs(*ends, width, pre, *rows, meanwhile)
    else:
        starts = (entering_by_rows(ends[0]),)

    def finish(after=()):
        args = (gain.reshape(1, channels), pre, decay, bc)
        outs = [array((tokens, channels), BF16)]
        return call(
            functools.partial(back_body, paired),
            outs,
            (*args, *starts),
            fixed=1,
            near_args=len(starts),
            after_far=after,
            scratch=room(args) + room(outs),
            sems=max(4, channels // (4 * HDIM)),
            flops=10**9,
            grant=16,
            name="back",
        )[0]

    return finish, late


TILE = 512


def join_body(a_ref, b_ref, out_ref, sems):
    rows = a_ref.shape[0]
    finished(
        started([a_ref, b_ref], [out_ref.at[pl.ds(0, rows), :], out_ref.at[pl.ds(rows, rows), :]], sems)
    )


def swapped(block, axis, bit):
    return lax.ppermute(block, axis, [(i, i ^ bit) for i in range(lax.axis_size(axis))])


def expert_body(part, w_gate, w_up, *refs):
    pieces, joined_ref, ids_ref, out_far = refs[:4], refs[4], refs[5], refs[6 + part]
    pick_ref, hid_ref, out_ref, sems = refs[7 + part :]
    length, hidden = out_ref.shape
    rows = pieces[0].shape[0] // 2
    depth = pieces[0].shape[1]
    me = lax.axis_index("exp")
    here = lax.axis_index("ctx")
    downs = [pl.ds(pl.multiple_of((me ^ k) * depth, depth), depth) for k in range(4)]
    pair = (here // 4) ^ part

    shape = (rows, rows)
    earlier = (iota(shape, 1) < iota(shape, 0)).astype(F32)
    across = iota(shape, 1)
    diagonal = iota(shape, 0) == across
    turns = [(here % 4) ^ (2 * (i % 2) + i // 2) for i in range(length // rows)]
    for i, block in enumerate(turns):
        line = ids_ref[pl.ds(4 * pair + block, 1), :]
        mine = me.astype(F32)
        named = ((line[:, :rows] == mine) | (line[:, rows:] == mine)).astype(F32)
        column = jnp.sum(jnp.where(diagonal, named, 0.0), axis=1, keepdims=True)
        position = jnp.sum(earlier * named, axis=1, keepdims=True).astype(jnp.int32)
        pick_ref[i] = jnp.where(position == across, column, 0.0).astype(BF16)

    out_copies = []
    out_rows = pl.ds(pl.multiple_of(pair * length, length), length)
    for n in range(hidden // TILE):
        cut = slice(n * TILE, (n + 1) * TILE)
        gate = upper = None
        for k in range(4):
            if k % 2 == 0:
                block = jnp.concatenate([piece[...] for piece in pieces[k : k + 2]], axis=0)
            else:
                block = joined_ref[k // 2 * length : (k // 2 + 1) * length]
            more = dot16(block, w_gate[0, downs[k], cut])
            gate = more if k == 0 else gate + more
            more = dot16(block, w_up[0, downs[k], cut])
            upper = more if k == 0 else upper + more
        hid_ref[...] = (silu(gate) * upper).astype(BF16)
        for i, block in enumerate(turns):
            picked = dot16(pick_ref[i], hid_ref[i * rows : (i + 1) * rows], FIRST)
            out_ref[pl.ds(pl.multiple_of(block * rows, rows), rows), cut] = picked.astype(BF16)
        out_copies += started([out_ref.at[:, cut]], [out_far.at[0, out_rows, cut]], sems, n)
    finished(out_copies)


def along_z(moe_input):
    rows, columns = moe_input.shape
    joined = call(
        join_body,
        [array((2 * rows, columns), BF16)],
        (moe_input, swapped(moe_input, "ctx", 2)),
        fixed=1,
        sems=2,
        name="join",
    )[0]
    return joined, swapped(joined, "ctx", 4)


def spread_rows(z, through):
    x, y = swapped(z, "ctx", 1), swapped(z, "exp", 2)
    d = swapped(y, "ctx", 1) if through else swapped(x, "exp", 2)
    return (z, x, y, d)


def experts_by_tokens(part, pieces, joined, ids, w_gate, w_up, so_far):
    rows = pieces[0].shape[0] // 2
    length = 4 * rows
    hidden = w_gate.shape[2]
    args = (w_gate, w_up, *pieces, swapped(joined, "exp", 1), ids)
    return call(
        functools.partial(expert_body, part),
        [pltpu.HBM((1, 2 * length, hidden), BF16)],
        args + ((so_far,) if part else ()),
        held=2,
        near_args=0,
        aliases={len(args): 0} if part else None,
        scratch=[
            pltpu.VMEM((length // rows, rows, rows), BF16),
            pltpu.VMEM((length, TILE), BF16),
            pltpu.VMEM((length, hidden), BF16),
        ],
        sems=hidden // TILE,
        flops=4 * length * w_gate.shape[1] * hidden,
        grant=16,
        spaces_of=[pltpu.VMEM] * len(args) + [pltpu.HBM] * part,
        name="experts",
    )[0]


def slot_matrix(pairs, expert, capacity):
    named = jnp.any(pairs == expert, axis=1).astype(jnp.int32)
    position = jnp.cumsum(named) - named
    hit = position[None, :] == jnp.arange(capacity, dtype=jnp.int32)[:, None]
    return (hit & (named[None, :] > 0)).astype(BF16)


def experts_by_slots(moe_input, pairs, w_gate, w_up):
    experts = lax.axis_size("exp")
    capacity = 4 * moe_input.shape[0] // experts
    pick = jax.vmap(lambda e: slot_matrix(pairs, e, capacity))(jnp.arange(experts))
    slots = jnp.einsum("eqt,td->eqd", pick, moe_input, preferred_element_type=F32)
    routed = lax.all_to_all(slots.astype(BF16), "exp", split_axis=0, concat_axis=2, tiled=True)
    rows = lax.all_gather(routed[0], "ctx", axis=0, tiled=True)
    gate = jnp.dot(rows, w_gate[0], preferred_element_type=F32)
    upper = jnp.dot(rows, w_up[0], preferred_element_type=F32)
    return (jax.nn.silu(gate) * upper).astype(BF16)[None]


def on_device(
    seq_input,
    b_input,
    c_input,
    conv_x,
    conv_bc,
    log_decay,
    skip_gain,
    norm_gain,
    moe_input,
    expert_ids,
    w_gate,
    w_up,
):
    ctx = lax.axis_size("ctx")
    by_tokens = lax.axis_size("exp") == 4 and ctx == 8
    tokens, channels = seq_input.shape
    ends = call(
        ends_body,
        [array((EDGE, channels + 2 * STATE), BF16)],
        (seq_input, b_input, c_input),
        fixed=3,
        sems=3,
        name="ends",
    )[0]
    before = lax.ppermute(ends, "ctx", [(i, i + 1) for i in range(ctx - 1)])
    pieces = meanwhile = None
    if by_tokens:
        near_rows, far_rows = along_z(moe_input)
        pieces = spread_rows(near_rows, 0), far_rows

        def meanwhile(ids, joined):
            return experts_by_tokens(0, pieces[0], joined, ids, w_gate, w_up, None)

    finish, late = mixing(
        pieces,
        meanwhile,
        seq_input,
        b_input,
        c_input,
        before,
        conv_x,
        conv_bc,
        log_decay,
        skip_gain,
        norm_gain,
        expert_ids,
    )
    if by_tokens:
        far_pieces, ids, joined, hidden = late
        hidden = experts_by_tokens(1, far_pieces, joined, ids, w_gate, w_up, hidden)
        mixed = finish((hidden,))
    else:
        mixed = finish()
        hidden = experts_by_slots(moe_input, expert_ids, w_gate, w_up)
    return (mixed, hidden)


def solution(mesh):
    in_specs = (
        P("ctx", "exp"),
        P("ctx", None),
        P("ctx", None),
        P(None, "exp"),
        P(),
        P("exp", "ctx"),
        P("exp"),
        P("exp"),
        P("ctx", "exp"),
        P("ctx", None),
        P("exp", None, "ctx"),
        P("exp", None, "ctx"),
    )
    out_specs = (P("ctx", "exp"), P("exp", None, "ctx"))
    return jax.shard_map(
        on_device, mesh=mesh, in_specs=in_specs, out_specs=out_specs, check_vma=False
    )
```

```python
import functools
import math

import jax
import jax.numpy as jnp
from jax import lax
from jax.experimental import pallas as pl
from jax.experimental.pallas import tpu as pltpu
from jax.sharding import PartitionSpec as P

HDIM = 64
STATE = 128
KCONV = 4
EDGE = 16
NOTES = 8

F32 = jnp.float32
BF16 = jnp.bfloat16


def dot16(a, b, contract=((1,), (0,))):
    return lax.dot_general(a, b, (contract, ((), ())), preferred_element_type=F32)


def halves(value):
    high = value.astype(BF16)
    return high, (value - high.astype(F32)).astype(BF16)


def dot(a, b, contract=((1,), (0,))):
    a_high, a_low = halves(a)
    b_high, b_low = halves(b)
    cross = dot16(a_high, b_low, contract) + dot16(a_low, b_high, contract)
    return dot16(a_high, b_high, contract) + cross


def dot_exact(a, b, contract=((1,), (0,))):
    high, rest = halves(a)
    low = (a - high.astype(F32) - rest.astype(F32)).astype(BF16)
    return dot16(high, b, contract) + (dot16(rest, b, contract) + dot16(low, b, contract))


def dot_left(a, b, contract=((1,), (0,))):
    high, low = halves(a)
    return dot16(high, b, contract) + dot16(low, b, contract)


FIRST = ((0,), (0,))


def iota(shape, axis):
    return lax.broadcasted_iota(jnp.int32, shape, axis)


def head_spread(heads):
    shape = (heads, heads * HDIM)
    return (iota(shape, 1) // HDIM == iota(shape, 0)).astype(BF16)


def upper_ones(length):
    return (iota((length, length), 0) <= iota((length, length), 1)).astype(BF16)


def silu(value):
    return value / (1.0 + jnp.exp(-value))


def one_minus_exp(value):
    series = jnp.ones_like(value)
    for n in range(8, 1, -1):
        series = 1.0 + value * series * (1.0 / n)
    return jnp.where(value > -0.25, -value * series, 1.0 - jnp.exp(value))


def started(sources, targets, sems, first=0):
    copies = []
    for i, (source, target) in enumerate(zip(sources, targets)):
        copies.append(pltpu.make_async_copy(source, target, sems.at[first + i]))
        copies[-1].start()
    return copies


def finished(copies):
    for copy in copies:
        copy.wait()


def following(body, count, skipped):
    return lambda *refs: body(*refs[:count], *refs[count + skipped :])


def call(
    body,
    outs,
    args,
    fixed=0,
    held=0,
    near_args=0,
    near_outs=0,
    after=(),
    after_far=(),
    aliases=None,
    scratch=(),
    sems=0,
    flops=0,
    grant=8,
    near=False,
    spaces_of=None,
    name=None,
):
    body = following(body, len(args), len(after) + len(after_far))
    moved = sum(math.prod(a.shape) * a.dtype.itemsize for a in (*args, *outs))
    scratch = list(scratch) + ([pltpu.SemaphoreType.DMA((sems,))] if sems else [])
    space = pltpu.VMEM if near else pl.ANY
    spaces = [pltpu.HBM] * fixed + [pltpu.VMEM] * held
    args = [
        pltpu.with_memory_space_constraint(a, spaces[i]) if i < len(spaces) else a
        for i, a in enumerate(args)
    ]
    spaces += [space] * (len(args) - near_args - len(spaces)) + [pltpu.VMEM] * near_args
    spaces = spaces_of or spaces
    args, spaces = [*args, *after], spaces + [pl.ANY] * len(after)
    args += [pltpu.with_memory_space_constraint(a, pltpu.HBM) for a in after_far]
    spaces += [pltpu.HBM] * len(after_far)
    out_spaces = [space] * (len(outs) - near_outs) + [pltpu.VMEM] * near_outs
    return pl.pallas_call(
        body,
        out_shape=outs,
        in_specs=[pl.BlockSpec(memory_space=s) for s in spaces],
        out_specs=[pl.BlockSpec(memory_space=s) for s in out_spaces],
        scratch_shapes=scratch,
        input_output_aliases=aliases or {},
        compiler_params=pltpu.CompilerParams(vmem_limit_bytes=grant * 2**20),
        cost_estimate=pl.CostEstimate(flops=flops, bytes_accessed=moved, transcendentals=0),
        name=name,
    )(*args)


def room(arrays):
    return [pltpu.VMEM(a.shape, a.dtype) for a in arrays]


def array(shape, dtype):
    return jax.ShapeDtypeStruct(shape, dtype)


def ends_body(x_ref, b_ref, c_ref, ends_ref, sems):
    tokens, channels = x_ref.shape
    cut = pl.ds(tokens - EDGE, EDGE)
    finished(
        started(
            [x_ref.at[cut, :], b_ref.at[cut, :], c_ref.at[cut, :]],
            [
                ends_ref.at[:, pl.ds(0, channels)],
                ends_ref.at[:, pl.ds(channels, STATE)],
                ends_ref.at[:, pl.ds(channels + STATE, STATE)],
            ],
            sems,
        )
    )


def front_body(paired, count, *refs):
    far, outs, rest = refs[:count], refs[count : count + 3], refs[count + 3 :]
    ends = rest[: 1 + paired]
    rest = rest[1 + paired :]
    near, scratch, pad_ref, sems = rest[:count], rest[count : count + 3], rest[-2], rest[-1]
    copies = started(far, near, sems)
    x_ref, b_ref, c_ref, taps_ref, taps_bc_ref, logs_ref, ids_ref, ends_ref = near
    xconv_ref, bc_ref, lines_ref = scratch
    tokens, channels = x_ref.shape
    heads = logs_ref.shape[0]
    finished(copies)
    pad_ref[0:8, :] = ends_ref[...].astype(F32)[EDGE - 8 : EDGE]
    pad_ref[8 : 8 + tokens, :channels] = x_ref[...].astype(F32)
    pad_ref[8 : 8 + tokens, channels : channels + STATE] = b_ref[...].astype(F32)
    pad_ref[8 : 8 + tokens, channels + STATE :] = c_ref[...].astype(F32)

    def conv(taps, start, stop):
        total = jnp.zeros((tokens, stop - start), F32)
        for k in range(KCONV):
            first = 8 - (KCONV - 1) + k
            total = total + taps[k : k + 1] * pad_ref[first : first + tokens, start:stop]
        return silu(total)

    bc = conv(taps_bc_ref[...], channels, channels + 2 * STATE)
    bc_ref[...] = bc
    xconv = conv(taps_ref[...], 0, channels)
    xconv_ref[...] = xconv
    logs = logs_ref[...]
    inflow = jnp.sqrt(one_minus_exp(2.0 * logs))
    row = dot_exact(logs, upper_ones(tokens))
    lines_ref[0] = row
    lines_ref[1] = inflow
    copies = started(scratch, outs, sems)
    total = row[:, tokens - 1 :]
    spread = head_spread(heads)
    fresh = xconv * dot_left(inflow * jnp.exp(total - row), spread, FIRST)
    state = dot(bc[:, :STATE], fresh, FIRST)
    total = jnp.broadcast_to(total, (heads, NOTES))
    if paired:
        total = dot_exact(total, spread, FIRST)
        half = channels // 2
        side = lax.axis_index("ctx") % 2
        ids = ids_ref[...].astype(F32)
        line = jnp.concatenate([ids[0:1], ids[1:2]], axis=1)
        line = jnp.concatenate([line] * (half // line.shape[1]), axis=1)
        for ref, first in ((ends[0], side == 0), (ends[1], side != 0)):
            mine = jnp.where(first, state[:, :half], state[:, half:])
            logsum = jnp.where(first, total[:1, :half], total[:1, half:])
            if ref is ends[0]:
                put(ref, mine, logsum, line)
            else:
                send(ref, mine, logsum, line)
    else:
        ends[0][:STATE] = state
        ends[0][STATE:] = dot_exact(jnp.exp(total), spread, FIRST)
    finished(copies)


def inner_body(skip_far, xconv_far, bc_far, lines_far, pre_far, decay_far, *rest):
    far = (skip_far, xconv_far, bc_far, lines_far)
    skip_ref, xconv_ref, bc_ref, lines_ref, pre_ref, decay_ref, sems = rest
    finished(started(far, rest[:4], sems))
    tokens, channels = xconv_ref.shape
    heads = channels // HDIM
    row = lines_ref[0]
    column = row.T
    spread = head_spread(heads)
    decay_ref[...] = dot_left(jnp.exp(row), spread, FIRST)
    copies = started([decay_ref], [decay_far], sems)
    inflow = dot_left(lines_ref[1], spread, FIRST)
    skip = dot_exact(skip_ref[...], spread)
    meet = dot(bc_ref[:, STATE:], bc_ref[:, :STATE], ((1,), (1,)))
    lower = iota((tokens, tokens), 0) >= iota((tokens, tokens), 1)
    left = iota((tokens, 2 * HDIM), 1) < HDIM
    for pair in range(heads // 2):
        cut = slice(pair * 2 * HDIM, (pair + 1) * 2 * HDIM)
        xconv = xconv_ref[:, cut]
        d_high, d_low = halves(xconv * inflow[:, cut])
        both = []
        for h in (2 * pair, 2 * pair + 1):
            gap = column[:, h : h + 1] - row[h : h + 1, :]
            mix = jnp.where(lower, jnp.exp(gap), 0.0) * meet
            m_high, m_low = halves(mix)
            both.append(dot16(m_high, d_high) + dot16(m_high, d_low) + dot16(m_low, d_high))
        pre_ref[:, cut] = skip[:, cut] * xconv + jnp.where(left, both[0], both[1])
    finished(copies + started([pre_ref], [pre_far], sems, 1))


def put(ref, state, logsum, line):
    ref[:STATE] = state
    at = iota((NOTES, state.shape[1]), 0)
    ref[STATE:] = jnp.where(at == 0, logsum, line)


def send(ref, state, logsum, line):
    largest = jnp.max(jnp.abs(state), axis=0, keepdims=True)
    power = jnp.ceil(jnp.log2(jnp.maximum(largest, 1e-30))) - 15.0
    whole = jnp.clip(jnp.round(state * jnp.exp2(-power)), -32767.0, 32767.0)
    ref[:STATE] = whole.astype(jnp.int32).astype(jnp.int16)
    logsum = jnp.round(jnp.maximum(logsum, -128.0) * 2.0**22).astype(jnp.int32)
    at = iota((16, state.shape[1]), 0)
    notes = jnp.where(at == 0, power.astype(jnp.int32), line.astype(jnp.int32))
    notes = jnp.where(at == 1, logsum >> 15, jnp.where(at == 2, logsum & 32767, notes))
    ref[STATE:] = notes.astype(jnp.int16)


def taken(ref):
    return ref[:STATE], ref[STATE : STATE + 1], ref[STATE + 1 : STATE + 2]


def received(ref):
    notes = ref[STATE:].astype(jnp.int32).astype(F32)
    state = ref[:STATE].astype(jnp.int32).astype(F32) * jnp.exp2(notes[0:1])
    return state, notes[1:2] * 2.0**-7 + notes[2:3] * 2.0**-22, notes[3:4]


def ordered(first, own, other):
    return [jnp.where(first, a, b) for a, b in zip(own, other)], [
        jnp.where(first, b, a) for a, b in zip(own, other)
    ]


def together(first, own, other, width):
    (a, a_log, a_line), (b, b_log, b_line) = ordered(first, own, other)
    line = jnp.concatenate([a_line[:, :width], b_line[:, :width]], axis=1)
    line = jnp.concatenate([line] * (a.shape[1] // line.shape[1]), axis=1)
    return jnp.exp(b_log) * a + b, a_log + b_log, line


def place():
    here = lax.axis_index("ctx")
    return here % 2, (here // 2) % 2, here // 4


def pair_body(
    width, own_ref, got_ref, rows_ref, a, b, c, d, pair_ref, sent_ref, same_rows_ref, joined_ref
):
    same_rows_ref[...] = rows_ref[...]
    join_rows((a, b, c, d), joined_ref)
    x, _, _ = place()
    pair = together(x == 0, taken(own_ref), received(got_ref), width)
    put(pair_ref, *pair)
    send(sent_ref, *pair)


def list_ids(ids_ref, early, late, width):
    at = iota(ids_ref.shape, 0)
    ids = jnp.zeros(ids_ref.shape, F32)
    for i in range(ids_ref.shape[0]):
        line = (early, late)[i // 4]
        ids = jnp.where(at == i, line[:, i % 4 * width : (i % 4 + 1) * width], ids)
    ids_ref[...] = ids


def join_rows(pieces, joined_ref):
    rows = pieces[0].shape[0]
    for i, piece in enumerate(pieces):
        joined_ref[i * rows : (i + 1) * rows] = piece[...]


def four_body(width, pair_ref, got_ref, sent_ref, ids_ref):
    _, z, _ = place()
    four = together(z == 0, taken(pair_ref), received(got_ref), 2 * width)
    send(sent_ref, *four)
    list_ids(ids_ref, four[2], four[2], width)


def turn_body(
    width,
    own_ref,
    got_ref,
    pair_ref,
    pair_got_ref,
    four_got_ref,
    a,
    b,
    c,
    d,
    mine_ref,
    sent_ref,
    ids_ref,
    joined_ref,
):
    join_rows((a, b, c, d), joined_ref)
    x, z, zz = place()
    pair, pair_got, four_got = taken(pair_ref), received(pair_got_ref), received(four_got_ref)
    line = together(z == 0, pair, pair_got, 2 * width)[2]
    (early,), (late,) = ordered(zz == 0, [line], [four_got[2]])
    list_ids(ids_ref, early, late, width)

    before = jnp.where(zz == 0, 0.0, four_got[0])
    before = jnp.where(z == 0, before, jnp.exp(pair_got[1]) * before + pair_got[0])
    (first, first_log), _ = ordered(x == 0, taken(own_ref)[:2], received(got_ref)[:2])
    after = jnp.exp(first_log) * before + first
    mine_ref[...] = jnp.where(x == 0, before, after)
    other = jnp.where(x == 0, after, before)
    send(sent_ref, other, jnp.zeros_like(first_log), jnp.zeros_like(first_log))


def prefix_body(parts_ref, starts_ref):
    ctx, rows, share = starts_ref.shape
    state = jnp.zeros((rows, share), F32)
    for i in range(ctx):
        starts_ref[i] = state
        if i < ctx - 1:
            state = parts_ref[i, STATE : STATE + 1] * state + parts_ref[i, :STATE]


def back_body(turn, gain_far, pre_far, decay_far, bc_far, start_ref, *rest):
    rest = rest[1:] if turn == 1 else rest
    out_far, gain_ref, pre_ref, decay_ref, bc_ref, out_ref, sems = rest
    channels = pre_ref.shape[1]
    half = pl.ds(0, channels)
    if turn is not None:
        side = (lax.axis_index("ctx") + turn) % 2
        half = pl.ds(pl.multiple_of(side * channels, channels), channels)
    far = (gain_far.at[:, half], pre_far.at[:, half], decay_far.at[:, half], bc_far)
    copies = started(far, (gain_ref, pre_ref, decay_ref, bc_ref), sems)
    width = min(channels, 4 * HDIM)
    group = (iota((width, width), 0) // HDIM == iota((width, width), 1) // HDIM).astype(BF16)
    start = received(start_ref)[0] if turn == 1 else start_ref[...]
    finished(copies)
    c_high, c_low = halves(bc_ref[:, STATE:])
    for i in range(channels // width):
        cut = slice(i * width, (i + 1) * width)
        s_high, s_low = halves(start[:, cut])
        carried = dot16(c_high, s_high) + dot16(c_high, s_low) + dot16(c_low, s_high)
        pre = pre_ref[:, cut] + carried * decay_ref[:, cut]
        mean = dot_left(pre * pre, group) * (1.0 / HDIM)
        out_ref[:, cut] = (pre * lax.rsqrt(mean + 1e-05) * gain_ref[:, cut]).astype(BF16)
    finished(started([out_ref], [out_far.at[:, half]], sems))


def entering_by_pairs(keep, sent, width, pre, near_pieces, far_rows, meanwhile):
    pair_array, sent_array = array(keep.shape, F32), array(sent.shape, jnp.int16)
    ids_array = array((8, width), F32)
    joined_array = array((4 * far_rows.shape[0], far_rows.shape[1]), BF16)
    got = swapped(sent, "ctx", 1)
    pair, sent, rows, joined = call(
        functools.partial(pair_body, width),
        [pair_array, sent_array, array(far_rows.shape, BF16), joined_array],
        (keep, got, far_rows, *near_pieces),
        near=True,
        after=(pre,),
        name="pair",
    )
    far_pieces = spread_rows(rows, 1)
    beside = swapped(joined, "exp", 1)
    pair_got = swapped(sent, "ctx", 2)
    sent, ids = call(
        functools.partial(four_body, width),
        [sent_array, ids_array],
        (pair, pair_got),
        near=True,
        after=(*far_pieces[1:3], beside),
        name="four",
    )
    four_got = swapped(sent, "ctx", 4)
    done = meanwhile(ids, beside)
    mine, sent, ids, joined = call(
        functools.partial(turn_body, width),
        [array((STATE, keep.shape[1]), F32), sent_array, ids_array, joined_array],
        (keep, got, pair, pair_got, four_got, *far_pieces),
        near=True,
        after_far=(done,),
        name="turn",
    )
    joined = swapped(joined, "exp", 1)
    return (mine, swapped(sent, "ctx", 1)), far_pieces, ids, joined, done


def entering_by_rows(state):
    ctx = lax.axis_size("ctx")
    rows, channels = state.shape
    slabs = state.reshape(rows, ctx, channels // ctx).transpose(1, 0, 2)
    parts = lax.all_to_all(slabs, "ctx", split_axis=0, concat_axis=0, tiled=True)
    (starts,) = call(
        prefix_body,
        [array((ctx, STATE, channels // ctx), F32)],
        (parts,),
        near=True,
        name="prefix",
    )
    start = lax.all_to_all(starts, "ctx", split_axis=0, concat_axis=0, tiled=True)
    return start.transpose(1, 0, 2).reshape(STATE, channels)


def mixing(
    rows, meanwhile, seq_input, b_input, c_input, before, conv_x, conv_bc, log_decay, skip, gain, ids
):
    tokens, channels = seq_input.shape
    heads = skip.shape[0]
    width = 2 * ids.shape[0]
    paired = rows is not None
    outs = [
        array((tokens, channels), F32),
        array((tokens, 2 * STATE), F32),
        array((2, heads, tokens), F32),
    ]
    if paired:
        ends = [array((STATE + NOTES, channels // 2), F32)]
        ends.append(array((STATE + 16, channels // 2), jnp.int16))
    else:
        ends = [array((STATE + NOTES, channels), F32)]
    args = (seq_input, b_input, c_input, conv_x, conv_bc, log_decay, ids.T, before)
    xconv, bc, lines, *ends = call(
        functools.partial(front_body, paired, len(args)),
        outs + ends,
        args,
        fixed=len(args) - 1,
        near_outs=len(ends),
        after=rows[0][:1] if paired else (),
        scratch=room(args) + room(outs) + [pltpu.VMEM((8 + tokens, channels + 2 * STATE), F32)],
        sems=len(args),
        flops=5 * 10**9,
        grant=20,
        name="front",
    )
    args = (skip.reshape(1, heads), xconv, bc, lines)
    outs = [array((tokens, channels), F32)] * 2
    pre, decay = call(
        inner_body,
        outs,
        args,
        fixed=1,
        scratch=room(args) + room(outs),
        sems=4,
        flops=4 * 10**9,
        grant=16,
        name="inner",
    )
    late = None
    if paired:
        starts, *late = entering_by_pairs(*ends, width, pre, *rows, meanwhile)
    else:
        starts = (entering_by_rows(ends[0]),)

    def finish(turn=None, so_far=None, after=()):
        args = (gain.reshape(1, channels), pre, decay, bc)
        parts = 1 if turn is None else 2
        shapes = [a.shape[:-1] + (a.shape[-1] // parts,) for a in args[:3]]
        inside = [array(shape, F32) for shape in shapes] + [bc, array(shapes[1], BF16)]
        start = starts[turn or 0]
        last = (so_far,) if turn == 1 else ()
        return call(
            functools.partial(back_body, turn),
            [pltpu.HBM((tokens, channels), BF16)],
            (*args, start, *last),
            fixed=1,
            spaces_of=[pltpu.HBM] + [pl.ANY] * 3 + [pltpu.VMEM] + [pltpu.HBM] * len(last),
            aliases={len(args) + 1: 0} if last else None,
            after_far=after,
            scratch=room(inside),
            sems=len(args),
            flops=10**9,
            grant=16,
            name="back",
        )[0]

    return finish, late


TILE = 512


def join_body(a_ref, b_ref, out_ref, sems):
    rows = a_ref.shape[0]
    finished(
        started([a_ref, b_ref], [out_ref.at[pl.ds(0, rows), :], out_ref.at[pl.ds(rows, rows), :]], sems)
    )


def swapped(block, axis, bit):
    return lax.ppermute(block, axis, [(i, i ^ bit) for i in range(lax.axis_size(axis))])


def expert_body(part, w_gate, w_up, *refs):
    pieces, joined_ref, ids_ref, out_far = refs[:4], refs[4], refs[5], refs[6 + part]
    pick_ref, hid_ref, out_ref, sems = refs[7 + part :]
    length, hidden = out_ref.shape
    rows = pieces[0].shape[0] // 2
    depth = pieces[0].shape[1]
    me = lax.axis_index("exp")
    here = lax.axis_index("ctx")
    downs = [pl.ds(pl.multiple_of((me ^ k) * depth, depth), depth) for k in range(4)]
    pair = (here // 4) ^ part

    shape = (rows, rows)
    earlier = (iota(shape, 1) < iota(shape, 0)).astype(F32)
    across = iota(shape, 1)
    diagonal = iota(shape, 0) == across
    turns = [(here % 4) ^ (2 * (i % 2) + i // 2) for i in range(length // rows)]
    for i, block in enumerate(turns):
        line = ids_ref[pl.ds(4 * pair + block, 1), :]
        mine = me.astype(F32)
        named = ((line[:, :rows] == mine) | (line[:, rows:] == mine)).astype(F32)
        column = jnp.sum(jnp.where(diagonal, named, 0.0), axis=1, keepdims=True)
        position = jnp.sum(earlier * named, axis=1, keepdims=True).astype(jnp.int32)
        pick_ref[i] = jnp.where(position == across, column, 0.0).astype(BF16)

    out_copies = []
    out_rows = pl.ds(pl.multiple_of(pair * length, length), length)
    for n in range(hidden // TILE):
        cut = slice(n * TILE, (n + 1) * TILE)
        gate = upper = None
        for k in range(4):
            if k % 2 == 0:
                block = jnp.concatenate([piece[...] for piece in pieces[k : k + 2]], axis=0)
            else:
                block = joined_ref[k // 2 * length : (k // 2 + 1) * length]
            more = dot16(block, w_gate[0, downs[k], cut])
            gate = more if k == 0 else gate + more
            more = dot16(block, w_up[0, downs[k], cut])
            upper = more if k == 0 else upper + more
        hid_ref[...] = (silu(gate) * upper).astype(BF16)
        for i, block in enumerate(turns):
            picked = dot16(pick_ref[i], hid_ref[i * rows : (i + 1) * rows], FIRST)
            out_ref[pl.ds(pl.multiple_of(block * rows, rows), rows), cut] = picked.astype(BF16)
        out_copies += started([out_ref.at[:, cut]], [out_far.at[0, out_rows, cut]], sems, n)
    finished(out_copies)


def along_z(moe_input):
    rows, columns = moe_input.shape
    joined = call(
        join_body,
        [array((2 * rows, columns), BF16)],
        (moe_input, swapped(moe_input, "ctx", 2)),
        fixed=1,
        sems=2,
        name="join",
    )[0]
    return joined, swapped(joined, "ctx", 4)


def spread_rows(z, through):
    x, y = swapped(z, "ctx", 1), swapped(z, "exp", 2)
    d = swapped(y, "ctx", 1) if through else swapped(x, "exp", 2)
    return (z, x, y, d)


def experts_by_tokens(part, pieces, joined, ids, w_gate, w_up, so_far, after=()):
    rows = pieces[0].shape[0] // 2
    length = 4 * rows
    hidden = w_gate.shape[2]
    args = (w_gate, w_up, *pieces, joined, ids)
    return call(
        functools.partial(expert_body, part),
        [pltpu.HBM((1, 2 * length, hidden), BF16)],
        args + ((so_far,) if part else ()),
        held=2,
        near_args=0,
        aliases={len(args): 0} if part else None,
        after_far=after,
        scratch=[
            pltpu.VMEM((length // rows, rows, rows), BF16),
            pltpu.VMEM((length, TILE), BF16),
            pltpu.VMEM((length, hidden), BF16),
        ],
        sems=hidden // TILE,
        flops=4 * length * w_gate.shape[1] * hidden,
        grant=16,
        spaces_of=[pltpu.VMEM] * len(args) + [pltpu.HBM] * part,
        name="experts",
    )[0]


def slot_matrix(pairs, expert, capacity):
    named = jnp.any(pairs == expert, axis=1).astype(jnp.int32)
    position = jnp.cumsum(named) - named
    hit = position[None, :] == jnp.arange(capacity, dtype=jnp.int32)[:, None]
    return (hit & (named[None, :] > 0)).astype(BF16)


def experts_by_slots(moe_input, pairs, w_gate, w_up):
    experts = lax.axis_size("exp")
    capacity = 4 * moe_input.shape[0] // experts
    pick = jax.vmap(lambda e: slot_matrix(pairs, e, capacity))(jnp.arange(experts))
    slots = jnp.einsum("eqt,td->eqd", pick, moe_input, preferred_element_type=F32)
    routed = lax.all_to_all(slots.astype(BF16), "exp", split_axis=0, concat_axis=2, tiled=True)
    rows = lax.all_gather(routed[0], "ctx", axis=0, tiled=True)
    gate = jnp.dot(rows, w_gate[0], preferred_element_type=F32)
    upper = jnp.dot(rows, w_up[0], preferred_element_type=F32)
    return (jax.nn.silu(gate) * upper).astype(BF16)[None]


def on_device(
    seq_input,
    b_input,
    c_input,
    conv_x,
    conv_bc,
    log_decay,
    skip_gain,
    norm_gain,
    moe_input,
    expert_ids,
    w_gate,
    w_up,
):
    ctx = lax.axis_size("ctx")
    by_tokens = lax.axis_size("exp") == 4 and ctx == 8
    tokens, channels = seq_input.shape
    ends = call(
        ends_body,
        [array((EDGE, channels + 2 * STATE), BF16)],
        (seq_input, b_input, c_input),
        fixed=3,
        sems=3,
        name="ends",
    )[0]
    before = lax.ppermute(ends, "ctx", [(i, i + 1) for i in range(ctx - 1)])
    pieces = meanwhile = None
    if by_tokens:
        near_rows, far_rows = along_z(moe_input)
        pieces = spread_rows(near_rows, 0), far_rows

        def meanwhile(ids, joined):
            return experts_by_tokens(0, pieces[0], joined, ids, w_gate, w_up, None)

    finish, late = mixing(
        pieces,
        meanwhile,
        seq_input,
        b_input,
        c_input,
        before,
        conv_x,
        conv_bc,
        log_decay,
        skip_gain,
        norm_gain,
        expert_ids,
    )
    if by_tokens:
        far_pieces, ids, joined, hidden = late
        mixed = finish(0)
        hidden = experts_by_tokens(1, far_pieces, joined, ids, w_gate, w_up, hidden, (mixed,))
        mixed = finish(1, mixed, (hidden,))
    else:
        mixed = finish()
        hidden = experts_by_slots(moe_input, expert_ids, w_gate, w_up)
    return (mixed, hidden)


def solution(mesh):
    in_specs = (
        P("ctx", "exp"),
        P("ctx", None),
        P("ctx", None),
        P(None, "exp"),
        P(),
        P("exp", "ctx"),
        P("exp"),
        P("exp"),
        P("ctx", "exp"),
        P("ctx", None),
        P("exp", None, "ctx"),
        P("exp", None, "ctx"),
    )
    out_specs = (P("ctx", "exp"), P("exp", None, "ctx"))
    return jax.shard_map(
        on_device, mesh=mesh, in_specs=in_specs, out_specs=out_specs, check_vma=False
    )
```

```python
import functools
import math

import jax
import jax.numpy as jnp
from jax import lax
from jax.experimental import pallas as pl
from jax.experimental.pallas import tpu as pltpu
from jax.sharding import PartitionSpec as P

HDIM = 64
STATE = 128
KCONV = 4
EDGE = 16
NOTES = 8

F32 = jnp.float32
BF16 = jnp.bfloat16


def dot16(a, b, contract=((1,), (0,))):
    return lax.dot_general(a, b, (contract, ((), ())), preferred_element_type=F32)


def halves(value):
    high = value.astype(BF16)
    return high, (value - high.astype(F32)).astype(BF16)


def dot(a, b, contract=((1,), (0,))):
    a_high, a_low = halves(a)
    b_high, b_low = halves(b)
    cross = dot16(a_high, b_low, contract) + dot16(a_low, b_high, contract)
    return dot16(a_high, b_high, contract) + cross


def dot_exact(a, b, contract=((1,), (0,))):
    high, rest = halves(a)
    low = (a - high.astype(F32) - rest.astype(F32)).astype(BF16)
    return dot16(high, b, contract) + (dot16(rest, b, contract) + dot16(low, b, contract))


def dot_left(a, b, contract=((1,), (0,))):
    high, low = halves(a)
    return dot16(high, b, contract) + dot16(low, b, contract)


FIRST = ((0,), (0,))


def iota(shape, axis):
    return lax.broadcasted_iota(jnp.int32, shape, axis)


def head_spread(heads):
    shape = (heads, heads * HDIM)
    return (iota(shape, 1) // HDIM == iota(shape, 0)).astype(BF16)


def upper_ones(length):
    return (iota((length, length), 0) <= iota((length, length), 1)).astype(BF16)


def silu(value):
    return value / (1.0 + jnp.exp(-value))


def one_minus_exp(value):
    series = jnp.ones_like(value)
    for n in range(8, 1, -1):
        series = 1.0 + value * series * (1.0 / n)
    return jnp.where(value > -0.25, -value * series, 1.0 - jnp.exp(value))


def started(sources, targets, sems, first=0):
    copies = []
    for i, (source, target) in enumerate(zip(sources, targets)):
        copies.append(pltpu.make_async_copy(source, target, sems.at[first + i]))
        copies[-1].start()
    return copies


def finished(copies):
    for copy in copies:
        copy.wait()


def following(body, count, skipped):
    return lambda *refs: body(*refs[:count], *refs[count + skipped :])


def call(
    body,
    outs,
    args,
    fixed=0,
    held=0,
    near_args=0,
    near_outs=0,
    after=(),
    after_far=(),
    aliases=None,
    scratch=(),
    sems=0,
    flops=0,
    grant=8,
    near=False,
    spaces_of=None,
    name=None,
):
    body = following(body, len(args), len(after) + len(after_far))
    moved = sum(math.prod(a.shape) * a.dtype.itemsize for a in (*args, *outs))
    scratch = list(scratch) + ([pltpu.SemaphoreType.DMA((sems,))] if sems else [])
    space = pltpu.VMEM if near else pl.ANY
    spaces = [pltpu.HBM] * fixed + [pltpu.VMEM] * held
    args = [
        pltpu.with_memory_space_constraint(a, spaces[i]) if i < len(spaces) else a
        for i, a in enumerate(args)
    ]
    spaces += [space] * (len(args) - near_args - len(spaces)) + [pltpu.VMEM] * near_args
    spaces = spaces_of or spaces
    args, spaces = [*args, *after], spaces + [pl.ANY] * len(after)
    args += [pltpu.with_memory_space_constraint(a, pltpu.HBM) for a in after_far]
    spaces += [pltpu.HBM] * len(after_far)
    out_spaces = [space] * (len(outs) - near_outs) + [pltpu.VMEM] * near_outs
    return pl.pallas_call(
        body,
        out_shape=outs,
        in_specs=[pl.BlockSpec(memory_space=s) for s in spaces],
        out_specs=[pl.BlockSpec(memory_space=s) for s in out_spaces],
        scratch_shapes=scratch,
        input_output_aliases=aliases or {},
        compiler_params=pltpu.CompilerParams(vmem_limit_bytes=grant * 2**20),
        cost_estimate=pl.CostEstimate(flops=flops, bytes_accessed=moved, transcendentals=0),
        name=name,
    )(*args)


def room(arrays):
    return [pltpu.VMEM(a.shape, a.dtype) for a in arrays]


def array(shape, dtype):
    return jax.ShapeDtypeStruct(shape, dtype)


def ends_body(x_ref, b_ref, c_ref, ends_ref, sems):
    tokens, channels = x_ref.shape
    cut = pl.ds(tokens - EDGE, EDGE)
    finished(
        started(
            [x_ref.at[cut, :], b_ref.at[cut, :], c_ref.at[cut, :]],
            [
                ends_ref.at[:, pl.ds(0, channels)],
                ends_ref.at[:, pl.ds(channels, STATE)],
                ends_ref.at[:, pl.ds(channels + STATE, STATE)],
            ],
            sems,
        )
    )


def front_body(paired, count, *refs):
    far, (xconv_ref, bc_ref, lines_ref), rest = refs[:count], refs[count : count + 3], refs[count + 3 :]
    ends, rest = rest[: 1 + paired], rest[1 + paired :]
    near, pad_ref, sems = rest[:count], rest[-2], rest[-1]
    copies = started(far, near, sems)
    x_ref, b_ref, c_ref, taps_ref, taps_bc_ref, logs_ref, ids_ref, ends_ref = near
    tokens, channels = x_ref.shape
    heads = logs_ref.shape[0]
    finished(copies)
    pad_ref[0:8, :] = ends_ref[...].astype(F32)[EDGE - 8 : EDGE]
    pad_ref[8 : 8 + tokens, :channels] = x_ref[...].astype(F32)
    pad_ref[8 : 8 + tokens, channels : channels + STATE] = b_ref[...].astype(F32)
    pad_ref[8 : 8 + tokens, channels + STATE :] = c_ref[...].astype(F32)

    def conv(taps, start, stop):
        total = jnp.zeros((tokens, stop - start), F32)
        for k in range(KCONV):
            first = 8 - (KCONV - 1) + k
            total = total + taps[k : k + 1] * pad_ref[first : first + tokens, start:stop]
        return silu(total)

    bc = conv(taps_bc_ref[...], channels, channels + 2 * STATE)
    bc_ref[...] = bc
    xconv = conv(taps_ref[...], 0, channels)
    xconv_ref[...] = xconv
    logs = logs_ref[...]
    inflow = jnp.sqrt(one_minus_exp(2.0 * logs))
    row = dot_exact(logs, upper_ones(tokens))
    lines_ref[0] = row
    lines_ref[1] = inflow
    total = row[:, tokens - 1 :]
    spread = head_spread(heads)
    fresh = xconv * dot_left(inflow * jnp.exp(total - row), spread, FIRST)
    state = dot(bc[:, :STATE], fresh, FIRST)
    total = jnp.broadcast_to(total, (heads, NOTES))
    if paired:
        total = dot_exact(total, spread, FIRST)
        half = channels // 2
        side = lax.axis_index("ctx") % 2
        ids = ids_ref[...].astype(F32)
        line = jnp.concatenate([ids[0:1], ids[1:2]], axis=1)
        line = jnp.concatenate([line] * (half // line.shape[1]), axis=1)
        for ref, first in ((ends[0], side == 0), (ends[1], side != 0)):
            mine = jnp.where(first, state[:, :half], state[:, half:])
            logsum = jnp.where(first, total[:1, :half], total[:1, half:])
            if ref is ends[0]:
                put(ref, mine, logsum, line)
            else:
                send(ref, mine, logsum, line)
    else:
        ends[0][:STATE] = state
        ends[0][STATE:] = dot_exact(jnp.exp(total), spread, FIRST)


def inner_body(
    skip_far,
    gain_far,
    xconv_ref,
    bc_ref,
    lines_ref,
    pre_ref,
    decay_ref,
    gain_ref,
    skip_ref,
    sems,
):
    copies = started([skip_far, gain_far], [skip_ref, gain_ref], sems)
    tokens, channels = xconv_ref.shape
    heads = channels // HDIM
    row = lines_ref[0]
    column = row.T
    spread = head_spread(heads)
    decay_ref[...] = dot_left(jnp.exp(row), spread, FIRST)
    inflow = dot_left(lines_ref[1], spread, FIRST)
    meet = dot(bc_ref[:, STATE:], bc_ref[:, :STATE], ((1,), (1,)))
    lower = iota((tokens, tokens), 0) >= iota((tokens, tokens), 1)
    left = iota((tokens, 2 * HDIM), 1) < HDIM
    finished(copies)
    skip = dot_exact(skip_ref[...], spread)
    for pair in range(heads // 2):
        cut = slice(pair * 2 * HDIM, (pair + 1) * 2 * HDIM)
        xconv = xconv_ref[:, cut]
        d_high, d_low = halves(xconv * inflow[:, cut])
        both = []
        for h in (2 * pair, 2 * pair + 1):
            gap = column[:, h : h + 1] - row[h : h + 1, :]
            mix = jnp.where(lower, jnp.exp(gap), 0.0) * meet
            m_high, m_low = halves(mix)
            both.append(dot16(m_high, d_high) + dot16(m_high, d_low) + dot16(m_low, d_high))
        pre_ref[:, cut] = skip[:, cut] * xconv + jnp.where(left, both[0], both[1])


def put(ref, state, logsum, line):
    ref[:STATE] = state
    at = iota((NOTES, state.shape[1]), 0)
    ref[STATE:] = jnp.where(at == 0, logsum, line)


def send(ref, state, logsum, line):
    largest = jnp.max(jnp.abs(state), axis=0, keepdims=True)
    power = jnp.ceil(jnp.log2(jnp.maximum(largest, 1e-30))) - 15.0
    whole = jnp.clip(jnp.round(state * jnp.exp2(-power)), -32767.0, 32767.0)
    ref[:STATE] = whole.astype(jnp.int32).astype(jnp.int16)
    logsum = jnp.round(jnp.maximum(logsum, -128.0) * 2.0**22).astype(jnp.int32)
    at = iota((16, state.shape[1]), 0)
    notes = jnp.where(at == 0, power.astype(jnp.int32), line.astype(jnp.int32))
    notes = jnp.where(at == 1, logsum >> 15, jnp.where(at == 2, logsum & 32767, notes))
    ref[STATE:] = notes.astype(jnp.int16)


def taken(ref):
    return ref[:STATE], ref[STATE : STATE + 1], ref[STATE + 1 : STATE + 2]


def received(ref):
    notes = ref[STATE:].astype(jnp.int32).astype(F32)
    state = ref[:STATE].astype(jnp.int32).astype(F32) * jnp.exp2(notes[0:1])
    return state, notes[1:2] * 2.0**-7 + notes[2:3] * 2.0**-22, notes[3:4]


def ordered(first, own, other):
    return [jnp.where(first, a, b) for a, b in zip(own, other)], [
        jnp.where(first, b, a) for a, b in zip(own, other)
    ]


def together(first, own, other, width):
    (a, a_log, a_line), (b, b_log, b_line) = ordered(first, own, other)
    line = jnp.concatenate([a_line[:, :width], b_line[:, :width]], axis=1)
    line = jnp.concatenate([line] * (a.shape[1] // line.shape[1]), axis=1)
    return jnp.exp(b_log) * a + b, a_log + b_log, line


def place():
    here = lax.axis_index("ctx")
    return here % 2, (here // 2) % 2, here // 4


def pair_body(width, own_ref, got_ref, rows_ref, pair_ref, sent_ref, same_rows_ref):
    same_rows_ref[...] = rows_ref[...]
    x, _, _ = place()
    pair = together(x == 0, taken(own_ref), received(got_ref), width)
    put(pair_ref, *pair)
    send(sent_ref, *pair)


def list_ids(ids_ref, early, late, width):
    at = iota(ids_ref.shape, 0)
    ids = jnp.zeros(ids_ref.shape, F32)
    for i in range(ids_ref.shape[0]):
        line = (early, late)[i // 4]
        ids = jnp.where(at == i, line[:, i % 4 * width : (i % 4 + 1) * width], ids)
    ids_ref[...] = ids


def join_rows(pieces, joined_ref):
    rows = pieces[0].shape[0]
    for i, piece in enumerate(pieces):
        joined_ref[i * rows : (i + 1) * rows] = piece[...]


def four_body(width, pair_ref, got_ref, a, b, c, d, sent_ref, ids_ref, joined_ref):
    join_rows((a, b, c, d), joined_ref)
    _, z, _ = place()
    four = together(z == 0, taken(pair_ref), received(got_ref), 2 * width)
    send(sent_ref, *four)
    list_ids(ids_ref, four[2], four[2], width)


def turn_body(
    width,
    own_ref,
    got_ref,
    pair_ref,
    pair_got_ref,
    four_got_ref,
    a,
    b,
    c,
    d,
    mine_ref,
    sent_ref,
    ids_ref,
    joined_ref,
):
    join_rows((a, b, c, d), joined_ref)
    x, z, zz = place()
    pair, pair_got, four_got = taken(pair_ref), received(pair_got_ref), received(four_got_ref)
    line = together(z == 0, pair, pair_got, 2 * width)[2]
    (early,), (late,) = ordered(zz == 0, [line], [four_got[2]])
    list_ids(ids_ref, early, late, width)

    before = jnp.where(zz == 0, 0.0, four_got[0])
    before = jnp.where(z == 0, before, jnp.exp(pair_got[1]) * before + pair_got[0])
    (first, first_log), _ = ordered(x == 0, taken(own_ref)[:2], received(got_ref)[:2])
    after = jnp.exp(first_log) * before + first
    mine_ref[...] = jnp.where(x == 0, before, after)
    other = jnp.where(x == 0, after, before)
    send(sent_ref, other, jnp.zeros_like(first_log), jnp.zeros_like(first_log))


def prefix_body(parts_ref, starts_ref):
    ctx, rows, share = starts_ref.shape
    state = jnp.zeros((rows, share), F32)
    for i in range(ctx):
        starts_ref[i] = state
        if i < ctx - 1:
            state = parts_ref[i, STATE : STATE + 1] * state + parts_ref[i, :STATE]


def back_body(paired, gain_ref, pre_ref, decay_ref, bc_ref, *rest):
    starts, (out_far, out_ref, sems) = rest[: 1 + paired], rest[1 + paired :]
    channels = pre_ref.shape[1]
    width = min(channels, 4 * HDIM)
    group = (iota((width, width), 0) // HDIM == iota((width, width), 1) // HDIM).astype(BF16)
    if paired:
        side = lax.axis_index("ctx") % 2
        mine, other = starts[0][...], received(starts[1])[0]
        start = [jnp.where(side == 0, mine, other), jnp.where(side == 0, other, mine)]
        start = jnp.concatenate(start, axis=1)
    else:
        start = starts[0][...]
    c_high, c_low = halves(bc_ref[:, STATE:])
    copies = []
    for i in range(channels // width):
        cut = slice(i * width, (i + 1) * width)
        s_high, s_low = halves(start[:, cut])
        carried = dot16(c_high, s_high) + dot16(c_high, s_low) + dot16(c_low, s_high)
        pre = pre_ref[:, cut] + carried * decay_ref[:, cut]
        mean = dot_left(pre * pre, group) * (1.0 / HDIM)
        out_ref[:, cut] = (pre * lax.rsqrt(mean + 1e-05) * gain_ref[:, cut]).astype(BF16)
        copies += started([out_ref.at[:, cut]], [out_far.at[:, cut]], sems, i)
    finished(copies)


def entering_by_pairs(keep, sent, width, pre, near_pieces, far_rows, meanwhile):
    pair_array, sent_array = array(keep.shape, F32), array(sent.shape, jnp.int16)
    ids_array = array((8, width), F32)
    joined_array = array((4 * far_rows.shape[0], far_rows.shape[1]), BF16)
    got = swapped(sent, "ctx", 1)
    pair, sent, rows = call(
        functools.partial(pair_body, width),
        [pair_array, sent_array, array(far_rows.shape, BF16)],
        (keep, got, far_rows),
        near=True,
        after=(*near_pieces[2:], pre),
        name="pair",
    )
    far_pieces = spread_rows(rows, 1)
    pair_got = swapped(sent, "ctx", 2)
    sent, ids, joined = call(
        functools.partial(four_body, width),
        [sent_array, ids_array, joined_array],
        (pair, pair_got, *near_pieces),
        near=True,
        after=far_pieces[1:3],
        name="four",
    )
    four_got = swapped(sent, "ctx", 4)
    done = meanwhile(ids, joined)
    mine, sent, ids, joined = call(
        functools.partial(turn_body, width),
        [array((STATE, keep.shape[1]), F32), sent_array, ids_array, joined_array],
        (keep, got, pair, pair_got, four_got, *far_pieces),
        near=True,
        after_far=(done,),
        name="turn",
    )
    return (mine, swapped(sent, "ctx", 1)), far_pieces, ids, joined, done


def entering_by_rows(state):
    ctx = lax.axis_size("ctx")
    rows, channels = state.shape
    slabs = state.reshape(rows, ctx, channels // ctx).transpose(1, 0, 2)
    parts = lax.all_to_all(slabs, "ctx", split_axis=0, concat_axis=0, tiled=True)
    (starts,) = call(
        prefix_body,
        [array((ctx, STATE, channels // ctx), F32)],
        (parts,),
        near=True,
        name="prefix",
    )
    start = lax.all_to_all(starts, "ctx", split_axis=0, concat_axis=0, tiled=True)
    return start.transpose(1, 0, 2).reshape(STATE, channels)


def mixing(
    rows, meanwhile, seq_input, b_input, c_input, before, conv_x, conv_bc, log_decay, skip, gain, ids
):
    tokens, channels = seq_input.shape
    heads = skip.shape[0]
    width = 2 * ids.shape[0]
    paired = rows is not None
    outs = [
        array((tokens, channels), F32),
        array((tokens, 2 * STATE), F32),
        array((2, heads, tokens), F32),
    ]
    if paired:
        ends = [array((STATE + NOTES, channels // 2), F32)]
        ends.append(array((STATE + 16, channels // 2), jnp.int16))
    else:
        ends = [array((STATE + NOTES, channels), F32)]
    args = (seq_input, b_input, c_input, conv_x, conv_bc, log_decay, ids.T, before)
    xconv, bc, lines, *ends = call(
        functools.partial(front_body, paired, len(args)),
        outs + ends,
        args,
        fixed=len(args) - 1,
        near_outs=len(outs + ends),
        after=rows[0][:1] if paired else (),
        scratch=room(args) + [pltpu.VMEM((8 + tokens, channels + 2 * STATE), F32)],
        sems=len(args),
        flops=5 * 10**9,
        grant=20,
        name="front",
    )
    args = (skip.reshape(1, heads), gain.reshape(1, channels), xconv, bc, lines)
    pre, decay, gain = call(
        inner_body,
        [array((tokens, channels), F32)] * 2 + [array((1, channels), F32)],
        args,
        fixed=2,
        near_args=3,
        near_outs=3,
        scratch=room(args[:1]),
        sems=2,
        flops=4 * 10**9,
        grant=16,
        name="inner",
    )
    late = None
    if paired:
        starts, *late = entering_by_pairs(*ends, width, pre, *rows, meanwhile)
    else:
        starts = (entering_by_rows(ends[0]),)

    def finish(after=()):
        outs = [array((tokens, channels), BF16)]
        args = (gain, pre, decay, bc, *starts)
        return call(
            functools.partial(back_body, paired),
            outs,
            args,
            near_args=len(args),
            after_far=after,
            scratch=room(outs),
            sems=max(1, channels // (4 * HDIM)),
            flops=10**9,
            grant=16,
            name="back",
        )[0]

    return finish, late


TILE = 512


def join_body(a_ref, b_ref, out_ref, sems):
    rows = a_ref.shape[0]
    finished(
        started([a_ref, b_ref], [out_ref.at[pl.ds(0, rows), :], out_ref.at[pl.ds(rows, rows), :]], sems)
    )


def swapped(block, axis, bit):
    return lax.ppermute(block, axis, [(i, i ^ bit) for i in range(lax.axis_size(axis))])


def expert_body(part, w_gate, w_up, *refs):
    pieces, joined_ref, ids_ref, out_far = refs[:4], refs[4], refs[5], refs[6 + part]
    pick_ref, hid_ref, out_ref, sems = refs[7 + part :]
    length, hidden = out_ref.shape
    rows = pieces[0].shape[0] // 2
    depth = pieces[0].shape[1]
    me = lax.axis_index("exp")
    here = lax.axis_index("ctx")
    downs = [pl.ds(pl.multiple_of((me ^ k) * depth, depth), depth) for k in range(4)]
    pair = (here // 4) ^ part

    shape = (rows, rows)
    earlier = (iota(shape, 1) < iota(shape, 0)).astype(F32)
    across = iota(shape, 1)
    diagonal = iota(shape, 0) == across
    turns = [(here % 4) ^ (2 * (i % 2) + i // 2) for i in range(length // rows)]
    for i, block in enumerate(turns):
        line = ids_ref[pl.ds(4 * pair + block, 1), :]
        mine = me.astype(F32)
        named = ((line[:, :rows] == mine) | (line[:, rows:] == mine)).astype(F32)
        column = jnp.sum(jnp.where(diagonal, named, 0.0), axis=1, keepdims=True)
        position = jnp.sum(earlier * named, axis=1, keepdims=True).astype(jnp.int32)
        pick_ref[i] = jnp.where(position == across, column, 0.0).astype(BF16)

    out_copies = []
    out_rows = pl.ds(pl.multiple_of(pair * length, length), length)
    for n in range(hidden // TILE):
        cut = slice(n * TILE, (n + 1) * TILE)
        gate = upper = None
        for k in range(4):
            if k % 2 == 0:
                block = jnp.concatenate([piece[...] for piece in pieces[k : k + 2]], axis=0)
            else:
                block = joined_ref[k // 2 * length : (k // 2 + 1) * length]
            more = dot16(block, w_gate[0, downs[k], cut])
            gate = more if k == 0 else gate + more
            more = dot16(block, w_up[0, downs[k], cut])
            upper = more if k == 0 else upper + more
        hid_ref[...] = (silu(gate) * upper).astype(BF16)
        for i, block in enumerate(turns):
            picked = dot16(pick_ref[i], hid_ref[i * rows : (i + 1) * rows], FIRST)
            out_ref[pl.ds(pl.multiple_of(block * rows, rows), rows), cut] = picked.astype(BF16)
        out_copies += started([out_ref.at[:, cut]], [out_far.at[0, out_rows, cut]], sems, n)
    finished(out_copies)


def along_z(moe_input):
    rows, columns = moe_input.shape
    joined = call(
        join_body,
        [array((2 * rows, columns), BF16)],
        (moe_input, swapped(moe_input, "ctx", 2)),
        fixed=1,
        sems=2,
        name="join",
    )[0]
    return joined, swapped(joined, "ctx", 4)


def spread_rows(z, through):
    x, y = swapped(z, "ctx", 1), swapped(z, "exp", 2)
    d = swapped(y, "ctx", 1) if through else swapped(x, "exp", 2)
    return (z, x, y, d)


def experts_by_tokens(part, pieces, joined, ids, w_gate, w_up, so_far):
    rows = pieces[0].shape[0] // 2
    length = 4 * rows
    hidden = w_gate.shape[2]
    args = (w_gate, w_up, *pieces, swapped(joined, "exp", 1), ids)
    return call(
        functools.partial(expert_body, part),
        [pltpu.HBM((1, 2 * length, hidden), BF16)],
        args + ((so_far,) if part else ()),
        held=2,
        near_args=0,
        aliases={len(args): 0} if part else None,
        scratch=[
            pltpu.VMEM((length // rows, rows, rows), BF16),
            pltpu.VMEM((length, TILE), BF16),
            pltpu.VMEM((length, hidden), BF16),
        ],
        sems=hidden // TILE,
        flops=4 * length * w_gate.shape[1] * hidden,
        grant=16,
        spaces_of=[pltpu.VMEM] * len(args) + [pltpu.HBM] * part,
        name="experts",
    )[0]


def slot_matrix(pairs, expert, capacity):
    named = jnp.any(pairs == expert, axis=1).astype(jnp.int32)
    position = jnp.cumsum(named) - named
    hit = position[None, :] == jnp.arange(capacity, dtype=jnp.int32)[:, None]
    return (hit & (named[None, :] > 0)).astype(BF16)


def experts_by_slots(moe_input, pairs, w_gate, w_up):
    experts = lax.axis_size("exp")
    capacity = 4 * moe_input.shape[0] // experts
    pick = jax.vmap(lambda e: slot_matrix(pairs, e, capacity))(jnp.arange(experts))
    slots = jnp.einsum("eqt,td->eqd", pick, moe_input, preferred_element_type=F32)
    routed = lax.all_to_all(slots.astype(BF16), "exp", split_axis=0, concat_axis=2, tiled=True)
    rows = lax.all_gather(routed[0], "ctx", axis=0, tiled=True)
    gate = jnp.dot(rows, w_gate[0], preferred_element_type=F32)
    upper = jnp.dot(rows, w_up[0], preferred_element_type=F32)
    return (jax.nn.silu(gate) * upper).astype(BF16)[None]


def on_device(
    seq_input,
    b_input,
    c_input,
    conv_x,
    conv_bc,
    log_decay,
    skip_gain,
    norm_gain,
    moe_input,
    expert_ids,
    w_gate,
    w_up,
):
    ctx = lax.axis_size("ctx")
    by_tokens = lax.axis_size("exp") == 4 and ctx == 8
    tokens, channels = seq_input.shape
    ends = call(
        ends_body,
        [array((EDGE, channels + 2 * STATE), BF16)],
        (seq_input, b_input, c_input),
        fixed=3,
        sems=3,
        name="ends",
    )[0]
    before = lax.ppermute(ends, "ctx", [(i, i + 1) for i in range(ctx - 1)])
    pieces = meanwhile = None
    if by_tokens:
        near_rows, far_rows = along_z(moe_input)
        pieces = spread_rows(near_rows, 0), far_rows

        def meanwhile(ids, joined):
            return experts_by_tokens(0, pieces[0], joined, ids, w_gate, w_up, None)

    finish, late = mixing(
        pieces,
        meanwhile,
        seq_input,
        b_input,
        c_input,
        before,
        conv_x,
        conv_bc,
        log_decay,
        skip_gain,
        norm_gain,
        expert_ids,
    )
    if by_tokens:
        far_pieces, ids, joined, hidden = late
        hidden = experts_by_tokens(1, far_pieces, joined, ids, w_gate, w_up, hidden)
        mixed = finish((hidden,))
    else:
        mixed = finish()
        hidden = experts_by_slots(moe_input, expert_ids, w_gate, w_up)
    return (mixed, hidden)


def solution(mesh):
    in_specs = (
        P("ctx", "exp"),
        P("ctx", None),
        P("ctx", None),
        P(None, "exp"),
        P(),
        P("exp", "ctx"),
        P("exp"),
        P("exp"),
        P("ctx", "exp"),
        P("ctx", None),
        P("exp", None, "ctx"),
        P("exp", None, "ctx"),
    )
    out_specs = (P("ctx", "exp"), P("exp", None, "ctx"))
    return jax.shard_map(
        on_device, mesh=mesh, in_specs=in_specs, out_specs=out_specs, check_vma=False
    )
```

```python
import functools
import math

import jax
import jax.numpy as jnp
from jax import lax
from jax.experimental import pallas as pl
from jax.experimental.pallas import tpu as pltpu
from jax.sharding import PartitionSpec as P

HDIM = 64
STATE = 128
KCONV = 4
EDGE = 16
NOTES = 8

F32 = jnp.float32
BF16 = jnp.bfloat16


def dot16(a, b, contract=((1,), (0,))):
    return lax.dot_general(a, b, (contract, ((), ())), preferred_element_type=F32)


def halves(value):
    high = value.astype(BF16)
    return high, (value - high.astype(F32)).astype(BF16)


def dot(a, b, contract=((1,), (0,))):
    a_high, a_low = halves(a)
    b_high, b_low = halves(b)
    cross = dot16(a_high, b_low, contract) + dot16(a_low, b_high, contract)
    return dot16(a_high, b_high, contract) + cross


def dot_exact(a, b, contract=((1,), (0,))):
    high, rest = halves(a)
    low = (a - high.astype(F32) - rest.astype(F32)).astype(BF16)
    return dot16(high, b, contract) + (dot16(rest, b, contract) + dot16(low, b, contract))


def dot_left(a, b, contract=((1,), (0,))):
    high, low = halves(a)
    return dot16(high, b, contract) + dot16(low, b, contract)


FIRST = ((0,), (0,))


def iota(shape, axis):
    return lax.broadcasted_iota(jnp.int32, shape, axis)


def head_spread(heads):
    shape = (heads, heads * HDIM)
    return (iota(shape, 1) // HDIM == iota(shape, 0)).astype(BF16)


def upper_ones(length):
    return (iota((length, length), 0) <= iota((length, length), 1)).astype(BF16)


def silu(value):
    return value / (1.0 + jnp.exp(-value))


def one_minus_exp(value):
    series = jnp.ones_like(value)
    for n in range(8, 1, -1):
        series = 1.0 + value * series * (1.0 / n)
    return jnp.where(value > -0.25, -value * series, 1.0 - jnp.exp(value))


def started(sources, targets, sems, first=0):
    copies = []
    for i, (source, target) in enumerate(zip(sources, targets)):
        copies.append(pltpu.make_async_copy(source, target, sems.at[first + i]))
        copies[-1].start()
    return copies


def finished(copies):
    for copy in copies:
        copy.wait()


def following(body, count, skipped):
    return lambda *refs: body(*refs[:count], *refs[count + skipped :])


def call(
    body,
    outs,
    args,
    fixed=0,
    held=0,
    near_args=0,
    near_outs=0,
    after=(),
    after_far=(),
    aliases=None,
    scratch=(),
    sems=0,
    flops=0,
    grant=8,
    near=False,
    spaces_of=None,
    name=None,
):
    body = following(body, len(args), len(after) + len(after_far))
    moved = sum(math.prod(a.shape) * a.dtype.itemsize for a in (*args, *outs))
    scratch = list(scratch) + ([pltpu.SemaphoreType.DMA((sems,))] if sems else [])
    space = pltpu.VMEM if near else pl.ANY
    spaces = [pltpu.HBM] * fixed + [pltpu.VMEM] * held
    args = [
        pltpu.with_memory_space_constraint(a, spaces[i]) if i < len(spaces) else a
        for i, a in enumerate(args)
    ]
    spaces += [space] * (len(args) - near_args - len(spaces)) + [pltpu.VMEM] * near_args
    spaces = spaces_of or spaces
    args, spaces = [*args, *after], spaces + [pl.ANY] * len(after)
    args += [pltpu.with_memory_space_constraint(a, pltpu.HBM) for a in after_far]
    spaces += [pltpu.HBM] * len(after_far)
    out_spaces = [space] * (len(outs) - near_outs) + [pltpu.VMEM] * near_outs
    return pl.pallas_call(
        body,
        out_shape=outs,
        in_specs=[pl.BlockSpec(memory_space=s) for s in spaces],
        out_specs=[pl.BlockSpec(memory_space=s) for s in out_spaces],
        scratch_shapes=scratch,
        input_output_aliases=aliases or {},
        compiler_params=pltpu.CompilerParams(vmem_limit_bytes=grant * 2**20),
        cost_estimate=pl.CostEstimate(flops=flops, bytes_accessed=moved, transcendentals=0),
        name=name,
    )(*args)


def room(arrays):
    return [pltpu.VMEM(a.shape, a.dtype) for a in arrays]


def array(shape, dtype):
    return jax.ShapeDtypeStruct(shape, dtype)


def ends_body(x_ref, b_ref, c_ref, ends_ref, sems):
    tokens, channels = x_ref.shape
    cut = pl.ds(tokens - EDGE, EDGE)
    finished(
        started(
            [x_ref.at[cut, :], b_ref.at[cut, :], c_ref.at[cut, :]],
            [
                ends_ref.at[:, pl.ds(0, channels)],
                ends_ref.at[:, pl.ds(channels, STATE)],
                ends_ref.at[:, pl.ds(channels + STATE, STATE)],
            ],
            sems,
        )
    )


def front_body(paired, count, *refs):
    far, (xconv_ref, bc_ref, lines_ref), rest = refs[:count], refs[count : count + 3], refs[count + 3 :]
    ends, rest = rest[: 1 + paired], rest[1 + paired :]
    near, pad_ref, sems = rest[:count], rest[-2], rest[-1]
    copies = started(far, near, sems)
    x_ref, b_ref, c_ref, taps_ref, taps_bc_ref, logs_ref, ids_ref, ends_ref = near
    tokens, channels = x_ref.shape
    heads = logs_ref.shape[0]
    finished(copies)
    pad_ref[0:8, :] = ends_ref[...].astype(F32)[EDGE - 8 : EDGE]
    pad_ref[8 : 8 + tokens, :channels] = x_ref[...].astype(F32)
    pad_ref[8 : 8 + tokens, channels : channels + STATE] = b_ref[...].astype(F32)
    pad_ref[8 : 8 + tokens, channels + STATE :] = c_ref[...].astype(F32)

    def conv(taps, start, stop):
        total = jnp.zeros((tokens, stop - start), F32)
        for k in range(KCONV):
            first = 8 - (KCONV - 1) + k
            total = total + taps[k : k + 1] * pad_ref[first : first + tokens, start:stop]
        return silu(total)

    bc = conv(taps_bc_ref[...], channels, channels + 2 * STATE)
    bc_ref[...] = bc
    xconv = conv(taps_ref[...], 0, channels)
    xconv_ref[...] = xconv
    logs = logs_ref[...]
    inflow = jnp.sqrt(one_minus_exp(2.0 * logs))
    row = dot_exact(logs, upper_ones(tokens))
    lines_ref[0] = row
    lines_ref[1] = inflow
    total = row[:, tokens - 1 :]
    spread = head_spread(heads)
    fresh = xconv * dot_left(inflow * jnp.exp(total - row), spread, FIRST)
    state = dot(bc[:, :STATE], fresh, FIRST)
    total = jnp.broadcast_to(total, (heads, NOTES))
    if paired:
        total = dot_exact(total, spread, FIRST)
        half = channels // 2
        side = lax.axis_index("ctx") % 2
        ids = ids_ref[...].astype(F32)
        line = jnp.concatenate([ids[0:1], ids[1:2]], axis=1)
        line = jnp.concatenate([line] * (half // line.shape[1]), axis=1)
        for ref, first in ((ends[0], side == 0), (ends[1], side != 0)):
            mine = jnp.where(first, state[:, :half], state[:, half:])
            logsum = jnp.where(first, total[:1, :half], total[:1, half:])
            if ref is ends[0]:
                put(ref, mine, logsum, line)
            else:
                send(ref, mine, logsum, line)
    else:
        ends[0][:STATE] = state
        ends[0][STATE:] = dot_exact(jnp.exp(total), spread, FIRST)


def inner_body(
    skip_far,
    gain_far,
    xconv_ref,
    bc_ref,
    lines_ref,
    pre_ref,
    decay_ref,
    gain_ref,
    skip_ref,
    sems,
):
    copies = started([skip_far, gain_far], [skip_ref, gain_ref], sems)
    tokens, channels = xconv_ref.shape
    heads = channels // HDIM
    row = lines_ref[0]
    column = row.T
    spread = head_spread(heads)
    decay_ref[...] = dot_left(jnp.exp(row), spread, FIRST)
    inflow = dot_left(lines_ref[1], spread, FIRST)
    meet = dot(bc_ref[:, STATE:], bc_ref[:, :STATE], ((1,), (1,)))
    lower = iota((tokens, tokens), 0) >= iota((tokens, tokens), 1)
    left = iota((tokens, 2 * HDIM), 1) < HDIM
    finished(copies)
    skip = dot_exact(skip_ref[...], spread)
    for pair in range(heads // 2):
        cut = slice(pair * 2 * HDIM, (pair + 1) * 2 * HDIM)
        xconv = xconv_ref[:, cut]
        d_high, d_low = halves(xconv * inflow[:, cut])
        both = []
        for h in (2 * pair, 2 * pair + 1):
            gap = column[:, h : h + 1] - row[h : h + 1, :]
            mix = jnp.where(lower, jnp.exp(gap), 0.0) * meet
            m_high, m_low = halves(mix)
            both.append(dot16(m_high, d_high) + dot16(m_high, d_low) + dot16(m_low, d_high))
        pre_ref[:, cut] = skip[:, cut] * xconv + jnp.where(left, both[0], both[1])


def put(ref, state, logsum, line):
    ref[:STATE] = state
    at = iota((NOTES, state.shape[1]), 0)
    ref[STATE:] = jnp.where(at == 0, logsum, line)


def send(ref, state, logsum, line):
    largest = jnp.max(jnp.abs(state), axis=0, keepdims=True)
    power = jnp.ceil(jnp.log2(jnp.maximum(largest, 1e-30))) - 15.0
    whole = jnp.clip(jnp.round(state * jnp.exp2(-power)), -32767.0, 32767.0)
    ref[:STATE] = whole.astype(jnp.int32).astype(jnp.int16)
    logsum = jnp.round(jnp.maximum(logsum, -128.0) * 2.0**22).astype(jnp.int32)
    at = iota((16, state.shape[1]), 0)
    notes = jnp.where(at == 0, power.astype(jnp.int32), line.astype(jnp.int32))
    notes = jnp.where(at == 1, logsum >> 15, jnp.where(at == 2, logsum & 32767, notes))
    ref[STATE:] = notes.astype(jnp.int16)


def taken(ref):
    return ref[:STATE], ref[STATE : STATE + 1], ref[STATE + 1 : STATE + 2]


def received(ref):
    notes = ref[STATE:].astype(jnp.int32).astype(F32)
    state = ref[:STATE].astype(jnp.int32).astype(F32) * jnp.exp2(notes[0:1])
    return state, notes[1:2] * 2.0**-7 + notes[2:3] * 2.0**-22, notes[3:4]


def ordered(first, own, other):
    return [jnp.where(first, a, b) for a, b in zip(own, other)], [
        jnp.where(first, b, a) for a, b in zip(own, other)
    ]


def together(first, own, other, width):
    (a, a_log, a_line), (b, b_log, b_line) = ordered(first, own, other)
    line = jnp.concatenate([a_line[:, :width], b_line[:, :width]], axis=1)
    line = jnp.concatenate([line] * (a.shape[1] // line.shape[1]), axis=1)
    return jnp.exp(b_log) * a + b, a_log + b_log, line


def place():
    here = lax.axis_index("ctx")
    return here % 2, (here // 2) % 2, here // 4


def pair_body(
    width, own_ref, got_ref, rows_ref, a, b, c, d, pair_ref, sent_ref, same_rows_ref, joined_ref
):
    same_rows_ref[...] = rows_ref[...]
    join_rows((a, b, c, d), joined_ref)
    x, _, _ = place()
    pair = together(x == 0, taken(own_ref), received(got_ref), width)
    put(pair_ref, *pair)
    send(sent_ref, *pair)


def list_ids(ids_ref, early, late, width):
    at = iota(ids_ref.shape, 0)
    ids = jnp.zeros(ids_ref.shape, F32)
    for i in range(ids_ref.shape[0]):
        line = (early, late)[i // 4]
        ids = jnp.where(at == i, line[:, i % 4 * width : (i % 4 + 1) * width], ids)
    ids_ref[...] = ids


def join_rows(pieces, joined_ref):
    rows = pieces[0].shape[0]
    for i, piece in enumerate(pieces):
        joined_ref[i * rows : (i + 1) * rows] = piece[...]


def four_body(width, pair_ref, got_ref, sent_ref, ids_ref):
    _, z, _ = place()
    four = together(z == 0, taken(pair_ref), received(got_ref), 2 * width)
    send(sent_ref, *four)
    list_ids(ids_ref, four[2], four[2], width)


def turn_body(
    width,
    own_ref,
    got_ref,
    pair_ref,
    pair_got_ref,
    four_got_ref,
    a,
    b,
    c,
    d,
    mine_ref,
    sent_ref,
    ids_ref,
    joined_ref,
):
    join_rows((a, b, c, d), joined_ref)
    x, z, zz = place()
    pair, pair_got, four_got = taken(pair_ref), received(pair_got_ref), received(four_got_ref)
    line = together(z == 0, pair, pair_got, 2 * width)[2]
    (early,), (late,) = ordered(zz == 0, [line], [four_got[2]])
    list_ids(ids_ref, early, late, width)

    before = jnp.where(zz == 0, 0.0, four_got[0])
    before = jnp.where(z == 0, before, jnp.exp(pair_got[1]) * before + pair_got[0])
    (first, first_log), _ = ordered(x == 0, taken(own_ref)[:2], received(got_ref)[:2])
    after = jnp.exp(first_log) * before + first
    mine_ref[...] = jnp.where(x == 0, before, after)
    other = jnp.where(x == 0, after, before)
    send(sent_ref, other, jnp.zeros_like(first_log), jnp.zeros_like(first_log))


def prefix_body(parts_ref, starts_ref):
    ctx, rows, share = starts_ref.shape
    state = jnp.zeros((rows, share), F32)
    for i in range(ctx):
        starts_ref[i] = state
        if i < ctx - 1:
            state = parts_ref[i, STATE : STATE + 1] * state + parts_ref[i, :STATE]


def back_body(paired, gain_ref, pre_ref, decay_ref, bc_ref, *rest):
    starts, (out_far, out_ref, sems) = rest[: 1 + paired], rest[1 + paired :]
    channels = pre_ref.shape[1]
    width = min(channels, 4 * HDIM)
    group = (iota((width, width), 0) // HDIM == iota((width, width), 1) // HDIM).astype(BF16)
    if paired:
        side = lax.axis_index("ctx") % 2
        mine, other = starts[0][...], received(starts[1])[0]
        start = [jnp.where(side == 0, mine, other), jnp.where(side == 0, other, mine)]
        start = jnp.concatenate(start, axis=1)
    else:
        start = starts[0][...]
    c_high, c_low = halves(bc_ref[:, STATE:])
    copies = []
    for i in range(channels // width):
        cut = slice(i * width, (i + 1) * width)
        s_high, s_low = halves(start[:, cut])
        carried = dot16(c_high, s_high) + dot16(c_high, s_low) + dot16(c_low, s_high)
        pre = pre_ref[:, cut] + carried * decay_ref[:, cut]
        mean = dot_left(pre * pre, group) * (1.0 / HDIM)
        out_ref[:, cut] = (pre * lax.rsqrt(mean + 1e-05) * gain_ref[:, cut]).astype(BF16)
        copies += started([out_ref.at[:, cut]], [out_far.at[:, cut]], sems, i)
    finished(copies)


def entering_by_pairs(keep, sent, width, pre, near_pieces, far_rows, meanwhile):
    pair_array, sent_array = array(keep.shape, F32), array(sent.shape, jnp.int16)
    ids_array = array((8, width), F32)
    joined_array = array((4 * far_rows.shape[0], far_rows.shape[1]), BF16)
    got = swapped(sent, "ctx", 1)
    pair, sent, rows, joined = call(
        functools.partial(pair_body, width),
        [pair_array, sent_array, array(far_rows.shape, BF16), joined_array],
        (keep, got, far_rows, *near_pieces),
        near=True,
        after=(pre,),
        name="pair",
    )
    far_pieces = spread_rows(rows, 1)
    pair_got = swapped(sent, "ctx", 2)
    sent, ids = call(
        functools.partial(four_body, width),
        [sent_array, ids_array],
        (pair, pair_got),
        near=True,
        after=far_pieces[1:3],
        name="four",
    )
    four_got = swapped(sent, "ctx", 4)
    done = meanwhile(ids, joined)
    mine, sent, ids, joined = call(
        functools.partial(turn_body, width),
        [array((STATE, keep.shape[1]), F32), sent_array, ids_array, joined_array],
        (keep, got, pair, pair_got, four_got, *far_pieces),
        near=True,
        after_far=(done,),
        name="turn",
    )
    return (mine, swapped(sent, "ctx", 1)), far_pieces, ids, joined, done


def entering_by_rows(state):
    ctx = lax.axis_size("ctx")
    rows, channels = state.shape
    slabs = state.reshape(rows, ctx, channels // ctx).transpose(1, 0, 2)
    parts = lax.all_to_all(slabs, "ctx", split_axis=0, concat_axis=0, tiled=True)
    (starts,) = call(
        prefix_body,
        [array((ctx, STATE, channels // ctx), F32)],
        (parts,),
        near=True,
        name="prefix",
    )
    start = lax.all_to_all(starts, "ctx", split_axis=0, concat_axis=0, tiled=True)
    return start.transpose(1, 0, 2).reshape(STATE, channels)


def mixing(
    rows, meanwhile, seq_input, b_input, c_input, before, conv_x, conv_bc, log_decay, skip, gain, ids
):
    tokens, channels = seq_input.shape
    heads = skip.shape[0]
    width = 2 * ids.shape[0]
    paired = rows is not None
    outs = [
        array((tokens, channels), F32),
        array((tokens, 2 * STATE), F32),
        array((2, heads, tokens), F32),
    ]
    if paired:
        ends = [array((STATE + NOTES, channels // 2), F32)]
        ends.append(array((STATE + 16, channels // 2), jnp.int16))
    else:
        ends = [array((STATE + NOTES, channels), F32)]
    args = (seq_input, b_input, c_input, conv_x, conv_bc, log_decay, ids.T, before)
    xconv, bc, lines, *ends = call(
        functools.partial(front_body, paired, len(args)),
        outs + ends,
        args,
        fixed=len(args) - 1,
        near_outs=len(outs + ends),
        after=rows[0][:1] if paired else (),
        scratch=room(args) + [pltpu.VMEM((8 + tokens, channels + 2 * STATE), F32)],
        sems=len(args),
        flops=5 * 10**9,
        grant=20,
        name="front",
    )
    args = (skip.reshape(1, heads), gain.reshape(1, channels), xconv, bc, lines)
    pre, decay, gain = call(
        inner_body,
        [array((tokens, channels), F32)] * 2 + [array((1, channels), F32)],
        args,
        fixed=2,
        near_args=3,
        near_outs=3,
        scratch=room(args[:1]),
        sems=2,
        flops=4 * 10**9,
        grant=16,
        name="inner",
    )
    late = None
    if paired:
        starts, *late = entering_by_pairs(*ends, width, pre, *rows, meanwhile)
    else:
        starts = (entering_by_rows(ends[0]),)

    def finish(after=()):
        outs = [array((tokens, channels), BF16)]
        args = (gain, pre, decay, bc, *starts)
        return call(
            functools.partial(back_body, paired),
            outs,
            args,
            near_args=len(args),
            after_far=after,
            scratch=room(outs),
            sems=max(1, channels // (4 * HDIM)),
            flops=10**9,
            grant=16,
            name="back",
        )[0]

    return finish, late


TILE = 512


def join_body(a_ref, b_ref, out_ref, sems):
    rows = a_ref.shape[0]
    finished(
        started([a_ref, b_ref], [out_ref.at[pl.ds(0, rows), :], out_ref.at[pl.ds(rows, rows), :]], sems)
    )


def swapped(block, axis, bit):
    return lax.ppermute(block, axis, [(i, i ^ bit) for i in range(lax.axis_size(axis))])


def expert_body(part, w_gate, w_up, *refs):
    pieces, joined_ref, ids_ref, out_far = refs[:4], refs[4], refs[5], refs[6 + part]
    pick_ref, hid_ref, out_ref, sems = refs[7 + part :]
    length, hidden = out_ref.shape
    rows = pieces[0].shape[0] // 2
    depth = pieces[0].shape[1]
    me = lax.axis_index("exp")
    here = lax.axis_index("ctx")
    downs = [pl.ds(pl.multiple_of((me ^ k) * depth, depth), depth) for k in range(4)]
    pair = (here // 4) ^ part

    shape = (rows, rows)
    earlier = (iota(shape, 1) < iota(shape, 0)).astype(F32)
    across = iota(shape, 1)
    diagonal = iota(shape, 0) == across
    turns = [(here % 4) ^ (2 * (i % 2) + i // 2) for i in range(length // rows)]
    for i, block in enumerate(turns):
        line = ids_ref[pl.ds(4 * pair + block, 1), :]
        mine = me.astype(F32)
        named = ((line[:, :rows] == mine) | (line[:, rows:] == mine)).astype(F32)
        column = jnp.sum(jnp.where(diagonal, named, 0.0), axis=1, keepdims=True)
        position = jnp.sum(earlier * named, axis=1, keepdims=True).astype(jnp.int32)
        pick_ref[i] = jnp.where(position == across, column, 0.0).astype(BF16)

    out_copies = []
    out_rows = pl.ds(pl.multiple_of(pair * length, length), length)
    for n in range(hidden // TILE):
        cut = slice(n * TILE, (n + 1) * TILE)
        gate = upper = None
        for k in range(4):
            if k % 2 == 0:
                block = jnp.concatenate([piece[...] for piece in pieces[k : k + 2]], axis=0)
            else:
                block = joined_ref[k // 2 * length : (k // 2 + 1) * length]
            more = dot16(block, w_gate[0, downs[k], cut])
            gate = more if k == 0 else gate + more
            more = dot16(block, w_up[0, downs[k], cut])
            upper = more if k == 0 else upper + more
        hid_ref[...] = (silu(gate) * upper).astype(BF16)
        for i, block in enumerate(turns):
            picked = dot16(pick_ref[i], hid_ref[i * rows : (i + 1) * rows], FIRST)
            out_ref[pl.ds(pl.multiple_of(block * rows, rows), rows), cut] = picked.astype(BF16)
        out_copies += started([out_ref.at[:, cut]], [out_far.at[0, out_rows, cut]], sems, n)
    finished(out_copies)


def along_z(moe_input):
    rows, columns = moe_input.shape
    joined = call(
        join_body,
        [array((2 * rows, columns), BF16)],
        (moe_input, swapped(moe_input, "ctx", 2)),
        fixed=1,
        sems=2,
        name="join",
    )[0]
    return joined, swapped(joined, "ctx", 4)


def spread_rows(z, through):
    x, y = swapped(z, "ctx", 1), swapped(z, "exp", 2)
    d = swapped(y, "ctx", 1) if through else swapped(x, "exp", 2)
    return (z, x, y, d)


def experts_by_tokens(part, pieces, joined, ids, w_gate, w_up, so_far):
    rows = pieces[0].shape[0] // 2
    length = 4 * rows
    hidden = w_gate.shape[2]
    args = (w_gate, w_up, *pieces, swapped(joined, "exp", 1), ids)
    return call(
        functools.partial(expert_body, part),
        [pltpu.HBM((1, 2 * length, hidden), BF16)],
        args + ((so_far,) if part else ()),
        held=2,
        near_args=0,
        aliases={len(args): 0} if part else None,
        scratch=[
            pltpu.VMEM((length // rows, rows, rows), BF16),
            pltpu.VMEM((length, TILE), BF16),
            pltpu.VMEM((length, hidden), BF16),
        ],
        sems=hidden // TILE,
        flops=4 * length * w_gate.shape[1] * hidden,
        grant=16,
        spaces_of=[pltpu.VMEM] * len(args) + [pltpu.HBM] * part,
        name="experts",
    )[0]


def slot_matrix(pairs, expert, capacity):
    named = jnp.any(pairs == expert, axis=1).astype(jnp.int32)
    position = jnp.cumsum(named) - named
    hit = position[None, :] == jnp.arange(capacity, dtype=jnp.int32)[:, None]
    return (hit & (named[None, :] > 0)).astype(BF16)


def experts_by_slots(moe_input, pairs, w_gate, w_up):
    experts = lax.axis_size("exp")
    capacity = 4 * moe_input.shape[0] // experts
    pick = jax.vmap(lambda e: slot_matrix(pairs, e, capacity))(jnp.arange(experts))
    slots = jnp.einsum("eqt,td->eqd", pick, moe_input, preferred_element_type=F32)
    routed = lax.all_to_all(slots.astype(BF16), "exp", split_axis=0, concat_axis=2, tiled=True)
    rows = lax.all_gather(routed[0], "ctx", axis=0, tiled=True)
    gate = jnp.dot(rows, w_gate[0], preferred_element_type=F32)
    upper = jnp.dot(rows, w_up[0], preferred_element_type=F32)
    return (jax.nn.silu(gate) * upper).astype(BF16)[None]


def on_device(
    seq_input,
    b_input,
    c_input,
    conv_x,
    conv_bc,
    log_decay,
    skip_gain,
    norm_gain,
    moe_input,
    expert_ids,
    w_gate,
    w_up,
):
    ctx = lax.axis_size("ctx")
    by_tokens = lax.axis_size("exp") == 4 and ctx == 8
    tokens, channels = seq_input.shape
    ends = call(
        ends_body,
        [array((EDGE, channels + 2 * STATE), BF16)],
        (seq_input, b_input, c_input),
        fixed=3,
        sems=3,
        name="ends",
    )[0]
    before = lax.ppermute(ends, "ctx", [(i, i + 1) for i in range(ctx - 1)])
    pieces = meanwhile = None
    if by_tokens:
        near_rows, far_rows = along_z(moe_input)
        pieces = spread_rows(near_rows, 0), far_rows

        def meanwhile(ids, joined):
            return experts_by_tokens(0, pieces[0], joined, ids, w_gate, w_up, None)

    finish, late = mixing(
        pieces,
        meanwhile,
        seq_input,
        b_input,
        c_input,
        before,
        conv_x,
        conv_bc,
        log_decay,
        skip_gain,
        norm_gain,
        expert_ids,
    )
    if by_tokens:
        far_pieces, ids, joined, hidden = late
        hidden = experts_by_tokens(1, far_pieces, joined, ids, w_gate, w_up, hidden)
        mixed = finish((hidden,))
    else:
        mixed = finish()
        hidden = experts_by_slots(moe_input, expert_ids, w_gate, w_up)
    return (mixed, hidden)


def solution(mesh):
    in_specs = (
        P("ctx", "exp"),
        P("ctx", None),
        P("ctx", None),
        P(None, "exp"),
        P(),
        P("exp", "ctx"),
        P("exp"),
        P("exp"),
        P("ctx", "exp"),
        P("ctx", None),
        P("exp", None, "ctx"),
        P("exp", None, "ctx"),
    )
    out_specs = (P("ctx", "exp"), P("exp", None, "ctx"))
    return jax.shard_map(
        on_device, mesh=mesh, in_specs=in_specs, out_specs=out_specs, check_vma=False
    )
```

```python
import functools
import math

import jax
import jax.numpy as jnp
from jax import lax
from jax.experimental import pallas as pl
from jax.experimental.pallas import tpu as pltpu
from jax.sharding import PartitionSpec as P

HDIM = 64
STATE = 128
KCONV = 4
EDGE = 16
NOTES = 8

F32 = jnp.float32
BF16 = jnp.bfloat16


def dot16(a, b, contract=((1,), (0,))):
    return lax.dot_general(a, b, (contract, ((), ())), preferred_element_type=F32)


def halves(value):
    high = value.astype(BF16)
    return high, (value - high.astype(F32)).astype(BF16)


def dot(a, b, contract=((1,), (0,))):
    a_high, a_low = halves(a)
    b_high, b_low = halves(b)
    cross = dot16(a_high, b_low, contract) + dot16(a_low, b_high, contract)
    return dot16(a_high, b_high, contract) + cross


def dot_exact(a, b, contract=((1,), (0,))):
    high, rest = halves(a)
    low = (a - high.astype(F32) - rest.astype(F32)).astype(BF16)
    return dot16(high, b, contract) + (dot16(rest, b, contract) + dot16(low, b, contract))


def dot_left(a, b, contract=((1,), (0,))):
    high, low = halves(a)
    return dot16(high, b, contract) + dot16(low, b, contract)


FIRST = ((0,), (0,))


def iota(shape, axis):
    return lax.broadcasted_iota(jnp.int32, shape, axis)


def head_spread(heads):
    shape = (heads, heads * HDIM)
    return (iota(shape, 1) // HDIM == iota(shape, 0)).astype(BF16)


def upper_ones(length):
    return (iota((length, length), 0) <= iota((length, length), 1)).astype(BF16)


def silu(value):
    return value / (1.0 + jnp.exp(-value))


def one_minus_exp(value):
    series = jnp.ones_like(value)
    for n in range(8, 1, -1):
        series = 1.0 + value * series * (1.0 / n)
    return jnp.where(value > -0.25, -value * series, 1.0 - jnp.exp(value))


def started(sources, targets, sems, first=0):
    copies = []
    for i, (source, target) in enumerate(zip(sources, targets)):
        copies.append(pltpu.make_async_copy(source, target, sems.at[first + i]))
        copies[-1].start()
    return copies


def finished(copies):
    for copy in copies:
        copy.wait()


def following(body, count, skipped):
    return lambda *refs: body(*refs[:count], *refs[count + skipped :])


def call(
    body,
    outs,
    args,
    fixed=0,
    held=0,
    near_args=0,
    near_outs=0,
    after=(),
    after_far=(),
    aliases=None,
    scratch=(),
    sems=0,
    flops=0,
    grant=8,
    near=False,
    spaces_of=None,
    name=None,
):
    body = following(body, len(args), len(after) + len(after_far))
    moved = sum(math.prod(a.shape) * a.dtype.itemsize for a in (*args, *outs))
    scratch = list(scratch) + ([pltpu.SemaphoreType.DMA((sems,))] if sems else [])
    space = pltpu.VMEM if near else pl.ANY
    spaces = [pltpu.HBM] * fixed + [pltpu.VMEM] * held
    args = [
        pltpu.with_memory_space_constraint(a, spaces[i]) if i < len(spaces) else a
        for i, a in enumerate(args)
    ]
    spaces += [space] * (len(args) - near_args - len(spaces)) + [pltpu.VMEM] * near_args
    spaces = spaces_of or spaces
    args, spaces = [*args, *after], spaces + [pl.ANY] * len(after)
    args += [pltpu.with_memory_space_constraint(a, pltpu.HBM) for a in after_far]
    spaces += [pltpu.HBM] * len(after_far)
    out_spaces = [space] * (len(outs) - near_outs) + [pltpu.VMEM] * near_outs
    return pl.pallas_call(
        body,
        out_shape=outs,
        in_specs=[pl.BlockSpec(memory_space=s) for s in spaces],
        out_specs=[pl.BlockSpec(memory_space=s) for s in out_spaces],
        scratch_shapes=scratch,
        input_output_aliases=aliases or {},
        compiler_params=pltpu.CompilerParams(vmem_limit_bytes=grant * 2**20),
        cost_estimate=pl.CostEstimate(flops=flops, bytes_accessed=moved, transcendentals=0),
        name=name,
    )(*args)


def room(arrays):
    return [pltpu.VMEM(a.shape, a.dtype) for a in arrays]


def array(shape, dtype):
    return jax.ShapeDtypeStruct(shape, dtype)


def ends_body(x_ref, b_ref, c_ref, ends_ref, sems):
    tokens, channels = x_ref.shape
    cut = pl.ds(tokens - EDGE, EDGE)
    finished(
        started(
            [x_ref.at[cut, :], b_ref.at[cut, :], c_ref.at[cut, :]],
            [
                ends_ref.at[:, pl.ds(0, channels)],
                ends_ref.at[:, pl.ds(channels, STATE)],
                ends_ref.at[:, pl.ds(channels + STATE, STATE)],
            ],
            sems,
        )
    )


def front_body(paired, count, *refs):
    far, (xconv_ref, bc_ref, lines_ref), rest = refs[:count], refs[count : count + 3], refs[count + 3 :]
    ends, rest = rest[: 1 + paired], rest[1 + paired :]
    near, pad_ref, sems = rest[:count], rest[-2], rest[-1]
    copies = started(far, near, sems)
    x_ref, b_ref, c_ref, taps_ref, taps_bc_ref, logs_ref, ids_ref, ends_ref = near
    tokens, channels = x_ref.shape
    heads = logs_ref.shape[0]
    finished(copies)
    pad_ref[0:8, :] = ends_ref[...].astype(F32)[EDGE - 8 : EDGE]
    pad_ref[8 : 8 + tokens, :channels] = x_ref[...].astype(F32)
    pad_ref[8 : 8 + tokens, channels : channels + STATE] = b_ref[...].astype(F32)
    pad_ref[8 : 8 + tokens, channels + STATE :] = c_ref[...].astype(F32)

    def conv(taps, start, stop):
        total = jnp.zeros((tokens, stop - start), F32)
        for k in range(KCONV):
            first = 8 - (KCONV - 1) + k
            total = total + taps[k : k + 1] * pad_ref[first : first + tokens, start:stop]
        return silu(total)

    bc = conv(taps_bc_ref[...], channels, channels + 2 * STATE)
    bc_ref[...] = bc
    xconv = conv(taps_ref[...], 0, channels)
    xconv_ref[...] = xconv
    logs = logs_ref[...]
    inflow = jnp.sqrt(one_minus_exp(2.0 * logs))
    row = dot_exact(logs, upper_ones(tokens))
    lines_ref[0] = row
    lines_ref[1] = inflow
    total = row[:, tokens - 1 :]
    spread = head_spread(heads)
    fresh = xconv * dot_left(inflow * jnp.exp(total - row), spread, FIRST)
    state = dot(bc[:, :STATE], fresh, FIRST)
    total = jnp.broadcast_to(total, (heads, NOTES))
    if paired:
        total = dot_exact(total, spread, FIRST)
        half = channels // 2
        side = lax.axis_index("ctx") % 2
        ids = ids_ref[...].astype(F32)
        line = jnp.concatenate([ids[0:1], ids[1:2]], axis=1)
        line = jnp.concatenate([line] * (half // line.shape[1]), axis=1)
        for ref, first in ((ends[0], side == 0), (ends[1], side != 0)):
            mine = jnp.where(first, state[:, :half], state[:, half:])
            logsum = jnp.where(first, total[:1, :half], total[:1, half:])
            if ref is ends[0]:
                put(ref, mine, logsum, line)
            else:
                send(ref, mine, logsum, line)
    else:
        ends[0][:STATE] = state
        ends[0][STATE:] = dot_exact(jnp.exp(total), spread, FIRST)


def inner_body(
    skip_far,
    gain_far,
    xconv_ref,
    bc_ref,
    lines_ref,
    pre_ref,
    decay_ref,
    gain_ref,
    skip_ref,
    sems,
):
    copies = started([skip_far, gain_far], [skip_ref, gain_ref], sems)
    tokens, channels = xconv_ref.shape
    heads = channels // HDIM
    row = lines_ref[0]
    column = row.T
    spread = head_spread(heads)
    decay_ref[...] = dot_left(jnp.exp(row), spread, FIRST)
    inflow = dot_left(lines_ref[1], spread, FIRST)
    meet = dot(bc_ref[:, STATE:], bc_ref[:, :STATE], ((1,), (1,)))
    lower = iota((tokens, tokens), 0) >= iota((tokens, tokens), 1)
    left = iota((tokens, 2 * HDIM), 1) < HDIM
    finished(copies)
    skip = dot_exact(skip_ref[...], spread)
    for pair in range(heads // 2):
        cut = slice(pair * 2 * HDIM, (pair + 1) * 2 * HDIM)
        xconv = xconv_ref[:, cut]
        d_high, d_low = halves(xconv * inflow[:, cut])
        both = []
        for h in (2 * pair, 2 * pair + 1):
            gap = column[:, h : h + 1] - row[h : h + 1, :]
            mix = jnp.where(lower, jnp.exp(gap), 0.0) * meet
            m_high, m_low = halves(mix)
            both.append(dot16(m_high, d_high) + dot16(m_high, d_low) + dot16(m_low, d_high))
        pre_ref[:, cut] = skip[:, cut] * xconv + jnp.where(left, both[0], both[1])


def put(ref, state, logsum, line):
    ref[:STATE] = state
    at = iota((NOTES, state.shape[1]), 0)
    ref[STATE:] = jnp.where(at == 0, logsum, line)


def send(ref, state, logsum, line):
    largest = jnp.max(jnp.abs(state), axis=0, keepdims=True)
    power = jnp.ceil(jnp.log2(jnp.maximum(largest, 1e-30))) - 15.0
    whole = jnp.clip(jnp.round(state * jnp.exp2(-power)), -32767.0, 32767.0)
    ref[:STATE] = whole.astype(jnp.int32).astype(jnp.int16)
    logsum = jnp.round(jnp.maximum(logsum, -128.0) * 2.0**22).astype(jnp.int32)
    at = iota((16, state.shape[1]), 0)
    notes = jnp.where(at == 0, power.astype(jnp.int32), line.astype(jnp.int32))
    notes = jnp.where(at == 1, logsum >> 15, jnp.where(at == 2, logsum & 32767, notes))
    ref[STATE:] = notes.astype(jnp.int16)


def taken(ref):
    return ref[:STATE], ref[STATE : STATE + 1], ref[STATE + 1 : STATE + 2]


def received(ref):
    notes = ref[STATE:].astype(jnp.int32).astype(F32)
    state = ref[:STATE].astype(jnp.int32).astype(F32) * jnp.exp2(notes[0:1])
    return state, notes[1:2] * 2.0**-7 + notes[2:3] * 2.0**-22, notes[3:4]


def ordered(first, own, other):
    return [jnp.where(first, a, b) for a, b in zip(own, other)], [
        jnp.where(first, b, a) for a, b in zip(own, other)
    ]


def together(first, own, other, width):
    (a, a_log, a_line), (b, b_log, b_line) = ordered(first, own, other)
    line = jnp.concatenate([a_line[:, :width], b_line[:, :width]], axis=1)
    line = jnp.concatenate([line] * (a.shape[1] // line.shape[1]), axis=1)
    return jnp.exp(b_log) * a + b, a_log + b_log, line


def place():
    here = lax.axis_index("ctx")
    return here % 2, (here // 2) % 2, here // 4


def pair_body(width, own_ref, got_ref, rows_ref, pair_ref, sent_ref, same_rows_ref):
    same_rows_ref[...] = rows_ref[...]
    x, _, _ = place()
    pair = together(x == 0, taken(own_ref), received(got_ref), width)
    put(pair_ref, *pair)
    send(sent_ref, *pair)


def list_ids(ids_ref, early, late, width):
    at = iota(ids_ref.shape, 0)
    ids = jnp.zeros(ids_ref.shape, F32)
    for i in range(ids_ref.shape[0]):
        line = (early, late)[i // 4]
        ids = jnp.where(at == i, line[:, i % 4 * width : (i % 4 + 1) * width], ids)
    ids_ref[...] = ids


def join_rows(pieces, joined_ref):
    rows = pieces[0].shape[0]
    for i, piece in enumerate(pieces):
        joined_ref[i * rows : (i + 1) * rows] = piece[...]


def four_body(
    width, pair_ref, got_ref, a, b, c, d, e, f, g, sent_ref, ids_ref, joined_ref, later_ref
):
    join_rows((a, b, c, d), joined_ref)
    join_rows((e, f, g), later_ref)
    _, z, _ = place()
    four = together(z == 0, taken(pair_ref), received(got_ref), 2 * width)
    send(sent_ref, *four)
    list_ids(ids_ref, four[2], four[2], width)


def turn_body(
    width,
    own_ref,
    got_ref,
    pair_ref,
    pair_got_ref,
    four_got_ref,
    rows_ref,
    mine_ref,
    sent_ref,
    ids_ref,
    same_rows_ref,
):
    same_rows_ref[...] = rows_ref[...]
    x, z, zz = place()
    pair, pair_got, four_got = taken(pair_ref), received(pair_got_ref), received(four_got_ref)
    line = together(z == 0, pair, pair_got, 2 * width)[2]
    (early,), (late,) = ordered(zz == 0, [line], [four_got[2]])
    list_ids(ids_ref, early, late, width)

    before = jnp.where(zz == 0, 0.0, four_got[0])
    before = jnp.where(z == 0, before, jnp.exp(pair_got[1]) * before + pair_got[0])
    (first, first_log), _ = ordered(x == 0, taken(own_ref)[:2], received(got_ref)[:2])
    after = jnp.exp(first_log) * before + first
    mine_ref[...] = jnp.where(x == 0, before, after)
    other = jnp.where(x == 0, after, before)
    send(sent_ref, other, jnp.zeros_like(first_log), jnp.zeros_like(first_log))


def prefix_body(parts_ref, starts_ref):
    ctx, rows, share = starts_ref.shape
    state = jnp.zeros((rows, share), F32)
    for i in range(ctx):
        starts_ref[i] = state
        if i < ctx - 1:
            state = parts_ref[i, STATE : STATE + 1] * state + parts_ref[i, :STATE]


def back_body(paired, gain_ref, pre_ref, decay_ref, bc_ref, *rest):
    starts, (out_far, out_ref, sems) = rest[: 1 + paired], rest[1 + paired :]
    channels = pre_ref.shape[1]
    width = min(channels, 4 * HDIM)
    group = (iota((width, width), 0) // HDIM == iota((width, width), 1) // HDIM).astype(BF16)
    if paired:
        side = lax.axis_index("ctx") % 2
        mine, other = starts[0][...], received(starts[1])[0]
        start = [jnp.where(side == 0, mine, other), jnp.where(side == 0, other, mine)]
        start = jnp.concatenate(start, axis=1)
    else:
        start = starts[0][...]
    c_high, c_low = halves(bc_ref[:, STATE:])
    copies = []
    for i in range(channels // width):
        cut = slice(i * width, (i + 1) * width)
        s_high, s_low = halves(start[:, cut])
        carried = dot16(c_high, s_high) + dot16(c_high, s_low) + dot16(c_low, s_high)
        pre = pre_ref[:, cut] + carried * decay_ref[:, cut]
        mean = dot_left(pre * pre, group) * (1.0 / HDIM)
        out_ref[:, cut] = (pre * lax.rsqrt(mean + 1e-05) * gain_ref[:, cut]).astype(BF16)
        copies += started([out_ref.at[:, cut]], [out_far.at[:, cut]], sems, i)
    finished(copies)


def entering_by_pairs(keep, sent, width, pre, near_pieces, far_rows, meanwhile):
    pair_array, sent_array = array(keep.shape, F32), array(sent.shape, jnp.int16)
    ids_array = array((8, width), F32)
    joined_array = array((4 * far_rows.shape[0], far_rows.shape[1]), BF16)
    got = swapped(sent, "ctx", 1)
    pair, sent, rows = call(
        functools.partial(pair_body, width),
        [pair_array, sent_array, array(far_rows.shape, BF16)],
        (keep, got, far_rows),
        near=True,
        after=(*near_pieces[2:], pre),
        name="pair",
    )
    far_pieces = spread_rows(rows, 1)
    pair_got = swapped(sent, "ctx", 2)
    later_array = array((3 * far_rows.shape[0], far_rows.shape[1]), BF16)
    sent, ids, joined, later = call(
        functools.partial(four_body, width),
        [sent_array, ids_array, joined_array, later_array],
        (pair, pair_got, *near_pieces, *far_pieces[:3]),
        near=True,
        name="four",
    )
    four_got = swapped(sent, "ctx", 4)
    done = meanwhile(ids, joined)
    mine, sent, ids, rows = call(
        functools.partial(turn_body, width),
        [array((STATE, keep.shape[1]), F32), sent_array, ids_array, array(rows.shape, BF16)],
        (keep, got, pair, pair_got, four_got, far_pieces[3]),
        near=True,
        after_far=(done,),
        name="turn",
    )
    return (mine, swapped(sent, "ctx", 1)), far_pieces, ids, (later, rows), done


def entering_by_rows(state):
    ctx = lax.axis_size("ctx")
    rows, channels = state.shape
    slabs = state.reshape(rows, ctx, channels // ctx).transpose(1, 0, 2)
    parts = lax.all_to_all(slabs, "ctx", split_axis=0, concat_axis=0, tiled=True)
    (starts,) = call(
        prefix_body,
        [array((ctx, STATE, channels // ctx), F32)],
        (parts,),
        near=True,
        name="prefix",
    )
    start = lax.all_to_all(starts, "ctx", split_axis=0, concat_axis=0, tiled=True)
    return start.transpose(1, 0, 2).reshape(STATE, channels)


def mixing(
    rows, meanwhile, seq_input, b_input, c_input, before, conv_x, conv_bc, log_decay, skip, gain, ids
):
    tokens, channels = seq_input.shape
    heads = skip.shape[0]
    width = 2 * ids.shape[0]
    paired = rows is not None
    outs = [
        array((tokens, channels), F32),
        array((tokens, 2 * STATE), F32),
        array((2, heads, tokens), F32),
    ]
    if paired:
        ends = [array((STATE + NOTES, channels // 2), F32)]
        ends.append(array((STATE + 16, channels // 2), jnp.int16))
    else:
        ends = [array((STATE + NOTES, channels), F32)]
    args = (seq_input, b_input, c_input, conv_x, conv_bc, log_decay, ids.T, before)
    xconv, bc, lines, *ends = call(
        functools.partial(front_body, paired, len(args)),
        outs + ends,
        args,
        fixed=len(args) - 1,
        near_outs=len(outs + ends),
        after=rows[0][:1] if paired else (),
        scratch=room(args) + [pltpu.VMEM((8 + tokens, channels + 2 * STATE), F32)],
        sems=len(args),
        flops=5 * 10**9,
        grant=20,
        name="front",
    )
    args = (skip.reshape(1, heads), gain.reshape(1, channels), xconv, bc, lines)
    pre, decay, gain = call(
        inner_body,
        [array((tokens, channels), F32)] * 2 + [array((1, channels), F32)],
        args,
        fixed=2,
        near_args=3,
        near_outs=3,
        scratch=room(args[:1]),
        sems=2,
        flops=4 * 10**9,
        grant=16,
        name="inner",
    )
    late = None
    if paired:
        starts, *late = entering_by_pairs(*ends, width, pre, *rows, meanwhile)
    else:
        starts = (entering_by_rows(ends[0]),)

    def finish(after=()):
        outs = [array((tokens, channels), BF16)]
        args = (gain, pre, decay, bc, *starts)
        return call(
            functools.partial(back_body, paired),
            outs,
            args,
            near_args=len(args),
            after_far=after,
            scratch=room(outs),
            sems=max(1, channels // (4 * HDIM)),
            flops=10**9,
            grant=16,
            name="back",
        )[0]

    return finish, late


TILE = 512


def join_body(a_ref, b_ref, out_ref, sems):
    rows = a_ref.shape[0]
    finished(
        started([a_ref, b_ref], [out_ref.at[pl.ds(0, rows), :], out_ref.at[pl.ds(rows, rows), :]], sems)
    )


def swapped(block, axis, bit):
    return lax.ppermute(block, axis, [(i, i ^ bit) for i in range(lax.axis_size(axis))])


def expert_body(part, w_gate, w_up, *refs):
    count = 1 + part
    pieces, beside, refs = refs[:4], refs[4 : 4 + count], refs[4 + count :]
    ids_ref, out_far = refs[0], refs[1 + part]
    pick_ref, hid_ref, out_ref, sems = refs[2 + part :]
    length, hidden = out_ref.shape
    rows = pieces[0].shape[0] // 2
    depth = pieces[0].shape[1]
    me = lax.axis_index("exp")
    here = lax.axis_index("ctx")
    downs = [pl.ds(pl.multiple_of((me ^ k) * depth, depth), depth) for k in range(4)]
    pair = (here // 4) ^ part

    shape = (rows, rows)
    earlier = (iota(shape, 1) < iota(shape, 0)).astype(F32)
    across = iota(shape, 1)
    diagonal = iota(shape, 0) == across
    turns = [(here % 4) ^ (2 * (i % 2) + i // 2) for i in range(length // rows)]
    for i, block in enumerate(turns):
        line = ids_ref[pl.ds(4 * pair + block, 1), :]
        mine = me.astype(F32)
        named = ((line[:, :rows] == mine) | (line[:, rows:] == mine)).astype(F32)
        column = jnp.sum(jnp.where(diagonal, named, 0.0), axis=1, keepdims=True)
        position = jnp.sum(earlier * named, axis=1, keepdims=True).astype(jnp.int32)
        pick_ref[i] = jnp.where(position == across, column, 0.0).astype(BF16)

    out_copies = []
    out_rows = pl.ds(pl.multiple_of(pair * length, length), length)
    for n in range(hidden // TILE):
        cut = slice(n * TILE, (n + 1) * TILE)
        gate = upper = None
        for k in range(4):
            if k % 2 == 0:
                block = jnp.concatenate([piece[...] for piece in pieces[k : k + 2]], axis=0)
            else:
                block = beside[0][k // 2 * length : min((k // 2 + 1) * length, beside[0].shape[0])]
                if block.shape[0] < length:
                    block = jnp.concatenate([block, beside[1][...]], axis=0)
            more = dot16(block, w_gate[0, downs[k], cut])
            gate = more if k == 0 else gate + more
            more = dot16(block, w_up[0, downs[k], cut])
            upper = more if k == 0 else upper + more
        hid_ref[...] = (silu(gate) * upper).astype(BF16)
        for i, block in enumerate(turns):
            picked = dot16(pick_ref[i], hid_ref[i * rows : (i + 1) * rows], FIRST)
            out_ref[pl.ds(pl.multiple_of(block * rows, rows), rows), cut] = picked.astype(BF16)
        out_copies += started([out_ref.at[:, cut]], [out_far.at[0, out_rows, cut]], sems, n)
    finished(out_copies)


def along_z(moe_input):
    rows, columns = moe_input.shape
    joined = call(
        join_body,
        [array((2 * rows, columns), BF16)],
        (moe_input, swapped(moe_input, "ctx", 2)),
        fixed=1,
        sems=2,
        name="join",
    )[0]
    return joined, swapped(joined, "ctx", 4)


def spread_rows(z, through):
    x, y = swapped(z, "ctx", 1), swapped(z, "exp", 2)
    d = swapped(y, "ctx", 1) if through else swapped(x, "exp", 2)
    return (z, x, y, d)


def experts_by_tokens(part, pieces, sent, ids, w_gate, w_up, so_far):
    rows = pieces[0].shape[0] // 2
    length = 4 * rows
    hidden = w_gate.shape[2]
    args = (w_gate, w_up, *pieces, *(swapped(a, "exp", 1) for a in sent), ids)
    return call(
        functools.partial(expert_body, part),
        [pltpu.HBM((1, 2 * length, hidden), BF16)],
        args + ((so_far,) if part else ()),
        held=2,
        near_args=0,
        aliases={len(args): 0} if part else None,
        scratch=[
            pltpu.VMEM((length // rows, rows, rows), BF16),
            pltpu.VMEM((length, TILE), BF16),
            pltpu.VMEM((length, hidden), BF16),
        ],
        sems=hidden // TILE,
        flops=4 * length * w_gate.shape[1] * hidden,
        grant=16,
        spaces_of=[pltpu.VMEM] * len(args) + [pltpu.HBM] * part,
        name="experts",
    )[0]


def slot_matrix(pairs, expert, capacity):
    named = jnp.any(pairs == expert, axis=1).astype(jnp.int32)
    position = jnp.cumsum(named) - named
    hit = position[None, :] == jnp.arange(capacity, dtype=jnp.int32)[:, None]
    return (hit & (named[None, :] > 0)).astype(BF16)


def experts_by_slots(moe_input, pairs, w_gate, w_up):
    experts = lax.axis_size("exp")
    capacity = 4 * moe_input.shape[0] // experts
    pick = jax.vmap(lambda e: slot_matrix(pairs, e, capacity))(jnp.arange(experts))
    slots = jnp.einsum("eqt,td->eqd", pick, moe_input, preferred_element_type=F32)
    routed = lax.all_to_all(slots.astype(BF16), "exp", split_axis=0, concat_axis=2, tiled=True)
    rows = lax.all_gather(routed[0], "ctx", axis=0, tiled=True)
    gate = jnp.dot(rows, w_gate[0], preferred_element_type=F32)
    upper = jnp.dot(rows, w_up[0], preferred_element_type=F32)
    return (jax.nn.silu(gate) * upper).astype(BF16)[None]


def on_device(
    seq_input,
    b_input,
    c_input,
    conv_x,
    conv_bc,
    log_decay,
    skip_gain,
    norm_gain,
    moe_input,
    expert_ids,
    w_gate,
    w_up,
):
    ctx = lax.axis_size("ctx")
    by_tokens = lax.axis_size("exp") == 4 and ctx == 8
    tokens, channels = seq_input.shape
    ends = call(
        ends_body,
        [array((EDGE, channels + 2 * STATE), BF16)],
        (seq_input, b_input, c_input),
        fixed=3,
        sems=3,
        name="ends",
    )[0]
    before = lax.ppermute(ends, "ctx", [(i, i + 1) for i in range(ctx - 1)])
    pieces = meanwhile = None
    if by_tokens:
        near_rows, far_rows = along_z(moe_input)
        pieces = spread_rows(near_rows, 0), far_rows

        def meanwhile(ids, joined):
            return experts_by_tokens(0, pieces[0], (joined,), ids, w_gate, w_up, None)

    finish, late = mixing(
        pieces,
        meanwhile,
        seq_input,
        b_input,
        c_input,
        before,
        conv_x,
        conv_bc,
        log_decay,
        skip_gain,
        norm_gain,
        expert_ids,
    )
    if by_tokens:
        far_pieces, ids, joined, hidden = late
        hidden = experts_by_tokens(1, far_pieces, joined, ids, w_gate, w_up, hidden)
        mixed = finish((hidden,))
    else:
        mixed = finish()
        hidden = experts_by_slots(moe_input, expert_ids, w_gate, w_up)
    return (mixed, hidden)


def solution(mesh):
    in_specs = (
        P("ctx", "exp"),
        P("ctx", None),
        P("ctx", None),
        P(None, "exp"),
        P(),
        P("exp", "ctx"),
        P("exp"),
        P("exp"),
        P("ctx", "exp"),
        P("ctx", None),
        P("exp", None, "ctx"),
        P("exp", None, "ctx"),
    )
    out_specs = (P("ctx", "exp"), P("exp", None, "ctx"))
    return jax.shard_map(
        on_device, mesh=mesh, in_specs=in_specs, out_specs=out_specs, check_vma=False
    )
```

```python
import functools
import math

import jax
import jax.numpy as jnp
from jax import lax
from jax.experimental import pallas as pl
from jax.experimental.pallas import tpu as pltpu
from jax.sharding import PartitionSpec as P

HDIM = 64
STATE = 128
KCONV = 4
EDGE = 16
NOTES = 8

F32 = jnp.float32
BF16 = jnp.bfloat16


def dot16(a, b, contract=((1,), (0,))):
    return lax.dot_general(a, b, (contract, ((), ())), preferred_element_type=F32)


def halves(value):
    high = value.astype(BF16)
    return high, (value - high.astype(F32)).astype(BF16)


def dot(a, b, contract=((1,), (0,))):
    a_high, a_low = halves(a)
    b_high, b_low = halves(b)
    cross = dot16(a_high, b_low, contract) + dot16(a_low, b_high, contract)
    return dot16(a_high, b_high, contract) + cross


def dot_exact(a, b, contract=((1,), (0,))):
    high, rest = halves(a)
    low = (a - high.astype(F32) - rest.astype(F32)).astype(BF16)
    return dot16(high, b, contract) + (dot16(rest, b, contract) + dot16(low, b, contract))


def dot_left(a, b, contract=((1,), (0,))):
    high, low = halves(a)
    return dot16(high, b, contract) + dot16(low, b, contract)


FIRST = ((0,), (0,))


def iota(shape, axis):
    return lax.broadcasted_iota(jnp.int32, shape, axis)


def head_spread(heads):
    shape = (heads, heads * HDIM)
    return (iota(shape, 1) // HDIM == iota(shape, 0)).astype(BF16)


def upper_ones(length):
    return (iota((length, length), 0) <= iota((length, length), 1)).astype(BF16)


def silu(value):
    return value / (1.0 + jnp.exp(-value))


def one_minus_exp(value):
    series = jnp.ones_like(value)
    for n in range(8, 1, -1):
        series = 1.0 + value * series * (1.0 / n)
    return jnp.where(value > -0.25, -value * series, 1.0 - jnp.exp(value))


def started(sources, targets, sems, first=0):
    copies = []
    for i, (source, target) in enumerate(zip(sources, targets)):
        copies.append(pltpu.make_async_copy(source, target, sems.at[first + i]))
        copies[-1].start()
    return copies


def finished(copies):
    for copy in copies:
        copy.wait()


def following(body, count, skipped):
    return lambda *refs: body(*refs[:count], *refs[count + skipped :])


def call(
    body,
    outs,
    args,
    fixed=0,
    held=0,
    near_args=0,
    near_outs=0,
    after=(),
    after_far=(),
    aliases=None,
    scratch=(),
    sems=0,
    flops=0,
    grant=8,
    near=False,
    spaces_of=None,
    name=None,
):
    body = following(body, len(args), len(after) + len(after_far))
    moved = sum(math.prod(a.shape) * a.dtype.itemsize for a in (*args, *outs))
    scratch = list(scratch) + ([pltpu.SemaphoreType.DMA((sems,))] if sems else [])
    space = pltpu.VMEM if near else pl.ANY
    spaces = [pltpu.HBM] * fixed + [pltpu.VMEM] * held
    args = [
        pltpu.with_memory_space_constraint(a, spaces[i]) if i < len(spaces) else a
        for i, a in enumerate(args)
    ]
    spaces += [space] * (len(args) - near_args - len(spaces)) + [pltpu.VMEM] * near_args
    spaces = spaces_of or spaces
    args, spaces = [*args, *after], spaces + [pl.ANY] * len(after)
    args += [pltpu.with_memory_space_constraint(a, pltpu.HBM) for a in after_far]
    spaces += [pltpu.HBM] * len(after_far)
    out_spaces = [space] * (len(outs) - near_outs) + [pltpu.VMEM] * near_outs
    return pl.pallas_call(
        body,
        out_shape=outs,
        in_specs=[pl.BlockSpec(memory_space=s) for s in spaces],
        out_specs=[pl.BlockSpec(memory_space=s) for s in out_spaces],
        scratch_shapes=scratch,
        input_output_aliases=aliases or {},
        compiler_params=pltpu.CompilerParams(vmem_limit_bytes=grant * 2**20),
        cost_estimate=pl.CostEstimate(flops=flops, bytes_accessed=moved, transcendentals=0),
        name=name,
    )(*args)


def room(arrays):
    return [pltpu.VMEM(a.shape, a.dtype) for a in arrays]


def array(shape, dtype):
    return jax.ShapeDtypeStruct(shape, dtype)


def ends_body(x_ref, b_ref, c_ref, rows_ref, ends_ref, held_ref, sems):
    tokens, channels = x_ref.shape
    cut = pl.ds(tokens - EDGE, EDGE)
    finished(
        started(
            [x_ref.at[cut, :], b_ref.at[cut, :], c_ref.at[cut, :], rows_ref],
            [
                ends_ref.at[:, pl.ds(0, channels)],
                ends_ref.at[:, pl.ds(channels, STATE)],
                ends_ref.at[:, pl.ds(channels + STATE, STATE)],
                held_ref,
            ],
            sems,
        )
    )


def front_body(paired, count, *refs):
    far, (xconv_ref, bc_ref, lines_ref), rest = refs[:count], refs[count : count + 3], refs[count + 3 :]
    ends, rest = rest[: 1 + paired], rest[1 + paired :]
    near, pad_ref, sems = rest[:count], rest[-2], rest[-1]
    copies = started(far, near, sems)
    x_ref, b_ref, c_ref, taps_ref, taps_bc_ref, logs_ref, ids_ref, ends_ref = near
    tokens, channels = x_ref.shape
    heads = logs_ref.shape[0]
    finished(copies)
    pad_ref[0:8, :] = ends_ref[...].astype(F32)[EDGE - 8 : EDGE]
    pad_ref[8 : 8 + tokens, :channels] = x_ref[...].astype(F32)
    pad_ref[8 : 8 + tokens, channels : channels + STATE] = b_ref[...].astype(F32)
    pad_ref[8 : 8 + tokens, channels + STATE :] = c_ref[...].astype(F32)

    def conv(taps, start, stop):
        total = jnp.zeros((tokens, stop - start), F32)
        for k in range(KCONV):
            first = 8 - (KCONV - 1) + k
            total = total + taps[k : k + 1] * pad_ref[first : first + tokens, start:stop]
        return silu(total)

    bc = conv(taps_bc_ref[...], channels, channels + 2 * STATE)
    bc_ref[...] = bc
    xconv = conv(taps_ref[...], 0, channels)
    xconv_ref[...] = xconv
    logs = logs_ref[...]
    inflow = jnp.sqrt(one_minus_exp(2.0 * logs))
    row = dot_exact(logs, upper_ones(tokens))
    lines_ref[0] = row
    lines_ref[1] = inflow
    total = row[:, tokens - 1 :]
    spread = head_spread(heads)
    fresh = xconv * dot_left(inflow * jnp.exp(total - row), spread, FIRST)
    state = dot(bc[:, :STATE], fresh, FIRST)
    total = jnp.broadcast_to(total, (heads, NOTES))
    if paired:
        total = dot_exact(total, spread, FIRST)
        half = channels // 2
        side = lax.axis_index("ctx") % 2
        ids = ids_ref[...].astype(F32)
        line = jnp.concatenate([ids[0:1], ids[1:2]], axis=1)
        line = jnp.concatenate([line] * (half // line.shape[1]), axis=1)
        for ref, first in ((ends[0], side == 0), (ends[1], side != 0)):
            mine = jnp.where(first, state[:, :half], state[:, half:])
            logsum = jnp.where(first, total[:1, :half], total[:1, half:])
            if ref is ends[0]:
                put(ref, mine, logsum, line)
            else:
                send(ref, mine, logsum, line)
    else:
        ends[0][:STATE] = state
        ends[0][STATE:] = dot_exact(jnp.exp(total), spread, FIRST)


def inner_body(
    skip_far,
    gain_far,
    xconv_ref,
    bc_ref,
    lines_ref,
    pre_ref,
    decay_ref,
    gain_ref,
    skip_ref,
    sems,
):
    copies = started([skip_far, gain_far], [skip_ref, gain_ref], sems)
    tokens, channels = xconv_ref.shape
    heads = channels // HDIM
    row = lines_ref[0]
    column = row.T
    spread = head_spread(heads)
    decay_ref[...] = dot_left(jnp.exp(row), spread, FIRST)
    inflow = dot_left(lines_ref[1], spread, FIRST)
    meet = dot(bc_ref[:, STATE:], bc_ref[:, :STATE], ((1,), (1,)))
    lower = iota((tokens, tokens), 0) >= iota((tokens, tokens), 1)
    left = iota((tokens, 2 * HDIM), 1) < HDIM
    finished(copies)
    skip = dot_exact(skip_ref[...], spread)
    for pair in range(heads // 2):
        cut = slice(pair * 2 * HDIM, (pair + 1) * 2 * HDIM)
        xconv = xconv_ref[:, cut]
        d_high, d_low = halves(xconv * inflow[:, cut])
        both = []
        for h in (2 * pair, 2 * pair + 1):
            gap = column[:, h : h + 1] - row[h : h + 1, :]
            mix = jnp.where(lower, jnp.exp(gap), 0.0) * meet
            m_high, m_low = halves(mix)
            both.append(dot16(m_high, d_high) + dot16(m_high, d_low) + dot16(m_low, d_high))
        pre_ref[:, cut] = skip[:, cut] * xconv + jnp.where(left, both[0], both[1])


def put(ref, state, logsum, line):
    ref[:STATE] = state
    at = iota((NOTES, state.shape[1]), 0)
    ref[STATE:] = jnp.where(at == 0, logsum, line)


def send(ref, state, logsum, line):
    largest = jnp.max(jnp.abs(state), axis=0, keepdims=True)
    power = jnp.ceil(jnp.log2(jnp.maximum(largest, 1e-30))) - 15.0
    whole = jnp.clip(jnp.round(state * jnp.exp2(-power)), -32767.0, 32767.0)
    ref[:STATE] = whole.astype(jnp.int32).astype(jnp.int16)
    logsum = jnp.round(jnp.maximum(logsum, -128.0) * 2.0**22).astype(jnp.int32)
    at = iota((16, state.shape[1]), 0)
    notes = jnp.where(at == 0, power.astype(jnp.int32), line.astype(jnp.int32))
    notes = jnp.where(at == 1, logsum >> 15, jnp.where(at == 2, logsum & 32767, notes))
    ref[STATE:] = notes.astype(jnp.int16)


def taken(ref):
    return ref[:STATE], ref[STATE : STATE + 1], ref[STATE + 1 : STATE + 2]


def received(ref):
    notes = ref[STATE:].astype(jnp.int32).astype(F32)
    state = ref[:STATE].astype(jnp.int32).astype(F32) * jnp.exp2(notes[0:1])
    return state, notes[1:2] * 2.0**-7 + notes[2:3] * 2.0**-22, notes[3:4]


def ordered(first, own, other):
    return [jnp.where(first, a, b) for a, b in zip(own, other)], [
        jnp.where(first, b, a) for a, b in zip(own, other)
    ]


def together(first, own, other, width):
    (a, a_log, a_line), (b, b_log, b_line) = ordered(first, own, other)
    line = jnp.concatenate([a_line[:, :width], b_line[:, :width]], axis=1)
    line = jnp.concatenate([line] * (a.shape[1] // line.shape[1]), axis=1)
    return jnp.exp(b_log) * a + b, a_log + b_log, line


def place():
    here = lax.axis_index("ctx")
    return here % 2, (here // 2) % 2, here // 4


def pair_body(width, own_ref, got_ref, rows_ref, pair_ref, sent_ref, same_rows_ref):
    same_rows_ref[...] = rows_ref[...]
    x, _, _ = place()
    pair = together(x == 0, taken(own_ref), received(got_ref), width)
    put(pair_ref, *pair)
    send(sent_ref, *pair)


def list_ids(ids_ref, early, late, width):
    at = iota(ids_ref.shape, 0)
    ids = jnp.zeros(ids_ref.shape, F32)
    for i in range(ids_ref.shape[0]):
        line = (early, late)[i // 4]
        ids = jnp.where(at == i, line[:, i % 4 * width : (i % 4 + 1) * width], ids)
    ids_ref[...] = ids


def join_rows(pieces, joined_ref):
    rows = pieces[0].shape[0]
    for i, piece in enumerate(pieces):
        joined_ref[i * rows : (i + 1) * rows] = piece[...]


def four_body(
    width, pair_ref, got_ref, a, b, c, d, e, f, g, sent_ref, ids_ref, joined_ref, later_ref
):
    join_rows((a, b, c, d), joined_ref)
    join_rows((e, f, g), later_ref)
    _, z, _ = place()
    four = together(z == 0, taken(pair_ref), received(got_ref), 2 * width)
    send(sent_ref, *four)
    list_ids(ids_ref, four[2], four[2], width)


def turn_body(
    width,
    own_ref,
    got_ref,
    pair_ref,
    pair_got_ref,
    four_got_ref,
    rows_ref,
    mine_ref,
    sent_ref,
    ids_ref,
    same_rows_ref,
):
    same_rows_ref[...] = rows_ref[...]
    x, z, zz = place()
    pair, pair_got, four_got = taken(pair_ref), received(pair_got_ref), received(four_got_ref)
    line = together(z == 0, pair, pair_got, 2 * width)[2]
    (early,), (late,) = ordered(zz == 0, [line], [four_got[2]])
    list_ids(ids_ref, early, late, width)

    before = jnp.where(zz == 0, 0.0, four_got[0])
    before = jnp.where(z == 0, before, jnp.exp(pair_got[1]) * before + pair_got[0])
    (first, first_log), _ = ordered(x == 0, taken(own_ref)[:2], received(got_ref)[:2])
    after = jnp.exp(first_log) * before + first
    mine_ref[...] = jnp.where(x == 0, before, after)
    other = jnp.where(x == 0, after, before)
    send(sent_ref, other, jnp.zeros_like(first_log), jnp.zeros_like(first_log))


def prefix_body(parts_ref, starts_ref):
    ctx, rows, share = starts_ref.shape
    state = jnp.zeros((rows, share), F32)
    for i in range(ctx):
        starts_ref[i] = state
        if i < ctx - 1:
            state = parts_ref[i, STATE : STATE + 1] * state + parts_ref[i, :STATE]


def back_body(paired, gain_ref, pre_ref, decay_ref, bc_ref, *rest):
    starts, (out_far, out_ref, sems) = rest[: 1 + paired], rest[1 + paired :]
    channels = pre_ref.shape[1]
    width = min(channels, 4 * HDIM)
    group = (iota((width, width), 0) // HDIM == iota((width, width), 1) // HDIM).astype(BF16)
    if paired:
        side = lax.axis_index("ctx") % 2
        mine, other = starts[0][...], received(starts[1])[0]
        start = [jnp.where(side == 0, mine, other), jnp.where(side == 0, other, mine)]
        start = jnp.concatenate(start, axis=1)
    else:
        start = starts[0][...]
    c_high, c_low = halves(bc_ref[:, STATE:])
    copies = []
    for i in range(channels // width):
        cut = slice(i * width, (i + 1) * width)
        s_high, s_low = halves(start[:, cut])
        carried = dot16(c_high, s_high) + dot16(c_high, s_low) + dot16(c_low, s_high)
        pre = pre_ref[:, cut] + carried * decay_ref[:, cut]
        mean = dot_left(pre * pre, group) * (1.0 / HDIM)
        out_ref[:, cut] = (pre * lax.rsqrt(mean + 1e-05) * gain_ref[:, cut]).astype(BF16)
        copies += started([out_ref.at[:, cut]], [out_far.at[:, cut]], sems, i)
    finished(copies)


def entering_by_pairs(keep, sent, width, pre, near_pieces, far_rows, meanwhile):
    pair_array, sent_array = array(keep.shape, F32), array(sent.shape, jnp.int16)
    ids_array = array((8, width), F32)
    joined_array = array((4 * far_rows.shape[0], far_rows.shape[1]), BF16)
    got = swapped(sent, "ctx", 1)
    pair, sent, rows = call(
        functools.partial(pair_body, width),
        [pair_array, sent_array, array(far_rows.shape, BF16)],
        (keep, got, far_rows),
        near=True,
        after=(*near_pieces[2:], pre),
        name="pair",
    )
    far_pieces = spread_rows(rows, 1)
    pair_got = swapped(sent, "ctx", 2)
    later_array = array((3 * far_rows.shape[0], far_rows.shape[1]), BF16)
    sent, ids, joined, later = call(
        functools.partial(four_body, width),
        [sent_array, ids_array, joined_array, later_array],
        (pair, pair_got, *near_pieces, *far_pieces[:3]),
        near=True,
        name="four",
    )
    four_got = swapped(sent, "ctx", 4)
    done = meanwhile(ids, joined)
    mine, sent, ids, rows = call(
        functools.partial(turn_body, width),
        [array((STATE, keep.shape[1]), F32), sent_array, ids_array, array(rows.shape, BF16)],
        (keep, got, pair, pair_got, four_got, far_pieces[3]),
        near=True,
        after_far=(done,),
        name="turn",
    )
    return (mine, swapped(sent, "ctx", 1)), far_pieces, ids, (later, rows), done


def entering_by_rows(state):
    ctx = lax.axis_size("ctx")
    rows, channels = state.shape
    slabs = state.reshape(rows, ctx, channels // ctx).transpose(1, 0, 2)
    parts = lax.all_to_all(slabs, "ctx", split_axis=0, concat_axis=0, tiled=True)
    (starts,) = call(
        prefix_body,
        [array((ctx, STATE, channels // ctx), F32)],
        (parts,),
        near=True,
        name="prefix",
    )
    start = lax.all_to_all(starts, "ctx", split_axis=0, concat_axis=0, tiled=True)
    return start.transpose(1, 0, 2).reshape(STATE, channels)


def mixing(
    rows, meanwhile, seq_input, b_input, c_input, before, conv_x, conv_bc, log_decay, skip, gain, ids
):
    tokens, channels = seq_input.shape
    heads = skip.shape[0]
    width = 2 * ids.shape[0]
    paired = rows is not None
    outs = [
        array((tokens, channels), F32),
        array((tokens, 2 * STATE), F32),
        array((2, heads, tokens), F32),
    ]
    if paired:
        ends = [array((STATE + NOTES, channels // 2), F32)]
        ends.append(array((STATE + 16, channels // 2), jnp.int16))
    else:
        ends = [array((STATE + NOTES, channels), F32)]
    args = (seq_input, b_input, c_input, conv_x, conv_bc, log_decay, ids.T, before)
    xconv, bc, lines, *ends = call(
        functools.partial(front_body, paired, len(args)),
        outs + ends,
        args,
        fixed=len(args) - 1,
        near_outs=len(outs + ends),
        after=rows[0][:1] if paired else (),
        scratch=room(args) + [pltpu.VMEM((8 + tokens, channels + 2 * STATE), F32)],
        sems=len(args),
        flops=5 * 10**9,
        grant=20,
        name="front",
    )
    args = (skip.reshape(1, heads), gain.reshape(1, channels), xconv, bc, lines)
    pre, decay, gain = call(
        inner_body,
        [array((tokens, channels), F32)] * 2 + [array((1, channels), F32)],
        args,
        fixed=2,
        near_args=3,
        near_outs=3,
        scratch=room(args[:1]),
        sems=2,
        flops=4 * 10**9,
        grant=16,
        name="inner",
    )
    late = None
    if paired:
        starts, *late = entering_by_pairs(*ends, width, pre, *rows, meanwhile)
    else:
        starts = (entering_by_rows(ends[0]),)

    def finish(after=()):
        outs = [array((tokens, channels), BF16)]
        args = (gain, pre, decay, bc, *starts)
        return call(
            functools.partial(back_body, paired),
            outs,
            args,
            near_args=len(args),
            after_far=after,
            scratch=room(outs),
            sems=max(1, channels // (4 * HDIM)),
            flops=10**9,
            grant=16,
            name="back",
        )[0]

    return finish, late


TILE = 512


def join_body(a, b, joined_ref):
    join_rows((a, b), joined_ref)


def swapped(block, axis, bit):
    return lax.ppermute(block, axis, [(i, i ^ bit) for i in range(lax.axis_size(axis))])


def expert_body(part, w_gate, w_up, *refs):
    count = 1 + part
    pieces, beside, refs = refs[:4], refs[4 : 4 + count], refs[4 + count :]
    ids_ref, out_far = refs[0], refs[1 + part]
    pick_ref, hid_ref, out_ref, sems = refs[2 + part :]
    length, hidden = out_ref.shape
    rows = pieces[0].shape[0] // 2
    depth = pieces[0].shape[1]
    me = lax.axis_index("exp")
    here = lax.axis_index("ctx")
    downs = [pl.ds(pl.multiple_of((me ^ k) * depth, depth), depth) for k in range(4)]
    pair = (here // 4) ^ part

    shape = (rows, rows)
    earlier = (iota(shape, 1) < iota(shape, 0)).astype(F32)
    across = iota(shape, 1)
    diagonal = iota(shape, 0) == across
    turns = [(here % 4) ^ (2 * (i % 2) + i // 2) for i in range(length // rows)]
    for i, block in enumerate(turns):
        line = ids_ref[pl.ds(4 * pair + block, 1), :]
        mine = me.astype(F32)
        named = ((line[:, :rows] == mine) | (line[:, rows:] == mine)).astype(F32)
        column = jnp.sum(jnp.where(diagonal, named, 0.0), axis=1, keepdims=True)
        position = jnp.sum(earlier * named, axis=1, keepdims=True).astype(jnp.int32)
        pick_ref[i] = jnp.where(position == across, column, 0.0).astype(BF16)

    out_copies = []
    out_rows = pl.ds(pl.multiple_of(pair * length, length), length)
    for n in range(hidden // TILE):
        cut = slice(n * TILE, (n + 1) * TILE)
        gate = upper = None
        for k in range(4):
            if k % 2 == 0:
                block = jnp.concatenate([piece[...] for piece in pieces[k : k + 2]], axis=0)
            else:
                block = beside[0][k // 2 * length : min((k // 2 + 1) * length, beside[0].shape[0])]
                if block.shape[0] < length:
                    block = jnp.concatenate([block, beside[1][...]], axis=0)
            more = dot16(block, w_gate[0, downs[k], cut])
            gate = more if k == 0 else gate + more
            more = dot16(block, w_up[0, downs[k], cut])
            upper = more if k == 0 else upper + more
        hid_ref[...] = (silu(gate) * upper).astype(BF16)
        for i, block in enumerate(turns):
            picked = dot16(pick_ref[i], hid_ref[i * rows : (i + 1) * rows], FIRST)
            out_ref[pl.ds(pl.multiple_of(block * rows, rows), rows), cut] = picked.astype(BF16)
        out_copies += started([out_ref.at[:, cut]], [out_far.at[0, out_rows, cut]], sems, n)
    finished(out_copies)


def along_z(moe_input, held):
    rows, columns = moe_input.shape
    (joined,) = call(
        join_body,
        [array((2 * rows, columns), BF16)],
        (held, swapped(moe_input, "ctx", 2)),
        near=True,
        name="join",
    )
    return joined, swapped(joined, "ctx", 4)


def spread_rows(z, through):
    x, y = swapped(z, "ctx", 1), swapped(z, "exp", 2)
    d = swapped(y, "ctx", 1) if through else swapped(x, "exp", 2)
    return (z, x, y, d)


def experts_by_tokens(part, pieces, sent, ids, w_gate, w_up, so_far):
    rows = pieces[0].shape[0] // 2
    length = 4 * rows
    hidden = w_gate.shape[2]
    args = (w_gate, w_up, *pieces, *(swapped(a, "exp", 1) for a in sent), ids)
    return call(
        functools.partial(expert_body, part),
        [pltpu.HBM((1, 2 * length, hidden), BF16)],
        args + ((so_far,) if part else ()),
        held=2,
        near_args=0,
        aliases={len(args): 0} if part else None,
        scratch=[
            pltpu.VMEM((length // rows, rows, rows), BF16),
            pltpu.VMEM((length, TILE), BF16),
            pltpu.VMEM((length, hidden), BF16),
        ],
        sems=hidden // TILE,
        flops=4 * length * w_gate.shape[1] * hidden,
        grant=16,
        spaces_of=[pltpu.VMEM] * len(args) + [pltpu.HBM] * part,
        name="experts",
    )[0]


def slot_matrix(pairs, expert, capacity):
    named = jnp.any(pairs == expert, axis=1).astype(jnp.int32)
    position = jnp.cumsum(named) - named
    hit = position[None, :] == jnp.arange(capacity, dtype=jnp.int32)[:, None]
    return (hit & (named[None, :] > 0)).astype(BF16)


def experts_by_slots(moe_input, pairs, w_gate, w_up):
    experts = lax.axis_size("exp")
    capacity = 4 * moe_input.shape[0] // experts
    pick = jax.vmap(lambda e: slot_matrix(pairs, e, capacity))(jnp.arange(experts))
    slots = jnp.einsum("eqt,td->eqd", pick, moe_input, preferred_element_type=F32)
    routed = lax.all_to_all(slots.astype(BF16), "exp", split_axis=0, concat_axis=2, tiled=True)
    rows = lax.all_gather(routed[0], "ctx", axis=0, tiled=True)
    gate = jnp.dot(rows, w_gate[0], preferred_element_type=F32)
    upper = jnp.dot(rows, w_up[0], preferred_element_type=F32)
    return (jax.nn.silu(gate) * upper).astype(BF16)[None]


def on_device(
    seq_input,
    b_input,
    c_input,
    conv_x,
    conv_bc,
    log_decay,
    skip_gain,
    norm_gain,
    moe_input,
    expert_ids,
    w_gate,
    w_up,
):
    ctx = lax.axis_size("ctx")
    by_tokens = lax.axis_size("exp") == 4 and ctx == 8
    tokens, channels = seq_input.shape
    ends, held = call(
        ends_body,
        [array((EDGE, channels + 2 * STATE), BF16), array(moe_input.shape, BF16)],
        (seq_input, b_input, c_input, moe_input),
        fixed=4,
        near_outs=1,
        sems=4,
        name="ends",
    )
    before = lax.ppermute(ends, "ctx", [(i, i + 1) for i in range(ctx - 1)])
    pieces = meanwhile = None
    if by_tokens:
        near_rows, far_rows = along_z(moe_input, held)
        pieces = spread_rows(near_rows, 0), far_rows

        def meanwhile(ids, joined):
            return experts_by_tokens(0, pieces[0], (joined,), ids, w_gate, w_up, None)

    finish, late = mixing(
        pieces,
        meanwhile,
        seq_input,
        b_input,
        c_input,
        before,
        conv_x,
        conv_bc,
        log_decay,
        skip_gain,
        norm_gain,
        expert_ids,
    )
    if by_tokens:
        far_pieces, ids, joined, hidden = late
        hidden = experts_by_tokens(1, far_pieces, joined, ids, w_gate, w_up, hidden)
        mixed = finish((hidden,))
    else:
        mixed = finish()
        hidden = experts_by_slots(moe_input, expert_ids, w_gate, w_up)
    return (mixed, hidden)


def solution(mesh):
    in_specs = (
        P("ctx", "exp"),
        P("ctx", None),
        P("ctx", None),
        P(None, "exp"),
        P(),
        P("exp", "ctx"),
        P("exp"),
        P("exp"),
        P("ctx", "exp"),
        P("ctx", None),
        P("exp", None, "ctx"),
        P("exp", None, "ctx"),
    )
    out_specs = (P("ctx", "exp"), P("exp", None, "ctx"))
    return jax.shard_map(
        on_device, mesh=mesh, in_specs=in_specs, out_specs=out_specs, check_vma=False
    )
```

```python
import functools
import math

import jax
import jax.numpy as jnp
from jax import lax
from jax.experimental import pallas as pl
from jax.experimental.pallas import tpu as pltpu
from jax.sharding import PartitionSpec as P

HDIM = 64
STATE = 128
KCONV = 4
EDGE = 16
NOTES = 8

F32 = jnp.float32
BF16 = jnp.bfloat16


def dot16(a, b, contract=((1,), (0,))):
    return lax.dot_general(a, b, (contract, ((), ())), preferred_element_type=F32)


def halves(value):
    high = value.astype(BF16)
    return high, (value - high.astype(F32)).astype(BF16)


def dot(a, b, contract=((1,), (0,))):
    a_high, a_low = halves(a)
    b_high, b_low = halves(b)
    cross = dot16(a_high, b_low, contract) + dot16(a_low, b_high, contract)
    return dot16(a_high, b_high, contract) + cross


def dot_exact(a, b, contract=((1,), (0,))):
    high, rest = halves(a)
    low = (a - high.astype(F32) - rest.astype(F32)).astype(BF16)
    return dot16(high, b, contract) + (dot16(rest, b, contract) + dot16(low, b, contract))


def dot_left(a, b, contract=((1,), (0,))):
    high, low = halves(a)
    return dot16(high, b, contract) + dot16(low, b, contract)


FIRST = ((0,), (0,))


def iota(shape, axis):
    return lax.broadcasted_iota(jnp.int32, shape, axis)


def head_spread(heads):
    shape = (heads, heads * HDIM)
    return (iota(shape, 1) // HDIM == iota(shape, 0)).astype(BF16)


def upper_ones(length):
    return (iota((length, length), 0) <= iota((length, length), 1)).astype(BF16)


def silu(value):
    return value / (1.0 + jnp.exp(-value))


def one_minus_exp(value):
    series = jnp.ones_like(value)
    for n in range(8, 1, -1):
        series = 1.0 + value * series * (1.0 / n)
    return jnp.where(value > -0.25, -value * series, 1.0 - jnp.exp(value))


def started(sources, targets, sems, first=0):
    copies = []
    for i, (source, target) in enumerate(zip(sources, targets)):
        copies.append(pltpu.make_async_copy(source, target, sems.at[first + i]))
        copies[-1].start()
    return copies


def finished(copies):
    for copy in copies:
        copy.wait()


def following(body, count, skipped):
    return lambda *refs: body(*refs[:count], *refs[count + skipped :])


def call(
    body,
    outs,
    args,
    fixed=0,
    held=0,
    near_args=0,
    near_outs=0,
    after=(),
    after_far=(),
    aliases=None,
    scratch=(),
    sems=0,
    flops=0,
    grant=8,
    near=False,
    spaces_of=None,
    name=None,
):
    body = following(body, len(args), len(after) + len(after_far))
    moved = sum(math.prod(a.shape) * a.dtype.itemsize for a in (*args, *outs))
    scratch = list(scratch) + ([pltpu.SemaphoreType.DMA((sems,))] if sems else [])
    space = pltpu.VMEM if near else pl.ANY
    spaces = [pltpu.HBM] * fixed + [pltpu.VMEM] * held
    args = [
        pltpu.with_memory_space_constraint(a, spaces[i]) if i < len(spaces) else a
        for i, a in enumerate(args)
    ]
    spaces += [space] * (len(args) - near_args - len(spaces)) + [pltpu.VMEM] * near_args
    spaces = spaces_of or spaces
    args, spaces = [*args, *after], spaces + [pl.ANY] * len(after)
    args += [pltpu.with_memory_space_constraint(a, pltpu.HBM) for a in after_far]
    spaces += [pltpu.HBM] * len(after_far)
    out_spaces = [space] * (len(outs) - near_outs) + [pltpu.VMEM] * near_outs
    return pl.pallas_call(
        body,
        out_shape=outs,
        in_specs=[pl.BlockSpec(memory_space=s) for s in spaces],
        out_specs=[pl.BlockSpec(memory_space=s) for s in out_spaces],
        scratch_shapes=scratch,
        input_output_aliases=aliases or {},
        compiler_params=pltpu.CompilerParams(vmem_limit_bytes=grant * 2**20),
        cost_estimate=pl.CostEstimate(flops=flops, bytes_accessed=moved, transcendentals=0),
        name=name,
    )(*args)


def room(arrays):
    return [pltpu.VMEM(a.shape, a.dtype) for a in arrays]


def array(shape, dtype):
    return jax.ShapeDtypeStruct(shape, dtype)


def ends_body(x_ref, b_ref, c_ref, rows_ref, ends_ref, held_ref, sems):
    tokens, channels = x_ref.shape
    cut = pl.ds(tokens - EDGE, EDGE)
    finished(
        started(
            [x_ref.at[cut, :], b_ref.at[cut, :], c_ref.at[cut, :], rows_ref],
            [
                ends_ref.at[:, pl.ds(0, channels)],
                ends_ref.at[:, pl.ds(channels, STATE)],
                ends_ref.at[:, pl.ds(channels + STATE, STATE)],
                held_ref,
            ],
            sems,
        )
    )


def front_body(paired, count, *refs):
    far, (xconv_ref, bc_ref, lines_ref), rest = refs[:count], refs[count : count + 3], refs[count + 3 :]
    ends, rest = rest[: 1 + paired], rest[1 + paired :]
    near, pad_ref, sems = rest[:count], rest[-2], rest[-1]
    copies = started(far, near, sems)
    x_ref, b_ref, c_ref, taps_ref, taps_bc_ref, logs_ref, ids_ref, ends_ref = near
    tokens, channels = x_ref.shape
    heads = logs_ref.shape[0]
    finished(copies)
    pad_ref[0:8, :] = ends_ref[...].astype(F32)[EDGE - 8 : EDGE]
    pad_ref[8 : 8 + tokens, :channels] = x_ref[...].astype(F32)
    pad_ref[8 : 8 + tokens, channels : channels + STATE] = b_ref[...].astype(F32)
    pad_ref[8 : 8 + tokens, channels + STATE :] = c_ref[...].astype(F32)

    def conv(taps, start, stop):
        total = jnp.zeros((tokens, stop - start), F32)
        for k in range(KCONV):
            first = 8 - (KCONV - 1) + k
            total = total + taps[k : k + 1] * pad_ref[first : first + tokens, start:stop]
        return silu(total)

    bc = conv(taps_bc_ref[...], channels, channels + 2 * STATE)
    bc_ref[...] = bc
    xconv = conv(taps_ref[...], 0, channels)
    xconv_ref[...] = xconv
    logs = logs_ref[...]
    inflow = jnp.sqrt(one_minus_exp(2.0 * logs))
    row = dot_exact(logs, upper_ones(tokens))
    lines_ref[0] = row
    lines_ref[1] = inflow
    total = row[:, tokens - 1 :]
    spread = head_spread(heads)
    fresh = xconv * dot_left(inflow * jnp.exp(total - row), spread, FIRST)
    state = dot(bc[:, :STATE], fresh, FIRST)
    total = jnp.broadcast_to(total, (heads, NOTES))
    if paired:
        total = dot_exact(total, spread, FIRST)
        half = channels // 2
        side = lax.axis_index("ctx") % 2
        ids = ids_ref[...].astype(F32)
        line = jnp.concatenate([ids[0:1], ids[1:2]], axis=1)
        line = jnp.concatenate([line] * (half // line.shape[1]), axis=1)
        for ref, first in ((ends[0], side == 0), (ends[1], side != 0)):
            mine = jnp.where(first, state[:, :half], state[:, half:])
            logsum = jnp.where(first, total[:1, :half], total[:1, half:])
            if ref is ends[0]:
                put(ref, mine, logsum, line)
            else:
                send(ref, mine, logsum, line)
    else:
        ends[0][:STATE] = state
        ends[0][STATE:] = dot_exact(jnp.exp(total), spread, FIRST)


def inner_body(
    skip_far,
    gain_far,
    xconv_ref,
    bc_ref,
    lines_ref,
    pre_ref,
    decay_ref,
    gain_ref,
    skip_ref,
    sems,
):
    copies = started([skip_far, gain_far], [skip_ref, gain_ref], sems)
    tokens, channels = xconv_ref.shape
    heads = channels // HDIM
    row = lines_ref[0]
    column = row.T
    spread = head_spread(heads)
    decay_ref[...] = dot_left(jnp.exp(row), spread, FIRST)
    inflow = dot_left(lines_ref[1], spread, FIRST)
    meet = dot(bc_ref[:, STATE:], bc_ref[:, :STATE], ((1,), (1,)))
    lower = iota((tokens, tokens), 0) >= iota((tokens, tokens), 1)
    left = iota((tokens, 2 * HDIM), 1) < HDIM
    finished(copies)
    skip = dot_exact(skip_ref[...], spread)
    for pair in range(heads // 2):
        cut = slice(pair * 2 * HDIM, (pair + 1) * 2 * HDIM)
        xconv = xconv_ref[:, cut]
        d_high, d_low = halves(xconv * inflow[:, cut])
        both = []
        for h in (2 * pair, 2 * pair + 1):
            gap = column[:, h : h + 1] - row[h : h + 1, :]
            mix = jnp.where(lower, jnp.exp(gap), 0.0) * meet
            m_high, m_low = halves(mix)
            both.append(dot16(m_high, d_high) + dot16(m_high, d_low) + dot16(m_low, d_high))
        pre_ref[:, cut] = skip[:, cut] * xconv + jnp.where(left, both[0], both[1])


def put(ref, state, logsum, line):
    ref[:STATE] = state
    at = iota((NOTES, state.shape[1]), 0)
    ref[STATE:] = jnp.where(at == 0, logsum, line)


def send(ref, state, logsum, line):
    largest = jnp.max(jnp.abs(state), axis=0, keepdims=True)
    power = jnp.ceil(jnp.log2(jnp.maximum(largest, 1e-30))) - 15.0
    whole = jnp.clip(jnp.round(state * jnp.exp2(-power)), -32767.0, 32767.0)
    ref[:STATE] = whole.astype(jnp.int32).astype(jnp.int16)
    logsum = jnp.round(jnp.maximum(logsum, -128.0) * 2.0**22).astype(jnp.int32)
    at = iota((16, state.shape[1]), 0)
    notes = jnp.where(at == 0, power.astype(jnp.int32), line.astype(jnp.int32))
    notes = jnp.where(at == 1, logsum >> 15, jnp.where(at == 2, logsum & 32767, notes))
    ref[STATE:] = notes.astype(jnp.int16)


def taken(ref):
    return ref[:STATE], ref[STATE : STATE + 1], ref[STATE + 1 : STATE + 2]


def received(ref):
    notes = ref[STATE:].astype(jnp.int32).astype(F32)
    state = ref[:STATE].astype(jnp.int32).astype(F32) * jnp.exp2(notes[0:1])
    return state, notes[1:2] * 2.0**-7 + notes[2:3] * 2.0**-22, notes[3:4]


def ordered(first, own, other):
    return [jnp.where(first, a, b) for a, b in zip(own, other)], [
        jnp.where(first, b, a) for a, b in zip(own, other)
    ]


def together(first, own, other, width):
    (a, a_log, a_line), (b, b_log, b_line) = ordered(first, own, other)
    line = jnp.concatenate([a_line[:, :width], b_line[:, :width]], axis=1)
    line = jnp.concatenate([line] * (a.shape[1] // line.shape[1]), axis=1)
    return jnp.exp(b_log) * a + b, a_log + b_log, line


def place():
    here = lax.axis_index("ctx")
    return here % 2, (here // 2) % 2, here // 4


def pair_body(width, own_ref, got_ref, rows_ref, pair_ref, sent_ref, same_rows_ref):
    same_rows_ref[...] = rows_ref[...]
    x, _, _ = place()
    pair = together(x == 0, taken(own_ref), received(got_ref), width)
    put(pair_ref, *pair)
    send(sent_ref, *pair)


def list_ids(ids_ref, early, late, width):
    at = iota(ids_ref.shape, 0)
    ids = jnp.zeros(ids_ref.shape, F32)
    for i in range(ids_ref.shape[0]):
        line = (early, late)[i // 4]
        ids = jnp.where(at == i, line[:, i % 4 * width : (i % 4 + 1) * width], ids)
    ids_ref[...] = ids


def join_rows(pieces, joined_ref):
    rows = pieces[0].shape[0]
    for i, piece in enumerate(pieces):
        joined_ref[i * rows : (i + 1) * rows] = piece[...]


def four_body(
    width, pair_ref, got_ref, a, b, c, d, e, f, g, sent_ref, ids_ref, joined_ref, later_ref
):
    join_rows((a, b, c, d), joined_ref)
    join_rows((e, f, g), later_ref)
    _, z, _ = place()
    four = together(z == 0, taken(pair_ref), received(got_ref), 2 * width)
    send(sent_ref, *four)
    list_ids(ids_ref, four[2], four[2], width)


def turn_body(
    width,
    own_ref,
    got_ref,
    pair_ref,
    pair_got_ref,
    four_got_ref,
    rows_ref,
    mine_ref,
    sent_ref,
    ids_ref,
    same_rows_ref,
):
    same_rows_ref[...] = rows_ref[...]
    x, z, zz = place()
    pair, pair_got, four_got = taken(pair_ref), received(pair_got_ref), received(four_got_ref)
    line = together(z == 0, pair, pair_got, 2 * width)[2]
    (early,), (late,) = ordered(zz == 0, [line], [four_got[2]])
    list_ids(ids_ref, early, late, width)

    before = jnp.where(zz == 0, 0.0, four_got[0])
    before = jnp.where(z == 0, before, jnp.exp(pair_got[1]) * before + pair_got[0])
    (first, first_log), _ = ordered(x == 0, taken(own_ref)[:2], received(got_ref)[:2])
    after = jnp.exp(first_log) * before + first
    mine_ref[...] = jnp.where(x == 0, before, after)
    other = jnp.where(x == 0, after, before)
    send(sent_ref, other, jnp.zeros_like(first_log), jnp.zeros_like(first_log))


def prefix_body(parts_ref, starts_ref):
    ctx, rows, share = starts_ref.shape
    state = jnp.zeros((rows, share), F32)
    for i in range(ctx):
        starts_ref[i] = state
        if i < ctx - 1:
            state = parts_ref[i, STATE : STATE + 1] * state + parts_ref[i, :STATE]


def back_body(paired, gain_ref, pre_ref, decay_ref, bc_ref, *rest):
    starts, (out_far, out_ref, sems) = rest[: 1 + paired], rest[1 + paired :]
    channels = pre_ref.shape[1]
    width = min(channels, 4 * HDIM)
    group = (iota((width, width), 0) // HDIM == iota((width, width), 1) // HDIM).astype(BF16)
    if paired:
        side = lax.axis_index("ctx") % 2
        mine, other = starts[0][...], received(starts[1])[0]
        start = [jnp.where(side == 0, mine, other), jnp.where(side == 0, other, mine)]
        start = jnp.concatenate(start, axis=1)
    else:
        start = starts[0][...]
    c_high, c_low = halves(bc_ref[:, STATE:])
    copies = []
    for i in range(channels // width):
        cut = slice(i * width, (i + 1) * width)
        s_high, s_low = halves(start[:, cut])
        carried = dot16(c_high, s_high) + dot16(c_high, s_low) + dot16(c_low, s_high)
        pre = pre_ref[:, cut] + carried * decay_ref[:, cut]
        mean = dot_left(pre * pre, group) * (1.0 / HDIM)
        out_ref[:, cut] = (pre * lax.rsqrt(mean + 1e-05) * gain_ref[:, cut]).astype(BF16)
        copies += started([out_ref.at[:, cut]], [out_far.at[:, cut]], sems, i)
    finished(copies)


def entering_by_pairs(keep, sent, width, pre, near_pieces, far_rows, meanwhile):
    pair_array, sent_array = array(keep.shape, F32), array(sent.shape, jnp.int16)
    ids_array = array((8, width), F32)
    joined_array = array((4 * far_rows.shape[0], far_rows.shape[1]), BF16)
    got = swapped(sent, "ctx", 1)
    pair, sent, rows = call(
        functools.partial(pair_body, width),
        [pair_array, sent_array, array(far_rows.shape, BF16)],
        (keep, got, far_rows),
        near=True,
        after=(*near_pieces[2:], pre),
        name="pair",
    )
    far_pieces = spread_rows(rows, 1)
    pair_got = swapped(sent, "ctx", 2)
    later_array = array((3 * far_rows.shape[0], far_rows.shape[1]), BF16)
    sent, ids, joined, later = call(
        functools.partial(four_body, width),
        [sent_array, ids_array, joined_array, later_array],
        (pair, pair_got, *near_pieces, *far_pieces[:3]),
        near=True,
        name="four",
    )
    four_got = swapped(sent, "ctx", 4)
    done = meanwhile(ids, joined)
    mine, sent, ids, rows = call(
        functools.partial(turn_body, width),
        [array((STATE, keep.shape[1]), F32), sent_array, ids_array, array(rows.shape, BF16)],
        (keep, got, pair, pair_got, four_got, far_pieces[3]),
        near=True,
        after_far=(done,),
        name="turn",
    )
    return (mine, swapped(sent, "ctx", 1)), far_pieces, ids, (later, rows), done


def entering_by_rows(state):
    ctx = lax.axis_size("ctx")
    rows, channels = state.shape
    slabs = state.reshape(rows, ctx, channels // ctx).transpose(1, 0, 2)
    parts = lax.all_to_all(slabs, "ctx", split_axis=0, concat_axis=0, tiled=True)
    (starts,) = call(
        prefix_body,
        [array((ctx, STATE, channels // ctx), F32)],
        (parts,),
        near=True,
        name="prefix",
    )
    start = lax.all_to_all(starts, "ctx", split_axis=0, concat_axis=0, tiled=True)
    return start.transpose(1, 0, 2).reshape(STATE, channels)


def mixing(
    rows, meanwhile, seq_input, b_input, c_input, before, conv_x, conv_bc, log_decay, skip, gain, ids
):
    tokens, channels = seq_input.shape
    heads = skip.shape[0]
    width = 2 * ids.shape[0]
    paired = rows is not None
    outs = [
        array((tokens, channels), F32),
        array((tokens, 2 * STATE), F32),
        array((2, heads, tokens), F32),
    ]
    if paired:
        ends = [array((STATE + NOTES, channels // 2), F32)]
        ends.append(array((STATE + 16, channels // 2), jnp.int16))
    else:
        ends = [array((STATE + NOTES, channels), F32)]
    args = (seq_input, b_input, c_input, conv_x, conv_bc, log_decay, ids.T, before)
    xconv, bc, lines, *ends = call(
        functools.partial(front_body, paired, len(args)),
        outs + ends,
        args,
        fixed=len(args) - 1,
        near_outs=len(outs + ends),
        after=rows[0][:1] if paired else (),
        scratch=room(args) + [pltpu.VMEM((8 + tokens, channels + 2 * STATE), F32)],
        sems=len(args),
        flops=5 * 10**9,
        grant=20,
        name="front",
    )
    args = (skip.reshape(1, heads), gain.reshape(1, channels), xconv, bc, lines)
    pre, decay, gain = call(
        inner_body,
        [array((tokens, channels), F32)] * 2 + [array((1, channels), F32)],
        args,
        fixed=2,
        near_args=3,
        near_outs=3,
        scratch=room(args[:1]),
        sems=2,
        flops=4 * 10**9,
        grant=16,
        name="inner",
    )
    late = None
    if paired:
        starts, *late = entering_by_pairs(*ends, width, pre, *rows, meanwhile)
    else:
        starts = (entering_by_rows(ends[0]),)

    def finish(after=()):
        outs = [array((tokens, channels), BF16)]
        args = (gain, pre, decay, bc, *starts)
        return call(
            functools.partial(back_body, paired),
            outs,
            args,
            near_args=len(args),
            after_far=after,
            scratch=room(outs),
            sems=max(1, channels // (4 * HDIM)),
            flops=10**9,
            grant=16,
            name="back",
        )[0]

    return finish, late


TILE = 1024


def join_body(a, b, joined_ref):
    join_rows((a, b), joined_ref)


def swapped(block, axis, bit):
    return lax.ppermute(block, axis, [(i, i ^ bit) for i in range(lax.axis_size(axis))])


def expert_body(part, w_gate, w_up, *refs):
    count = 1 + part
    pieces, beside, refs = refs[:4], refs[4 : 4 + count], refs[4 + count :]
    ids_ref, out_far = refs[0], refs[1 + part]
    pick_ref, hid_ref, out_ref, sems = refs[2 + part :]
    length, hidden = out_ref.shape
    rows = pieces[0].shape[0] // 2
    depth = pieces[0].shape[1]
    me = lax.axis_index("exp")
    here = lax.axis_index("ctx")
    downs = [pl.ds(pl.multiple_of((me ^ k) * depth, depth), depth) for k in range(4)]
    pair = (here // 4) ^ part

    shape = (rows, rows)
    earlier = (iota(shape, 1) < iota(shape, 0)).astype(F32)
    across = iota(shape, 1)
    diagonal = iota(shape, 0) == across
    turns = [(here % 4) ^ (2 * (i % 2) + i // 2) for i in range(length // rows)]
    for i, block in enumerate(turns):
        line = ids_ref[pl.ds(4 * pair + block, 1), :]
        mine = me.astype(F32)
        named = ((line[:, :rows] == mine) | (line[:, rows:] == mine)).astype(F32)
        column = jnp.sum(jnp.where(diagonal, named, 0.0), axis=1, keepdims=True)
        position = jnp.sum(earlier * named, axis=1, keepdims=True).astype(jnp.int32)
        pick_ref[i] = jnp.where(position == across, column, 0.0).astype(BF16)

    out_copies = []
    out_rows = pl.ds(pl.multiple_of(pair * length, length), length)
    for n in range(hidden // TILE):
        cut = slice(n * TILE, (n + 1) * TILE)
        gate = upper = None
        for k in range(4):
            if k % 2 == 0:
                block = jnp.concatenate([piece[...] for piece in pieces[k : k + 2]], axis=0)
            else:
                block = beside[0][k // 2 * length : min((k // 2 + 1) * length, beside[0].shape[0])]
                if block.shape[0] < length:
                    block = jnp.concatenate([block, beside[1][...]], axis=0)
            more = dot16(block, w_gate[0, downs[k], cut])
            gate = more if k == 0 else gate + more
            more = dot16(block, w_up[0, downs[k], cut])
            upper = more if k == 0 else upper + more
        hid_ref[...] = (silu(gate) * upper).astype(BF16)
        for i, block in enumerate(turns):
            picked = dot16(pick_ref[i], hid_ref[i * rows : (i + 1) * rows], FIRST)
            out_ref[pl.ds(pl.multiple_of(block * rows, rows), rows), cut] = picked.astype(BF16)
        out_copies += started([out_ref.at[:, cut]], [out_far.at[0, out_rows, cut]], sems, n)
    finished(out_copies)


def along_z(moe_input, held):
    rows, columns = moe_input.shape
    (joined,) = call(
        join_body,
        [array((2 * rows, columns), BF16)],
        (held, swapped(moe_input, "ctx", 2)),
        near=True,
        name="join",
    )
    return joined, swapped(joined, "ctx", 4)


def spread_rows(z, through):
    x, y = swapped(z, "ctx", 1), swapped(z, "exp", 2)
    d = swapped(y, "ctx", 1) if through else swapped(x, "exp", 2)
    return (z, x, y, d)


def experts_by_tokens(part, pieces, sent, ids, w_gate, w_up, so_far):
    rows = pieces[0].shape[0] // 2
    length = 4 * rows
    hidden = w_gate.shape[2]
    args = (w_gate, w_up, *pieces, *(swapped(a, "exp", 1) for a in sent), ids)
    return call(
        functools.partial(expert_body, part),
        [pltpu.HBM((1, 2 * length, hidden), BF16)],
        args + ((so_far,) if part else ()),
        held=2,
        near_args=0,
        aliases={len(args): 0} if part else None,
        scratch=[
            pltpu.VMEM((length // rows, rows, rows), BF16),
            pltpu.VMEM((length, TILE), BF16),
            pltpu.VMEM((length, hidden), BF16),
        ],
        sems=hidden // TILE,
        flops=4 * length * w_gate.shape[1] * hidden,
        grant=16,
        spaces_of=[pltpu.VMEM] * len(args) + [pltpu.HBM] * part,
        name="experts",
    )[0]


def slot_matrix(pairs, expert, capacity):
    named = jnp.any(pairs == expert, axis=1).astype(jnp.int32)
    position = jnp.cumsum(named) - named
    hit = position[None, :] == jnp.arange(capacity, dtype=jnp.int32)[:, None]
    return (hit & (named[None, :] > 0)).astype(BF16)


def experts_by_slots(moe_input, pairs, w_gate, w_up):
    experts = lax.axis_size("exp")
    capacity = 4 * moe_input.shape[0] // experts
    pick = jax.vmap(lambda e: slot_matrix(pairs, e, capacity))(jnp.arange(experts))
    slots = jnp.einsum("eqt,td->eqd", pick, moe_input, preferred_element_type=F32)
    routed = lax.all_to_all(slots.astype(BF16), "exp", split_axis=0, concat_axis=2, tiled=True)
    rows = lax.all_gather(routed[0], "ctx", axis=0, tiled=True)
    gate = jnp.dot(rows, w_gate[0], preferred_element_type=F32)
    upper = jnp.dot(rows, w_up[0], preferred_element_type=F32)
    return (jax.nn.silu(gate) * upper).astype(BF16)[None]


def on_device(
    seq_input,
    b_input,
    c_input,
    conv_x,
    conv_bc,
    log_decay,
    skip_gain,
    norm_gain,
    moe_input,
    expert_ids,
    w_gate,
    w_up,
):
    ctx = lax.axis_size("ctx")
    by_tokens = lax.axis_size("exp") == 4 and ctx == 8
    tokens, channels = seq_input.shape
    ends, held = call(
        ends_body,
        [array((EDGE, channels + 2 * STATE), BF16), array(moe_input.shape, BF16)],
        (seq_input, b_input, c_input, moe_input),
        fixed=4,
        near_outs=1,
        sems=4,
        name="ends",
    )
    before = lax.ppermute(ends, "ctx", [(i, i + 1) for i in range(ctx - 1)])
    pieces = meanwhile = None
    if by_tokens:
        near_rows, far_rows = along_z(moe_input, held)
        pieces = spread_rows(near_rows, 0), far_rows

        def meanwhile(ids, joined):
            return experts_by_tokens(0, pieces[0], (joined,), ids, w_gate, w_up, None)

    finish, late = mixing(
        pieces,
        meanwhile,
        seq_input,
        b_input,
        c_input,
        before,
        conv_x,
        conv_bc,
        log_decay,
        skip_gain,
        norm_gain,
        expert_ids,
    )
    if by_tokens:
        far_pieces, ids, joined, hidden = late
        hidden = experts_by_tokens(1, far_pieces, joined, ids, w_gate, w_up, hidden)
        mixed = finish((hidden,))
    else:
        mixed = finish()
        hidden = experts_by_slots(moe_input, expert_ids, w_gate, w_up)
    return (mixed, hidden)


def solution(mesh):
    in_specs = (
        P("ctx", "exp"),
        P("ctx", None),
        P("ctx", None),
        P(None, "exp"),
        P(),
        P("exp", "ctx"),
        P("exp"),
        P("exp"),
        P("ctx", "exp"),
        P("ctx", None),
        P("exp", None, "ctx"),
        P("exp", None, "ctx"),
    )
    out_specs = (P("ctx", "exp"), P("exp", None, "ctx"))
    return jax.shard_map(
        on_device, mesh=mesh, in_specs=in_specs, out_specs=out_specs, check_vma=False
    )
```

```python
import functools
import math

import jax
import jax.numpy as jnp
from jax import lax
from jax.experimental import pallas as pl
from jax.experimental.pallas import tpu as pltpu
from jax.sharding import PartitionSpec as P

HDIM = 64
STATE = 128
KCONV = 4
EDGE = 16
NOTES = 8

F32 = jnp.float32
BF16 = jnp.bfloat16


def dot16(a, b, contract=((1,), (0,))):
    return lax.dot_general(a, b, (contract, ((), ())), preferred_element_type=F32)


def halves(value):
    high = value.astype(BF16)
    return high, (value - high.astype(F32)).astype(BF16)


def dot(a, b, contract=((1,), (0,))):
    a_high, a_low = halves(a)
    b_high, b_low = halves(b)
    cross = dot16(a_high, b_low, contract) + dot16(a_low, b_high, contract)
    return dot16(a_high, b_high, contract) + cross


def dot_exact(a, b, contract=((1,), (0,))):
    high, rest = halves(a)
    low = (a - high.astype(F32) - rest.astype(F32)).astype(BF16)
    return dot16(high, b, contract) + (dot16(rest, b, contract) + dot16(low, b, contract))


def dot_left(a, b, contract=((1,), (0,))):
    high, low = halves(a)
    return dot16(high, b, contract) + dot16(low, b, contract)


FIRST = ((0,), (0,))


def iota(shape, axis):
    return lax.broadcasted_iota(jnp.int32, shape, axis)


def head_spread(heads):
    shape = (heads, heads * HDIM)
    return (iota(shape, 1) // HDIM == iota(shape, 0)).astype(BF16)


def upper_ones(length):
    return (iota((length, length), 0) <= iota((length, length), 1)).astype(BF16)


def silu(value):
    return value / (1.0 + jnp.exp(-value))


def one_minus_exp(value):
    series = jnp.ones_like(value)
    for n in range(8, 1, -1):
        series = 1.0 + value * series * (1.0 / n)
    return jnp.where(value > -0.25, -value * series, 1.0 - jnp.exp(value))


def started(sources, targets, sems, first=0):
    copies = []
    for i, (source, target) in enumerate(zip(sources, targets)):
        copies.append(pltpu.make_async_copy(source, target, sems.at[first + i]))
        copies[-1].start()
    return copies


def finished(copies):
    for copy in copies:
        copy.wait()


def following(body, count, skipped):
    return lambda *refs: body(*refs[:count], *refs[count + skipped :])


def call(
    body,
    outs,
    args,
    fixed=0,
    held=0,
    near_args=0,
    near_outs=0,
    after=(),
    after_far=(),
    aliases=None,
    scratch=(),
    sems=0,
    flops=0,
    grant=8,
    near=False,
    spaces_of=None,
    name=None,
):
    body = following(body, len(args), len(after) + len(after_far))
    moved = sum(math.prod(a.shape) * a.dtype.itemsize for a in (*args, *outs))
    scratch = list(scratch) + ([pltpu.SemaphoreType.DMA((sems,))] if sems else [])
    space = pltpu.VMEM if near else pl.ANY
    spaces = [pltpu.HBM] * fixed + [pltpu.VMEM] * held
    args = [
        pltpu.with_memory_space_constraint(a, spaces[i]) if i < len(spaces) else a
        for i, a in enumerate(args)
    ]
    spaces += [space] * (len(args) - near_args - len(spaces)) + [pltpu.VMEM] * near_args
    spaces = spaces_of or spaces
    args, spaces = [*args, *after], spaces + [pl.ANY] * len(after)
    args += [pltpu.with_memory_space_constraint(a, pltpu.HBM) for a in after_far]
    spaces += [pltpu.HBM] * len(after_far)
    out_spaces = [space] * (len(outs) - near_outs) + [pltpu.VMEM] * near_outs
    return pl.pallas_call(
        body,
        out_shape=outs,
        in_specs=[pl.BlockSpec(memory_space=s) for s in spaces],
        out_specs=[pl.BlockSpec(memory_space=s) for s in out_spaces],
        scratch_shapes=scratch,
        input_output_aliases=aliases or {},
        compiler_params=pltpu.CompilerParams(vmem_limit_bytes=grant * 2**20),
        cost_estimate=pl.CostEstimate(flops=flops, bytes_accessed=moved, transcendentals=0),
        name=name,
    )(*args)


def room(arrays):
    return [pltpu.VMEM(a.shape, a.dtype) for a in arrays]


def array(shape, dtype):
    return jax.ShapeDtypeStruct(shape, dtype)


def ends_body(count, *refs):
    far, ends_ref, near, sems = refs[:count], refs[count], refs[count + 1 : -1], refs[-1]
    tokens, channels = far[0].shape
    cut = pl.ds(tokens - EDGE, EDGE)
    finished(
        started(
            [*(a.at[cut, :] for a in far[:3]), *far],
            [
                ends_ref.at[:, pl.ds(0, channels)],
                ends_ref.at[:, pl.ds(channels, STATE)],
                ends_ref.at[:, pl.ds(channels + STATE, STATE)],
                *near,
            ],
            sems,
        )
    )


def front_body(paired, *refs):
    x_ref, b_ref, c_ref, taps_ref, taps_bc_ref, logs_ref, ids_ref, ends_ref = refs[:8]
    xconv_ref, bc_ref, lines_ref = refs[8:11]
    ends, pad_ref = refs[11:-1], refs[-1]
    tokens, channels = x_ref.shape
    heads = logs_ref.shape[0]
    pad_ref[0:8, :] = ends_ref[...].astype(F32)[EDGE - 8 : EDGE]
    pad_ref[8 : 8 + tokens, :channels] = x_ref[...].astype(F32)
    pad_ref[8 : 8 + tokens, channels : channels + STATE] = b_ref[...].astype(F32)
    pad_ref[8 : 8 + tokens, channels + STATE :] = c_ref[...].astype(F32)

    def conv(taps, start, stop):
        total = jnp.zeros((tokens, stop - start), F32)
        for k in range(KCONV):
            first = 8 - (KCONV - 1) + k
            total = total + taps[k : k + 1] * pad_ref[first : first + tokens, start:stop]
        return silu(total)

    bc = conv(taps_bc_ref[...], channels, channels + 2 * STATE)
    bc_ref[...] = bc
    xconv = conv(taps_ref[...], 0, channels)
    xconv_ref[...] = xconv
    logs = logs_ref[...]
    inflow = jnp.sqrt(one_minus_exp(2.0 * logs))
    row = dot_exact(logs, upper_ones(tokens))
    lines_ref[0] = row
    lines_ref[1] = inflow
    total = row[:, tokens - 1 :]
    spread = head_spread(heads)
    fresh = xconv * dot_left(inflow * jnp.exp(total - row), spread, FIRST)
    state = dot(bc[:, :STATE], fresh, FIRST)
    total = jnp.broadcast_to(total, (heads, NOTES))
    if paired:
        total = dot_exact(total, spread, FIRST)
        half = channels // 2
        side = lax.axis_index("ctx") % 2
        ids = ids_ref[...].astype(F32)
        line = jnp.concatenate([ids[0:1], ids[1:2]], axis=1)
        line = jnp.concatenate([line] * (half // line.shape[1]), axis=1)
        for ref, first in ((ends[0], side == 0), (ends[1], side != 0)):
            mine = jnp.where(first, state[:, :half], state[:, half:])
            logsum = jnp.where(first, total[:1, :half], total[:1, half:])
            if ref is ends[0]:
                put(ref, mine, logsum, line)
            else:
                send(ref, mine, logsum, line)
    else:
        ends[0][:STATE] = state
        ends[0][STATE:] = dot_exact(jnp.exp(total), spread, FIRST)


def inner_body(
    skip_far,
    gain_far,
    xconv_ref,
    bc_ref,
    lines_ref,
    pre_ref,
    decay_ref,
    gain_ref,
    skip_ref,
    sems,
):
    copies = started([skip_far, gain_far], [skip_ref, gain_ref], sems)
    tokens, channels = xconv_ref.shape
    heads = channels // HDIM
    row = lines_ref[0]
    column = row.T
    spread = head_spread(heads)
    decay_ref[...] = dot_left(jnp.exp(row), spread, FIRST)
    inflow = dot_left(lines_ref[1], spread, FIRST)
    meet = dot(bc_ref[:, STATE:], bc_ref[:, :STATE], ((1,), (1,)))
    lower = iota((tokens, tokens), 0) >= iota((tokens, tokens), 1)
    left = iota((tokens, 2 * HDIM), 1) < HDIM
    finished(copies)
    skip = dot_exact(skip_ref[...], spread)
    for pair in range(heads // 2):
        cut = slice(pair * 2 * HDIM, (pair + 1) * 2 * HDIM)
        xconv = xconv_ref[:, cut]
        d_high, d_low = halves(xconv * inflow[:, cut])
        both = []
        for h in (2 * pair, 2 * pair + 1):
            gap = column[:, h : h + 1] - row[h : h + 1, :]
            mix = jnp.where(lower, jnp.exp(gap), 0.0) * meet
            m_high, m_low = halves(mix)
            both.append(dot16(m_high, d_high) + dot16(m_high, d_low) + dot16(m_low, d_high))
        pre_ref[:, cut] = skip[:, cut] * xconv + jnp.where(left, both[0], both[1])


def put(ref, state, logsum, line):
    ref[:STATE] = state
    at = iota((NOTES, state.shape[1]), 0)
    ref[STATE:] = jnp.where(at == 0, logsum, line)


def send(ref, state, logsum, line):
    largest = jnp.max(jnp.abs(state), axis=0, keepdims=True)
    power = jnp.ceil(jnp.log2(jnp.maximum(largest, 1e-30))) - 15.0
    whole = jnp.clip(jnp.round(state * jnp.exp2(-power)), -32767.0, 32767.0)
    ref[:STATE] = whole.astype(jnp.int32).astype(jnp.int16)
    logsum = jnp.round(jnp.maximum(logsum, -128.0) * 2.0**22).astype(jnp.int32)
    at = iota((16, state.shape[1]), 0)
    notes = jnp.where(at == 0, power.astype(jnp.int32), line.astype(jnp.int32))
    notes = jnp.where(at == 1, logsum >> 15, jnp.where(at == 2, logsum & 32767, notes))
    ref[STATE:] = notes.astype(jnp.int16)


def taken(ref):
    return ref[:STATE], ref[STATE : STATE + 1], ref[STATE + 1 : STATE + 2]


def received(ref):
    notes = ref[STATE:].astype(jnp.int32).astype(F32)
    state = ref[:STATE].astype(jnp.int32).astype(F32) * jnp.exp2(notes[0:1])
    return state, notes[1:2] * 2.0**-7 + notes[2:3] * 2.0**-22, notes[3:4]


def ordered(first, own, other):
    return [jnp.where(first, a, b) for a, b in zip(own, other)], [
        jnp.where(first, b, a) for a, b in zip(own, other)
    ]


def together(first, own, other, width):
    (a, a_log, a_line), (b, b_log, b_line) = ordered(first, own, other)
    line = jnp.concatenate([a_line[:, :width], b_line[:, :width]], axis=1)
    line = jnp.concatenate([line] * (a.shape[1] // line.shape[1]), axis=1)
    return jnp.exp(b_log) * a + b, a_log + b_log, line


def place():
    here = lax.axis_index("ctx")
    return here % 2, (here // 2) % 2, here // 4


def pair_body(width, own_ref, got_ref, rows_ref, pair_ref, sent_ref, same_rows_ref):
    same_rows_ref[...] = rows_ref[...]
    x, _, _ = place()
    pair = together(x == 0, taken(own_ref), received(got_ref), width)
    put(pair_ref, *pair)
    send(sent_ref, *pair)


def list_ids(ids_ref, early, late, width):
    at = iota(ids_ref.shape, 0)
    ids = jnp.zeros(ids_ref.shape, F32)
    for i in range(ids_ref.shape[0]):
        line = (early, late)[i // 4]
        ids = jnp.where(at == i, line[:, i % 4 * width : (i % 4 + 1) * width], ids)
    ids_ref[...] = ids


def join_rows(pieces, joined_ref):
    rows = pieces[0].shape[0]
    for i, piece in enumerate(pieces):
        joined_ref[i * rows : (i + 1) * rows] = piece[...]


def four_body(
    width, pair_ref, got_ref, a, b, c, d, e, f, g, sent_ref, ids_ref, joined_ref, later_ref
):
    join_rows((a, b, c, d), joined_ref)
    join_rows((e, f, g), later_ref)
    _, z, _ = place()
    four = together(z == 0, taken(pair_ref), received(got_ref), 2 * width)
    send(sent_ref, *four)
    list_ids(ids_ref, four[2], four[2], width)


def turn_body(
    width,
    own_ref,
    got_ref,
    pair_ref,
    pair_got_ref,
    four_got_ref,
    rows_ref,
    mine_ref,
    sent_ref,
    ids_ref,
    same_rows_ref,
):
    same_rows_ref[...] = rows_ref[...]
    x, z, zz = place()
    pair, pair_got, four_got = taken(pair_ref), received(pair_got_ref), received(four_got_ref)
    line = together(z == 0, pair, pair_got, 2 * width)[2]
    (early,), (late,) = ordered(zz == 0, [line], [four_got[2]])
    list_ids(ids_ref, early, late, width)

    before = jnp.where(zz == 0, 0.0, four_got[0])
    before = jnp.where(z == 0, before, jnp.exp(pair_got[1]) * before + pair_got[0])
    (first, first_log), _ = ordered(x == 0, taken(own_ref)[:2], received(got_ref)[:2])
    after = jnp.exp(first_log) * before + first
    mine_ref[...] = jnp.where(x == 0, before, after)
    other = jnp.where(x == 0, after, before)
    send(sent_ref, other, jnp.zeros_like(first_log), jnp.zeros_like(first_log))


def prefix_body(parts_ref, starts_ref):
    ctx, rows, share = starts_ref.shape
    state = jnp.zeros((rows, share), F32)
    for i in range(ctx):
        starts_ref[i] = state
        if i < ctx - 1:
            state = parts_ref[i, STATE : STATE + 1] * state + parts_ref[i, :STATE]


def back_body(paired, gain_ref, pre_ref, decay_ref, bc_ref, *rest):
    starts, (out_far, out_ref, sems) = rest[: 1 + paired], rest[1 + paired :]
    channels = pre_ref.shape[1]
    width = min(channels, 4 * HDIM)
    group = (iota((width, width), 0) // HDIM == iota((width, width), 1) // HDIM).astype(BF16)
    if paired:
        side = lax.axis_index("ctx") % 2
        mine, other = starts[0][...], received(starts[1])[0]
        start = [jnp.where(side == 0, mine, other), jnp.where(side == 0, other, mine)]
        start = jnp.concatenate(start, axis=1)
    else:
        start = starts[0][...]
    c_high, c_low = halves(bc_ref[:, STATE:])
    copies = []
    for i in range(channels // width):
        cut = slice(i * width, (i + 1) * width)
        s_high, s_low = halves(start[:, cut])
        carried = dot16(c_high, s_high) + dot16(c_high, s_low) + dot16(c_low, s_high)
        pre = pre_ref[:, cut] + carried * decay_ref[:, cut]
        mean = dot_left(pre * pre, group) * (1.0 / HDIM)
        out_ref[:, cut] = (pre * lax.rsqrt(mean + 1e-05) * gain_ref[:, cut]).astype(BF16)
        copies += started([out_ref.at[:, cut]], [out_far.at[:, cut]], sems, i)
    finished(copies)


def entering_by_pairs(keep, sent, width, pre, near_pieces, far_rows, meanwhile):
    pair_array, sent_array = array(keep.shape, F32), array(sent.shape, jnp.int16)
    ids_array = array((8, width), F32)
    joined_array = array((4 * far_rows.shape[0], far_rows.shape[1]), BF16)
    got = swapped(sent, "ctx", 1)
    pair, sent, rows = call(
        functools.partial(pair_body, width),
        [pair_array, sent_array, array(far_rows.shape, BF16)],
        (keep, got, far_rows),
        near=True,
        after=(*near_pieces[2:], pre),
        name="pair",
    )
    far_pieces = spread_rows(rows, 1)
    pair_got = swapped(sent, "ctx", 2)
    later_array = array((3 * far_rows.shape[0], far_rows.shape[1]), BF16)
    sent, ids, joined, later = call(
        functools.partial(four_body, width),
        [sent_array, ids_array, joined_array, later_array],
        (pair, pair_got, *near_pieces, *far_pieces[:3]),
        near=True,
        name="four",
    )
    four_got = swapped(sent, "ctx", 4)
    done = meanwhile(ids, joined)
    mine, sent, ids, rows = call(
        functools.partial(turn_body, width),
        [array((STATE, keep.shape[1]), F32), sent_array, ids_array, array(rows.shape, BF16)],
        (keep, got, pair, pair_got, four_got, far_pieces[3]),
        near=True,
        after_far=(done,),
        name="turn",
    )
    return (mine, swapped(sent, "ctx", 1)), far_pieces, ids, (later, rows), done


def entering_by_rows(state):
    ctx = lax.axis_size("ctx")
    rows, channels = state.shape
    slabs = state.reshape(rows, ctx, channels // ctx).transpose(1, 0, 2)
    parts = lax.all_to_all(slabs, "ctx", split_axis=0, concat_axis=0, tiled=True)
    (starts,) = call(
        prefix_body,
        [array((ctx, STATE, channels // ctx), F32)],
        (parts,),
        near=True,
        name="prefix",
    )
    start = lax.all_to_all(starts, "ctx", split_axis=0, concat_axis=0, tiled=True)
    return start.transpose(1, 0, 2).reshape(STATE, channels)


def mixing(
    rows, meanwhile, seq_input, b_input, c_input, before, conv_x, conv_bc, log_decay, skip, gain, ids
):
    tokens, channels = seq_input.shape
    heads = skip.shape[0]
    width = 2 * ids.shape[1]
    paired = rows is not None
    outs = [
        array((tokens, channels), F32),
        array((tokens, 2 * STATE), F32),
        array((2, heads, tokens), F32),
    ]
    if paired:
        ends = [array((STATE + NOTES, channels // 2), F32)]
        ends.append(array((STATE + 16, channels // 2), jnp.int16))
    else:
        ends = [array((STATE + NOTES, channels), F32)]
    xconv, bc, lines, *ends = call(
        functools.partial(front_body, paired),
        outs + ends,
        (seq_input, b_input, c_input, conv_x, conv_bc, log_decay, ids, before),
        near=True,
        after=rows[0][:1] if paired else (),
        scratch=[pltpu.VMEM((8 + tokens, channels + 2 * STATE), F32)],
        flops=5 * 10**9,
        grant=20,
        name="front",
    )
    args = (skip.reshape(1, heads), gain.reshape(1, channels), xconv, bc, lines)
    pre, decay, gain = call(
        inner_body,
        [array((tokens, channels), F32)] * 2 + [array((1, channels), F32)],
        args,
        fixed=2,
        near_args=3,
        near_outs=3,
        scratch=room(args[:1]),
        sems=2,
        flops=4 * 10**9,
        grant=16,
        name="inner",
    )
    late = None
    if paired:
        starts, *late = entering_by_pairs(*ends, width, pre, *rows, meanwhile)
    else:
        starts = (entering_by_rows(ends[0]),)

    def finish(after=()):
        outs = [array((tokens, channels), BF16)]
        args = (gain, pre, decay, bc, *starts)
        return call(
            functools.partial(back_body, paired),
            outs,
            args,
            near_args=len(args),
            after_far=after,
            scratch=room(outs),
            sems=max(1, channels // (4 * HDIM)),
            flops=10**9,
            grant=16,
            name="back",
        )[0]

    return finish, late


TILE = 1024


def join_body(a, b, joined_ref):
    join_rows((a, b), joined_ref)


def swapped(block, axis, bit):
    return lax.ppermute(block, axis, [(i, i ^ bit) for i in range(lax.axis_size(axis))])


def expert_body(part, w_gate, w_up, *refs):
    count = 1 + part
    pieces, beside, refs = refs[:4], refs[4 : 4 + count], refs[4 + count :]
    ids_ref, out_far = refs[0], refs[1 + part]
    pick_ref, hid_ref, out_ref, sems = refs[2 + part :]
    length, hidden = out_ref.shape
    rows = pieces[0].shape[0] // 2
    depth = pieces[0].shape[1]
    me = lax.axis_index("exp")
    here = lax.axis_index("ctx")
    downs = [pl.ds(pl.multiple_of((me ^ k) * depth, depth), depth) for k in range(4)]
    pair = (here // 4) ^ part

    shape = (rows, rows)
    earlier = (iota(shape, 1) < iota(shape, 0)).astype(F32)
    across = iota(shape, 1)
    diagonal = iota(shape, 0) == across
    turns = [(here % 4) ^ (2 * (i % 2) + i // 2) for i in range(length // rows)]
    for i, block in enumerate(turns):
        line = ids_ref[pl.ds(4 * pair + block, 1), :]
        mine = me.astype(F32)
        named = ((line[:, :rows] == mine) | (line[:, rows:] == mine)).astype(F32)
        column = jnp.sum(jnp.where(diagonal, named, 0.0), axis=1, keepdims=True)
        position = jnp.sum(earlier * named, axis=1, keepdims=True).astype(jnp.int32)
        pick_ref[i] = jnp.where(position == across, column, 0.0).astype(BF16)

    out_copies = []
    out_rows = pl.ds(pl.multiple_of(pair * length, length), length)
    for n in range(hidden // TILE):
        cut = slice(n * TILE, (n + 1) * TILE)
        gate = upper = None
        for k in range(4):
            if k % 2 == 0:
                block = jnp.concatenate([piece[...] for piece in pieces[k : k + 2]], axis=0)
            else:
                block = beside[0][k // 2 * length : min((k // 2 + 1) * length, beside[0].shape[0])]
                if block.shape[0] < length:
                    block = jnp.concatenate([block, beside[1][...]], axis=0)
            more = dot16(block, w_gate[0, downs[k], cut])
            gate = more if k == 0 else gate + more
            more = dot16(block, w_up[0, downs[k], cut])
            upper = more if k == 0 else upper + more
        hid_ref[...] = (silu(gate) * upper).astype(BF16)
        for i, block in enumerate(turns):
            picked = dot16(pick_ref[i], hid_ref[i * rows : (i + 1) * rows], FIRST)
            out_ref[pl.ds(pl.multiple_of(block * rows, rows), rows), cut] = picked.astype(BF16)
        out_copies += started([out_ref.at[:, cut]], [out_far.at[0, out_rows, cut]], sems, n)
    finished(out_copies)


def along_z(moe_input, held):
    rows, columns = moe_input.shape
    (joined,) = call(
        join_body,
        [array((2 * rows, columns), BF16)],
        (held, swapped(moe_input, "ctx", 2)),
        near=True,
        name="join",
    )
    return joined, swapped(joined, "ctx", 4)


def spread_rows(z, through):
    x, y = swapped(z, "ctx", 1), swapped(z, "exp", 2)
    d = swapped(y, "ctx", 1) if through else swapped(x, "exp", 2)
    return (z, x, y, d)


def experts_by_tokens(part, pieces, sent, ids, w_gate, w_up, so_far):
    rows = pieces[0].shape[0] // 2
    length = 4 * rows
    hidden = w_gate.shape[2]
    args = (w_gate, w_up, *pieces, *(swapped(a, "exp", 1) for a in sent), ids)
    return call(
        functools.partial(expert_body, part),
        [pltpu.HBM((1, 2 * length, hidden), BF16)],
        args + ((so_far,) if part else ()),
        held=2,
        near_args=0,
        aliases={len(args): 0} if part else None,
        scratch=[
            pltpu.VMEM((length // rows, rows, rows), BF16),
            pltpu.VMEM((length, TILE), BF16),
            pltpu.VMEM((length, hidden), BF16),
        ],
        sems=hidden // TILE,
        flops=4 * length * w_gate.shape[1] * hidden,
        grant=16,
        spaces_of=[pltpu.VMEM] * len(args) + [pltpu.HBM] * part,
        name="experts",
    )[0]


def slot_matrix(pairs, expert, capacity):
    named = jnp.any(pairs == expert, axis=1).astype(jnp.int32)
    position = jnp.cumsum(named) - named
    hit = position[None, :] == jnp.arange(capacity, dtype=jnp.int32)[:, None]
    return (hit & (named[None, :] > 0)).astype(BF16)


def experts_by_slots(moe_input, pairs, w_gate, w_up):
    experts = lax.axis_size("exp")
    capacity = 4 * moe_input.shape[0] // experts
    pick = jax.vmap(lambda e: slot_matrix(pairs, e, capacity))(jnp.arange(experts))
    slots = jnp.einsum("eqt,td->eqd", pick, moe_input, preferred_element_type=F32)
    routed = lax.all_to_all(slots.astype(BF16), "exp", split_axis=0, concat_axis=2, tiled=True)
    rows = lax.all_gather(routed[0], "ctx", axis=0, tiled=True)
    gate = jnp.dot(rows, w_gate[0], preferred_element_type=F32)
    upper = jnp.dot(rows, w_up[0], preferred_element_type=F32)
    return (jax.nn.silu(gate) * upper).astype(BF16)[None]


def on_device(
    seq_input,
    b_input,
    c_input,
    conv_x,
    conv_bc,
    log_decay,
    skip_gain,
    norm_gain,
    moe_input,
    expert_ids,
    w_gate,
    w_up,
):
    ctx = lax.axis_size("ctx")
    by_tokens = lax.axis_size("exp") == 4 and ctx == 8
    tokens, channels = seq_input.shape
    far = (seq_input, b_input, c_input, moe_input, conv_x, conv_bc, log_decay, expert_ids.T)
    ends, *near = call(
        functools.partial(ends_body, len(far)),
        [array((EDGE, channels + 2 * STATE), BF16)] + [array(a.shape, a.dtype) for a in far],
        far,
        fixed=len(far),
        near_outs=len(far),
        sems=3 + len(far),
        name="ends",
    )
    seq_input, b_input, c_input, held, conv_x, conv_bc, log_decay, ids = near
    before = lax.ppermute(ends, "ctx", [(i, i + 1) for i in range(ctx - 1)])
    pieces = meanwhile = None
    if by_tokens:
        near_rows, far_rows = along_z(moe_input, held)
        pieces = spread_rows(near_rows, 0), far_rows

        def meanwhile(ids, joined):
            return experts_by_tokens(0, pieces[0], (joined,), ids, w_gate, w_up, None)

    finish, late = mixing(
        pieces,
        meanwhile,
        seq_input,
        b_input,
        c_input,
        before,
        conv_x,
        conv_bc,
        log_decay,
        skip_gain,
        norm_gain,
        ids,
    )
    if by_tokens:
        far_pieces, ids, joined, hidden = late
        hidden = experts_by_tokens(1, far_pieces, joined, ids, w_gate, w_up, hidden)
        mixed = finish((hidden,))
    else:
        mixed = finish()
        hidden = experts_by_slots(moe_input, expert_ids, w_gate, w_up)
    return (mixed, hidden)


def solution(mesh):
    in_specs = (
        P("ctx", "exp"),
        P("ctx", None),
        P("ctx", None),
        P(None, "exp"),
        P(),
        P("exp", "ctx"),
        P("exp"),
        P("exp"),
        P("ctx", "exp"),
        P("ctx", None),
        P("exp", None, "ctx"),
        P("exp", None, "ctx"),
    )
    out_specs = (P("ctx", "exp"), P("exp", None, "ctx"))
    return jax.shard_map(
        on_device, mesh=mesh, in_specs=in_specs, out_specs=out_specs, check_vma=False
    )
```

```python
import functools
import math

import jax
import jax.numpy as jnp
from jax import lax
from jax.experimental import pallas as pl
from jax.experimental.pallas import tpu as pltpu
from jax.sharding import PartitionSpec as P

HDIM = 64
STATE = 128
KCONV = 4
EDGE = 16
NOTES = 8

F32 = jnp.float32
BF16 = jnp.bfloat16


def dot16(a, b, contract=((1,), (0,))):
    return lax.dot_general(a, b, (contract, ((), ())), preferred_element_type=F32)


def halves(value):
    high = value.astype(BF16)
    return high, (value - high.astype(F32)).astype(BF16)


def dot(a, b, contract=((1,), (0,))):
    a_high, a_low = halves(a)
    b_high, b_low = halves(b)
    cross = dot16(a_high, b_low, contract) + dot16(a_low, b_high, contract)
    return dot16(a_high, b_high, contract) + cross


def dot_exact(a, b, contract=((1,), (0,))):
    high, rest = halves(a)
    low = (a - high.astype(F32) - rest.astype(F32)).astype(BF16)
    return dot16(high, b, contract) + (dot16(rest, b, contract) + dot16(low, b, contract))


def dot_left(a, b, contract=((1,), (0,))):
    high, low = halves(a)
    return dot16(high, b, contract) + dot16(low, b, contract)


FIRST = ((0,), (0,))


def iota(shape, axis):
    return lax.broadcasted_iota(jnp.int32, shape, axis)


def head_spread(heads):
    shape = (heads, heads * HDIM)
    return (iota(shape, 1) // HDIM == iota(shape, 0)).astype(BF16)


def upper_ones(length):
    return (iota((length, length), 0) <= iota((length, length), 1)).astype(BF16)


def silu(value):
    return value / (1.0 + jnp.exp(-value))


def one_minus_exp(value):
    series = jnp.ones_like(value)
    for n in range(8, 1, -1):
        series = 1.0 + value * series * (1.0 / n)
    return jnp.where(value > -0.25, -value * series, 1.0 - jnp.exp(value))


def started(sources, targets, sems, first=0):
    copies = []
    for i, (source, target) in enumerate(zip(sources, targets)):
        copies.append(pltpu.make_async_copy(source, target, sems.at[first + i]))
        copies[-1].start()
    return copies


def finished(copies):
    for copy in copies:
        copy.wait()


def following(body, count, skipped):
    return lambda *refs: body(*refs[:count], *refs[count + skipped :])


def call(
    body,
    outs,
    args,
    fixed=0,
    held=0,
    near_args=0,
    near_outs=0,
    after=(),
    after_far=(),
    aliases=None,
    scratch=(),
    sems=0,
    flops=0,
    grant=8,
    near=False,
    spaces_of=None,
    name=None,
):
    body = following(body, len(args), len(after) + len(after_far))
    moved = sum(math.prod(a.shape) * a.dtype.itemsize for a in (*args, *outs))
    scratch = list(scratch) + ([pltpu.SemaphoreType.DMA((sems,))] if sems else [])
    space = pltpu.VMEM if near else pl.ANY
    spaces = [pltpu.HBM] * fixed + [pltpu.VMEM] * held
    args = [
        pltpu.with_memory_space_constraint(a, spaces[i]) if i < len(spaces) else a
        for i, a in enumerate(args)
    ]
    spaces += [space] * (len(args) - near_args - len(spaces)) + [pltpu.VMEM] * near_args
    spaces = spaces_of or spaces
    args, spaces = [*args, *after], spaces + [pl.ANY] * len(after)
    args += [pltpu.with_memory_space_constraint(a, pltpu.HBM) for a in after_far]
    spaces += [pltpu.HBM] * len(after_far)
    out_spaces = [space] * (len(outs) - near_outs) + [pltpu.VMEM] * near_outs
    return pl.pallas_call(
        body,
        out_shape=outs,
        in_specs=[pl.BlockSpec(memory_space=s) for s in spaces],
        out_specs=[pl.BlockSpec(memory_space=s) for s in out_spaces],
        scratch_shapes=scratch,
        input_output_aliases=aliases or {},
        compiler_params=pltpu.CompilerParams(vmem_limit_bytes=grant * 2**20),
        cost_estimate=pl.CostEstimate(flops=flops, bytes_accessed=moved, transcendentals=0),
        name=name,
    )(*args)


def room(arrays):
    return [pltpu.VMEM(a.shape, a.dtype) for a in arrays]


def array(shape, dtype):
    return jax.ShapeDtypeStruct(shape, dtype)


def ends_body(count, *refs):
    far, ends_ref, near, sems = refs[:count], refs[count], refs[count + 1 : -1], refs[-1]
    tokens, channels = far[0].shape
    cut = pl.ds(tokens - EDGE, EDGE)
    finished(
        started(
            [*(a.at[cut, :] for a in far[:3]), *far],
            [
                ends_ref.at[:, pl.ds(0, channels)],
                ends_ref.at[:, pl.ds(channels, STATE)],
                ends_ref.at[:, pl.ds(channels + STATE, STATE)],
                *near,
            ],
            sems,
        )
    )


def front_body(paired, *refs):
    x_ref, b_ref, c_ref, taps_ref, taps_bc_ref, logs_ref, ids_ref, ends_ref = refs[:8]
    xconv_ref, bc_ref, lines_ref = refs[8:11]
    ends, pad_ref = refs[11:-1], refs[-1]
    tokens, channels = x_ref.shape
    heads = logs_ref.shape[0]
    pad_ref[0:8, :] = ends_ref[...].astype(F32)[EDGE - 8 : EDGE]
    pad_ref[8 : 8 + tokens, :channels] = x_ref[...].astype(F32)
    pad_ref[8 : 8 + tokens, channels : channels + STATE] = b_ref[...].astype(F32)
    pad_ref[8 : 8 + tokens, channels + STATE :] = c_ref[...].astype(F32)

    def conv(taps, start, stop):
        total = jnp.zeros((tokens, stop - start), F32)
        for k in range(KCONV):
            first = 8 - (KCONV - 1) + k
            total = total + taps[k : k + 1] * pad_ref[first : first + tokens, start:stop]
        return silu(total)

    bc = conv(taps_bc_ref[...], channels, channels + 2 * STATE)
    bc_ref[...] = bc
    xconv = conv(taps_ref[...], 0, channels)
    xconv_ref[...] = xconv
    logs = logs_ref[...]
    inflow = jnp.sqrt(one_minus_exp(2.0 * logs))
    row = dot_exact(logs, upper_ones(tokens))
    lines_ref[0] = row
    lines_ref[1] = inflow
    total = row[:, tokens - 1 :]
    spread = head_spread(heads)
    fresh = xconv * dot_left(inflow * jnp.exp(total - row), spread, FIRST)
    state = dot(bc[:, :STATE], fresh, FIRST)
    total = jnp.broadcast_to(total, (heads, NOTES))
    if paired:
        total = dot_exact(total, spread, FIRST)
        half = channels // 2
        side = lax.axis_index("ctx") % 2
        ids = ids_ref[...].astype(F32)
        line = jnp.concatenate([ids[0:1], ids[1:2]], axis=1)
        line = jnp.concatenate([line] * (half // line.shape[1]), axis=1)
        for ref, first in ((ends[0], side == 0), (ends[1], side != 0)):
            mine = jnp.where(first, state[:, :half], state[:, half:])
            logsum = jnp.where(first, total[:1, :half], total[:1, half:])
            if ref is ends[0]:
                put(ref, mine, logsum, line)
            else:
                send(ref, mine, logsum, line)
    else:
        ends[0][:STATE] = state
        ends[0][STATE:] = dot_exact(jnp.exp(total), spread, FIRST)


def inner_body(
    skip_far,
    gain_far,
    xconv_ref,
    bc_ref,
    lines_ref,
    pre_ref,
    decay_ref,
    gain_ref,
    skip_ref,
    sems,
):
    copies = started([skip_far, gain_far], [skip_ref, gain_ref], sems)
    tokens, channels = xconv_ref.shape
    heads = channels // HDIM
    row = lines_ref[0]
    column = row.T
    spread = head_spread(heads)
    decay_ref[...] = dot_left(jnp.exp(row), spread, FIRST)
    inflow = dot_left(lines_ref[1], spread, FIRST)
    meet = dot(bc_ref[:, STATE:], bc_ref[:, :STATE], ((1,), (1,)))
    lower = iota((tokens, tokens), 0) >= iota((tokens, tokens), 1)
    left = iota((tokens, 2 * HDIM), 1) < HDIM
    finished(copies)
    skip = dot_exact(skip_ref[...], spread)
    for pair in range(heads // 2):
        cut = slice(pair * 2 * HDIM, (pair + 1) * 2 * HDIM)
        xconv = xconv_ref[:, cut]
        d_high, d_low = halves(xconv * inflow[:, cut])
        both = []
        for h in (2 * pair, 2 * pair + 1):
            gap = column[:, h : h + 1] - row[h : h + 1, :]
            mix = jnp.where(lower, jnp.exp(gap), 0.0) * meet
            m_high, m_low = halves(mix)
            both.append(dot16(m_high, d_high) + dot16(m_high, d_low) + dot16(m_low, d_high))
        pre_ref[:, cut] = skip[:, cut] * xconv + jnp.where(left, both[0], both[1])


def put(ref, state, logsum, line):
    ref[:STATE] = state
    at = iota((NOTES, state.shape[1]), 0)
    ref[STATE:] = jnp.where(at == 0, logsum, line)


def send(ref, state, logsum, line):
    largest = jnp.max(jnp.abs(state), axis=0, keepdims=True)
    power = jnp.ceil(jnp.log2(jnp.maximum(largest, 1e-30))) - 15.0
    whole = jnp.clip(jnp.round(state * jnp.exp2(-power)), -32767.0, 32767.0)
    ref[:STATE] = whole.astype(jnp.int32).astype(jnp.int16)
    logsum = jnp.round(jnp.maximum(logsum, -128.0) * 2.0**22).astype(jnp.int32)
    at = iota((16, state.shape[1]), 0)
    notes = jnp.where(at == 0, power.astype(jnp.int32), line.astype(jnp.int32))
    notes = jnp.where(at == 1, logsum >> 15, jnp.where(at == 2, logsum & 32767, notes))
    ref[STATE:] = notes.astype(jnp.int16)


def taken(ref):
    return ref[:STATE], ref[STATE : STATE + 1], ref[STATE + 1 : STATE + 2]


def received(ref):
    notes = ref[STATE:].astype(jnp.int32).astype(F32)
    state = ref[:STATE].astype(jnp.int32).astype(F32) * jnp.exp2(notes[0:1])
    return state, notes[1:2] * 2.0**-7 + notes[2:3] * 2.0**-22, notes[3:4]


def ordered(first, own, other):
    return [jnp.where(first, a, b) for a, b in zip(own, other)], [
        jnp.where(first, b, a) for a, b in zip(own, other)
    ]


def together(first, own, other, width):
    (a, a_log, a_line), (b, b_log, b_line) = ordered(first, own, other)
    line = jnp.concatenate([a_line[:, :width], b_line[:, :width]], axis=1)
    line = jnp.concatenate([line] * (a.shape[1] // line.shape[1]), axis=1)
    return jnp.exp(b_log) * a + b, a_log + b_log, line


def place():
    here = lax.axis_index("ctx")
    return here % 2, (here // 2) % 2, here // 4


def pair_body(width, own_ref, got_ref, rows_ref, pair_ref, sent_ref, same_rows_ref):
    same_rows_ref[...] = rows_ref[...]
    x, _, _ = place()
    pair = together(x == 0, taken(own_ref), received(got_ref), width)
    put(pair_ref, *pair)
    send(sent_ref, *pair)


def list_ids(ids_ref, early, late, width):
    at = iota(ids_ref.shape, 0)
    ids = jnp.zeros(ids_ref.shape, F32)
    for i in range(ids_ref.shape[0]):
        line = (early, late)[i // 4]
        ids = jnp.where(at == i, line[:, i % 4 * width : (i % 4 + 1) * width], ids)
    ids_ref[...] = ids


def join_rows(pieces, joined_ref):
    rows = pieces[0].shape[0]
    for i, piece in enumerate(pieces):
        joined_ref[i * rows : (i + 1) * rows] = piece[...]


def four_body(
    width, pair_ref, got_ref, a, b, c, d, e, f, g, sent_ref, ids_ref, joined_ref, later_ref
):
    join_rows((a, b, c, d), joined_ref)
    join_rows((e, f, g), later_ref)
    _, z, _ = place()
    four = together(z == 0, taken(pair_ref), received(got_ref), 2 * width)
    send(sent_ref, *four)
    list_ids(ids_ref, four[2], four[2], width)


def turn_body(
    width,
    own_ref,
    got_ref,
    pair_ref,
    pair_got_ref,
    four_got_ref,
    rows_ref,
    mine_ref,
    sent_ref,
    ids_ref,
    same_rows_ref,
):
    same_rows_ref[...] = rows_ref[...]
    x, z, zz = place()
    pair, pair_got, four_got = taken(pair_ref), received(pair_got_ref), received(four_got_ref)
    line = together(z == 0, pair, pair_got, 2 * width)[2]
    (early,), (late,) = ordered(zz == 0, [line], [four_got[2]])
    list_ids(ids_ref, early, late, width)

    before = jnp.where(zz == 0, 0.0, four_got[0])
    before = jnp.where(z == 0, before, jnp.exp(pair_got[1]) * before + pair_got[0])
    (first, first_log), _ = ordered(x == 0, taken(own_ref)[:2], received(got_ref)[:2])
    after = jnp.exp(first_log) * before + first
    mine_ref[...] = jnp.where(x == 0, before, after)
    other = jnp.where(x == 0, after, before)
    send(sent_ref, other, jnp.zeros_like(first_log), jnp.zeros_like(first_log))


def prefix_body(parts_ref, starts_ref):
    ctx, rows, share = starts_ref.shape
    state = jnp.zeros((rows, share), F32)
    for i in range(ctx):
        starts_ref[i] = state
        if i < ctx - 1:
            state = parts_ref[i, STATE : STATE + 1] * state + parts_ref[i, :STATE]


def back_body(paired, gain_ref, pre_ref, decay_ref, bc_ref, *rest):
    starts, (out_far, out_ref, sems) = rest[: 1 + paired], rest[1 + paired :]
    channels = pre_ref.shape[1]
    width = min(channels, 4 * HDIM)
    group = (iota((width, width), 0) // HDIM == iota((width, width), 1) // HDIM).astype(BF16)
    if paired:
        side = lax.axis_index("ctx") % 2
        mine, other = starts[0][...], received(starts[1])[0]
        start = [jnp.where(side == 0, mine, other), jnp.where(side == 0, other, mine)]
        start = jnp.concatenate(start, axis=1)
    else:
        start = starts[0][...]
    c_high, c_low = halves(bc_ref[:, STATE:])
    copies = []
    for i in range(channels // width):
        cut = slice(i * width, (i + 1) * width)
        s_high, s_low = halves(start[:, cut])
        carried = dot16(c_high, s_high) + dot16(c_high, s_low) + dot16(c_low, s_high)
        pre = pre_ref[:, cut] + carried * decay_ref[:, cut]
        mean = dot_left(pre * pre, group) * (1.0 / HDIM)
        out_ref[:, cut] = (pre * lax.rsqrt(mean + 1e-05) * gain_ref[:, cut]).astype(BF16)
        copies += started([out_ref.at[:, cut]], [out_far.at[:, cut]], sems, i)
    finished(copies)


def entering_by_pairs(keep, sent, width, pre, near_pieces, far_rows, meanwhile):
    pair_array, sent_array = array(keep.shape, F32), array(sent.shape, jnp.int16)
    ids_array = array((8, width), F32)
    joined_array = array((4 * far_rows.shape[0], far_rows.shape[1]), BF16)
    got = swapped(sent, "ctx", 1)
    pair, sent, rows = call(
        functools.partial(pair_body, width),
        [pair_array, sent_array, array(far_rows.shape, BF16)],
        (keep, got, far_rows),
        near=True,
        after=(near_pieces[2], pre),
        name="pair",
    )
    far_pieces = spread_rows(rows, 1)
    pair_got = swapped(sent, "ctx", 2)
    later_array = array((3 * far_rows.shape[0], far_rows.shape[1]), BF16)
    sent, ids, joined, later = call(
        functools.partial(four_body, width),
        [sent_array, ids_array, joined_array, later_array],
        (pair, pair_got, *near_pieces, *far_pieces[:3]),
        near=True,
        name="four",
    )
    four_got = swapped(sent, "ctx", 4)
    done = meanwhile(ids, joined)
    mine, sent, ids, rows = call(
        functools.partial(turn_body, width),
        [array((STATE, keep.shape[1]), F32), sent_array, ids_array, array(rows.shape, BF16)],
        (keep, got, pair, pair_got, four_got, far_pieces[3]),
        near=True,
        after_far=(done,),
        name="turn",
    )
    return (mine, swapped(sent, "ctx", 1)), far_pieces, ids, (later, rows), done


def entering_by_rows(state):
    ctx = lax.axis_size("ctx")
    rows, channels = state.shape
    slabs = state.reshape(rows, ctx, channels // ctx).transpose(1, 0, 2)
    parts = lax.all_to_all(slabs, "ctx", split_axis=0, concat_axis=0, tiled=True)
    (starts,) = call(
        prefix_body,
        [array((ctx, STATE, channels // ctx), F32)],
        (parts,),
        near=True,
        name="prefix",
    )
    start = lax.all_to_all(starts, "ctx", split_axis=0, concat_axis=0, tiled=True)
    return start.transpose(1, 0, 2).reshape(STATE, channels)


def mixing(
    rows, meanwhile, seq_input, b_input, c_input, before, conv_x, conv_bc, log_decay, skip, gain, ids
):
    tokens, channels = seq_input.shape
    heads = skip.shape[0]
    width = 2 * ids.shape[1]
    paired = rows is not None
    outs = [
        array((tokens, channels), F32),
        array((tokens, 2 * STATE), F32),
        array((2, heads, tokens), F32),
    ]
    if paired:
        ends = [array((STATE + NOTES, channels // 2), F32)]
        ends.append(array((STATE + 16, channels // 2), jnp.int16))
    else:
        ends = [array((STATE + NOTES, channels), F32)]
    xconv, bc, lines, *ends = call(
        functools.partial(front_body, paired),
        outs + ends,
        (seq_input, b_input, c_input, conv_x, conv_bc, log_decay, ids, before),
        near=True,
        after=rows[0][:1] if paired else (),
        scratch=[pltpu.VMEM((8 + tokens, channels + 2 * STATE), F32)],
        flops=5 * 10**9,
        grant=20,
        name="front",
    )
    args = (skip.reshape(1, heads), gain.reshape(1, channels), xconv, bc, lines)
    pre, decay, gain = call(
        inner_body,
        [array((tokens, channels), F32)] * 2 + [array((1, channels), F32)],
        args,
        fixed=2,
        near_args=3,
        near_outs=3,
        scratch=room(args[:1]),
        sems=2,
        flops=4 * 10**9,
        grant=16,
        name="inner",
    )
    late = None
    if paired:
        starts, *late = entering_by_pairs(*ends, width, pre, *rows, meanwhile)
    else:
        starts = (entering_by_rows(ends[0]),)

    def finish(after=()):
        outs = [array((tokens, channels), BF16)]
        args = (gain, pre, decay, bc, *starts)
        return call(
            functools.partial(back_body, paired),
            outs,
            args,
            near_args=len(args),
            after_far=after,
            scratch=room(outs),
            sems=max(1, channels // (4 * HDIM)),
            flops=10**9,
            grant=16,
            name="back",
        )[0]

    return finish, late


TILE = 1024


def join_body(a, b, joined_ref):
    join_rows((a, b), joined_ref)


def swapped(block, axis, bit):
    return lax.ppermute(block, axis, [(i, i ^ bit) for i in range(lax.axis_size(axis))])


def expert_body(part, w_gate, w_up, *refs):
    count = 1 + part
    pieces, beside, refs = refs[:4], refs[4 : 4 + count], refs[4 + count :]
    ids_ref, out_far = refs[0], refs[1 + part]
    pick_ref, hid_ref, out_ref, sems = refs[2 + part :]
    length, hidden = out_ref.shape
    rows = pieces[0].shape[0] // 2
    depth = pieces[0].shape[1]
    me = lax.axis_index("exp")
    here = lax.axis_index("ctx")
    downs = [pl.ds(pl.multiple_of((me ^ k) * depth, depth), depth) for k in range(4)]
    pair = (here // 4) ^ part

    shape = (rows, rows)
    earlier = (iota(shape, 1) < iota(shape, 0)).astype(F32)
    across = iota(shape, 1)
    diagonal = iota(shape, 0) == across
    turns = [(here % 4) ^ (2 * (i % 2) + i // 2) for i in range(length // rows)]
    for i, block in enumerate(turns):
        line = ids_ref[pl.ds(4 * pair + block, 1), :]
        mine = me.astype(F32)
        named = ((line[:, :rows] == mine) | (line[:, rows:] == mine)).astype(F32)
        column = jnp.sum(jnp.where(diagonal, named, 0.0), axis=1, keepdims=True)
        position = jnp.sum(earlier * named, axis=1, keepdims=True).astype(jnp.int32)
        pick_ref[i] = jnp.where(position == across, column, 0.0).astype(BF16)

    out_copies = []
    out_rows = pl.ds(pl.multiple_of(pair * length, length), length)
    for n in range(hidden // TILE):
        cut = slice(n * TILE, (n + 1) * TILE)
        gate = upper = None
        for k in range(4):
            if k % 2 == 0:
                block = jnp.concatenate([piece[...] for piece in pieces[k : k + 2]], axis=0)
            else:
                block = beside[0][k // 2 * length : min((k // 2 + 1) * length, beside[0].shape[0])]
                if block.shape[0] < length:
                    block = jnp.concatenate([block, beside[1][...]], axis=0)
            more = dot16(block, w_gate[0, downs[k], cut])
            gate = more if k == 0 else gate + more
            more = dot16(block, w_up[0, downs[k], cut])
            upper = more if k == 0 else upper + more
        hid_ref[...] = (silu(gate) * upper).astype(BF16)
        for i, block in enumerate(turns):
            picked = dot16(pick_ref[i], hid_ref[i * rows : (i + 1) * rows], FIRST)
            out_ref[pl.ds(pl.multiple_of(block * rows, rows), rows), cut] = picked.astype(BF16)
        out_copies += started([out_ref.at[:, cut]], [out_far.at[0, out_rows, cut]], sems, n)
    finished(out_copies)


def along_z(moe_input, held):
    rows, columns = moe_input.shape
    (joined,) = call(
        join_body,
        [array((2 * rows, columns), BF16)],
        (held, swapped(moe_input, "ctx", 2)),
        near=True,
        name="join",
    )
    return joined, swapped(joined, "ctx", 4)


def spread_rows(z, through):
    x, y = swapped(z, "ctx", 1), swapped(z, "exp", 2)
    d = swapped(y, "ctx", 1) if through else swapped(x, "exp", 2)
    return (z, x, y, d)


def experts_by_tokens(part, pieces, sent, ids, w_gate, w_up, so_far):
    rows = pieces[0].shape[0] // 2
    length = 4 * rows
    hidden = w_gate.shape[2]
    args = (w_gate, w_up, *pieces, *(swapped(a, "exp", 1) for a in sent), ids)
    return call(
        functools.partial(expert_body, part),
        [pltpu.HBM((1, 2 * length, hidden), BF16)],
        args + ((so_far,) if part else ()),
        held=2,
        near_args=0,
        aliases={len(args): 0} if part else None,
        scratch=[
            pltpu.VMEM((length // rows, rows, rows), BF16),
            pltpu.VMEM((length, TILE), BF16),
            pltpu.VMEM((length, hidden), BF16),
        ],
        sems=hidden // TILE,
        flops=4 * length * w_gate.shape[1] * hidden,
        grant=16,
        spaces_of=[pltpu.VMEM] * len(args) + [pltpu.HBM] * part,
        name="experts",
    )[0]


def slot_matrix(pairs, expert, capacity):
    named = jnp.any(pairs == expert, axis=1).astype(jnp.int32)
    position = jnp.cumsum(named) - named
    hit = position[None, :] == jnp.arange(capacity, dtype=jnp.int32)[:, None]
    return (hit & (named[None, :] > 0)).astype(BF16)


def experts_by_slots(moe_input, pairs, w_gate, w_up):
    experts = lax.axis_size("exp")
    capacity = 4 * moe_input.shape[0] // experts
    pick = jax.vmap(lambda e: slot_matrix(pairs, e, capacity))(jnp.arange(experts))
    slots = jnp.einsum("eqt,td->eqd", pick, moe_input, preferred_element_type=F32)
    routed = lax.all_to_all(slots.astype(BF16), "exp", split_axis=0, concat_axis=2, tiled=True)
    rows = lax.all_gather(routed[0], "ctx", axis=0, tiled=True)
    gate = jnp.dot(rows, w_gate[0], preferred_element_type=F32)
    upper = jnp.dot(rows, w_up[0], preferred_element_type=F32)
    return (jax.nn.silu(gate) * upper).astype(BF16)[None]


def on_device(
    seq_input,
    b_input,
    c_input,
    conv_x,
    conv_bc,
    log_decay,
    skip_gain,
    norm_gain,
    moe_input,
    expert_ids,
    w_gate,
    w_up,
):
    ctx = lax.axis_size("ctx")
    by_tokens = lax.axis_size("exp") == 4 and ctx == 8
    tokens, channels = seq_input.shape
    far = (seq_input, b_input, c_input, moe_input, conv_x, conv_bc, log_decay, expert_ids.T)
    ends, *near = call(
        functools.partial(ends_body, len(far)),
        [array((EDGE, channels + 2 * STATE), BF16)] + [array(a.shape, a.dtype) for a in far],
        far,
        fixed=len(far),
        near_outs=len(far),
        sems=3 + len(far),
        name="ends",
    )
    seq_input, b_input, c_input, held, conv_x, conv_bc, log_decay, ids = near
    before = lax.ppermute(ends, "ctx", [(i, i + 1) for i in range(ctx - 1)])
    pieces = meanwhile = None
    if by_tokens:
        near_rows, far_rows = along_z(moe_input, held)
        pieces = spread_rows(near_rows, 0), far_rows

        def meanwhile(ids, joined):
            return experts_by_tokens(0, pieces[0], (joined,), ids, w_gate, w_up, None)

    finish, late = mixing(
        pieces,
        meanwhile,
        seq_input,
        b_input,
        c_input,
        before,
        conv_x,
        conv_bc,
        log_decay,
        skip_gain,
        norm_gain,
        ids,
    )
    if by_tokens:
        far_pieces, ids, joined, hidden = late
        hidden = experts_by_tokens(1, far_pieces, joined, ids, w_gate, w_up, hidden)
        mixed = finish((hidden,))
    else:
        mixed = finish()
        hidden = experts_by_slots(moe_input, expert_ids, w_gate, w_up)
    return (mixed, hidden)


def solution(mesh):
    in_specs = (
        P("ctx", "exp"),
        P("ctx", None),
        P("ctx", None),
        P(None, "exp"),
        P(),
        P("exp", "ctx"),
        P("exp"),
        P("exp"),
        P("ctx", "exp"),
        P("ctx", None),
        P("exp", None, "ctx"),
        P("exp", None, "ctx"),
    )
    out_specs = (P("ctx", "exp"), P("exp", None, "ctx"))
    return jax.shard_map(
        on_device, mesh=mesh, in_specs=in_specs, out_specs=out_specs, check_vma=False
    )
```
